32 devices in a mesh: group: 8 (over z, y), head: 4 (over x, core).
Axes of the slice: x: 2, y: 2, z: 4, core: 2. Of those that a mesh axis runs over, the one named last changes fastest.
Arguments:
- tokens: bfloat16 [4, 1024, 1536], P(None, 'group'), may hold values from -6 to 6
- parents: int32 [3, 1024], P(None, 'group'), may hold values from 0 to 7
- page_request: int32 [384], P('group'), may hold values from 0 to 127, as said below
- page_fill: int32 [384], P('group'), may hold values from 1 to 128, as said below
- keys_pool: bfloat16 [384, 1536, 128], P('group', 'head'), may hold values from -600 to 600
- values_pool: bfloat16 [384, 1536, 128], P('group', 'head'), may hold values from -6 to 6
- decay_pool: bfloat16 [384, 24, 128], P('group', 'head'), may hold values from -494.52 to 0
- gain_attn: float32 [1536], replicated, may hold values from 0.1 to 1.9
- w_query: bfloat16 [1536, 1536], P('head'), may hold values from -0.15625 to 0.15625
- w_key: bfloat16 [1536, 1536], P('head'), may hold values from -0.15625 to 0.15625
- w_value: bfloat16 [1536, 1536], P('head'), may hold values from -0.15625 to 0.15625
- w_forget: bfloat16 [1536, 24], P(None, 'head'), may hold values from -0.15625 to 0.15625
- forget_bias: float32 [24], P('head'), may hold values from -2 to 6
- w_out: bfloat16 [1536, 1536], P('head'), may hold values from -0.15625 to 0.15625
- gain_ffn: float32 [1536], replicated, may hold values from 0.1 to 1.9
- w_gate: bfloat16 [1536, 4096], P(None, 'head'), may hold values from -0.15625 to 0.15625
- w_up: bfloat16 [1536, 4096], P(None, 'head'), may hold values from -0.15625 to 0.15625
- w_down: bfloat16 [4096, 1536], P('head'), may hold values from -0.09375 to 0.09375
Outputs:
- outputs: bfloat16 [4, 1024, 1536], P(None, 'group')
The draws below stay inside these ranges and needn't reach their ends.
Inputs may be any that keep to these rules, and one draw needn't show every extreme that they name: `page_request`: request ids g * 16 to g * 16 + 15 are the requests owned by group g, and pages g * 48 to g * 48 + 47 are the page slots of group g. The first 32 slots of a group hold pages of its own requests; its other 16 slots hold pages of other groups' requests, at most 3 from the requests of one group. Every request has at least one page. `page_fill`: the valid positions of a page are its first ones.
All inputs are finite; a program needn't handle non-finite values.
Results may differ from the reference program's by a relative error of at most 0.0095.
Values may be sent and summed in bfloat16 or wider, within the bound.
No kernel may reach another device: no remote copies, remote signals or barrier semaphores. Data moves between devices by JAX's collectives and lax.ppermute only.
A program may use at most 192 MiB of HBM per device.

```python
import math
import jax
import jax.numpy as jnp
from jax import lax

D = 1536
HEAD_TOTAL = 24
DH = 64
FF = 4096
BEAMS = 8
STEPS = 4
PAGE_POSITIONS = 128
REQ_DEV = 16
OWNED_SLOTS = 32
SPILL = 16
ROWS = 1024
PAGES_DEV = 48
PAGES = 384
N_GROUP = 8


def layout(key):
    layout_key = jax.random.fold_in(key, 7001)
    groups = N_GROUP
    rank_group = jax.random.permutation(jax.random.fold_in(layout_key, 1), groups).astype(jnp.int32)
    rank_of = jnp.zeros((groups,), jnp.int32).at[rank_group].set(jnp.arange(groups, dtype=jnp.int32))
    long_index = jax.random.randint(jax.random.fold_in(layout_key, 2), (groups,), 0, REQ_DEV)
    long_own = jax.random.randint(jax.random.fold_in(layout_key, 3), (groups,), OWNED_SLOTS // 2, OWNED_SLOTS - REQ_DEV + 2)
    last_fills = jax.random.randint(jax.random.fold_in(layout_key, 4), (groups, REQ_DEV), 1, PAGE_POSITIONS + 1)
    last_fills = last_fills.at[rank_group[0], 0].set(1)
    page_ids = jnp.arange(groups * PAGES_DEV, dtype=jnp.int32)
    holder = page_ids // PAGES_DEV
    slot_ids = page_ids % PAGES_DEV
    first_own = long_own[holder]
    others = OWNED_SLOTS - first_own
    other_index = jnp.maximum(slot_ids - first_own, 0) * (REQ_DEV - 1) // others
    other_local = other_index + (other_index >= long_index[holder]).astype(jnp.int32)
    end_other = first_own + ((other_index + 1) * others + REQ_DEV - 2) // (REQ_DEV - 1)
    is_long = slot_ids < first_own
    own_local = jnp.where(is_long, long_index[holder], other_local)
    own_remain = jnp.where(is_long, first_own + SPILL - 1 - slot_ids, end_other - 1 - slot_ids)
    spill_slot = jnp.maximum(slot_ids - OWNED_SLOTS, 0)
    owner_rank = jnp.mod(rank_of[holder] - 1 - spill_slot % (groups - 1), groups)
    owner_group = rank_group[owner_rank]
    is_own = slot_ids < OWNED_SLOTS
    group_of = jnp.where(is_own, holder, owner_group)
    local_index = jnp.where(is_own, own_local, long_index[owner_group])
    remain = jnp.where(is_own, own_remain, SPILL - 1 - spill_slot)
    last_fill = last_fills[group_of, local_index]
    page_fills = jnp.where(remain == 0, last_fill, PAGE_POSITIONS)
    current_request = group_of * REQ_DEV + local_index
    return (current_request.astype(jnp.int32), page_fills.astype(jnp.int32), remain.astype(jnp.int32), last_fill.astype(jnp.int32))


def draw_page_request(key, part):
    current_request, page_fills, remain, last_fill = layout(key)
    return current_request


def draw_page_fill(key, part):
    current_request, page_fills, remain, last_fill = layout(key)
    return page_fills


def draw_decay_pool(key, part):
    current_request, page_fills, remain, last_fill = layout(key)
    request_total_count = N_GROUP * REQ_DEV
    log_rate = jax.random.uniform(jax.random.fold_in(key, 8101), (request_total_count, HEAD_TOTAL), minval=math.log(0.0003), maxval=math.log(0.08))
    decay_rate = jnp.exp(log_rate)[current_request]
    spike_threshold = jax.random.randint(jax.random.fold_in(key, 8104), (request_total_count, 3), 0, OWNED_SLOTS * PAGE_POSITIONS)[current_request]
    spike_discard = jax.random.uniform(jax.random.fold_in(key, 8105), (request_total_count, HEAD_TOTAL, 3), minval=0.22, maxval=0.69)[current_request]
    offset = jnp.arange(PAGE_POSITIONS, dtype=jnp.int32)
    position_gap = jnp.maximum(remain[:, None] * PAGE_POSITIONS + last_fill[:, None] - 1 - offset[None, :], 0)
    logarithm_decay = -decay_rate[:, :, None] * position_gap[:, None, :].astype(jnp.float32)
    for spike_position_index in range(3):
        spike_struck = (position_gap > spike_threshold[:, spike_position_index:spike_position_index + 1]).astype(jnp.float32)
        logarithm_decay = logarithm_decay - spike_discard[:, :, spike_position_index:spike_position_index + 1] * spike_struck[:, None, :]
    return logarithm_decay.astype(jnp.bfloat16)


def draw_keys_pool(key, part):
    page_total = N_GROUP * PAGES_DEV
    shape = (page_total, HEAD_TOTAL * DH, PAGE_POSITIONS)
    drawn_keys = jnp.clip(jax.random.normal(jax.random.fold_in(key, 8204), shape), -6.0, 6.0)
    return drawn_keys.astype(jnp.bfloat16)


def place_ends(drawn, key, low, largest):
    dims = drawn.shape
    place = [jax.random.randint(jax.random.fold_in(key, axis), (), 0, dims[axis]) for axis in range(len(dims))]
    drawn = drawn.at[tuple(place)].set(low)
    longest = dims.index(max(dims))
    place[longest] = (place[longest] + 1) % dims[longest]
    return drawn.at[tuple(place)].set(largest)


def block_levels(rng, dims, cuts, low, largest):
    level = 1.0
    for dim, blocks in cuts:
        draws = jax.random.uniform(jax.random.fold_in(jax.random.fold_in(rng, 6), dim), (blocks,), jnp.float32, low / len(cuts), largest / len(cuts))
        level = level * jnp.repeat(jnp.exp(draws), dims[dim] // blocks).reshape((-1,) + (1,) * (len(dims) - 1 - dim))
    return level


def centred(own_key, extent, width, most, pieces=(), kind=jnp.bfloat16):
    values = width * jax.random.normal(own_key, extent, jnp.float32)
    if pieces:
        values = values * block_levels(own_key, extent, pieces, -0.22, 0.18)
    return jnp.clip(values, -most, most).astype(kind)


def setup_inputs(seed: int = 0) -> dict:
    arg_keys = jax.random.split(jax.random.key(seed), 19)
    tokens = centred(arg_keys[0], (STEPS, ROWS, D), 1.0, 6.0, ((1, 8),))
    parents = place_ends(jax.random.randint(arg_keys[1], (STEPS - 1, ROWS), 0, BEAMS), jax.random.fold_in(arg_keys[1], 1), 0, BEAMS - 1).astype(jnp.int32)
    page_request = draw_page_request(jax.random.fold_in(arg_keys[18], 71), 0)
    page_fill = draw_page_fill(jax.random.fold_in(arg_keys[18], 71), 0)
    keys_pool = draw_keys_pool(jax.random.fold_in(arg_keys[18], 71), 0)
    values_pool = centred(arg_keys[5], (PAGES, HEAD_TOTAL * DH, PAGE_POSITIONS), 1.0, 6.0, ((0, 8), (1, 4)))
    decay_pool = draw_decay_pool(jax.random.fold_in(arg_keys[18], 71), 0)
    gain_attn = jnp.clip(1.0 + 0.18 * jax.random.normal(arg_keys[7], (D,), jnp.float32), 0.1, 1.9)
    w_query = centred(arg_keys[8], (HEAD_TOTAL * DH, D), D ** -0.5, 0.15625, ((0, 4),))
    w_key = centred(arg_keys[9], (HEAD_TOTAL * DH, D), D ** -0.5, 0.15625, ((0, 4),))
    w_value = centred(arg_keys[10], (HEAD_TOTAL * DH, D), D ** -0.5, 0.15625, ((0, 4),))
    w_forget = centred(arg_keys[11], (D, HEAD_TOTAL), D ** -0.5, 0.15625, ((1, 4),))
    forget_bias = jnp.clip(-2.0 + 8.0 * jax.random.uniform(arg_keys[12], (HEAD_TOTAL,), jnp.float32) ** block_levels(arg_keys[12], (HEAD_TOTAL,), ((0, 4),), -0.2, 0.2), -2.0, 6.0)
    w_out = centred(arg_keys[13], (HEAD_TOTAL * DH, D), (HEAD_TOTAL * DH) ** -0.5, 0.15625, ((0, 4),))
    gain_ffn = jnp.clip(1.0 + 0.18 * jax.random.normal(arg_keys[14], (D,), jnp.float32), 0.1, 1.9)
    w_gate = centred(arg_keys[15], (D, FF), D ** -0.5, 0.15625, ((1, 4),))
    w_up = centred(arg_keys[16], (D, FF), D ** -0.5, 0.15625, ((1, 4),))
    w_down = centred(arg_keys[17], (FF, D), FF ** -0.5, 0.09375, ((0, 4),))
    return {"tokens": tokens, "parents": parents, "page_request": page_request, "page_fill": page_fill, "keys_pool": keys_pool, "values_pool": values_pool, "decay_pool": decay_pool, "gain_attn": gain_attn, "w_query": w_query, "w_key": w_key, "w_value": w_value, "w_forget": w_forget, "forget_bias": forget_bias, "w_out": w_out, "gain_ffn": gain_ffn, "w_gate": w_gate, "w_up": w_up, "w_down": w_down}


epsilon = 1e-05
masked_score = -1e+30

def rms_scale(values, gain_vector):
    widened = values.astype(jnp.float32)
    return widened * lax.rsqrt(lax.optimization_barrier(jnp.mean(widened * widened, axis=-1, keepdims=True)) + epsilon) * gain_vector.astype(jnp.float32)

def page_block(asked_all, page_keys, page_values, page_decay, current_request, fill_count):
    page_count = page_keys.shape[0]
    asked_rows = asked_all[current_request].astype(jnp.float32)
    keys_split = page_keys.reshape(page_count, HEAD_TOTAL, DH, PAGE_POSITIONS).astype(jnp.float32)
    values_split = page_values.reshape(page_count, HEAD_TOTAL, DH, PAGE_POSITIONS).astype(jnp.float32)
    scores = jnp.einsum('psbhd,phdt->psbht', asked_rows, keys_split) * DH ** (-0.5)
    scores = scores + page_decay.astype(jnp.float32)[:, None, None, :, :]
    valid_mask = jnp.arange(PAGE_POSITIONS)[None, :] < fill_count[:, None]
    scores = jnp.where(valid_mask[:, None, None, None, :], scores, masked_score)
    page_top = lax.optimization_barrier(jnp.max(scores, axis=-1))
    weights = jnp.exp(scores - page_top[..., None])
    page_total = lax.optimization_barrier(jnp.sum(weights, axis=-1))
    rounded = lax.optimization_barrier(weights.astype(jnp.bfloat16)).astype(jnp.float32)
    numerator = jnp.einsum('psbht,phdt->psbhd', rounded, values_split)
    return (page_top, page_total, numerator)

def reference(tokens, parents, page_request, page_fill, keys_pool, values_pool, decay_pool, gain_attn, w_query, w_key, w_value, w_forget, forget_bias, w_out, gain_ffn, w_gate, w_up, w_down):
    requests = N_GROUP * REQ_DEV
    row_count = requests * BEAMS
    inner_width = HEAD_TOTAL * DH
    flat_tokens = tokens.reshape(STEPS * row_count, D)
    normed = rms_scale(flat_tokens, gain_attn).astype(jnp.bfloat16)

    def project(weight):
        return jnp.dot(normed, weight.T, preferred_element_type=jnp.float32).astype(jnp.bfloat16).reshape(STEPS, row_count, -1)
    queries = project(w_query)
    key_new = project(w_key)
    value_new = project(w_value)
    forget = jax.nn.log_sigmoid(jnp.dot(normed, w_forget, preferred_element_type=jnp.float32) + forget_bias.astype(jnp.float32)).reshape(STEPS, row_count, HEAD_TOTAL)
    asked_all = queries.reshape(STEPS, requests, BEAMS, HEAD_TOTAL, DH).transpose(1, 0, 2, 3, 4)
    blocks = (keys_pool.reshape(N_GROUP, PAGES_DEV, inner_width, PAGE_POSITIONS), values_pool.reshape(N_GROUP, PAGES_DEV, inner_width, PAGE_POSITIONS), decay_pool.reshape(N_GROUP, PAGES_DEV, HEAD_TOTAL, PAGE_POSITIONS), page_request.reshape(N_GROUP, PAGES_DEV).astype(jnp.int32), page_fill.reshape(N_GROUP, PAGES_DEV).astype(jnp.int32))

    def absorb(carry, block):
        carry_top, carry_total, carry_numer = carry
        block_keys, block_values, block_decay, block_request, block_fill = block
        page_top, page_total, numerator = page_block(asked_all, block_keys, block_values, block_decay, block_request, block_fill)
        new_top = carry_top.at[block_request].max(page_top)
        keep = jnp.exp(carry_top - new_top)
        factor = jnp.exp(page_top - new_top[block_request])
        new_total = carry_total * keep + jnp.zeros_like(carry_total).at[block_request].add(page_total * factor)
        new_numer = carry_numer * keep[..., None] + jnp.zeros_like(carry_numer).at[block_request].add(numerator * factor[..., None])
        return ((new_top, new_total, new_numer), None)
    start = (jnp.full((requests, STEPS, BEAMS, HEAD_TOTAL), masked_score, jnp.float32), jnp.zeros((requests, STEPS, BEAMS, HEAD_TOTAL), jnp.float32), jnp.zeros((requests, STEPS, BEAMS, HEAD_TOTAL, DH), jnp.float32))
    (prefix_top, prefix_total, prefix_numer), _ = lax.scan(absorb, start, blocks)
    base_rows = jnp.arange(row_count) // BEAMS * BEAMS
    hist_keys = jnp.zeros((0, row_count, inner_width), jnp.bfloat16)
    hist_values = jnp.zeros((0, row_count, inner_width), jnp.bfloat16)
    hist_totals = jnp.zeros((0, row_count, HEAD_TOTAL), jnp.float32)
    running = jnp.zeros((row_count, HEAD_TOTAL), jnp.float32)
    results = []
    for step_index in range(STEPS):
        if step_index > 0:
            source = base_rows + parents[step_index - 1]
            hist_keys = hist_keys[:, source]
            hist_values = hist_values[:, source]
            hist_totals = hist_totals[:, source]
            running = running[source]
        running = running + forget[step_index]
        hist_keys = jnp.concatenate([hist_keys, key_new[step_index][None]], axis=0)
        hist_values = jnp.concatenate([hist_values, value_new[step_index][None]], axis=0)
        hist_totals = jnp.concatenate([hist_totals, running[None]], axis=0)
        asked_now = queries[step_index].reshape(row_count, HEAD_TOTAL, DH).astype(jnp.float32)
        keys_now = hist_keys.reshape(step_index + 1, row_count, HEAD_TOTAL, DH).astype(jnp.float32)
        values_now = hist_values.reshape(step_index + 1, row_count, HEAD_TOTAL, DH).astype(jnp.float32)
        scores = jnp.einsum('rhd,urhd->rhu', asked_now, keys_now) * DH ** (-0.5) - hist_totals.transpose(1, 2, 0)
        history_top = lax.optimization_barrier(jnp.max(scores, axis=-1))
        weights = jnp.exp(scores - history_top[..., None])
        history_total = lax.optimization_barrier(jnp.sum(weights, axis=-1))
        rounded = lax.optimization_barrier(weights.astype(jnp.bfloat16)).astype(jnp.float32)
        history_numer = jnp.einsum('rhu,urhd->rhd', rounded, values_now)
        page_top = prefix_top[:, step_index].reshape(row_count, HEAD_TOTAL)
        page_total = prefix_total[:, step_index].reshape(row_count, HEAD_TOTAL)
        page_numer = prefix_numer[:, step_index].reshape(row_count, HEAD_TOTAL, DH)
        best_top = jnp.maximum(page_top, history_top)
        page_scale = jnp.exp(page_top - best_top)
        history_scale = jnp.exp(history_top - best_top)
        total_sum = page_total * page_scale + history_total * history_scale
        numer_sum = page_numer * page_scale[..., None] + history_numer * history_scale[..., None]
        attended = (numer_sum / total_sum[..., None]).astype(jnp.bfloat16).reshape(row_count, inner_width)
        residual = tokens[step_index].astype(jnp.float32) + jnp.dot(attended, w_out, preferred_element_type=jnp.float32)
        normed_ffn = rms_scale(residual, gain_ffn).astype(jnp.bfloat16)
        gate_proj = jnp.dot(normed_ffn, w_gate, preferred_element_type=jnp.float32)
        up_proj = jnp.dot(normed_ffn, w_up, preferred_element_type=jnp.float32)
        hidden = (jax.nn.silu(gate_proj) * up_proj).astype(jnp.bfloat16)
        results.append((residual + jnp.dot(hidden, w_down, preferred_element_type=jnp.float32)).astype(jnp.bfloat16))
    return jnp.stack(results, axis=0)
```

```python
import functools

import jax
import jax.numpy as jnp
from jax import lax
from jax.experimental import pallas as pl
from jax.experimental.pallas import tpu as pltpu
from jax.sharding import PartitionSpec as P

BEAMS = 8
OWNED_SLOTS = 32
SPILL = 16
PAGE_BLOCK = 4
TAIL_ROWS = 16
MIB = 1 << 20

epsilon = 1e-05
masked_score = -1e30
f32 = jnp.float32
bf16 = jnp.bfloat16

NN = (((1,), (0,)), ((), ()))
NT = (((1,), (1,)), ((), ()))
SMEM = pl.BlockSpec(memory_space=pltpu.SMEM)


def dot(a, b, dims=NN):
    return lax.dot_general(a, b, dims, preferred_element_type=f32)


def lanes(shape):
    return lax.broadcasted_iota(jnp.int32, shape, len(shape) - 1)


def sublanes(shape):
    return lax.broadcasted_iota(jnp.int32, shape, len(shape) - 2)


def route_kernel(local_count, capacity, request_ref, table_ref, slot_ref, count_ref):
    for owner in range(count_ref.shape[0]):
        count_ref[owner] = 0
    for slot in range(table_ref.shape[0]):
        table_ref[slot] = -1
    for page in range(SPILL):
        request = request_ref[OWNED_SLOTS + page]
        owner = request // local_count
        rank = count_ref[owner]
        slot = owner * capacity + rank
        table_ref[slot] = request - owner * local_count
        slot_ref[page] = slot
        count_ref[owner] = rank + 1


def route(page_request, groups, local_count, capacity):
    return pl.pallas_call(
        functools.partial(route_kernel, local_count, capacity),
        in_specs=[SMEM],
        out_specs=[SMEM, SMEM],
        out_shape=[
            jax.ShapeDtypeStruct((groups * capacity,), jnp.int32),
            jax.ShapeDtypeStruct((SPILL,), jnp.int32),
        ],
        scratch_shapes=[pltpu.SMEM((groups,), jnp.int32)],
        name="route",
    )(page_request)


def project_kernel(
    tokens_ref, gain_ref, wq_ref, wk_ref, wv_ref, wf_ref, bias_ref,
    q_ref, k_ref, v_ref, forget_ref, normed_ref,
):
    steps, rows, _ = tokens_ref.shape
    span = steps * BEAMS
    gain = gain_ref[...]

    def pair(index, carry):
        slabs = []
        for step in range(steps):
            x = tokens_ref[step, pl.ds(pl.multiple_of(index * 16, 16), 16), :].astype(f32)
            scale = lax.rsqrt(jnp.mean(x * x, axis=-1, keepdims=True) + epsilon)
            slabs.append(x * scale * gain)
        for half in range(2):
            part = jnp.concatenate([s[half * 8 : half * 8 + 8] for s in slabs], axis=0)
            start = pl.multiple_of((index * 2 + half) * span, span)
            normed_ref[pl.ds(start, span), :] = part.astype(bf16)
        return carry

    lax.fori_loop(0, rows // 16, pair, 0)
    normed = normed_ref[...]
    query = dot(normed, wq_ref[...], NT).astype(bf16)
    q_ref[...] = (query.astype(f32) * 0.125).astype(bf16)
    k_ref[...] = dot(normed, wk_ref[...], NT).astype(bf16)
    v_ref[...] = dot(normed, wv_ref[...], NT).astype(bf16)
    gate = dot(normed, wf_ref[...]) + bias_ref[...]
    forget = jnp.minimum(gate, 0.0) - jnp.log1p(jnp.exp(-jnp.abs(gate)))
    forget_ref[...] = jnp.zeros_like(forget_ref)
    forget_ref[:, : forget.shape[1]] = forget


def project(tokens, gain, w_query, w_key, w_value, w_forget, forget_bias):
    steps, rows, width = tokens.shape
    inner = w_query.shape[0]
    total = steps * rows
    flat = jax.ShapeDtypeStruct((total, inner), bf16)
    flops = 2 * total * width * inner * 3
    return pl.pallas_call(
        project_kernel,
        out_shape=[flat, flat, flat, jax.ShapeDtypeStruct((total, 128), f32)],
        scratch_shapes=[pltpu.VMEM((total, width), bf16)],
        compiler_params=pltpu.CompilerParams(vmem_limit_bytes=32 * MIB),
        cost_estimate=pl.CostEstimate(
            flops=flops, bytes_accessed=8 * MIB, transcendentals=total
        ),
        name="project",
    )(
        tokens, gain.reshape(1, -1), w_query, w_key, w_value, w_forget,
        forget_bias.reshape(1, -1),
    )


def half_masks(rows):
    low = lanes((rows, 128)) < 64
    return low.astype(f32).astype(bf16), jnp.logical_not(low).astype(f32).astype(bf16)


def stacked(pair_rows, masks):
    return jnp.concatenate([pair_rows * masks[0], pair_rows * masks[1]], axis=0)


def side_by_side(values, rows):
    low = lanes((rows, 128)) < 64
    top = jnp.broadcast_to(values[:rows], (rows, 128))
    bottom = jnp.broadcast_to(values[rows:], (rows, 128))
    return jnp.where(low, top, bottom)


def page_pair(query_pair, keys_pair, values_pair, decay_low, decay_high, masks):
    rows = query_pair.shape[0]
    raw = dot(stacked(query_pair, masks), keys_pair)
    scores = jnp.concatenate([raw[:rows] + decay_low, raw[rows:] + decay_high], axis=0)
    top = jnp.max(scores, axis=-1, keepdims=True)
    weights = jnp.exp(scores - top)
    total = jnp.sum(weights, axis=-1, keepdims=True)
    numer = dot(weights.astype(bf16), values_pair, NT)
    return top, total, side_by_side(numer, rows)


def absorb(state, rows, columns, top, total, numer):
    top_ref, total_ref, numer_ref = state
    old = top_ref[rows, columns]
    new = jnp.maximum(old, top)
    keep = jnp.exp(old - new)
    add = jnp.exp(top - new)
    top_ref[rows, columns] = new
    total_ref[rows, columns] = total_ref[rows, columns] * keep + total * add
    numer_ref[rows, columns] = numer_ref[rows, columns] * keep + numer * add


def history(parents_ref, q_ref, k_ref, v_ref, forget_ref, state):
    transitions, rows = parents_ref.shape
    span = (transitions + 1) * BEAMS
    pack = 128 // span
    square = (128, 128)
    down, across = sublanes(square), lanes(square)
    diagonal = down == across
    columns = []
    for step in range(transitions):
        row = parents_ref[step : step + 1, :].astype(f32)
        columns.append(
            jnp.sum(jnp.where(diagonal, jnp.broadcast_to(row, square), 0.0), axis=1, keepdims=True)
        )
    lane8 = lanes((8, 128)).astype(f32)
    masks = half_masks(128)
    top_ref, total_ref, numer_ref = state
    for group in range(rows // BEAMS // pack):
        slabs = []
        for member in range(pack):
            first = (group * pack + member) * BEAMS
            slabs.append(jnp.zeros((8, 128), f32))
            for step in range(transitions):
                wanted = columns[step][first : first + 8] + float(member * span + step * 8)
                slabs.append(jnp.where(lane8 == wanted, 1.0, 0.0))
        parent = jnp.concatenate(slabs, axis=0)
        same = diagonal.astype(f32)
        parent16 = parent.astype(bf16)
        one = same + parent
        two = dot(parent16, parent16)
        ancestors = one + dot(two.astype(bf16), one.astype(bf16))
        here = pl.ds(group * 128, 128)
        running = lax.dot_general(
            ancestors, forget_ref[here, :], NN,
            precision=lax.Precision.HIGHEST, preferred_element_type=f32,
        ).T
        hidden = jnp.where(ancestors > 0.5, 0.0, masked_score)
        for pair in range(q_ref.shape[1] // 128):
            cols = pl.ds(pair * 128, 128)
            raw = dot(stacked(q_ref[here, cols], masks), k_ref[here, cols], NT)
            low = raw[:128] + (hidden - running[2 * pair : 2 * pair + 1])
            high = raw[128:] + (hidden - running[2 * pair + 1 : 2 * pair + 2])
            scores = jnp.concatenate([low, high], axis=0)
            top = jnp.max(scores, axis=-1, keepdims=True)
            weights = jnp.exp(scores - top)
            total = jnp.sum(weights, axis=-1, keepdims=True)
            numer = dot(weights.astype(bf16), v_ref[here, cols])
            top_ref[here, cols] = side_by_side(top, 128)
            total_ref[here, cols] = side_by_side(total, 128)
            numer_ref[here, cols] = side_by_side(numer, 128)


def masked_decay(decay, fill):
    valid = lanes(decay.shape) < fill
    return jnp.where(valid, decay.astype(f32), masked_score)


def own_kernel(
    request_ref, fill_ref, parents_ref, q_ref, k_ref, v_ref, forget_ref,
    keys_ref, values_ref, decay_ref, top_ref, total_ref, numer_ref,
):
    state = (top_ref, total_ref, numer_ref)
    block = pl.program_id(0)
    local_count = parents_ref.shape[1] // BEAMS
    span = (parents_ref.shape[0] + 1) * BEAMS

    @pl.when(block == 0)
    def _():
        history(parents_ref, q_ref, k_ref, v_ref, forget_ref, state)

    masks = half_masks(span)
    pairs = q_ref.shape[1] // 128
    found = []
    for page in range(PAGE_BLOCK):
        index = block * PAGE_BLOCK + page
        local = lax.rem(request_ref[index], local_count)
        rows = pl.ds(pl.multiple_of(local * span, span), span)
        decay = masked_decay(decay_ref[page], fill_ref[index])
        for pair in range(pairs):
            cols = pl.ds(pair * 128, 128)
            top, total, numer = page_pair(
                q_ref[rows, cols],
                keys_ref[page, cols, :],
                values_ref[page, cols, :],
                decay[2 * pair : 2 * pair + 1],
                decay[2 * pair + 1 : 2 * pair + 2],
                masks,
            )
            found.append(
                (rows, cols, side_by_side(top, span), side_by_side(total, span), numer)
            )
    for rows, cols, top, total, numer in found:
        absorb(state, rows, cols, top, total, numer)


def whole(array):
    return pl.BlockSpec(array.shape, lambda *_: (0,) * array.ndim)


def page_specs(keys, decay, first):
    shift = first // PAGE_BLOCK
    pool = pl.BlockSpec((PAGE_BLOCK,) + keys.shape[1:], lambda i: (i + shift, 0, 0))
    return [pool, pool, pl.BlockSpec((PAGE_BLOCK,) + decay.shape[1:], lambda i: (i + shift, 0, 0))]


def page_cost(pages, keys, rows):
    inner, length = keys.shape[1:]
    return pl.CostEstimate(
        flops=pages * rows * inner * length * 8,
        bytes_accessed=pages * inner * length * 4,
        transcendentals=pages * rows * inner * length // 64,
    )


def own_pages(request, fill, parents, q, k, v, forget, keys, values, decay):
    state = jax.ShapeDtypeStruct(q.shape, f32)
    out_spec = pl.BlockSpec(q.shape, lambda *_: (0, 0))
    return pl.pallas_call(
        own_kernel,
        grid=(OWNED_SLOTS // PAGE_BLOCK,),
        in_specs=[SMEM, SMEM, whole(parents), whole(q), whole(k), whole(v), whole(forget)]
        + page_specs(keys, decay, 0),
        out_specs=[out_spec] * 3,
        out_shape=[state] * 3,
        compiler_params=pltpu.CompilerParams(vmem_limit_bytes=32 * MIB),
        cost_estimate=page_cost(OWNED_SLOTS, keys, 64),
        name="own_pages",
    )(request, fill, parents, q, k, v, forget, keys, values, decay)


def ask_kernel(asked_ref, q_ref, out_ref):
    slots, span, _ = out_ref.shape
    for slot in range(slots):
        local = jnp.maximum(asked_ref[slot], 0)
        out_ref[slot] = q_ref[pl.ds(pl.multiple_of(local * span, span), span), :]


def ask(asked, q, span):
    slots = asked.shape[0]
    return pl.pallas_call(
        ask_kernel,
        in_specs=[SMEM, pl.BlockSpec(memory_space=pltpu.VMEM)],
        out_shape=jax.ShapeDtypeStruct((slots, span, q.shape[1]), bf16),
        name="ask",
    )(asked, q)


def hosted_kernel(
    capacity, fill_ref, slot_ref, q_ref, keys_ref, values_ref, decay_ref, out_ref, tail_ref
):
    block = pl.program_id(0)
    span = q_ref.shape[1]
    inner = q_ref.shape[2]
    pairs = inner // 128
    heads = inner // 64

    @pl.when(block == 0)
    def _():
        out_ref[...] = jnp.zeros_like(out_ref)
        tail_ref[...] = jnp.zeros_like(tail_ref)

    masks = half_masks(span)
    lane = lanes((span, 128))
    found = []
    for page in range(PAGE_BLOCK):
        index = block * PAGE_BLOCK + page
        slot = slot_ref[index]
        decay = masked_decay(decay_ref[page], fill_ref[OWNED_SLOTS + index])
        logs, averages = [], []
        for pair in range(pairs):
            cols = pl.ds(pair * 128, 128)
            top, total, numer = page_pair(
                q_ref[slot, :, cols],
                keys_ref[page, cols, :],
                values_ref[page, cols, :],
                decay[2 * pair : 2 * pair + 1],
                decay[2 * pair + 1 : 2 * pair + 2],
                masks,
            )
            averages.append((numer / side_by_side(total, span)).astype(bf16))
            log_total = top + jnp.log(total)
            logs.extend([log_total[:span], log_total[span:]])
        found.append((slot, logs, averages))
    for slot, logs, averages in found:
        owner = slot // capacity
        rank = slot - owner * capacity
        for pair in range(pairs):
            out_ref[owner, pl.ds(pl.multiple_of(rank * span, span), span), pl.ds(pair * 128, 128)] = averages[pair]
        tail = tail_ref[owner]
        base = rank * (3 * heads)
        for head, value in enumerate(logs):
            rest = jnp.broadcast_to(value, (span, 128))
            for piece in range(3):
                part = rest.astype(bf16).astype(f32)
                rest = rest - part
                tail = jnp.where(lane == base + piece * heads + head, part, tail)
        tail_ref[owner] = tail

    @pl.when(block == pl.num_programs(0) - 1)
    def _():
        first = capacity * span
        for owner in range(out_ref.shape[0]):
            tail = tail_ref[owner].astype(bf16)
            for part in range(span // TAIL_ROWS):
                out_ref[owner, first : first + TAIL_ROWS, part * 128 : part * 128 + 128] = tail[
                    part * TAIL_ROWS : part * TAIL_ROWS + TAIL_ROWS
                ]


def hosted_pages(fill, slots, asked_rows, keys, values, decay, groups, capacity):
    count, span, inner = asked_rows.shape
    out_shape = (groups, capacity * span + TAIL_ROWS, inner)
    return pl.pallas_call(
        functools.partial(hosted_kernel, capacity),
        grid=(SPILL // PAGE_BLOCK,),
        in_specs=[SMEM, SMEM, whole(asked_rows)] + page_specs(keys, decay, OWNED_SLOTS),
        out_specs=pl.BlockSpec(out_shape, lambda *_: (0, 0, 0)),
        out_shape=jax.ShapeDtypeStruct(out_shape, bf16),
        scratch_shapes=[pltpu.VMEM((groups, span, 128), f32)],
        compiler_params=pltpu.CompilerParams(vmem_limit_bytes=32 * MIB),
        cost_estimate=page_cost(SPILL, keys, 64),
        name="hosted_pages",
    )(fill, slots, asked_rows, keys, values, decay)


def merge_kernel(capacity, steps, asked_ref, back_ref, top_in, total_in, numer_in, out_ref,
                 top_ref, total_ref, numer_ref):
    groups, _, inner = back_ref.shape
    span = steps * BEAMS
    heads = inner // 64
    state = (top_ref, total_ref, numer_ref)
    top_ref[...] = top_in[...]
    total_ref[...] = total_in[...]
    numer_ref[...] = numer_in[...]
    source, target = sublanes((128, inner)), lanes((128, inner)) // 64
    spread = []
    for rank in range(capacity):
        hit = source < 0
        for piece in range(3):
            hit = hit | (source == target + (rank * 3 + piece) * heads)
        spread.append(hit.astype(f32).astype(bf16))

    for owner in range(groups):
        first = capacity * span
        for rank in range(capacity):
            local = asked_ref[owner * capacity + rank]

            @pl.when(local >= 0)
            def _():
                tail = jnp.concatenate(
                    [
                        back_ref[owner, first : first + TAIL_ROWS, part * 128 : part * 128 + 128]
                        for part in range(span // TAIL_ROWS)
                    ],
                    axis=0,
                )
                top = dot(tail, spread[rank])
                average = back_ref[owner, rank * span : rank * span + span, :].astype(f32)
                rows = pl.ds(pl.multiple_of(local * span, span), span)
                absorb(state, rows, slice(None), top, 1.0, average)

    for index in range(out_ref.shape[1] // 16):
        parts = []
        for half in range(2):
            rows = slice((index * 2 + half) * span, (index * 2 + half + 1) * span)
            parts.append(numer_ref[rows, :] / total_ref[rows, :])
        for step in range(steps):
            both = jnp.concatenate([p[step * 8 : step * 8 + 8] for p in parts], axis=0)
            out_ref[step, index * 16 : index * 16 + 16, :] = both.astype(bf16)


def merge(asked, back, top, total, numer, steps, capacity):
    rows, inner = top.shape
    vmem = pl.BlockSpec(memory_space=pltpu.VMEM)
    return pl.pallas_call(
        functools.partial(merge_kernel, capacity, steps),
        in_specs=[SMEM, vmem, vmem, vmem, vmem],
        out_shape=jax.ShapeDtypeStruct((steps, rows // steps, inner), bf16),
        scratch_shapes=[pltpu.VMEM((rows, inner), f32)] * 3,
        compiler_params=pltpu.CompilerParams(vmem_limit_bytes=32 * MIB),
        name="merge",
    )(asked, back, top, total, numer)


def rms_scale(values, gain_vector):
    return (
        values
        * lax.rsqrt(jnp.mean(values * values, axis=-1, keepdims=True) + epsilon)
        * gain_vector
    )


def swap_core(value):
    return lax.ppermute(value, "head", [(i, i ^ 1) for i in range(4)])


def swap_chip(value):
    return lax.ppermute(value, "head", [(i, i ^ 2) for i in range(4)])


def shards(
    tokens, parents, page_request, page_fill, keys_pool, values_pool, decay_pool,
    gain_attn, w_query, w_key, w_value, w_forget, forget_bias, w_out,
    gain_ffn, w_gate, w_up, w_down,
):
    steps, rows, width = tokens.shape
    inner = w_query.shape[0]
    local_count = rows // BEAMS
    span = steps * BEAMS
    groups = lax.axis_size("group")
    capacity = (SPILL + groups - 2) // (groups - 1)
    core = lax.axis_index("head") % 2

    table, slots = route(page_request, groups, local_count, capacity)
    asked = lax.all_to_all(
        table.reshape(groups, 1, capacity), "group", split_axis=0, concat_axis=0, tiled=True
    ).reshape(groups * capacity)
    w_out_far = swap_chip(w_out)
    q, k, v, forget = project(tokens, gain_attn, w_query, w_key, w_value, w_forget, forget_bias)
    asked_rows = lax.all_to_all(
        ask(asked, q, span).reshape(groups, capacity * span, inner),
        "group", split_axis=0, concat_axis=0, tiled=True,
    ).reshape(groups * capacity, span, inner)
    top, total, numer = own_pages(
        page_request, page_fill, parents, q, k, v, forget, keys_pool, values_pool, decay_pool
    )
    back = lax.all_to_all(
        hosted_pages(
            page_fill, slots, asked_rows, keys_pool, values_pool, decay_pool, groups, capacity
        ),
        "group", split_axis=0, concat_axis=0, tiled=True,
    )
    w_out_near, w_out_cross = swap_core(w_out), swap_core(w_out_far)
    attended = merge(asked, back, top, total, numer, steps, capacity).reshape(steps * rows, inner)
    far = swap_chip(attended)
    near, cross = swap_core(attended), swap_core(far)

    mixed = (dot(attended, w_out) + dot(near, w_out_near)) + (
        dot(far, w_out_far) + dot(cross, w_out_cross)
    )
    residual = tokens.reshape(steps * rows, width).astype(f32) + mixed
    normed = rms_scale(residual, gain_ffn).astype(bf16)
    hidden = (jax.nn.silu(dot(normed, w_gate)) * dot(normed, w_up)).astype(bf16)
    partial = dot(hidden, w_down)
    half = steps * rows // 2
    mine = lax.dynamic_slice_in_dim(partial, core * half, half, 0)
    other = lax.dynamic_slice_in_dim(partial, (1 - core) * half, half, 0).astype(bf16)
    chip = (mine + swap_core(other).astype(f32)).astype(bf16)
    both = chip.astype(f32) + swap_chip(chip).astype(f32)
    done = (lax.dynamic_slice_in_dim(residual, core * half, half, 0) + both).astype(bf16)
    theirs = swap_core(done)
    first = jnp.where(core == 0, done, theirs)
    second = jnp.where(core == 0, theirs, done)
    return jnp.concatenate([first, second], axis=0).reshape(steps, rows, width)


def solution(mesh):
    return jax.shard_map(
        shards,
        mesh=mesh,
        in_specs=(
            P(None, "group", None),
            P(None, "group"),
            P("group"),
            P("group"),
            P("group", "head", None),
            P("group", "head", None),
            P("group", "head", None),
            P(),
            P("head", None),
            P("head", None),
            P("head", None),
            P(None, "head"),
            P("head"),
            P("head", None),
            P(),
            P(None, "head"),
            P(None, "head"),
            P("head", None),
        ),
        out_specs=P(None, "group", None),
        check_vma=False,
    )
```

```python
import functools

import jax
import jax.numpy as jnp
from jax import lax
from jax.experimental import pallas as pl
from jax.experimental.pallas import tpu as pltpu
from jax.sharding import PartitionSpec as P

BEAMS = 8
OWNED_SLOTS = 32
SPILL = 16
PAGE_BLOCK = 16
TAIL_ROWS = 16
MIB = 1 << 20

epsilon = 1e-05
masked_score = -1e30
f32 = jnp.float32
bf16 = jnp.bfloat16

NN = (((1,), (0,)), ((), ()))
NT = (((1,), (1,)), ((), ()))
SMEM = pl.BlockSpec(memory_space=pltpu.SMEM)


def dot(a, b, dims=NN):
    return lax.dot_general(a, b, dims, preferred_element_type=f32)


def lanes(shape):
    return lax.broadcasted_iota(jnp.int32, shape, len(shape) - 1)


def sublanes(shape):
    return lax.broadcasted_iota(jnp.int32, shape, len(shape) - 2)


def in_hbm(array):
    return pltpu.with_memory_space_constraint(array, pltpu.HBM)


def in_vmem(array):
    return pltpu.with_memory_space_constraint(array, pltpu.VMEM)


def start_all(pairs, sems):
    copies = [pltpu.make_async_copy(s, t, sems.at[i]) for i, (s, t) in enumerate(pairs)]
    for copy in copies:
        copy.start()
    return copies


def fill_table(local_count, capacity, first, ids_ref, table_ref):
    groups, _, spill = ids_ref.shape
    for slot in range(groups * capacity):
        table_ref[slot] = -1

    def group(index, carry):
        rank = jnp.int32(0)
        for page in range(spill):
            local = ids_ref[index, 0, page] - first
            mine = (local >= 0) & (local < local_count)

            @pl.when(mine)
            def _():
                table_ref[index * capacity + rank] = local

            rank = rank + mine.astype(jnp.int32)
        return carry

    lax.fori_loop(0, groups, group, 0)


def query_kernel(
    capacity, request_ref, ids_ref, tokens_hbm, gain_ref, wq_hbm,
    asked_ref, table_ref, q_hbm, normed_hbm,
    tokens_ref, wq_ref, normed_ref, q_ref, sems, out_sems,
):
    steps, rows, _ = tokens_ref.shape
    span = steps * BEAMS
    local_count = rows // BEAMS
    copies = start_all([(tokens_hbm, tokens_ref), (wq_hbm, wq_ref)], sems)
    first = request_ref[0] // local_count * local_count
    fill_table(local_count, capacity, first, ids_ref, table_ref)
    copies[0].wait()
    gain = gain_ref[...]

    def pair(index, carry):
        slabs = []
        for step in range(steps):
            x = tokens_ref[step, pl.ds(pl.multiple_of(index * 16, 16), 16), :].astype(f32)
            scale = lax.rsqrt(jnp.mean(x * x, axis=-1, keepdims=True) + epsilon)
            slabs.append(x * scale * gain)
        for half in range(2):
            part = jnp.concatenate([s[half * 8 : half * 8 + 8] for s in slabs], axis=0)
            start = pl.multiple_of((index * 2 + half) * span, span)
            normed_ref[pl.ds(start, span), :] = part.astype(bf16)
        return carry

    lax.fori_loop(0, rows // 16, pair, 0, unroll=2)
    leaving = start_all([(normed_ref, normed_hbm)], out_sems)
    copies[1].wait()
    query = dot(normed_ref[...], wq_ref[...], NT).astype(bf16)
    q_ref[...] = (query.astype(f32) * 0.125).astype(bf16)
    last = pltpu.make_async_copy(q_ref, q_hbm, out_sems.at[1])
    last.start()
    for slot in range(asked_ref.shape[0]):
        local = jnp.maximum(table_ref[slot], 0)
        asked_ref[slot] = q_ref[pl.ds(pl.multiple_of(local * span, span), span), :]
    leaving[0].wait()
    last.wait()


def queries_of(request, ids, tokens, gain, w_query, capacity):
    steps, rows, width = tokens.shape
    inner = w_query.shape[0]
    total = steps * rows
    slots = ids.shape[0] * capacity
    hbm = pl.BlockSpec(memory_space=pltpu.HBM)
    vmem = pl.BlockSpec(memory_space=pltpu.VMEM)
    return pl.pallas_call(
        functools.partial(query_kernel, capacity),
        in_specs=[SMEM, SMEM, hbm, vmem, hbm],
        out_specs=[vmem, SMEM, hbm, hbm],
        out_shape=[
            jax.ShapeDtypeStruct((slots, steps * BEAMS, inner), bf16),
            jax.ShapeDtypeStruct((slots,), jnp.int32),
            pltpu.HBM((total, inner), bf16),
            pltpu.HBM((total, width), bf16),
        ],
        scratch_shapes=[
            pltpu.VMEM(tokens.shape, bf16),
            pltpu.VMEM(w_query.shape, bf16),
            pltpu.VMEM((total, width), bf16),
            pltpu.VMEM((total, inner), bf16),
            pltpu.SemaphoreType.DMA((2,)),
            pltpu.SemaphoreType.DMA((2,)),
        ],
        compiler_params=pltpu.CompilerParams(vmem_limit_bytes=16 * MIB),
        cost_estimate=pl.CostEstimate(
            flops=2 * total * width * inner, bytes_accessed=6 * MIB, transcendentals=total
        ),
        name="queries",
    )(request, ids, in_hbm(tokens), gain.reshape(1, -1), in_hbm(w_query))


def half_masks(rows):
    low = lanes((rows, 128)) < 64
    return low.astype(f32).astype(bf16), jnp.logical_not(low).astype(f32).astype(bf16)


def stacked(pair_rows, masks):
    return jnp.concatenate([pair_rows * masks[0], pair_rows * masks[1]], axis=0)


def side_by_side(values, rows):
    low = lanes((rows, 128)) < 64
    top = jnp.broadcast_to(values[:rows], (rows, 128))
    bottom = jnp.broadcast_to(values[rows:], (rows, 128))
    return jnp.where(low, top, bottom)


def absorb(state, rows, columns, top, total, numer):
    top_ref, total_ref, numer_ref = state
    old = top_ref[rows, columns]
    new = jnp.maximum(old, top)
    keep = jnp.exp(old - new)
    add = jnp.exp(top - new)
    top_ref[rows, columns] = new
    total_ref[rows, columns] = total_ref[rows, columns] * keep + total * add
    numer_ref[rows, columns] = numer_ref[rows, columns] * keep + numer * add


def history(parents_ref, q_ref, k_ref, v_ref, forget_ref, state):
    top_ref, total_ref, numer_ref = state
    transitions, rows = parents_ref.shape
    span = (transitions + 1) * BEAMS
    pack = 128 // span
    square = (128, 128)
    down, across = sublanes(square), lanes(square)
    diagonal = down == across
    columns = []
    for step in range(transitions):
        row = parents_ref[step : step + 1, :].astype(f32)
        columns.append(
            jnp.sum(jnp.where(diagonal, jnp.broadcast_to(row, square), 0.0), axis=1, keepdims=True)
        )
    lane8 = lanes((8, 128)).astype(f32)
    masks = half_masks(128)
    for group in range(rows // BEAMS // pack):
        slabs = []
        for member in range(pack):
            first = (group * pack + member) * BEAMS
            slabs.append(jnp.zeros((8, 128), f32))
            for step in range(transitions):
                wanted = columns[step][first : first + 8] + float(member * span + step * 8)
                slabs.append(jnp.where(lane8 == wanted, 1.0, 0.0))
        parent = jnp.concatenate(slabs, axis=0)
        same = diagonal.astype(f32)
        parent16 = parent.astype(bf16)
        one = same + parent
        two = dot(parent16, parent16)
        ancestors = one + dot(two.astype(bf16), one.astype(bf16))
        here = pl.ds(group * 128, 128)
        running = lax.dot_general(
            ancestors, forget_ref[here, :], NN,
            precision=lax.Precision.HIGHEST, preferred_element_type=f32,
        ).T
        hidden = jnp.where(ancestors > 0.5, 0.0, masked_score)
        for pair in range(q_ref.shape[1] // 128):
            cols = pl.ds(pair * 128, 128)
            raw = dot(stacked(q_ref[here, cols], masks), k_ref[here, cols], NT)
            low = raw[:128] + (hidden - running[2 * pair : 2 * pair + 1])
            high = raw[128:] + (hidden - running[2 * pair + 1 : 2 * pair + 2])
            scores = jnp.concatenate([low, high], axis=0)
            top = jnp.max(scores, axis=-1, keepdims=True)
            weights = jnp.exp(scores - top)
            total = jnp.sum(weights, axis=-1, keepdims=True)
            numer = dot(weights.astype(bf16), v_ref[here, cols])
            top_ref[here, cols] = side_by_side(top, 128)
            total_ref[here, cols] = side_by_side(total, 128)
            numer_ref[here, cols] = side_by_side(numer, 128)


def fresh_kernel(
    parents_ref, bias_ref, normed_hbm, wk_hbm, wv_hbm, wf_hbm, q_hbm, top_hbm, total_hbm, numer_hbm,
    log_hbm, average_hbm,
    normed_ref, wk_ref, wv_ref, wf_ref, q_ref, top_own, total_own, numer_own,
    k_ref, v_ref, forget_ref, top_ref, total_ref, numer_ref, sems, out_sems,
):
    copies = start_all(
        [
            (normed_hbm, normed_ref), (wk_hbm, wk_ref), (wv_hbm, wv_ref), (wf_hbm, wf_ref),
            (q_hbm, q_ref), (top_hbm, top_own), (total_hbm, total_own), (numer_hbm, numer_own),
        ],
        sems,
    )
    copies[0].wait()
    copies[1].wait()
    k_ref[...] = dot(normed_ref[...], wk_ref[...], NT).astype(bf16)
    copies[2].wait()
    v_ref[...] = dot(normed_ref[...], wv_ref[...], NT).astype(bf16)
    copies[3].wait()
    gate = dot(normed_ref[...], wf_ref[...], NT) + bias_ref[...]
    forget = jnp.minimum(gate, 0.0) - jnp.log1p(jnp.exp(-jnp.abs(gate)))
    forget_ref[...] = jnp.zeros_like(forget_ref)
    forget_ref[:, : forget.shape[1]] = forget
    copies[4].wait()
    state = (top_ref, total_ref, numer_ref)
    history(parents_ref, q_ref, k_ref, v_ref, forget_ref, state)
    for copy in copies[5:]:
        copy.wait()

    def join(index, carry):
        rows = pl.ds(pl.multiple_of(index * 32, 32), 32)
        absorb(state, rows, slice(None), top_own[rows, :], total_own[rows, :], numer_own[rows, :])
        total = total_ref[rows, :]
        top_ref[rows, :] = top_ref[rows, :] + jnp.log(total)
        numer_ref[rows, :] = numer_ref[rows, :] / total
        return carry

    lax.fori_loop(0, top_ref.shape[0] // 32, join, 0, unroll=2)
    for copy in start_all([(top_ref, log_hbm), (numer_ref, average_hbm)], out_sems):
        copy.wait()


def fresh(parents, bias, normed, w_key, w_value, w_forget, q, own):
    rows, inner = q.shape
    vmem = pl.BlockSpec(memory_space=pltpu.VMEM)
    hbm = pl.BlockSpec(memory_space=pltpu.HBM)
    big = [normed, w_key, w_value, w_forget.T, q, *own]
    wide = pltpu.VMEM((rows, inner), f32)
    return pl.pallas_call(
        fresh_kernel,
        in_specs=[vmem, vmem] + [hbm] * len(big),
        out_specs=[hbm] * 2,
        out_shape=[pltpu.HBM((rows, inner), f32)] * 2,
        scratch_shapes=[pltpu.VMEM(x.shape, x.dtype) for x in big]
        + [pltpu.VMEM((rows, inner), bf16)] * 2
        + [pltpu.VMEM((rows, 128), f32), wide, wide, wide]
        + [pltpu.SemaphoreType.DMA((len(big),)), pltpu.SemaphoreType.DMA((2,))],
        compiler_params=pltpu.CompilerParams(vmem_limit_bytes=24 * MIB),
        cost_estimate=pl.CostEstimate(
            flops=4 * rows * normed.shape[1] * inner, bytes_accessed=12 * MIB,
            transcendentals=8 * rows * inner,
        ),
        name="fresh",
    )(parents, bias.reshape(1, -1), *[in_hbm(x) for x in big])


def page_weights(queries, fills, keys_ref, decay_ref, scores_ref, weights_ref, tops_ref):
    span = queries[0][0].shape[0]
    masks = half_masks(span)
    lane = lanes((1, 128))
    decay = [decay_ref[head].astype(f32) for head in range(decay_ref.shape[0])]
    for page, pairs in enumerate(queries):
        valid = lane < fills[page]
        for pair, query in enumerate(pairs):
            raw = dot(stacked(query, masks), keys_ref[page, pl.ds(pair * 128, 128), :])
            for half in range(2):
                head = pair * 2 + half
                bias = jnp.where(valid, decay[head][page : page + 1], masked_score)
                scores_ref[page, pl.ds(head * span, span), :] = (
                    raw[half * span : half * span + span] + bias
                )
    for page in range(len(queries)):
        for head in range(decay_ref.shape[0]):
            rows = pl.ds(head * span, span)
            scores = scores_ref[page, rows, :]
            top = jnp.broadcast_to(jnp.max(scores, axis=-1, keepdims=True), scores.shape)
            tops_ref[page, rows, :] = top
            weights = jnp.exp(scores - top)
            weights_ref[page, rows, :] = weights.astype(bf16)
            scores_ref[page, rows, :] = jnp.broadcast_to(
                jnp.sum(weights, axis=-1, keepdims=True), scores.shape
            )


def page_sums(page, pair, span, values_ref, scores_ref, weights_ref, tops_ref):
    low = lanes((span, 128)) < 64
    first, second = pl.ds(pair * 2 * span, span), pl.ds((pair * 2 + 1) * span, span)
    numer = dot(
        weights_ref[page, pl.ds(pair * 2 * span, 2 * span), :],
        values_ref[page, pl.ds(pair * 128, 128), :],
        NT,
    )
    top = jnp.where(low, tops_ref[page, first, :], tops_ref[page, second, :])
    total = jnp.where(low, scores_ref[page, first, :], scores_ref[page, second, :])
    return top, total, jnp.where(low, numer[:span], numer[span:])


def page_scratch(pages, span, heads):
    rows = span * heads
    return [
        pltpu.VMEM((pages, rows, 128), f32),
        pltpu.VMEM((pages, rows, 128), bf16),
        pltpu.VMEM((pages, rows, 128), f32),
    ]


def own_kernel(
    request_ref, fill_ref, q_ref, keys_ref, values_ref, decay_ref,
    top_ref, total_ref, numer_ref, *scratch,
):
    state = (top_ref, total_ref, numer_ref)
    block = pl.program_id(0)
    span = scratch[0].shape[1] // decay_ref.shape[0]
    local_count = q_ref.shape[0] // span
    pairs = q_ref.shape[1] // 128

    @pl.when(block == 0)
    def _():
        top_ref[...] = jnp.full_like(top_ref, masked_score)
        total_ref[...] = jnp.zeros_like(total_ref)
        numer_ref[...] = jnp.zeros_like(numer_ref)

    places, queries, fills = [], [], []
    for page in range(PAGE_BLOCK):
        index = block * PAGE_BLOCK + page
        local = lax.rem(request_ref[index], local_count)
        rows = pl.ds(pl.multiple_of(local * span, span), span)
        places.append(rows)
        queries.append([q_ref[rows, pl.ds(pair * 128, 128)] for pair in range(pairs)])
        fills.append(fill_ref[index])
    page_weights(queries, fills, keys_ref, decay_ref, *scratch)
    for page, rows in enumerate(places):
        for pair in range(pairs):
            sums = page_sums(page, pair, span, values_ref, *scratch)
            absorb(state, rows, pl.ds(pair * 128, 128), *sums)


def whole(array):
    return pl.BlockSpec(array.shape, lambda *_: (0,) * array.ndim)


def page_specs(keys, decay, first):
    shift = first // PAGE_BLOCK
    pool = pl.BlockSpec((PAGE_BLOCK,) + keys.shape[1:], lambda i: (i + shift, 0, 0))
    return [
        pool,
        pool,
        pl.BlockSpec((decay.shape[0], PAGE_BLOCK, decay.shape[2]), lambda i: (0, i + shift, 0)),
    ]


def page_cost(pages, keys, rows):
    inner, length = keys.shape[1:]
    return pl.CostEstimate(
        flops=pages * rows * inner * length * 8,
        bytes_accessed=pages * inner * length * 4,
        transcendentals=pages * rows * inner * length // 64,
    )


def own_pages(request, fill, q, keys, values, decay, span):
    out_spec = pl.BlockSpec(q.shape, lambda *_: (0, 0))
    return pl.pallas_call(
        own_kernel,
        grid=(OWNED_SLOTS // PAGE_BLOCK,),
        in_specs=[SMEM, SMEM, whole(q)] + page_specs(keys, decay, 0),
        out_specs=[out_spec] * 3,
        out_shape=[pltpu.HBM(q.shape, f32)] * 3,
        scratch_shapes=page_scratch(PAGE_BLOCK, span, decay.shape[0]),
        compiler_params=pltpu.CompilerParams(vmem_limit_bytes=24 * MIB),
        cost_estimate=page_cost(OWNED_SLOTS, keys, 64),
        name="own_pages",
    )(request, fill, in_hbm(q), in_hbm(keys), in_hbm(values), decay)


def hosted_kernel(
    local_count, capacity, request_ref, fill_ref, q_ref, keys_ref, values_ref, decay_ref,
    out_ref, tail_ref, count_ref, *scratch,
):
    span, inner = q_ref.shape[1:]
    pairs = inner // 128
    heads = decay_ref.shape[0]
    groups = out_ref.shape[0]
    out_ref[...] = jnp.zeros_like(out_ref)
    tail_ref[...] = jnp.zeros_like(tail_ref)
    for owner in range(groups):
        count_ref[owner] = 0
    places, queries, fills = [], [], []
    for page in range(SPILL):
        owner = request_ref[OWNED_SLOTS + page] // local_count
        rank = count_ref[owner]
        count_ref[owner] = rank + 1
        places.append((owner, rank))
        slot = owner * capacity + rank
        queries.append([q_ref[slot, :, pl.ds(pair * 128, 128)] for pair in range(pairs)])
        fills.append(fill_ref[OWNED_SLOTS + page])
    page_weights(queries, fills, keys_ref, decay_ref, *scratch)
    scores_ref, _, tops_ref = scratch
    lane = lanes((span, 128))
    for page, (owner, rank) in enumerate(places):
        here = pl.ds(pl.multiple_of(rank * span, span), span)
        for pair in range(pairs):
            _, total, numer = page_sums(page, pair, span, values_ref, *scratch)
            out_ref[owner, here, pl.ds(pair * 128, 128)] = (numer / total).astype(bf16)
        tail = tail_ref[owner]
        base = rank * (3 * heads)
        for head in range(heads):
            rows = pl.ds(head * span, span)
            rest = tops_ref[page, rows, :] + jnp.log(scores_ref[page, rows, :])
            for piece in range(3):
                part = rest.astype(bf16).astype(f32)
                rest = rest - part
                tail = jnp.where(lane == base + piece * heads + head, part, tail)
        tail_ref[owner] = tail
    first = capacity * span
    for owner in range(groups):
        tail = tail_ref[owner].astype(bf16)
        for part in range(span // TAIL_ROWS):
            out_ref[owner, first : first + TAIL_ROWS, part * 128 : part * 128 + 128] = tail[
                part * TAIL_ROWS : part * TAIL_ROWS + TAIL_ROWS
            ]


def hosted_pages(request, fill, asked_rows, keys, values, decay, groups, capacity, local_count):
    count, span, inner = asked_rows.shape
    out_shape = (groups, capacity * span + TAIL_ROWS, inner)
    return pl.pallas_call(
        functools.partial(hosted_kernel, local_count, capacity),
        grid=(1,),
        in_specs=[SMEM, SMEM, whole(asked_rows)] + page_specs(keys, decay, OWNED_SLOTS),
        out_specs=pl.BlockSpec(out_shape, lambda *_: (0, 0, 0)),
        out_shape=jax.ShapeDtypeStruct(out_shape, bf16),
        scratch_shapes=[pltpu.VMEM((groups, span, 128), f32), pltpu.SMEM((groups,), jnp.int32)]
        + page_scratch(SPILL, span, decay.shape[0]),
        compiler_params=pltpu.CompilerParams(vmem_limit_bytes=24 * MIB),
        cost_estimate=page_cost(SPILL, keys, 64),
        name="hosted_pages",
    )(request, fill, asked_rows, in_hbm(keys), in_hbm(values), decay)


def merge_kernel(
    capacity, steps, table_ref, back_ref, log_hbm, average_hbm, out_ref,
    top_ref, total_ref, numer_ref, sems,
):
    groups, _, inner = back_ref.shape
    span = steps * BEAMS
    heads = inner // 64
    state = (top_ref, total_ref, numer_ref)
    copies = start_all([(log_hbm, top_ref), (average_hbm, numer_ref)], sems)
    total_ref[...] = jnp.ones_like(total_ref)
    source, target = sublanes((128, inner)), lanes((128, inner)) // 64
    spread = []
    for rank in range(capacity):
        hit = source < 0
        for piece in range(3):
            hit = hit | (source == target + (rank * 3 + piece) * heads)
        spread.append(hit.astype(f32).astype(bf16))
    for copy in copies:
        copy.wait()

    for owner in range(groups):
        first = capacity * span
        for rank in range(capacity):
            local = table_ref[owner * capacity + rank]

            @pl.when(local >= 0)
            def _():
                tail = jnp.concatenate(
                    [
                        back_ref[owner, first : first + TAIL_ROWS, part * 128 : part * 128 + 128]
                        for part in range(span // TAIL_ROWS)
                    ],
                    axis=0,
                )
                top = dot(tail, spread[rank])
                average = back_ref[owner, rank * span : rank * span + span, :].astype(f32)
                rows = pl.ds(pl.multiple_of(local * span, span), span)
                absorb(state, rows, slice(None), top, 1.0, average)

    for index in range(top_ref.shape[0] // (2 * span)):
        parts = []
        for half in range(2):
            rows = slice((index * 2 + half) * span, (index * 2 + half + 1) * span)
            parts.append(numer_ref[rows, :] / total_ref[rows, :])
        for step in range(steps):
            both = jnp.concatenate([p[step * 8 : step * 8 + 8] for p in parts], axis=0)
            out_ref[step, index * 16 : index * 16 + 16, :] = both.astype(bf16)


def merge(table, back, logs, averages, steps, capacity):
    rows, inner = logs.shape
    vmem = pl.BlockSpec(memory_space=pltpu.VMEM)
    hbm = pl.BlockSpec(memory_space=pltpu.HBM)
    return pl.pallas_call(
        functools.partial(merge_kernel, capacity, steps),
        in_specs=[SMEM, vmem, hbm, hbm],
        out_shape=jax.ShapeDtypeStruct((steps, rows // steps, inner), bf16),
        scratch_shapes=[pltpu.VMEM((rows, inner), f32)] * 3 + [pltpu.SemaphoreType.DMA((2,))],
        compiler_params=pltpu.CompilerParams(vmem_limit_bytes=16 * MIB),
        cost_estimate=pl.CostEstimate(
            flops=40 * rows * inner, bytes_accessed=8 * MIB, transcendentals=4 * rows * inner
        ),
        name="merge",
    )(table, back, in_hbm(logs), in_hbm(averages))


def mix_kernel(
    first, att0, att1, att2, att3, w0, w1, w2, w3, tokens_hbm, gain_ref,
    residual_out, normed_ref, residual_ref, tokens_ref, sems,
):
    rows, width = residual_ref.shape
    half = rows // 2
    core = lax.axis_index("head") % 2
    near = pl.ds(pl.multiple_of(core * half, half), half)
    copies = start_all([(tokens_hbm.at[first : first + rows], tokens_ref)], sems)
    for start in range(0, width, 512):
        cols = slice(start, start + 512)
        mixed = (dot(att0[...], w0[:, cols]) + dot(att1[...], w1[:, cols])) + (
            dot(att2[...], w2[:, cols]) + dot(att3[...], w3[:, cols])
        )
        residual_ref[:, cols] = mixed
    copies[0].wait()
    gain = gain_ref[...]

    def norm(index, carry):
        here = pl.ds(pl.multiple_of(index * 32, 32), 32)
        x = tokens_ref[here, :].astype(f32) + residual_ref[here, :]
        residual_ref[here, :] = x
        scale = lax.rsqrt(jnp.mean(x * x, axis=-1, keepdims=True) + epsilon)
        normed_ref[here, :] = (x * scale * gain).astype(bf16)
        return carry

    lax.fori_loop(0, rows // 32, norm, 0, unroll=2)
    residual_out[...] = residual_ref[near, :]


def mix(first, attended, weights, tokens, gain):
    rows, inner = attended[0].shape
    width = tokens.shape[1]
    vmem = pl.BlockSpec(memory_space=pltpu.VMEM)
    return pl.pallas_call(
        functools.partial(mix_kernel, first),
        in_specs=[vmem] * 8 + [pl.BlockSpec(memory_space=pltpu.HBM), vmem],
        out_specs=[vmem] * 2,
        out_shape=[
            jax.ShapeDtypeStruct((rows // 2, width), f32),
            pltpu.VMEM((rows, width), bf16),
        ],
        scratch_shapes=[
            pltpu.VMEM((rows, width), f32),
            pltpu.VMEM((rows, width), bf16),
            pltpu.SemaphoreType.DMA((1,)),
        ],
        compiler_params=pltpu.CompilerParams(vmem_limit_bytes=10 * MIB),
        cost_estimate=pl.CostEstimate(
            flops=8 * rows * width * inner, bytes_accessed=8 * MIB, transcendentals=rows
        ),
        name="mix",
    )(*attended, *[in_vmem(w) for w in weights], in_hbm(tokens), gain.reshape(1, -1))


def ffn_kernel(normed_ref, gate_ref, up_ref, down_ref, mine_ref, other_ref, hidden_ref, sums_ref):
    rows, width = normed_ref.shape
    half = rows // 2
    core = lax.axis_index("head") % 2
    near = pl.ds(pl.multiple_of(core * half, half), half)
    away = pl.ds(pl.multiple_of((1 - core) * half, half), half)
    for first in range(0, gate_ref.shape[1], 256):
        cols = slice(first, first + 256)
        gate = dot(normed_ref[...], gate_ref[:, cols])
        up = dot(normed_ref[...], up_ref[:, cols])
        hidden_ref[:, cols] = (gate / (1.0 + jnp.exp(-gate)) * up).astype(bf16)
    for first in range(0, width, 512):
        cols = slice(first, first + 512)
        sums_ref[...] = dot(hidden_ref[...], down_ref[:, cols])
        mine_ref[:, cols] = sums_ref[near, :]
        other_ref[:, cols] = sums_ref[away, :].astype(bf16)


def ffn(normed, w_gate, w_up, w_down):
    rows, width = normed.shape
    hidden = w_gate.shape[1]
    vmem = pl.BlockSpec(memory_space=pltpu.VMEM)
    return pl.pallas_call(
        ffn_kernel,
        in_specs=[vmem] * 4,
        out_specs=[vmem] * 2,
        out_shape=[
            jax.ShapeDtypeStruct((rows // 2, width), f32),
            jax.ShapeDtypeStruct((rows // 2, width), bf16),
        ],
        scratch_shapes=[pltpu.VMEM((rows, hidden), bf16), pltpu.VMEM((rows, 512), f32)],
        compiler_params=pltpu.CompilerParams(vmem_limit_bytes=10 * MIB),
        cost_estimate=pl.CostEstimate(
            flops=6 * rows * width * hidden, bytes_accessed=10 * MIB, transcendentals=rows * hidden
        ),
        name="ffn",
    )(in_vmem(normed), in_vmem(w_gate), in_vmem(w_up), in_vmem(w_down))


def finish_kernel(*refs):
    parts, out_ref = refs[:-1], refs[-1]
    core = lax.axis_index("head") % 2
    for index, part in enumerate(parts):
        step = index // 2 * 2 + (core if index % 2 == 0 else 1 - core)
        out_ref[step] = part[...]


def finish(parts):
    vmem = pl.BlockSpec(memory_space=pltpu.VMEM)
    return pl.pallas_call(
        finish_kernel,
        in_specs=[vmem] * len(parts),
        out_specs=vmem,
        out_shape=jax.ShapeDtypeStruct((len(parts),) + parts[0].shape, parts[0].dtype),
        compiler_params=pltpu.CompilerParams(vmem_limit_bytes=12 * MIB),
        name="finish",
    )(*parts)


def swap_core(value):
    return lax.ppermute(value, "head", [(i, i ^ 1) for i in range(4)])


def swap_chip(value):
    return lax.ppermute(value, "head", [(i, i ^ 2) for i in range(4)])


def shards(
    tokens, parents, page_request, page_fill, keys_pool, values_pool, decay_pool,
    gain_attn, w_query, w_key, w_value, w_forget, forget_bias, w_out,
    gain_ffn, w_gate, w_up, w_down,
):
    steps, rows, width = tokens.shape
    inner = w_query.shape[0]
    local_count = rows // BEAMS
    span = steps * BEAMS
    groups = lax.axis_size("group")
    capacity = (SPILL + groups - 2) // (groups - 1)
    decay = decay_pool.transpose(1, 0, 2)

    hosted = page_request[OWNED_SLOTS:]
    ids = lax.all_to_all(
        jnp.broadcast_to(hosted, (groups, 1, SPILL)), "group", split_axis=0, concat_axis=0, tiled=True
    )
    w_out_far = swap_chip(w_out)
    asked, table, q, normed = queries_of(page_request, ids, tokens, gain_attn, w_query, capacity)
    asked_rows = lax.all_to_all(
        asked.reshape(groups, capacity * span, inner),
        "group", split_axis=0, concat_axis=0, tiled=True,
    ).reshape(groups * capacity, span, inner)
    own = own_pages(page_request, page_fill, q, keys_pool, values_pool, decay, span)
    asked_rows, own = lax.optimization_barrier((asked_rows, own))
    payload = hosted_pages(
        page_request, page_fill, asked_rows, keys_pool, values_pool, decay, groups, capacity, local_count
    )
    payload, normed = lax.optimization_barrier((payload, normed))
    back = lax.all_to_all(payload, "group", split_axis=0, concat_axis=0, tiled=True)
    logs, averages = fresh(parents, forget_bias, normed, w_key, w_value, w_forget, q, own)
    weights = [w_out, swap_core(w_out), w_out_far, swap_core(w_out_far)]
    attended = merge(table, back, logs, averages, steps, capacity)

    flat = tokens.reshape(steps * rows, width)
    heres = [attended[step : step + 2].reshape(2 * rows, inner) for step in range(0, steps, 2)]
    fars = [swap_chip(here) for here in heres]
    done = [None, None]
    residual, mine, other, chip = [[None, None] for _ in range(4)]
    for index, (here, far) in enumerate(zip(heres, fars)):
        gathered = [here, swap_core(here), far, swap_core(far)]
        if index:
            gathered, other[0] = lax.optimization_barrier((gathered, other[0]))
        residual[index], normed = mix(2 * index * rows, gathered, weights, flat, gain_ffn)
        if index:
            chip[0] = (mine[0] + swap_core(other[0]).astype(f32)).astype(bf16)
            chip[0], normed = lax.optimization_barrier((chip[0], normed))
        mine[index], other[index] = ffn(normed, w_gate, w_up, w_down)
    chip[1] = (mine[1] + swap_core(other[1]).astype(f32)).astype(bf16)
    parts = []
    for index in range(2):
        both = chip[index].astype(f32) + swap_chip(chip[index]).astype(f32)
        done = (residual[index] + both).astype(bf16)
        parts.extend([done, swap_core(done)])
    return finish(parts)


def solution(mesh):
    return jax.shard_map(
        shards,
        mesh=mesh,
        in_specs=(
            P(None, "group", None),
            P(None, "group"),
            P("group"),
            P("group"),
            P("group", "head", None),
            P("group", "head", None),
            P("group", "head", None),
            P(),
            P("head", None),
            P("head", None),
            P("head", None),
            P(None, "head"),
            P("head"),
            P("head", None),
            P(),
            P(None, "head"),
            P(None, "head"),
            P("head", None),
        ),
        out_specs=P(None, "group", None),
        check_vma=False,
    )
```

```python
import functools

import jax
import jax.numpy as jnp
from jax import lax
from jax.experimental import pallas as pl
from jax.experimental.pallas import tpu as pltpu
from jax.sharding import PartitionSpec as P

BEAMS = 8
OWNED_SLOTS = 32
SPILL = 16
PAGE_BLOCK = 16
PARTS = 2
TAIL_ROWS = 16
MIB = 1 << 20

epsilon = 1e-05
masked_score = -1e30
f32 = jnp.float32
bf16 = jnp.bfloat16

NN = (((1,), (0,)), ((), ()))
NT = (((1,), (1,)), ((), ()))
SMEM = pl.BlockSpec(memory_space=pltpu.SMEM)


def dot(a, b, dims=NN):
    return lax.dot_general(a, b, dims, preferred_element_type=f32)


def lanes(shape):
    return lax.broadcasted_iota(jnp.int32, shape, len(shape) - 1)


def sublanes(shape):
    return lax.broadcasted_iota(jnp.int32, shape, len(shape) - 2)


def in_hbm(array):
    return pltpu.with_memory_space_constraint(array, pltpu.HBM)


def in_vmem(array):
    return pltpu.with_memory_space_constraint(array, pltpu.VMEM)


def start_all(pairs, sems):
    copies = [pltpu.make_async_copy(s, t, sems.at[i]) for i, (s, t) in enumerate(pairs)]
    for copy in copies:
        copy.start()
    return copies


def fill_table(local_count, capacity, first, ids_ref, table_ref):
    groups = ids_ref.shape[0]
    for slot in range(groups * capacity):
        table_ref[slot] = -1

    def group(index, carry):
        rank = jnp.int32(0)
        for page in range(SPILL):
            local = ids_ref[index, 0, OWNED_SLOTS + page] - first
            mine = (local >= 0) & (local < local_count)

            @pl.when(mine)
            def _():
                table_ref[index * capacity + rank] = local

            rank = rank + mine.astype(jnp.int32)
        return carry

    lax.fori_loop(0, groups, group, 0)


def query_kernel(
    tokens_hbm, gain_ref, wq_hbm, q_ref, q_hbm, normed_hbm,
    tokens_ref, wq_ref, normed_ref, sems, out_sems,
):
    steps, rows, _ = tokens_ref.shape
    span = steps * BEAMS
    cut = rows // 2
    copies = start_all(
        [
            (tokens_hbm.at[:, :cut], tokens_ref.at[:, :cut]),
            (tokens_hbm.at[:, cut:], tokens_ref.at[:, cut:]),
            (wq_hbm, wq_ref),
        ],
        sems,
    )
    gain = gain_ref[...]

    def pair(index, carry):
        slabs = []
        for step in range(steps):
            x = tokens_ref[step, pl.ds(pl.multiple_of(index * 16, 16), 16), :].astype(f32)
            scale = lax.rsqrt(jnp.mean(x * x, axis=-1, keepdims=True) + epsilon)
            slabs.append(x * scale * gain)
        for half in range(2):
            part = jnp.concatenate([s[half * 8 : half * 8 + 8] for s in slabs], axis=0)
            start = pl.multiple_of((index * 2 + half) * span, span)
            normed_ref[pl.ds(start, span), :] = part.astype(bf16)
        return carry

    copies[0].wait()
    lax.fori_loop(0, cut // 16, pair, 0, unroll=2)
    copies[1].wait()
    lax.fori_loop(cut // 16, rows // 16, pair, 0, unroll=2)
    leaving = start_all([(normed_ref, normed_hbm)], out_sems)
    copies[2].wait()
    query = dot(normed_ref[...], wq_ref[...], NT).astype(bf16)
    q_ref[...] = (query.astype(f32) * 0.125).astype(bf16)
    last = pltpu.make_async_copy(q_ref, q_hbm, out_sems.at[1])
    last.start()
    leaving[0].wait()
    last.wait()


def queries_of(tokens, gain, w_query):
    steps, rows, width = tokens.shape
    inner = w_query.shape[0]
    total = steps * rows
    hbm = pl.BlockSpec(memory_space=pltpu.HBM)
    vmem = pl.BlockSpec(memory_space=pltpu.VMEM)
    return pl.pallas_call(
        query_kernel,
        in_specs=[hbm, vmem, hbm],
        out_specs=[vmem, hbm, hbm],
        out_shape=[
            pltpu.VMEM((total, inner), bf16),
            pltpu.HBM((total, inner), bf16),
            pltpu.HBM((total, width), bf16),
        ],
        scratch_shapes=[
            pltpu.VMEM(tokens.shape, bf16),
            pltpu.VMEM(w_query.shape, bf16),
            pltpu.VMEM((total, width), bf16),
            pltpu.SemaphoreType.DMA((3,)),
            pltpu.SemaphoreType.DMA((2,)),
        ],
        compiler_params=pltpu.CompilerParams(vmem_limit_bytes=12 * MIB),
        cost_estimate=pl.CostEstimate(
            flops=2 * total * width * inner, bytes_accessed=6 * MIB, transcendentals=total
        ),
        name="queries",
    )(in_hbm(tokens), gain.reshape(1, -1), in_hbm(w_query))


def ask_kernel(capacity, request_ref, ids_ref, q_ref, table_ref, *out_refs):
    slots, part, _ = out_refs[0].shape
    span = part * len(out_refs)
    local_count = q_ref.shape[0] // span
    first = request_ref[0] // local_count * local_count
    fill_table(local_count, capacity, first, ids_ref, table_ref)
    for slot in range(slots):
        start = jnp.maximum(table_ref[slot], 0) * span
        for index, out_ref in enumerate(out_refs):
            out_ref[slot] = q_ref[pl.ds(pl.multiple_of(start + index * part, part), part), :]


def ask(request, ids, q, span, capacity):
    slots = ids.shape[0] * capacity
    vmem = pl.BlockSpec(memory_space=pltpu.VMEM)
    return pl.pallas_call(
        functools.partial(ask_kernel, capacity),
        in_specs=[SMEM, SMEM, vmem],
        out_specs=[SMEM] + [vmem] * PARTS,
        out_shape=[jax.ShapeDtypeStruct((slots,), jnp.int32)]
        + [jax.ShapeDtypeStruct((slots, span // PARTS, q.shape[1]), bf16)] * PARTS,
        compiler_params=pltpu.CompilerParams(vmem_limit_bytes=8 * MIB),
        name="ask",
    )(request, ids, in_vmem(q))


def half_masks(rows):
    low = lanes((rows, 128)) < 64
    return low.astype(f32).astype(bf16), jnp.logical_not(low).astype(f32).astype(bf16)


def stacked(pair_rows, masks):
    return jnp.concatenate([pair_rows * masks[0], pair_rows * masks[1]], axis=0)


def side_by_side(values, rows):
    low = lanes((rows, 128)) < 64
    top = jnp.broadcast_to(values[:rows], (rows, 128))
    bottom = jnp.broadcast_to(values[rows:], (rows, 128))
    return jnp.where(low, top, bottom)


def absorb(state, rows, columns, top, total, numer):
    top_ref, total_ref, numer_ref = state
    old = top_ref[rows, columns]
    new = jnp.maximum(old, top)
    keep = jnp.exp(old - new)
    add = jnp.exp(top - new)
    top_ref[rows, columns] = new
    total_ref[rows, columns] = total_ref[rows, columns] * keep + total * add
    numer_ref[rows, columns] = numer_ref[rows, columns] * keep + numer * add


def history(parents_ref, q_ref, k_ref, v_ref, forget_ref, state, scores_ref, weights_ref):
    transitions, rows = parents_ref.shape
    span = (transitions + 1) * BEAMS
    pack = 128 // span
    square = (128, 128)
    diagonal = sublanes(square) == lanes(square)
    columns = []
    for step in range(transitions):
        row = parents_ref[step : step + 1, :].astype(f32)
        columns.append(
            jnp.sum(jnp.where(diagonal, jnp.broadcast_to(row, square), 0.0), axis=1, keepdims=True)
        )
    lane8 = lanes((8, 128)).astype(f32)
    masks = half_masks(128)
    low = lanes(square) < 64
    top_ref, total_ref, numer_ref = state
    groups = rows // BEAMS // pack
    pairs = q_ref.shape[1] // 128
    for group in range(groups):
        slabs = []
        for member in range(pack):
            first = (group * pack + member) * BEAMS
            slabs.append(jnp.zeros((8, 128), f32))
            for step in range(transitions):
                wanted = columns[step][first : first + 8] + float(member * span + step * 8)
                slabs.append(jnp.where(lane8 == wanted, 1.0, 0.0))
        parent = jnp.concatenate(slabs, axis=0)
        parent16 = parent.astype(bf16)
        one = diagonal.astype(f32) + parent
        two = dot(parent16, parent16)
        ancestors = one + dot(two.astype(bf16), one.astype(bf16))
        here = pl.ds(group * 128, 128)
        running = lax.dot_general(
            ancestors, forget_ref[here, :], NN,
            precision=lax.Precision.HIGHEST, preferred_element_type=f32,
        ).T
        hidden = jnp.where(ancestors > 0.5, 0.0, masked_score)
        for pair in range(pairs):
            cols = pl.ds(pair * 128, 128)
            raw = dot(stacked(q_ref[here, cols], masks), k_ref[here, cols], NT)
            for half in range(2):
                head = pair * 2 + half
                scores_ref[group * pairs + pair, half] = raw[half * 128 : half * 128 + 128] + (
                    hidden - running[head : head + 1]
                )
    for group in range(groups):
        here = pl.ds(group * 128, 128)
        for pair in range(pairs):
            cols = pl.ds(pair * 128, 128)
            tops, totals = [], []
            for half in range(2):
                scores = scores_ref[group * pairs + pair, half]
                top = jnp.broadcast_to(jnp.max(scores, axis=-1, keepdims=True), square)
                weights = jnp.exp(scores - top)
                weights_ref[group * pairs + pair, pl.ds(half * 128, 128), :] = weights.astype(bf16)
                tops.append(top)
                totals.append(jnp.broadcast_to(jnp.sum(weights, axis=-1, keepdims=True), square))
            top_ref[here, cols] = jnp.where(low, *tops)
            total_ref[here, cols] = jnp.where(low, *totals)
    for group in range(groups):
        here = pl.ds(group * 128, 128)
        for pair in range(pairs):
            cols = pl.ds(pair * 128, 128)
            numer = dot(weights_ref[group * pairs + pair], v_ref[here, cols])
            numer_ref[here, cols] = jnp.where(low, numer[:128], numer[128:])


def fresh_kernel(
    parents_ref, bias_ref, normed_hbm, wk_hbm, wv_hbm, wf_hbm, q_hbm, top_hbm, total_hbm, numer_hbm,
    logs_hbm, averages_hbm,
    normed_ref, wk_ref, wv_ref, wf_ref, q_ref, top_own, total_own, numer_own,
    k_ref, v_ref, forget_ref, top_ref, total_ref, numer_ref, scores_ref, weights_ref,
    logs_ref, averages_ref, sems, out_sems,
):
    copies = start_all(
        [
            (normed_hbm, normed_ref), (wk_hbm, wk_ref), (wv_hbm, wv_ref), (wf_hbm, wf_ref),
            (q_hbm, q_ref), (top_hbm, top_own), (total_hbm, total_own), (numer_hbm, numer_own),
        ],
        sems,
    )
    copies[0].wait()
    copies[1].wait()
    k_ref[...] = dot(normed_ref[...], wk_ref[...], NT).astype(bf16)
    copies[2].wait()
    v_ref[...] = dot(normed_ref[...], wv_ref[...], NT).astype(bf16)
    copies[3].wait()
    gate = dot(normed_ref[...], wf_ref[...], NT) + bias_ref[...]
    forget = jnp.minimum(gate, 0.0) - jnp.log1p(jnp.exp(-jnp.abs(gate)))
    forget_ref[...] = jnp.zeros_like(forget_ref)
    forget_ref[:, : forget.shape[1]] = forget
    copies[4].wait()
    state = (top_ref, total_ref, numer_ref)
    history(parents_ref, q_ref, k_ref, v_ref, forget_ref, state, scores_ref, weights_ref)
    for copy in copies[5:]:
        copy.wait()

    parts, _, part = logs_ref.shape[:3]
    span = parts * part

    def join(index, carry):
        rows = pl.ds(pl.multiple_of(index * span, span), span)
        absorb(state, rows, slice(None), top_own[rows, :], total_own[rows, :], numer_own[rows, :])
        total = total_ref[rows, :]
        logs = top_ref[rows, :] + jnp.log(total)
        averages = numer_ref[rows, :] / total
        for number in range(parts):
            logs_ref[number, index] = logs[number * part : number * part + part]
            averages_ref[number, index] = averages[number * part : number * part + part]
        return carry

    lax.fori_loop(0, logs_ref.shape[1], join, 0, unroll=2)
    for copy in start_all([(logs_ref, logs_hbm), (averages_ref, averages_hbm)], out_sems):
        copy.wait()


def fresh(parents, bias, normed, w_key, w_value, w_forget, q, own):
    rows, inner = q.shape
    span = (parents.shape[0] + 1) * BEAMS
    vmem = pl.BlockSpec(memory_space=pltpu.VMEM)
    hbm = pl.BlockSpec(memory_space=pltpu.HBM)
    big = [normed, w_key, w_value, w_forget.T, q, *own]
    wide = pltpu.VMEM((rows, inner), f32)
    out = (PARTS, rows // span, span // PARTS, inner)
    tiles = rows * inner // (128 * 128)
    return pl.pallas_call(
        fresh_kernel,
        in_specs=[vmem, vmem] + [hbm] * len(big),
        out_specs=[hbm] * 2,
        out_shape=[pltpu.HBM(out, f32)] * 2,
        scratch_shapes=[pltpu.VMEM(x.shape, x.dtype) for x in big]
        + [pltpu.VMEM((rows, inner), bf16)] * 2
        + [pltpu.VMEM((rows, 128), f32), wide, wide, wide]
        + [pltpu.VMEM((tiles, 2, 128, 128), f32), pltpu.VMEM((tiles, 256, 128), bf16)]
        + [pltpu.VMEM(out, f32)] * 2
        + [pltpu.SemaphoreType.DMA((len(big),)), pltpu.SemaphoreType.DMA((2,))],
        compiler_params=pltpu.CompilerParams(vmem_limit_bytes=24 * MIB),
        cost_estimate=pl.CostEstimate(
            flops=4 * rows * normed.shape[1] * inner, bytes_accessed=12 * MIB,
            transcendentals=8 * rows * inner,
        ),
        name="fresh",
    )(parents, bias.reshape(1, -1), *[in_hbm(x) for x in big])


def page_weights(queries, fills, keys_ref, decay_ref, scores_ref, weights_ref, tops_ref):
    span = queries[0][0].shape[0]
    masks = half_masks(span)
    lane = lanes((1, 128))
    decay = [decay_ref[head].astype(f32) for head in range(decay_ref.shape[0])]
    for page, pairs in enumerate(queries):
        valid = lane < fills[page]
        for pair, query in enumerate(pairs):
            raw = dot(stacked(query, masks), keys_ref[page, pl.ds(pair * 128, 128), :])
            for half in range(2):
                head = pair * 2 + half
                bias = jnp.where(valid, decay[head][page : page + 1], masked_score)
                scores_ref[page, pl.ds(head * span, span), :] = (
                    raw[half * span : half * span + span] + bias
                )
    for page in range(len(queries)):
        for head in range(decay_ref.shape[0]):
            rows = pl.ds(head * span, span)
            scores = scores_ref[page, rows, :]
            top = jnp.broadcast_to(jnp.max(scores, axis=-1, keepdims=True), scores.shape)
            tops_ref[page, rows, :] = top
            weights = jnp.exp(scores - top)
            weights_ref[page, rows, :] = weights.astype(bf16)
            scores_ref[page, rows, :] = jnp.broadcast_to(
                jnp.sum(weights, axis=-1, keepdims=True), scores.shape
            )


def page_sums(page, pair, span, values_ref, scores_ref, weights_ref, tops_ref):
    low = lanes((span, 128)) < 64
    first, second = pl.ds(pair * 2 * span, span), pl.ds((pair * 2 + 1) * span, span)
    numer = dot(
        weights_ref[page, pl.ds(pair * 2 * span, 2 * span), :],
        values_ref[page, pl.ds(pair * 128, 128), :],
        NT,
    )
    top = jnp.where(low, tops_ref[page, first, :], tops_ref[page, second, :])
    total = jnp.where(low, scores_ref[page, first, :], scores_ref[page, second, :])
    return top, total, jnp.where(low, numer[:span], numer[span:])


def page_scratch(pages, span, heads):
    rows = span * heads
    return [
        pltpu.VMEM((pages, rows, 128), f32),
        pltpu.VMEM((pages, rows, 128), bf16),
        pltpu.VMEM((pages, rows, 128), f32),
    ]


def own_kernel(
    request_ref, fill_ref, q_ref, keys_ref, values_ref, decay_ref,
    top_ref, total_ref, numer_ref, *scratch,
):
    state = (top_ref, total_ref, numer_ref)
    span = scratch[0].shape[1] // decay_ref.shape[0]
    local_count = q_ref.shape[0] // span
    pairs = q_ref.shape[1] // 128

    top_ref[...] = jnp.full_like(top_ref, masked_score)
    total_ref[...] = jnp.zeros_like(total_ref)
    numer_ref[...] = jnp.zeros_like(numer_ref)

    def block(number, carry):
        start = pl.multiple_of(number * PAGE_BLOCK, PAGE_BLOCK)
        pages = pl.ds(start, PAGE_BLOCK)
        places, queries, fills = [], [], []
        for page in range(PAGE_BLOCK):
            local = lax.rem(request_ref[start + page], local_count)
            rows = pl.ds(pl.multiple_of(local * span, span), span)
            places.append(rows)
            queries.append([q_ref[rows, pl.ds(pair * 128, 128)] for pair in range(pairs)])
            fills.append(fill_ref[start + page])
        values = values_ref.at[pages]
        page_weights(queries, fills, keys_ref.at[pages], decay_ref.at[:, pages], *scratch)
        for page, rows in enumerate(places):
            for pair in range(pairs):
                sums = page_sums(page, pair, span, values, *scratch)
                absorb(state, rows, pl.ds(pair * 128, 128), *sums)
        return carry

    lax.fori_loop(0, OWNED_SLOTS // PAGE_BLOCK, block, 0)


def page_cost(pages, keys, rows):
    inner, length = keys.shape[1:]
    return pl.CostEstimate(
        flops=pages * rows * inner * length * 8,
        bytes_accessed=pages * inner * length * 4,
        transcendentals=pages * rows * inner * length // 64,
    )


def own_pages(request, fill, q, keys, values, decay, span):
    vmem = pl.BlockSpec(memory_space=pltpu.VMEM)
    return pl.pallas_call(
        own_kernel,
        in_specs=[SMEM, SMEM, vmem, vmem, vmem, vmem],
        out_specs=[vmem] * 3,
        out_shape=[jax.ShapeDtypeStruct(q.shape, f32)] * 3,
        scratch_shapes=page_scratch(PAGE_BLOCK, span, decay.shape[0]),
        compiler_params=pltpu.CompilerParams(vmem_limit_bytes=12 * MIB),
        cost_estimate=page_cost(OWNED_SLOTS, keys, 64),
        name="own_pages",
    )(request, fill, in_vmem(q), in_vmem(keys), in_vmem(values), decay)


def hosted_kernel(
    local_count, capacity, request_ref, fill_ref, q_ref, keys_ref, values_ref, decay_ref,
    out_ref, tail_ref, count_ref, *scratch,
):
    span, inner = q_ref.shape[1:]
    pairs = inner // 128
    heads = decay_ref.shape[0]
    groups = out_ref.shape[0]
    out_ref[...] = jnp.zeros_like(out_ref)
    tail_ref[...] = jnp.zeros_like(tail_ref)
    for owner in range(groups):
        count_ref[owner] = 0
    places, queries, fills = [], [], []
    for page in range(SPILL):
        owner = request_ref[OWNED_SLOTS + page] // local_count
        rank = count_ref[owner]
        count_ref[owner] = rank + 1
        places.append((owner, rank))
        slot = owner * capacity + rank
        queries.append([q_ref[slot, :, pl.ds(pair * 128, 128)] for pair in range(pairs)])
        fills.append(fill_ref[OWNED_SLOTS + page])
    hosted = pl.ds(OWNED_SLOTS, SPILL)
    values = values_ref.at[hosted]
    page_weights(queries, fills, keys_ref.at[hosted], decay_ref.at[:, hosted], *scratch)
    scores_ref, _, tops_ref = scratch
    lane = lanes((span, 128))
    for page, (owner, rank) in enumerate(places):
        here = pl.ds(pl.multiple_of(rank * span, span), span)
        for pair in range(pairs):
            _, total, numer = page_sums(page, pair, span, values, *scratch)
            out_ref[owner, here, pl.ds(pair * 128, 128)] = (numer / total).astype(bf16)
        tail = tail_ref[owner]
        base = rank * (3 * heads)
        for head in range(heads):
            rows = pl.ds(head * span, span)
            rest = tops_ref[page, rows, :] + jnp.log(scores_ref[page, rows, :])
            for piece in range(3):
                part = rest.astype(bf16).astype(f32)
                rest = rest - part
                tail = jnp.where(lane == base + piece * heads + head, part, tail)
        tail_ref[owner] = tail
    first = capacity * span
    for owner in range(groups):
        tail = tail_ref[owner].astype(bf16)
        for part in range(span // TAIL_ROWS):
            out_ref[owner, first : first + TAIL_ROWS, part * 128 : part * 128 + 128] = tail[
                part * TAIL_ROWS : part * TAIL_ROWS + TAIL_ROWS
            ]


def hosted_pages(request, fill, asked_rows, keys, values, decay, groups, capacity, local_count):
    count, span, inner = asked_rows.shape
    vmem = pl.BlockSpec(memory_space=pltpu.VMEM)
    return pl.pallas_call(
        functools.partial(hosted_kernel, local_count, capacity),
        in_specs=[SMEM, SMEM, vmem, vmem, vmem, vmem],
        out_specs=vmem,
        out_shape=jax.ShapeDtypeStruct((groups, capacity * span + TAIL_ROWS, inner), bf16),
        scratch_shapes=[pltpu.VMEM((groups, span, 128), f32), pltpu.SMEM((groups,), jnp.int32)]
        + page_scratch(SPILL, span, decay.shape[0]),
        compiler_params=pltpu.CompilerParams(vmem_limit_bytes=12 * MIB),
        cost_estimate=page_cost(SPILL, keys, 64),
        name="hosted_pages",
    )(request, fill, asked_rows, in_vmem(keys), in_vmem(values), decay)


def merge_kernel(
    capacity, steps, part, table_ref, back_ref, log_hbm, average_hbm, out_ref,
    top_ref, total_ref, numer_ref, sems,
):
    groups, _, inner = back_ref.shape
    span = steps * BEAMS
    heads = inner // 64
    state = (top_ref, total_ref, numer_ref)
    copies = start_all([(log_hbm.at[part], top_ref), (average_hbm.at[part], numer_ref)], sems)
    total_ref[...] = jnp.ones_like(total_ref)
    source, target = sublanes((128, inner)), lanes((128, inner)) // 64
    spread = []
    for rank in range(capacity):
        hit = source < 0
        for piece in range(3):
            hit = hit | (source == target + (rank * 3 + piece) * heads)
        spread.append(hit.astype(f32).astype(bf16))
    for copy in copies:
        copy.wait()

    for owner in range(groups):
        first = capacity * span
        for rank in range(capacity):
            local = table_ref[owner * capacity + rank]

            @pl.when(local >= 0)
            def _():
                tail = jnp.concatenate(
                    [
                        back_ref[owner, first : first + TAIL_ROWS, part * 128 : part * 128 + 128]
                        for part in range(span // TAIL_ROWS)
                    ],
                    axis=0,
                )
                top = dot(tail, spread[rank])
                average = back_ref[owner, rank * span : rank * span + span, :].astype(f32)
                rows = pl.ds(pl.multiple_of(local * span, span), span)
                absorb(state, rows, slice(None), top, 1.0, average)

    for index in range(top_ref.shape[0] // (2 * span)):
        parts = []
        for half in range(2):
            rows = slice((index * 2 + half) * span, (index * 2 + half + 1) * span)
            parts.append(numer_ref[rows, :] / total_ref[rows, :])
        for step in range(steps):
            both = jnp.concatenate([p[step * 8 : step * 8 + 8] for p in parts], axis=0)
            out_ref[step, index * 16 : index * 16 + 16, :] = both.astype(bf16)


def merge(part, table, back, logs, averages, steps, capacity):
    _, requests, span, inner = logs.shape
    rows = requests * span
    logs, averages = (x.reshape(PARTS, rows, inner) for x in (logs, averages))
    vmem = pl.BlockSpec(memory_space=pltpu.VMEM)
    hbm = pl.BlockSpec(memory_space=pltpu.HBM)
    return pl.pallas_call(
        functools.partial(merge_kernel, capacity, steps, part),
        in_specs=[SMEM, vmem, hbm, hbm],
        out_shape=jax.ShapeDtypeStruct((steps, rows // steps, inner), bf16),
        scratch_shapes=[pltpu.VMEM((rows, inner), f32)] * 3 + [pltpu.SemaphoreType.DMA((2,))],
        compiler_params=pltpu.CompilerParams(vmem_limit_bytes=10 * MIB),
        cost_estimate=pl.CostEstimate(
            flops=40 * rows * inner, bytes_accessed=8 * MIB, transcendentals=4 * rows * inner
        ),
        name="merge",
    )(table, back, in_hbm(logs), in_hbm(averages))


def mix_kernel(
    first, att0, att1, att2, att3, w0, w1, w2, w3, tokens_hbm, gain_ref,
    residual_out, normed_ref, residual_ref, tokens_ref, sems,
):
    rows, width = residual_ref.shape
    half = rows // 2
    head = lax.axis_index("head")
    near = pl.ds(pl.multiple_of(head % 2 * half, half), half)
    copies = start_all([(tokens_hbm.at[first : first + rows], tokens_ref)], sems)
    for own in range(4):

        @pl.when(head == own)
        def _():
            order = [own ^ other for other in range(4)]
            attended = jnp.concatenate([(att0, att1, att2, att3)[k][...] for k in order], axis=1)
            for start in range(0, width, 512):
                cols = slice(start, start + 512)
                weight = jnp.concatenate([(w0, w1, w2, w3)[k][:, cols] for k in order], axis=0)
                residual_ref[:, cols] = dot(attended, weight)

    copies[0].wait()
    gain = gain_ref[...]

    def norm(index, carry):
        here = pl.ds(pl.multiple_of(index * 32, 32), 32)
        x = tokens_ref[here, :].astype(f32) + residual_ref[here, :]
        residual_ref[here, :] = x
        scale = lax.rsqrt(jnp.mean(x * x, axis=-1, keepdims=True) + epsilon)
        normed_ref[here, :] = (x * scale * gain).astype(bf16)
        return carry

    lax.fori_loop(0, rows // 32, norm, 0, unroll=2)
    residual_out[...] = residual_ref[near, :]


def mix(first, attended, weights, tokens, gain):
    rows, inner = attended[0].shape
    width = tokens.shape[1]
    vmem = pl.BlockSpec(memory_space=pltpu.VMEM)
    return pl.pallas_call(
        functools.partial(mix_kernel, first),
        in_specs=[vmem] * 8 + [pl.BlockSpec(memory_space=pltpu.HBM), vmem],
        out_specs=[vmem] * 2,
        out_shape=[
            jax.ShapeDtypeStruct((rows // 2, width), f32),
            pltpu.VMEM((rows, width), bf16),
        ],
        scratch_shapes=[
            pltpu.VMEM((rows, width), f32),
            pltpu.VMEM((rows, width), bf16),
            pltpu.SemaphoreType.DMA((1,)),
        ],
        compiler_params=pltpu.CompilerParams(vmem_limit_bytes=10 * MIB),
        cost_estimate=pl.CostEstimate(
            flops=8 * rows * width * inner, bytes_accessed=8 * MIB, transcendentals=rows
        ),
        name="mix",
    )(*attended, *[in_vmem(w) for w in weights], in_hbm(tokens), gain.reshape(1, -1))


def ffn_kernel(normed_ref, gate_ref, up_ref, down_ref, mine_ref, other_ref, hidden_ref, sums_ref):
    rows, width = normed_ref.shape
    half = rows // 2
    core = lax.axis_index("head") % 2
    near = pl.ds(pl.multiple_of(core * half, half), half)
    away = pl.ds(pl.multiple_of((1 - core) * half, half), half)
    for first in range(0, gate_ref.shape[1], 256):
        cols = slice(first, first + 256)
        gate = dot(normed_ref[...], gate_ref[:, cols])
        up = dot(normed_ref[...], up_ref[:, cols])
        hidden_ref[:, cols] = (gate / (1.0 + jnp.exp(-gate)) * up).astype(bf16)
    for first in range(0, width, 512):
        cols = slice(first, first + 512)
        sums_ref[...] = dot(hidden_ref[...], down_ref[:, cols])
        mine_ref[:, cols] = sums_ref[near, :]
        other_ref[:, cols] = sums_ref[away, :].astype(bf16)


def ffn(normed, w_gate, w_up, w_down):
    rows, width = normed.shape
    hidden = w_gate.shape[1]
    vmem = pl.BlockSpec(memory_space=pltpu.VMEM)
    return pl.pallas_call(
        ffn_kernel,
        in_specs=[vmem] * 4,
        out_specs=[vmem] * 2,
        out_shape=[
            jax.ShapeDtypeStruct((rows // 2, width), f32),
            jax.ShapeDtypeStruct((rows // 2, width), bf16),
        ],
        scratch_shapes=[pltpu.VMEM((rows, hidden), bf16), pltpu.VMEM((rows, 512), f32)],
        compiler_params=pltpu.CompilerParams(vmem_limit_bytes=10 * MIB),
        cost_estimate=pl.CostEstimate(
            flops=6 * rows * width * hidden, bytes_accessed=10 * MIB, transcendentals=rows * hidden
        ),
        name="ffn",
    )(in_vmem(normed), in_vmem(w_gate), in_vmem(w_up), in_vmem(w_down))


def finish_kernel(*refs):
    parts, out_ref = refs[:-1], refs[-1]
    core = lax.axis_index("head") % 2
    for index, part in enumerate(parts):
        step = index // 2 * 2 + (core if index % 2 == 0 else 1 - core)
        out_ref[step] = part[...]


def finish(parts):
    vmem = pl.BlockSpec(memory_space=pltpu.VMEM)
    return pl.pallas_call(
        finish_kernel,
        in_specs=[vmem] * len(parts),
        out_specs=vmem,
        out_shape=jax.ShapeDtypeStruct((len(parts),) + parts[0].shape, parts[0].dtype),
        compiler_params=pltpu.CompilerParams(vmem_limit_bytes=12 * MIB),
        name="finish",
    )(*parts)


def swap_core(value):
    return lax.ppermute(value, "head", [(i, i ^ 1) for i in range(4)])


def swap_chip(value):
    return lax.ppermute(value, "head", [(i, i ^ 2) for i in range(4)])


def shards(
    tokens, parents, page_request, page_fill, keys_pool, values_pool, decay_pool,
    gain_attn, w_query, w_key, w_value, w_forget, forget_bias, w_out,
    gain_ffn, w_gate, w_up, w_down,
):
    steps, rows, width = tokens.shape
    inner = w_query.shape[0]
    local_count = rows // BEAMS
    span = steps * BEAMS
    groups = lax.axis_size("group")
    capacity = (SPILL + groups - 2) // (groups - 1)
    decay = decay_pool.transpose(1, 0, 2)

    def exchange(value):
        return lax.all_to_all(value, "group", split_axis=0, concat_axis=0, tiled=True)

    ids = exchange(jnp.broadcast_to(page_request, (groups, 1, page_request.shape[0])))
    w_out_far = swap_chip(w_out)
    q_near, q, normed = queries_of(tokens, gain_attn, w_query)
    table, *asked = ask(page_request, ids, q_near, span, capacity)
    part = span // PARTS
    asked_rows = [
        exchange(x.reshape(groups, capacity * part, inner)).reshape(groups * capacity, part, inner)
        for x in asked
    ]
    own = own_pages(page_request, page_fill, q, keys_pool, values_pool, decay, span)
    asked_rows[0], own = lax.optimization_barrier((asked_rows[0], own))
    back = []
    for index in range(PARTS):
        if index:
            asked_rows[index], payload = lax.optimization_barrier((asked_rows[index], payload))
        payload = hosted_pages(
            page_request, page_fill, asked_rows[index], keys_pool, values_pool, decay,
            groups, capacity, local_count,
        )
        back.append(exchange(payload))
    payload, normed = lax.optimization_barrier((payload, normed))
    logs, averages = fresh(parents, forget_bias, normed, w_key, w_value, w_forget, q, own)
    weights = [w_out, swap_core(w_out), w_out_far, swap_core(w_out_far)]

    flat = tokens.reshape(steps * rows, width)
    each = steps // PARTS
    heres = [
        merge(index, table, back[index], logs, averages, each, capacity).reshape(each * rows, inner)
        for index in range(PARTS)
    ]
    fars = [swap_chip(here) for here in heres]
    residual, mine, other, chip, far_chip = [[None] * PARTS for _ in range(5)]
    for index, (here, far) in enumerate(zip(heres, fars)):
        gathered = [here, swap_core(here), far, swap_core(far)]
        if index:
            gathered, other[0] = lax.optimization_barrier((gathered, other[0]))
        residual[index], normed = mix(index * each * rows, gathered, weights, flat, gain_ffn)
        if index:
            chip[0] = (mine[0] + swap_core(other[0]).astype(f32)).astype(bf16)
            chip[0], normed = lax.optimization_barrier((chip[0], normed))
        mine[index], other[index] = ffn(normed, w_gate, w_up, w_down)
    far_chip[0] = swap_chip(chip[0])
    chip[1] = (mine[1] + swap_core(other[1]).astype(f32)).astype(bf16)
    chip[1], far_chip[0] = lax.optimization_barrier((chip[1], far_chip[0]))
    far_chip[1] = swap_chip(chip[1])
    parts = []
    for index in range(PARTS):
        both = chip[index].astype(f32) + far_chip[index].astype(f32)
        done = (residual[index] + both).astype(bf16)
        parts.extend([done, swap_core(done)])
    return finish(parts)


def solution(mesh):
    return jax.shard_map(
        shards,
        mesh=mesh,
        in_specs=(
            P(None, "group", None),
            P(None, "group"),
            P("group"),
            P("group"),
            P("group", "head", None),
            P("group", "head", None),
            P("group", "head", None),
            P(),
            P("head", None),
            P("head", None),
            P("head", None),
            P(None, "head"),
            P("head"),
            P("head", None),
            P(),
            P(None, "head"),
            P(None, "head"),
            P("head", None),
        ),
        out_specs=P(None, "group", None),
        check_vma=False,
    )
```

```python
import functools

import jax
import jax.numpy as jnp
from jax import lax
from jax.experimental import pallas as pl
from jax.experimental.pallas import tpu as pltpu
from jax.sharding import PartitionSpec as P

BEAMS = 8
OWNED_SLOTS = 32
SPILL = 16
PAGE_BLOCK = 16
PARTS = 2
TAIL_ROWS = 16
MIB = 1 << 20

epsilon = 1e-05
masked_score = -1e30
f32 = jnp.float32
bf16 = jnp.bfloat16

NN = (((1,), (0,)), ((), ()))
NT = (((1,), (1,)), ((), ()))
SMEM = pl.BlockSpec(memory_space=pltpu.SMEM)


def dot(a, b, dims=NN):
    return lax.dot_general(a, b, dims, preferred_element_type=f32)


def lanes(shape):
    return lax.broadcasted_iota(jnp.int32, shape, len(shape) - 1)


def sublanes(shape):
    return lax.broadcasted_iota(jnp.int32, shape, len(shape) - 2)


def in_hbm(array):
    return pltpu.with_memory_space_constraint(array, pltpu.HBM)


def in_vmem(array):
    return pltpu.with_memory_space_constraint(array, pltpu.VMEM)


def start_all(pairs, sems):
    copies = [pltpu.make_async_copy(s, t, sems.at[i]) for i, (s, t) in enumerate(pairs)]
    for copy in copies:
        copy.start()
    return copies


def fill_table(local_count, capacity, first, ids_ref, table_ref):
    groups = ids_ref.shape[0]
    for slot in range(groups * capacity):
        table_ref[slot] = -1

    def group(index, carry):
        rank = jnp.int32(0)
        for page in range(SPILL):
            local = ids_ref[index, 0, OWNED_SLOTS + page] - first
            mine = (local >= 0) & (local < local_count)

            @pl.when(mine)
            def _():
                table_ref[index * capacity + rank] = local

            rank = rank + mine.astype(jnp.int32)
        return carry

    lax.fori_loop(0, groups, group, 0)


def query_kernel(
    tokens_hbm, gain_ref, wq_hbm, q_ref, q_hbm, normed_hbm,
    tokens_ref, wq_ref, normed_ref, sems, out_sems,
):
    steps, rows, _ = tokens_ref.shape
    span = steps * BEAMS
    cut = rows // 2
    copies = start_all(
        [
            (tokens_hbm.at[:, :cut], tokens_ref.at[:, :cut]),
            (tokens_hbm.at[:, cut:], tokens_ref.at[:, cut:]),
            (wq_hbm, wq_ref),
        ],
        sems,
    )
    gain = gain_ref[...]

    def pair(index, carry):
        slabs = []
        for step in range(steps):
            x = tokens_ref[step, pl.ds(pl.multiple_of(index * 16, 16), 16), :].astype(f32)
            scale = lax.rsqrt(jnp.mean(x * x, axis=-1, keepdims=True) + epsilon)
            slabs.append(x * scale * gain)
        for half in range(2):
            part = jnp.concatenate([s[half * 8 : half * 8 + 8] for s in slabs], axis=0)
            start = pl.multiple_of((index * 2 + half) * span, span)
            normed_ref[pl.ds(start, span), :] = part.astype(bf16)
        return carry

    copies[0].wait()
    lax.fori_loop(0, cut // 16, pair, 0, unroll=2)
    copies[1].wait()
    lax.fori_loop(cut // 16, rows // 16, pair, 0, unroll=2)
    leaving = start_all([(normed_ref, normed_hbm)], out_sems)
    copies[2].wait()
    query = dot(normed_ref[...], wq_ref[...], NT).astype(bf16)
    q_ref[...] = (query.astype(f32) * 0.125).astype(bf16)
    last = pltpu.make_async_copy(q_ref, q_hbm, out_sems.at[1])
    last.start()
    leaving[0].wait()
    last.wait()


def queries_of(tokens, gain, w_query):
    steps, rows, width = tokens.shape
    inner = w_query.shape[0]
    total = steps * rows
    hbm = pl.BlockSpec(memory_space=pltpu.HBM)
    vmem = pl.BlockSpec(memory_space=pltpu.VMEM)
    return pl.pallas_call(
        query_kernel,
        in_specs=[hbm, vmem, hbm],
        out_specs=[vmem, hbm, hbm],
        out_shape=[
            pltpu.VMEM((total, inner), bf16),
            pltpu.HBM((total, inner), bf16),
            pltpu.HBM((total, width), bf16),
        ],
        scratch_shapes=[
            pltpu.VMEM(tokens.shape, bf16),
            pltpu.VMEM(w_query.shape, bf16),
            pltpu.VMEM((total, width), bf16),
            pltpu.SemaphoreType.DMA((3,)),
            pltpu.SemaphoreType.DMA((2,)),
        ],
        compiler_params=pltpu.CompilerParams(vmem_limit_bytes=12 * MIB),
        cost_estimate=pl.CostEstimate(
            flops=2 * total * width * inner, bytes_accessed=6 * MIB, transcendentals=total
        ),
        name="queries",
    )(in_hbm(tokens), gain.reshape(1, -1), in_hbm(w_query))


def ask_kernel(capacity, request_ref, ids_ref, q_ref, table_ref, out_ref):
    slots, span, _ = out_ref.shape
    local_count = q_ref.shape[0] // span
    first = request_ref[0] // local_count * local_count
    fill_table(local_count, capacity, first, ids_ref, table_ref)
    for slot in range(slots):
        start = jnp.maximum(table_ref[slot], 0) * span
        out_ref[slot] = q_ref[pl.ds(pl.multiple_of(start, span), span), :]


def ask(request, ids, q, span, capacity):
    slots = ids.shape[0] * capacity
    vmem = pl.BlockSpec(memory_space=pltpu.VMEM)
    return pl.pallas_call(
        functools.partial(ask_kernel, capacity),
        in_specs=[SMEM, SMEM, vmem],
        out_specs=[SMEM, vmem],
        out_shape=[
            jax.ShapeDtypeStruct((slots,), jnp.int32),
            jax.ShapeDtypeStruct((slots, span, q.shape[1]), bf16),
        ],
        compiler_params=pltpu.CompilerParams(vmem_limit_bytes=8 * MIB),
        name="ask",
    )(request, ids, in_vmem(q))


def half_masks(rows):
    low = lanes((rows, 128)) < 64
    return low.astype(f32).astype(bf16), jnp.logical_not(low).astype(f32).astype(bf16)


def stacked(pair_rows, masks):
    return jnp.concatenate([pair_rows * masks[0], pair_rows * masks[1]], axis=0)


def side_by_side(values, rows):
    low = lanes((rows, 128)) < 64
    top = jnp.broadcast_to(values[:rows], (rows, 128))
    bottom = jnp.broadcast_to(values[rows:], (rows, 128))
    return jnp.where(low, top, bottom)


def absorb(state, rows, columns, top, total, numer):
    top_ref, total_ref, numer_ref = state
    old = top_ref[rows, columns]
    new = jnp.maximum(old, top)
    keep = jnp.exp(old - new)
    add = jnp.exp(top - new)
    top_ref[rows, columns] = new
    total_ref[rows, columns] = total_ref[rows, columns] * keep + total * add
    numer_ref[rows, columns] = numer_ref[rows, columns] * keep + numer * add


def history(parents_ref, q_ref, k_ref, v_ref, forget_ref, state, scores_ref, weights_ref):
    transitions, rows = parents_ref.shape
    span = (transitions + 1) * BEAMS
    pack = 128 // span
    square = (128, 128)
    diagonal = sublanes(square) == lanes(square)
    columns = []
    for step in range(transitions):
        row = parents_ref[step : step + 1, :].astype(f32)
        columns.append(
            jnp.sum(jnp.where(diagonal, jnp.broadcast_to(row, square), 0.0), axis=1, keepdims=True)
        )
    lane8 = lanes((8, 128)).astype(f32)
    masks = half_masks(128)
    low = lanes(square) < 64
    top_ref, total_ref, numer_ref = state
    groups = rows // BEAMS // pack
    pairs = q_ref.shape[1] // 128
    for group in range(groups):
        slabs = []
        for member in range(pack):
            first = (group * pack + member) * BEAMS
            slabs.append(jnp.zeros((8, 128), f32))
            for step in range(transitions):
                wanted = columns[step][first : first + 8] + float(member * span + step * 8)
                slabs.append(jnp.where(lane8 == wanted, 1.0, 0.0))
        parent = jnp.concatenate(slabs, axis=0)
        parent16 = parent.astype(bf16)
        one = diagonal.astype(f32) + parent
        two = dot(parent16, parent16)
        ancestors = one + dot(two.astype(bf16), one.astype(bf16))
        here = pl.ds(group * 128, 128)
        running = lax.dot_general(
            ancestors, forget_ref[here, :], NN,
            precision=lax.Precision.HIGHEST, preferred_element_type=f32,
        ).T
        hidden = jnp.where(ancestors > 0.5, 0.0, masked_score)
        for pair in range(pairs):
            cols = pl.ds(pair * 128, 128)
            raw = dot(stacked(q_ref[here, cols], masks), k_ref[here, cols], NT)
            for half in range(2):
                head = pair * 2 + half
                scores_ref[group * pairs + pair, half] = raw[half * 128 : half * 128 + 128] + (
                    hidden - running[head : head + 1]
                )
    for group in range(groups):
        here = pl.ds(group * 128, 128)
        for pair in range(pairs):
            cols = pl.ds(pair * 128, 128)
            tops, totals = [], []
            for half in range(2):
                scores = scores_ref[group * pairs + pair, half]
                top = jnp.broadcast_to(jnp.max(scores, axis=-1, keepdims=True), square)
                weights = jnp.exp(scores - top)
                weights_ref[group * pairs + pair, pl.ds(half * 128, 128), :] = weights.astype(bf16)
                tops.append(top)
                totals.append(jnp.broadcast_to(jnp.sum(weights, axis=-1, keepdims=True), square))
            top_ref[here, cols] = jnp.where(low, *tops)
            total_ref[here, cols] = jnp.where(low, *totals)
    for group in range(groups):
        here = pl.ds(group * 128, 128)
        for pair in range(pairs):
            cols = pl.ds(pair * 128, 128)
            numer = dot(weights_ref[group * pairs + pair], v_ref[here, cols])
            numer_ref[here, cols] = jnp.where(low, numer[:128], numer[128:])


def fresh_kernel(
    parents_ref, bias_ref, normed_hbm, wk_hbm, wv_hbm, wf_hbm, q_hbm, top_hbm, total_hbm, numer_hbm,
    logs_hbm, averages_hbm,
    normed_ref, wk_ref, wv_ref, wf_ref, q_ref, top_own, total_own, numer_own,
    k_ref, v_ref, forget_ref, top_ref, total_ref, numer_ref, scores_ref, weights_ref,
    logs_ref, averages_ref, sems, out_sems,
):
    copies = start_all(
        [
            (normed_hbm, normed_ref), (wk_hbm, wk_ref), (wv_hbm, wv_ref), (wf_hbm, wf_ref),
            (q_hbm, q_ref), (top_hbm, top_own), (total_hbm, total_own), (numer_hbm, numer_own),
        ],
        sems,
    )
    copies[0].wait()
    copies[1].wait()
    k_ref[...] = dot(normed_ref[...], wk_ref[...], NT).astype(bf16)
    copies[2].wait()
    v_ref[...] = dot(normed_ref[...], wv_ref[...], NT).astype(bf16)
    copies[3].wait()
    gate = dot(normed_ref[...], wf_ref[...], NT) + bias_ref[...]
    forget = jnp.minimum(gate, 0.0) - jnp.log1p(jnp.exp(-jnp.abs(gate)))
    forget_ref[...] = jnp.zeros_like(forget_ref)
    forget_ref[:, : forget.shape[1]] = forget
    copies[4].wait()
    state = (top_ref, total_ref, numer_ref)
    history(parents_ref, q_ref, k_ref, v_ref, forget_ref, state, scores_ref, weights_ref)
    for copy in copies[5:]:
        copy.wait()

    parts, _, part = logs_ref.shape[:3]
    span = parts * part

    def join(index, carry):
        rows = pl.ds(pl.multiple_of(index * span, span), span)
        absorb(state, rows, slice(None), top_own[rows, :], total_own[rows, :], numer_own[rows, :])
        total = total_ref[rows, :]
        logs = top_ref[rows, :] + jnp.log(total)
        averages = numer_ref[rows, :] / total
        for number in range(parts):
            logs_ref[number, index] = logs[number * part : number * part + part]
            averages_ref[number, index] = averages[number * part : number * part + part]
        return carry

    lax.fori_loop(0, logs_ref.shape[1], join, 0, unroll=2)
    for copy in start_all([(logs_ref, logs_hbm), (averages_ref, averages_hbm)], out_sems):
        copy.wait()


def fresh(parents, bias, normed, w_key, w_value, w_forget, q, own):
    rows, inner = q.shape
    span = (parents.shape[0] + 1) * BEAMS
    vmem = pl.BlockSpec(memory_space=pltpu.VMEM)
    hbm = pl.BlockSpec(memory_space=pltpu.HBM)
    big = [normed, w_key, w_value, w_forget.T, q, *own]
    wide = pltpu.VMEM((rows, inner), f32)
    out = (PARTS, rows // span, span // PARTS, inner)
    tiles = rows * inner // (128 * 128)
    return pl.pallas_call(
        fresh_kernel,
        in_specs=[vmem, vmem] + [hbm] * len(big),
        out_specs=[hbm] * 2,
        out_shape=[pltpu.HBM(out, f32)] * 2,
        scratch_shapes=[pltpu.VMEM(x.shape, x.dtype) for x in big]
        + [pltpu.VMEM((rows, inner), bf16)] * 2
        + [pltpu.VMEM((rows, 128), f32), wide, wide, wide]
        + [pltpu.VMEM((tiles, 2, 128, 128), f32), pltpu.VMEM((tiles, 256, 128), bf16)]
        + [pltpu.VMEM(out, f32)] * 2
        + [pltpu.SemaphoreType.DMA((len(big),)), pltpu.SemaphoreType.DMA((2,))],
        compiler_params=pltpu.CompilerParams(vmem_limit_bytes=24 * MIB),
        cost_estimate=pl.CostEstimate(
            flops=4 * rows * normed.shape[1] * inner, bytes_accessed=12 * MIB,
            transcendentals=8 * rows * inner,
        ),
        name="fresh",
    )(parents, bias.reshape(1, -1), *[in_hbm(x) for x in big])


def page_weights(
    queries, fills, keys_ref, decay_ref, scores_ref, weights_ref, tops_ref, arrival=lambda page: None
):
    span = queries[0][0].shape[0]
    masks = half_masks(span)
    lane = lanes((1, 128))
    decay = [decay_ref[head].astype(f32) for head in range(decay_ref.shape[0])]
    for page, pairs in enumerate(queries):
        arrival(page)
        valid = lane < fills[page]
        for pair, query in enumerate(pairs):
            raw = dot(stacked(query, masks), keys_ref[page, pl.ds(pair * 128, 128), :])
            for half in range(2):
                head = pair * 2 + half
                bias = jnp.where(valid, decay[head][page : page + 1], masked_score)
                scores_ref[page, pl.ds(head * span, span), :] = (
                    raw[half * span : half * span + span] + bias
                )
    for page in range(len(queries)):
        for head in range(decay_ref.shape[0]):
            rows = pl.ds(head * span, span)
            scores = scores_ref[page, rows, :]
            top = jnp.broadcast_to(jnp.max(scores, axis=-1, keepdims=True), scores.shape)
            tops_ref[page, rows, :] = top
            weights = jnp.exp(scores - top)
            weights_ref[page, rows, :] = weights.astype(bf16)
            scores_ref[page, rows, :] = jnp.broadcast_to(
                jnp.sum(weights, axis=-1, keepdims=True), scores.shape
            )


def page_sums(page, pair, span, values_ref, scores_ref, weights_ref, tops_ref):
    low = lanes((span, 128)) < 64
    first, second = pl.ds(pair * 2 * span, span), pl.ds((pair * 2 + 1) * span, span)
    numer = dot(
        weights_ref[page, pl.ds(pair * 2 * span, 2 * span), :],
        values_ref[page, pl.ds(pair * 128, 128), :],
        NT,
    )
    top = jnp.where(low, tops_ref[page, first, :], tops_ref[page, second, :])
    total = jnp.where(low, scores_ref[page, first, :], scores_ref[page, second, :])
    return top, total, jnp.where(low, numer[:span], numer[span:])


def page_scratch(pages, span, heads):
    rows = span * heads
    return [
        pltpu.VMEM((pages, rows, 128), f32),
        pltpu.VMEM((pages, rows, 128), bf16),
        pltpu.VMEM((pages, rows, 128), f32),
    ]


def own_kernel(
    request_ref, fill_ref, q_ref, keys_ref, values_ref, decay_ref,
    top_ref, total_ref, numer_ref, *scratch,
):
    state = (top_ref, total_ref, numer_ref)
    span = scratch[0].shape[1] // decay_ref.shape[0]
    local_count = q_ref.shape[0] // span
    pairs = q_ref.shape[1] // 128

    block = pl.program_id(0)

    @pl.when(block == 0)
    def _():
        top_ref[...] = jnp.full_like(top_ref, masked_score)
        total_ref[...] = jnp.zeros_like(total_ref)
        numer_ref[...] = jnp.zeros_like(numer_ref)

    places, queries, fills = [], [], []
    for page in range(PAGE_BLOCK):
        index = block * PAGE_BLOCK + page
        local = lax.rem(request_ref[index], local_count)
        rows = pl.ds(pl.multiple_of(local * span, span), span)
        places.append(rows)
        queries.append([q_ref[rows, pl.ds(pair * 128, 128)] for pair in range(pairs)])
        fills.append(fill_ref[index])
    page_weights(queries, fills, keys_ref, decay_ref, *scratch)
    for page, rows in enumerate(places):
        for pair in range(pairs):
            sums = page_sums(page, pair, span, values_ref, *scratch)
            absorb(state, rows, pl.ds(pair * 128, 128), *sums)


def page_cost(pages, keys, rows):
    inner, length = keys.shape[1:]
    return pl.CostEstimate(
        flops=pages * rows * inner * length * 8,
        bytes_accessed=pages * inner * length * 4,
        transcendentals=pages * rows * inner * length // 64,
    )


def own_pages(request, fill, q, keys, values, decay, span):
    pool = pl.BlockSpec((PAGE_BLOCK,) + keys.shape[1:], lambda i: (i, 0, 0))
    decay_spec = pl.BlockSpec((decay.shape[0], PAGE_BLOCK, decay.shape[2]), lambda i: (0, i, 0))
    rows = pl.BlockSpec(q.shape, lambda i: (0, 0))
    return pl.pallas_call(
        own_kernel,
        grid=(OWNED_SLOTS // PAGE_BLOCK,),
        in_specs=[SMEM, SMEM, rows, pool, pool, decay_spec],
        out_specs=[rows] * 3,
        out_shape=[pltpu.HBM(q.shape, f32)] * 3,
        scratch_shapes=page_scratch(PAGE_BLOCK, span, decay.shape[0]),
        compiler_params=pltpu.CompilerParams(vmem_limit_bytes=20 * MIB),
        cost_estimate=page_cost(OWNED_SLOTS, keys, 64),
        name="own_pages",
    )(request, fill, in_hbm(q), in_hbm(keys), in_hbm(values), decay)


def hosted_kernel(
    local_count, capacity, request_ref, fill_ref, q_ref, keys_hbm, values_hbm, decay_ref,
    out_ref, keys_ref, values_ref, sems, tail_ref, count_ref, *scratch,
):
    pieces = sems.shape[0] // 2
    chunk = SPILL // pieces
    copies = start_all(
        [
            (pool.at[pl.ds(OWNED_SLOTS + piece * chunk, chunk)], target.at[pl.ds(piece * chunk, chunk)])
            for pool, target in ((keys_hbm, keys_ref), (values_hbm, values_ref))
            for piece in range(pieces)
        ],
        sems,
    )
    span, inner = q_ref.shape[1:]
    pairs = inner // 128
    heads = decay_ref.shape[0]
    groups = out_ref.shape[0]
    out_ref[...] = jnp.zeros_like(out_ref)
    tail_ref[...] = jnp.zeros_like(tail_ref)
    for owner in range(groups):
        count_ref[owner] = 0
    places, queries, fills = [], [], []
    for page in range(SPILL):
        owner = request_ref[OWNED_SLOTS + page] // local_count
        rank = count_ref[owner]
        count_ref[owner] = rank + 1
        places.append((owner, rank))
        slot = owner * capacity + rank
        queries.append([q_ref[slot, :, pl.ds(pair * 128, 128)] for pair in range(pairs)])
        fills.append(fill_ref[OWNED_SLOTS + page])

    def arrival(page):
        if page % chunk == 0:
            copies[page // chunk].wait()

    hosted = decay_ref.at[:, pl.ds(OWNED_SLOTS, SPILL)]
    page_weights(queries, fills, keys_ref, hosted, *scratch, arrival=arrival)
    for copy in copies[pieces:]:
        copy.wait()
    scores_ref, _, tops_ref = scratch
    lane = lanes((span, 128))
    for page, (owner, rank) in enumerate(places):
        here = pl.ds(pl.multiple_of(rank * span, span), span)
        for pair in range(pairs):
            _, total, numer = page_sums(page, pair, span, values_ref, *scratch)
            out_ref[owner, here, pl.ds(pair * 128, 128)] = (numer / total).astype(bf16)
        tail = tail_ref[owner]
        base = rank * (3 * heads)
        for head in range(heads):
            rows = pl.ds(head * span, span)
            rest = tops_ref[page, rows, :] + jnp.log(scores_ref[page, rows, :])
            for piece in range(3):
                part = rest.astype(bf16).astype(f32)
                rest = rest - part
                tail = jnp.where(lane == base + piece * heads + head, part, tail)
        tail_ref[owner] = tail
    first = capacity * span
    for owner in range(groups):
        tail = tail_ref[owner].astype(bf16)
        for part in range(span // TAIL_ROWS):
            out_ref[owner, first : first + TAIL_ROWS, part * 128 : part * 128 + 128] = tail[
                part * TAIL_ROWS : part * TAIL_ROWS + TAIL_ROWS
            ]


def hosted_pages(request, fill, asked_rows, keys, values, decay, groups, capacity, local_count):
    count, span, inner = asked_rows.shape
    vmem = pl.BlockSpec(memory_space=pltpu.VMEM)
    hbm = pl.BlockSpec(memory_space=pltpu.HBM)
    pages = pltpu.VMEM((SPILL,) + keys.shape[1:], bf16)
    return pl.pallas_call(
        functools.partial(hosted_kernel, local_count, capacity),
        in_specs=[SMEM, SMEM, vmem, hbm, hbm, vmem],
        out_specs=vmem,
        out_shape=jax.ShapeDtypeStruct((groups, capacity * span + TAIL_ROWS, inner), bf16),
        scratch_shapes=[pages, pages, pltpu.SemaphoreType.DMA((8,))]
        + [pltpu.VMEM((groups, span, 128), f32), pltpu.SMEM((groups,), jnp.int32)]
        + page_scratch(SPILL, span, decay.shape[0]),
        compiler_params=pltpu.CompilerParams(vmem_limit_bytes=14 * MIB),
        cost_estimate=page_cost(SPILL, keys, 64),
        name="hosted_pages",
    )(request, fill, asked_rows, in_hbm(keys), in_hbm(values), decay)


def merge_kernel(
    capacity, steps, part, table_ref, back_ref, log_hbm, average_hbm, out_ref,
    top_ref, total_ref, numer_ref, tops_ref, sems,
):
    groups, _, inner = back_ref.shape
    rows = steps * BEAMS
    span = PARTS * rows
    heads = inner // 64
    state = (top_ref, total_ref, numer_ref)
    copies = start_all([(log_hbm.at[part], top_ref), (average_hbm.at[part], numer_ref)], sems)
    total_ref[...] = jnp.ones_like(total_ref)
    first = capacity * span
    tails = jnp.concatenate(
        [
            back_ref[owner, first : first + TAIL_ROWS, part * 128 : part * 128 + 128]
            for owner in range(groups)
        ],
        axis=0,
    )
    source, target = sublanes((128, inner)), lanes((128, inner)) // 64
    for rank in range(capacity):
        hit = source < 0
        for piece in range(3):
            hit = hit | (source == target + (rank * 3 + piece) * heads)
        tops_ref[:, rank * inner : rank * inner + inner] = dot(tails, hit.astype(f32).astype(bf16))
    for copy in copies:
        copy.wait()
    for owner in range(groups):
        for rank in range(capacity):
            local = table_ref[owner * capacity + rank]
            bias = jnp.where(local >= 0, 0.0, masked_score)
            top = tops_ref[owner * rows : owner * rows + rows, rank * inner : rank * inner + inner]
            start = rank * span + part * rows
            average = back_ref[owner, start : start + rows, :].astype(f32)
            here = pl.ds(pl.multiple_of(jnp.maximum(local, 0) * rows, rows), rows)
            absorb(state, here, slice(None), top + bias, 1.0, average)
    for index in range(top_ref.shape[0] // (2 * rows)):
        parts = []
        for half in range(2):
            here = slice((index * 2 + half) * rows, (index * 2 + half + 1) * rows)
            parts.append(numer_ref[here, :] / total_ref[here, :])
        for step in range(steps):
            both = jnp.concatenate([p[step * 8 : step * 8 + 8] for p in parts], axis=0)
            out_ref[step, index * 16 : index * 16 + 16, :] = both.astype(bf16)


def merge(part, table, back, logs, averages, steps, capacity):
    _, requests, span, inner = logs.shape
    rows = requests * span
    logs, averages = (x.reshape(PARTS, rows, inner) for x in (logs, averages))
    vmem = pl.BlockSpec(memory_space=pltpu.VMEM)
    hbm = pl.BlockSpec(memory_space=pltpu.HBM)
    return pl.pallas_call(
        functools.partial(merge_kernel, capacity, steps, part),
        in_specs=[SMEM, vmem, hbm, hbm],
        out_shape=jax.ShapeDtypeStruct((steps, rows // steps, inner), bf16),
        scratch_shapes=[pltpu.VMEM((rows, inner), f32)] * 3
        + [pltpu.VMEM((back.shape[0] * span, capacity * inner), f32), pltpu.SemaphoreType.DMA((2,))],
        compiler_params=pltpu.CompilerParams(vmem_limit_bytes=10 * MIB),
        cost_estimate=pl.CostEstimate(
            flops=40 * rows * inner, bytes_accessed=8 * MIB, transcendentals=4 * rows * inner
        ),
        name="merge",
    )(table, back, in_hbm(logs), in_hbm(averages))


def mix_kernel(
    first, att0, att1, att2, att3, w0, w1, w2, w3, tokens_hbm, gain_ref,
    residual_out, normed_ref, residual_ref, tokens_ref, attended_ref, weight_ref, sems,
):
    rows, width = residual_ref.shape
    inner = att0.shape[1]
    half = rows // 2
    head = lax.axis_index("head")
    near = pl.ds(pl.multiple_of(head % 2 * half, half), half)
    places = [pl.ds(pl.multiple_of((head ^ other) * inner, inner), inner) for other in range(4)]
    step = width // 3
    columns = [slice(start, start + step) for start in range(0, width, step)]
    pairs = [
        (weight.at[:, cols], weight_ref.at[place, cols])
        for cols in columns
        for weight, place in zip((w0, w1, w2, w3), places)
    ]
    copies = start_all(pairs + [(tokens_hbm.at[first : first + rows], tokens_ref)], sems)
    for att, place in zip((att0, att1, att2, att3), places):
        attended_ref[:, place] = att[...]
    for index, cols in enumerate(columns):
        for copy in copies[index * 4 : index * 4 + 4]:
            copy.wait()
        residual_ref[:, cols] = dot(attended_ref[...], weight_ref[:, cols])
    copies[-1].wait()
    gain = gain_ref[...]

    def norm(index, carry):
        here = pl.ds(pl.multiple_of(index * 32, 32), 32)
        x = tokens_ref[here, :].astype(f32) + residual_ref[here, :]
        residual_ref[here, :] = x
        scale = lax.rsqrt(jnp.mean(x * x, axis=-1, keepdims=True) + epsilon)
        normed_ref[here, :] = (x * scale * gain).astype(bf16)
        return carry

    lax.fori_loop(0, rows // 32, norm, 0, unroll=2)
    residual_out[...] = residual_ref[near, :]


def mix(first, attended, weights, tokens, gain):
    rows, inner = attended[0].shape
    width = tokens.shape[1]
    vmem = pl.BlockSpec(memory_space=pltpu.VMEM)
    hbm = pl.BlockSpec(memory_space=pltpu.HBM)
    return pl.pallas_call(
        functools.partial(mix_kernel, first),
        in_specs=[vmem] * 4 + [hbm] * 5 + [vmem],
        out_specs=[vmem] * 2,
        out_shape=[
            jax.ShapeDtypeStruct((rows // 2, width), f32),
            jax.ShapeDtypeStruct((rows, width), bf16),
        ],
        scratch_shapes=[
            pltpu.VMEM((rows, width), f32),
            pltpu.VMEM((rows, width), bf16),
            pltpu.VMEM((rows, 4 * inner), bf16),
            pltpu.VMEM((4 * inner, width), bf16),
            pltpu.SemaphoreType.DMA((13,)),
        ],
        compiler_params=pltpu.CompilerParams(vmem_limit_bytes=14 * MIB),
        cost_estimate=pl.CostEstimate(
            flops=8 * rows * width * inner, bytes_accessed=8 * MIB, transcendentals=rows
        ),
        name="mix",
    )(*attended, *[in_hbm(w) for w in weights], in_hbm(tokens), gain.reshape(1, -1))


def ffn_kernel(normed_ref, gate_ref, up_ref, down_ref, mine_ref, other_ref, hidden_ref, sums_ref):
    rows, width = normed_ref.shape
    half = rows // 2
    core = lax.axis_index("head") % 2
    near = pl.ds(pl.multiple_of(core * half, half), half)
    away = pl.ds(pl.multiple_of((1 - core) * half, half), half)
    for first in range(0, gate_ref.shape[1], 256):
        cols = slice(first, first + 256)
        gate = dot(normed_ref[...], gate_ref[:, cols])
        up = dot(normed_ref[...], up_ref[:, cols])
        hidden_ref[:, cols] = (gate / (1.0 + jnp.exp(-gate)) * up).astype(bf16)
    for first in range(0, width, 512):
        cols = slice(first, first + 512)
        sums_ref[...] = dot(hidden_ref[...], down_ref[:, cols])
        mine_ref[:, cols] = sums_ref[near, :]
        other_ref[:, cols] = sums_ref[away, :].astype(bf16)


def ffn(normed, w_gate, w_up, w_down):
    rows, width = normed.shape
    hidden = w_gate.shape[1]
    vmem = pl.BlockSpec(memory_space=pltpu.VMEM)
    return pl.pallas_call(
        ffn_kernel,
        in_specs=[vmem] * 4,
        out_specs=[vmem] * 2,
        out_shape=[
            jax.ShapeDtypeStruct((rows // 2, width), f32),
            jax.ShapeDtypeStruct((rows // 2, width), bf16),
        ],
        scratch_shapes=[pltpu.VMEM((rows, hidden), bf16), pltpu.VMEM((rows, 512), f32)],
        compiler_params=pltpu.CompilerParams(vmem_limit_bytes=10 * MIB),
        cost_estimate=pl.CostEstimate(
            flops=6 * rows * width * hidden, bytes_accessed=10 * MIB, transcendentals=rows * hidden
        ),
        name="ffn",
    )(in_vmem(normed), in_vmem(w_gate), in_vmem(w_up), in_vmem(w_down))


def finish_kernel(*refs):
    parts, out_ref = refs[:-1], refs[-1]
    core = lax.axis_index("head") % 2
    for index, part in enumerate(parts):
        step = index // 2 * 2 + (core if index % 2 == 0 else 1 - core)
        out_ref[step] = part[...]


def finish(parts):
    vmem = pl.BlockSpec(memory_space=pltpu.VMEM)
    return pl.pallas_call(
        finish_kernel,
        in_specs=[vmem] * len(parts),
        out_specs=vmem,
        out_shape=jax.ShapeDtypeStruct((len(parts),) + parts[0].shape, parts[0].dtype),
        compiler_params=pltpu.CompilerParams(vmem_limit_bytes=12 * MIB),
        name="finish",
    )(*parts)


def swap_core(value):
    return lax.ppermute(value, "head", [(i, i ^ 1) for i in range(4)])


def swap_chip(value):
    return lax.ppermute(value, "head", [(i, i ^ 2) for i in range(4)])


def shards(
    tokens, parents, page_request, page_fill, keys_pool, values_pool, decay_pool,
    gain_attn, w_query, w_key, w_value, w_forget, forget_bias, w_out,
    gain_ffn, w_gate, w_up, w_down,
):
    steps, rows, width = tokens.shape
    inner = w_query.shape[0]
    local_count = rows // BEAMS
    span = steps * BEAMS
    groups = lax.axis_size("group")
    capacity = (SPILL + groups - 2) // (groups - 1)
    decay = decay_pool.transpose(1, 0, 2)

    def exchange(value):
        return lax.all_to_all(value, "group", split_axis=0, concat_axis=0, tiled=True)

    ids = exchange(jnp.broadcast_to(page_request, (groups, 1, page_request.shape[0])))
    w_out_far = swap_chip(w_out)
    q_near, q, normed = queries_of(tokens, gain_attn, w_query)
    table, asked = ask(page_request, ids, q_near, span, capacity)
    asked_rows = exchange(asked.reshape(groups, capacity * span, inner)).reshape(asked.shape)
    own = own_pages(page_request, page_fill, q, keys_pool, values_pool, decay, span)
    asked_rows, own = lax.optimization_barrier((asked_rows, own))
    payload = hosted_pages(
        page_request, page_fill, asked_rows, keys_pool, values_pool, decay, groups, capacity, local_count
    )
    payload, normed = lax.optimization_barrier((payload, normed))
    back = exchange(payload)
    logs, averages = fresh(parents, forget_bias, normed, w_key, w_value, w_forget, q, own)
    weights = [w_out, swap_core(w_out), w_out_far, swap_core(w_out_far)]

    flat = tokens.reshape(steps * rows, width)
    each = steps // PARTS
    heres = [
        merge(index, table, back, logs, averages, each, capacity).reshape(each * rows, inner)
        for index in range(PARTS)
    ]
    fars = [swap_chip(here) for here in heres]
    residual, mine, other, chip, far_chip = [[None] * PARTS for _ in range(5)]
    for index, (here, far) in enumerate(zip(heres, fars)):
        gathered = [here, swap_core(here), far, swap_core(far)]
        if index:
            gathered, other[0] = lax.optimization_barrier((gathered, other[0]))
        residual[index], normed = mix(index * each * rows, gathered, weights, flat, gain_ffn)
        if index:
            chip[0] = (mine[0] + swap_core(other[0]).astype(f32)).astype(bf16)
            chip[0], normed = lax.optimization_barrier((chip[0], normed))
        mine[index], other[index] = ffn(normed, w_gate, w_up, w_down)
    far_chip[0] = swap_chip(chip[0])
    other[1], far_chip[0] = lax.optimization_barrier((other[1], far_chip[0]))
    chip[1] = (mine[1] + swap_core(other[1]).astype(f32)).astype(bf16)
    far_chip[1] = swap_chip(chip[1])
    parts = []
    for index in range(PARTS):
        both = chip[index].astype(f32) + far_chip[index].astype(f32)
        done = (residual[index] + both).astype(bf16)
        parts.extend([done, swap_core(done)])
    return finish(parts)


def solution(mesh):
    return jax.shard_map(
        shards,
        mesh=mesh,
        in_specs=(
            P(None, "group", None),
            P(None, "group"),
            P("group"),
            P("group"),
            P("group", "head", None),
            P("group", "head", None),
            P("group", "head", None),
            P(),
            P("head", None),
            P("head", None),
            P("head", None),
            P(None, "head"),
            P("head"),
            P("head", None),
            P(),
            P(None, "head"),
            P(None, "head"),
            P("head", None),
        ),
        out_specs=P(None, "group", None),
        check_vma=False,
    )
```

```python
import functools

import jax
import jax.numpy as jnp
from jax import lax
from jax.experimental import pallas as pl
from jax.experimental.pallas import tpu as pltpu
from jax.sharding import PartitionSpec as P

BEAMS = 8
OWNED_SLOTS = 32
SPILL = 16
PAGE_BLOCK = 16
PARTS = 2
TAIL_ROWS = 16
MIB = 1 << 20

epsilon = 1e-05
masked_score = -1e30
f32 = jnp.float32
bf16 = jnp.bfloat16

NN = (((1,), (0,)), ((), ()))
NT = (((1,), (1,)), ((), ()))
SMEM = pl.BlockSpec(memory_space=pltpu.SMEM)


def dot(a, b, dims=NN):
    return lax.dot_general(a, b, dims, preferred_element_type=f32)


def lanes(shape):
    return lax.broadcasted_iota(jnp.int32, shape, len(shape) - 1)


def sublanes(shape):
    return lax.broadcasted_iota(jnp.int32, shape, len(shape) - 2)


def in_hbm(array):
    return pltpu.with_memory_space_constraint(array, pltpu.HBM)


def in_vmem(array):
    return pltpu.with_memory_space_constraint(array, pltpu.VMEM)


def start_all(pairs, sems):
    copies = [pltpu.make_async_copy(s, t, sems.at[i]) for i, (s, t) in enumerate(pairs)]
    for copy in copies:
        copy.start()
    return copies


def fill_table(local_count, capacity, first, ids_ref, table_ref):
    groups = ids_ref.shape[0]
    for slot in range(groups * capacity):
        table_ref[slot] = -1

    def group(index, carry):
        rank = jnp.int32(0)
        for page in range(SPILL):
            local = ids_ref[index, 0, OWNED_SLOTS + page] - first
            mine = (local >= 0) & (local < local_count)

            @pl.when(mine)
            def _():
                table_ref[index * capacity + rank] = local

            rank = rank + mine.astype(jnp.int32)
        return carry

    lax.fori_loop(0, groups, group, 0)


def query_kernel(
    tokens_hbm, gain_ref, wq_hbm, q_ref, q_hbm, normed_hbm,
    tokens_ref, wq_ref, normed_ref, sems, out_sems,
):
    steps, rows, _ = tokens_ref.shape
    span = steps * BEAMS
    cut = rows // 2
    copies = start_all(
        [
            (tokens_hbm.at[:, :cut], tokens_ref.at[:, :cut]),
            (tokens_hbm.at[:, cut:], tokens_ref.at[:, cut:]),
            (wq_hbm, wq_ref),
        ],
        sems,
    )
    gain = gain_ref[...].reshape(1, -1)

    def pair(index, carry):
        slabs = []
        for step in range(steps):
            x = tokens_ref[step, pl.ds(pl.multiple_of(index * 16, 16), 16), :].astype(f32)
            scale = lax.rsqrt(jnp.mean(x * x, axis=-1, keepdims=True) + epsilon)
            slabs.append(x * scale * gain)
        for half in range(2):
            part = jnp.concatenate([s[half * 8 : half * 8 + 8] for s in slabs], axis=0)
            start = pl.multiple_of((index * 2 + half) * span, span)
            normed_ref[pl.ds(start, span), :] = part.astype(bf16)
        return carry

    copies[0].wait()
    lax.fori_loop(0, cut // 16, pair, 0, unroll=2)
    copies[1].wait()
    lax.fori_loop(cut // 16, rows // 16, pair, 0, unroll=2)
    leaving = start_all([(normed_ref, normed_hbm)], out_sems)
    copies[2].wait()
    query = dot(normed_ref[...], wq_ref[...], NT).astype(bf16)
    q_ref[...] = (query.astype(f32) * 0.125).astype(bf16)
    last = pltpu.make_async_copy(q_ref, q_hbm, out_sems.at[1])
    last.start()
    leaving[0].wait()
    last.wait()


def queries_of(tokens, gain, w_query):
    steps, rows, width = tokens.shape
    inner = w_query.shape[0]
    total = steps * rows
    hbm = pl.BlockSpec(memory_space=pltpu.HBM)
    vmem = pl.BlockSpec(memory_space=pltpu.VMEM)
    return pl.pallas_call(
        query_kernel,
        in_specs=[hbm, vmem, hbm],
        out_specs=[vmem, hbm, hbm],
        out_shape=[
            pltpu.VMEM((total, inner), bf16),
            pltpu.HBM((total, inner), bf16),
            pltpu.HBM((total, width), bf16),
        ],
        scratch_shapes=[
            pltpu.VMEM(tokens.shape, bf16),
            pltpu.VMEM(w_query.shape, bf16),
            pltpu.VMEM((total, width), bf16),
            pltpu.SemaphoreType.DMA((3,)),
            pltpu.SemaphoreType.DMA((2,)),
        ],
        compiler_params=pltpu.CompilerParams(vmem_limit_bytes=12 * MIB),
        cost_estimate=pl.CostEstimate(
            flops=2 * total * width * inner, bytes_accessed=6 * MIB, transcendentals=total
        ),
        name="queries",
    )(in_hbm(tokens), gain, in_hbm(w_query))


def ask_kernel(capacity, request_ref, ids_ref, q_ref, table_ref, out_ref):
    slots, span, _ = out_ref.shape
    local_count = q_ref.shape[0] // span
    first = request_ref[0] // local_count * local_count
    fill_table(local_count, capacity, first, ids_ref, table_ref)
    for slot in range(slots):
        start = jnp.maximum(table_ref[slot], 0) * span
        out_ref[slot] = q_ref[pl.ds(pl.multiple_of(start, span), span), :]


def ask(request, ids, q, span, capacity):
    slots = ids.shape[0] * capacity
    vmem = pl.BlockSpec(memory_space=pltpu.VMEM)
    return pl.pallas_call(
        functools.partial(ask_kernel, capacity),
        in_specs=[SMEM, SMEM, vmem],
        out_specs=[SMEM, vmem],
        out_shape=[
            jax.ShapeDtypeStruct((slots,), jnp.int32),
            jax.ShapeDtypeStruct((slots, span, q.shape[1]), bf16),
        ],
        compiler_params=pltpu.CompilerParams(vmem_limit_bytes=8 * MIB),
        name="ask",
    )(request, ids, in_vmem(q))


def half_masks(rows):
    low = lanes((rows, 128)) < 64
    return low.astype(f32).astype(bf16), jnp.logical_not(low).astype(f32).astype(bf16)


def stacked(pair_rows, masks):
    return jnp.concatenate([pair_rows * masks[0], pair_rows * masks[1]], axis=0)


def side_by_side(values, rows):
    low = lanes((rows, 128)) < 64
    top = jnp.broadcast_to(values[:rows], (rows, 128))
    bottom = jnp.broadcast_to(values[rows:], (rows, 128))
    return jnp.where(low, top, bottom)


def absorb(state, rows, columns, top, total, numer):
    top_ref, total_ref, numer_ref = state
    old = top_ref[rows, columns]
    new = jnp.maximum(old, top)
    keep = jnp.exp(old - new)
    add = jnp.exp(top - new)
    top_ref[rows, columns] = new
    total_ref[rows, columns] = total_ref[rows, columns] * keep + total * add
    numer_ref[rows, columns] = numer_ref[rows, columns] * keep + numer * add


def history(parents_ref, q_ref, k_ref, v_ref, forget_ref, state, scores_ref, weights_ref):
    transitions, rows = parents_ref.shape
    span = (transitions + 1) * BEAMS
    pack = 128 // span
    square = (128, 128)
    diagonal = sublanes(square) == lanes(square)
    columns = []
    for step in range(transitions):
        row = parents_ref[step : step + 1, :].astype(f32)
        columns.append(
            jnp.sum(jnp.where(diagonal, jnp.broadcast_to(row, square), 0.0), axis=1, keepdims=True)
        )
    lane8 = lanes((8, 128)).astype(f32)
    masks = half_masks(128)
    low = lanes(square) < 64
    top_ref, total_ref, numer_ref = state
    groups = rows // BEAMS // pack
    pairs = q_ref.shape[1] // 128
    for group in range(groups):
        slabs = []
        for member in range(pack):
            first = (group * pack + member) * BEAMS
            slabs.append(jnp.zeros((8, 128), f32))
            for step in range(transitions):
                wanted = columns[step][first : first + 8] + float(member * span + step * 8)
                slabs.append(jnp.where(lane8 == wanted, 1.0, 0.0))
        parent = jnp.concatenate(slabs, axis=0)
        parent16 = parent.astype(bf16)
        one = diagonal.astype(f32) + parent
        two = dot(parent16, parent16)
        ancestors = one + dot(two.astype(bf16), one.astype(bf16))
        here = pl.ds(group * 128, 128)
        running = lax.dot_general(
            ancestors, forget_ref[here, :], NN,
            precision=lax.Precision.HIGHEST, preferred_element_type=f32,
        ).T
        hidden = jnp.where(ancestors > 0.5, 0.0, masked_score)
        for pair in range(pairs):
            cols = pl.ds(pair * 128, 128)
            raw = dot(stacked(q_ref[here, cols], masks), k_ref[here, cols], NT)
            for half in range(2):
                head = pair * 2 + half
                scores_ref[group * pairs + pair, half] = raw[half * 128 : half * 128 + 128] + (
                    hidden - running[head : head + 1]
                )
    for group in range(groups):
        here = pl.ds(group * 128, 128)
        for pair in range(pairs):
            cols = pl.ds(pair * 128, 128)
            tops, totals = [], []
            for half in range(2):
                scores = scores_ref[group * pairs + pair, half]
                top = jnp.broadcast_to(jnp.max(scores, axis=-1, keepdims=True), square)
                weights = jnp.exp(scores - top)
                weights_ref[group * pairs + pair, pl.ds(half * 128, 128), :] = weights.astype(bf16)
                tops.append(top)
                totals.append(jnp.broadcast_to(jnp.sum(weights, axis=-1, keepdims=True), square))
            top_ref[here, cols] = jnp.where(low, *tops)
            total_ref[here, cols] = jnp.where(low, *totals)
    for group in range(groups):
        here = pl.ds(group * 128, 128)
        for pair in range(pairs):
            cols = pl.ds(pair * 128, 128)
            numer = dot(weights_ref[group * pairs + pair], v_ref[here, cols])
            numer_ref[here, cols] = jnp.where(low, numer[:128], numer[128:])


def fresh_kernel(
    parents_ref, bias_ref, normed_hbm, wk_hbm, wv_hbm, wf_hbm, q_hbm, top_hbm, total_hbm, numer_hbm,
    logs_hbm, averages_hbm,
    normed_ref, wk_ref, wv_ref, wf_ref, q_ref, top_own, total_own, numer_own,
    k_ref, v_ref, forget_ref, top_ref, total_ref, numer_ref, scores_ref, weights_ref,
    logs_ref, averages_ref, sems, out_sems,
):
    copies = start_all(
        [
            (normed_hbm, normed_ref), (wk_hbm, wk_ref), (wv_hbm, wv_ref), (wf_hbm, wf_ref),
            (q_hbm, q_ref), (top_hbm, top_own), (total_hbm, total_own), (numer_hbm, numer_own),
        ],
        sems,
    )
    copies[0].wait()
    copies[1].wait()
    k_ref[...] = dot(normed_ref[...], wk_ref[...], NT).astype(bf16)
    copies[2].wait()
    v_ref[...] = dot(normed_ref[...], wv_ref[...], NT).astype(bf16)
    copies[3].wait()
    gate = dot(normed_ref[...], wf_ref[...], NT) + bias_ref[...]
    forget = jnp.minimum(gate, 0.0) - jnp.log1p(jnp.exp(-jnp.abs(gate)))
    forget_ref[...] = jnp.zeros_like(forget_ref)
    forget_ref[:, : forget.shape[1]] = forget
    copies[4].wait()
    state = (top_ref, total_ref, numer_ref)
    history(parents_ref, q_ref, k_ref, v_ref, forget_ref, state, scores_ref, weights_ref)
    for copy in copies[5:]:
        copy.wait()

    parts, _, part = logs_ref.shape[:3]
    span = parts * part

    def join(index, carry):
        rows = pl.ds(pl.multiple_of(index * span, span), span)
        absorb(state, rows, slice(None), top_own[rows, :], total_own[rows, :], numer_own[rows, :])
        total = total_ref[rows, :]
        logs = top_ref[rows, :] + jnp.log(total)
        averages = numer_ref[rows, :] / total
        for number in range(parts):
            logs_ref[number, index] = logs[number * part : number * part + part]
            averages_ref[number, index] = averages[number * part : number * part + part]
        return carry

    lax.fori_loop(0, logs_ref.shape[1], join, 0, unroll=2)
    for copy in start_all([(logs_ref, logs_hbm), (averages_ref, averages_hbm)], out_sems):
        copy.wait()


def fresh(parents, bias, normed, w_key, w_value, w_forget, q, own):
    rows, inner = q.shape
    span = (parents.shape[0] + 1) * BEAMS
    vmem = pl.BlockSpec(memory_space=pltpu.VMEM)
    hbm = pl.BlockSpec(memory_space=pltpu.HBM)
    big = [normed, w_key, w_value, w_forget.T, q, *own]
    wide = pltpu.VMEM((rows, inner), f32)
    out = (PARTS, rows // span, span // PARTS, inner)
    tiles = rows * inner // (128 * 128)
    return pl.pallas_call(
        fresh_kernel,
        in_specs=[vmem, vmem] + [hbm] * len(big),
        out_specs=[hbm] * 2,
        out_shape=[pltpu.HBM(out, f32)] * 2,
        scratch_shapes=[pltpu.VMEM(x.shape, x.dtype) for x in big]
        + [pltpu.VMEM((rows, inner), bf16)] * 2
        + [pltpu.VMEM((rows, 128), f32), wide, wide, wide]
        + [pltpu.VMEM((tiles, 2, 128, 128), f32), pltpu.VMEM((tiles, 256, 128), bf16)]
        + [pltpu.VMEM(out, f32)] * 2
        + [pltpu.SemaphoreType.DMA((len(big),)), pltpu.SemaphoreType.DMA((2,))],
        compiler_params=pltpu.CompilerParams(vmem_limit_bytes=24 * MIB),
        cost_estimate=pl.CostEstimate(
            flops=4 * rows * normed.shape[1] * inner, bytes_accessed=12 * MIB,
            transcendentals=8 * rows * inner,
        ),
        name="fresh",
    )(parents, bias.reshape(1, -1), *[in_hbm(x) for x in big])


def page_weights(queries, fills, keys_ref, decay_ref, scores_ref, weights_ref, tops_ref):
    span = queries[0][0].shape[0]
    masks = half_masks(span)
    lane = lanes((1, 128))
    decay = [decay_ref[head].astype(f32) for head in range(decay_ref.shape[0])]
    for page, pairs in enumerate(queries):
        valid = lane < fills[page]
        for pair, query in enumerate(pairs):
            raw = dot(stacked(query, masks), keys_ref[page, pl.ds(pair * 128, 128), :])
            for half in range(2):
                head = pair * 2 + half
                bias = jnp.where(valid, decay[head][page : page + 1], masked_score)
                scores_ref[page, pl.ds(head * span, span), :] = (
                    raw[half * span : half * span + span] + bias
                )
    for page in range(len(queries)):
        for head in range(decay_ref.shape[0]):
            rows = pl.ds(head * span, span)
            scores = scores_ref[page, rows, :]
            top = jnp.broadcast_to(jnp.max(scores, axis=-1, keepdims=True), scores.shape)
            tops_ref[page, rows, :] = top
            weights = jnp.exp(scores - top)
            weights_ref[page, rows, :] = weights.astype(bf16)
            scores_ref[page, rows, :] = jnp.broadcast_to(
                jnp.sum(weights, axis=-1, keepdims=True), scores.shape
            )


def page_sums(page, pair, span, values_ref, scores_ref, weights_ref, tops_ref):
    low = lanes((span, 128)) < 64
    first, second = pl.ds(pair * 2 * span, span), pl.ds((pair * 2 + 1) * span, span)
    numer = dot(
        weights_ref[page, pl.ds(pair * 2 * span, 2 * span), :],
        values_ref[page, pl.ds(pair * 128, 128), :],
        NT,
    )
    top = jnp.where(low, tops_ref[page, first, :], tops_ref[page, second, :])
    total = jnp.where(low, scores_ref[page, first, :], scores_ref[page, second, :])
    return top, total, jnp.where(low, numer[:span], numer[span:])


def page_scratch(pages, span, heads):
    rows = span * heads
    return [
        pltpu.VMEM((pages, rows, 128), f32),
        pltpu.VMEM((pages, rows, 128), bf16),
        pltpu.VMEM((pages, rows, 128), f32),
    ]


def own_kernel(
    request_ref, fill_ref, q_ref, keys_ref, values_ref, decay_ref,
    top_ref, total_ref, numer_ref, *scratch,
):
    state = (top_ref, total_ref, numer_ref)
    span = scratch[0].shape[1] // decay_ref.shape[0]
    local_count = q_ref.shape[0] // span
    pairs = q_ref.shape[1] // 128

    block = pl.program_id(0)

    @pl.when(block == 0)
    def _():
        top_ref[...] = jnp.full_like(top_ref, masked_score)
        total_ref[...] = jnp.zeros_like(total_ref)
        numer_ref[...] = jnp.zeros_like(numer_ref)

    places, queries, fills = [], [], []
    for page in range(PAGE_BLOCK):
        index = block * PAGE_BLOCK + page
        local = lax.rem(request_ref[index], local_count)
        rows = pl.ds(pl.multiple_of(local * span, span), span)
        places.append(rows)
        queries.append([q_ref[rows, pl.ds(pair * 128, 128)] for pair in range(pairs)])
        fills.append(fill_ref[index])
    page_weights(queries, fills, keys_ref, decay_ref, *scratch)
    for page, rows in enumerate(places):
        for pair in range(pairs):
            sums = page_sums(page, pair, span, values_ref, *scratch)
            absorb(state, rows, pl.ds(pair * 128, 128), *sums)


def page_cost(pages, keys, rows):
    inner, length = keys.shape[1:]
    return pl.CostEstimate(
        flops=pages * rows * inner * length * 8,
        bytes_accessed=pages * inner * length * 4,
        transcendentals=pages * rows * inner * length // 64,
    )


def own_pages(request, fill, q, keys, values, decay, span):
    pool = pl.BlockSpec((PAGE_BLOCK,) + keys.shape[1:], lambda i: (i, 0, 0))
    decay_spec = pl.BlockSpec((decay.shape[0], PAGE_BLOCK, decay.shape[2]), lambda i: (0, i, 0))
    rows = pl.BlockSpec(q.shape, lambda i: (0, 0))
    return pl.pallas_call(
        own_kernel,
        grid=(OWNED_SLOTS // PAGE_BLOCK,),
        in_specs=[SMEM, SMEM, rows, pool, pool, decay_spec],
        out_specs=[rows] * 3,
        out_shape=[pltpu.HBM(q.shape, f32)] * 3,
        scratch_shapes=page_scratch(PAGE_BLOCK, span, decay.shape[0]),
        compiler_params=pltpu.CompilerParams(vmem_limit_bytes=20 * MIB),
        cost_estimate=page_cost(OWNED_SLOTS, keys, 64),
        name="own_pages",
    )(request, fill, in_hbm(q), in_hbm(keys), in_hbm(values), decay)


def hosted_kernel(
    local_count, capacity, request_ref, fill_ref, q_ref, keys_ref, values_ref, decay_ref,
    out_ref, tail_ref, count_ref, *scratch,
):
    span, inner = q_ref.shape[1:]
    pairs = inner // 128
    heads = decay_ref.shape[0]
    groups = out_ref.shape[0]
    out_ref[...] = jnp.zeros_like(out_ref)
    tail_ref[...] = jnp.zeros_like(tail_ref)
    for owner in range(groups):
        count_ref[owner] = 0
    places, queries, fills = [], [], []
    for page in range(SPILL):
        owner = request_ref[OWNED_SLOTS + page] // local_count
        rank = count_ref[owner]
        count_ref[owner] = rank + 1
        places.append((owner, rank))
        slot = owner * capacity + rank
        queries.append([q_ref[slot, :, pl.ds(pair * 128, 128)] for pair in range(pairs)])
        fills.append(fill_ref[OWNED_SLOTS + page])
    page_weights(queries, fills, keys_ref, decay_ref, *scratch)
    scores_ref, _, tops_ref = scratch
    lane = lanes((span, 128))
    for page, (owner, rank) in enumerate(places):
        here = pl.ds(pl.multiple_of(rank * span, span), span)
        for pair in range(pairs):
            _, total, numer = page_sums(page, pair, span, values_ref, *scratch)
            out_ref[owner, here, pl.ds(pair * 128, 128)] = (numer / total).astype(bf16)
        tail = tail_ref[owner]
        base = rank * (3 * heads)
        for head in range(heads):
            rows = pl.ds(head * span, span)
            rest = tops_ref[page, rows, :] + jnp.log(scores_ref[page, rows, :])
            for piece in range(3):
                part = rest.astype(bf16).astype(f32)
                rest = rest - part
                tail = jnp.where(lane == base + piece * heads + head, part, tail)
        tail_ref[owner] = tail
    first = capacity * span
    for owner in range(groups):
        tail = tail_ref[owner].astype(bf16)
        for part in range(span // TAIL_ROWS):
            out_ref[owner, first : first + TAIL_ROWS, part * 128 : part * 128 + 128] = tail[
                part * TAIL_ROWS : part * TAIL_ROWS + TAIL_ROWS
            ]


def hosted_pages(request, fill, asked_rows, keys, values, decay, groups, capacity, local_count):
    count, span, inner = asked_rows.shape
    shift = OWNED_SLOTS // SPILL
    pool = pl.BlockSpec((SPILL,) + keys.shape[1:], lambda i: (shift, 0, 0))
    decay_spec = pl.BlockSpec((decay.shape[0], SPILL, decay.shape[2]), lambda i: (0, shift, 0))
    out_shape = (groups, capacity * span + TAIL_ROWS, inner)
    return pl.pallas_call(
        functools.partial(hosted_kernel, local_count, capacity),
        grid=(1,),
        in_specs=[
            SMEM, SMEM, pl.BlockSpec(asked_rows.shape, lambda i: (0, 0, 0)), pool, pool, decay_spec
        ],
        out_specs=pl.BlockSpec(out_shape, lambda i: (0, 0, 0)),
        out_shape=jax.ShapeDtypeStruct(out_shape, bf16),
        scratch_shapes=[pltpu.VMEM((groups, span, 128), f32), pltpu.SMEM((groups,), jnp.int32)]
        + page_scratch(SPILL, span, decay.shape[0]),
        compiler_params=pltpu.CompilerParams(vmem_limit_bytes=24 * MIB),
        cost_estimate=page_cost(SPILL, keys, 64),
        name="hosted_pages",
    )(request, fill, asked_rows, in_hbm(keys), in_hbm(values), decay)


def merge_kernel(
    capacity, steps, part, table_ref, back_ref, log_hbm, average_hbm, *refs
):
    out_refs, (top_ref, total_ref, numer_ref, tops_ref, sems) = refs[:steps], refs[steps:]
    groups, _, inner = back_ref.shape
    rows = steps * BEAMS
    span = PARTS * rows
    heads = inner // 64
    state = (top_ref, total_ref, numer_ref)
    copies = start_all([(log_hbm.at[part], top_ref), (average_hbm.at[part], numer_ref)], sems)
    total_ref[...] = jnp.ones_like(total_ref)
    first = capacity * span
    tails = jnp.concatenate(
        [
            back_ref[owner, first : first + TAIL_ROWS, part * 128 : part * 128 + 128]
            for owner in range(groups)
        ],
        axis=0,
    )
    source, target = sublanes((128, inner)), lanes((128, inner)) // 64
    for rank in range(capacity):
        hit = source < 0
        for piece in range(3):
            hit = hit | (source == target + (rank * 3 + piece) * heads)
        tops_ref[:, rank * inner : rank * inner + inner] = dot(tails, hit.astype(f32).astype(bf16))
    for copy in copies:
        copy.wait()
    for owner in range(groups):
        for rank in range(capacity):
            local = table_ref[owner * capacity + rank]
            bias = jnp.where(local >= 0, 0.0, masked_score)
            top = tops_ref[owner * rows : owner * rows + rows, rank * inner : rank * inner + inner]
            start = rank * span + part * rows
            average = back_ref[owner, start : start + rows, :].astype(f32)
            here = pl.ds(pl.multiple_of(jnp.maximum(local, 0) * rows, rows), rows)
            absorb(state, here, slice(None), top + bias, 1.0, average)
    for index in range(top_ref.shape[0] // (2 * rows)):
        parts = []
        for half in range(2):
            here = slice((index * 2 + half) * rows, (index * 2 + half + 1) * rows)
            parts.append(numer_ref[here, :] / total_ref[here, :])
        for step in range(steps):
            both = jnp.concatenate([p[step * 8 : step * 8 + 8] for p in parts], axis=0)
            out_refs[step][index * 16 : index * 16 + 16, :] = both.astype(bf16)


def merge(part, table, back, logs, averages, steps, capacity):
    _, requests, span, inner = logs.shape
    rows = requests * span
    logs, averages = (x.reshape(PARTS, rows, inner) for x in (logs, averages))
    vmem = pl.BlockSpec(memory_space=pltpu.VMEM)
    hbm = pl.BlockSpec(memory_space=pltpu.HBM)
    return pl.pallas_call(
        functools.partial(merge_kernel, capacity, steps, part),
        in_specs=[SMEM, vmem, hbm, hbm],
        out_shape=[jax.ShapeDtypeStruct((rows // steps, inner), bf16)] * steps,
        scratch_shapes=[pltpu.VMEM((rows, inner), f32)] * 3
        + [pltpu.VMEM((back.shape[0] * span, capacity * inner), f32), pltpu.SemaphoreType.DMA((2,))],
        compiler_params=pltpu.CompilerParams(vmem_limit_bytes=10 * MIB),
        cost_estimate=pl.CostEstimate(
            flops=40 * rows * inner, bytes_accessed=8 * MIB, transcendentals=4 * rows * inner
        ),
        name="merge",
    )(table, back, in_hbm(logs), in_hbm(averages))


def arrange_kernel(w0, w1, w2, w3, out_ref, sems):
    inner = w0.shape[0]
    head = lax.axis_index("head")
    pairs = [
        (weight, out_ref.at[pl.ds(pl.multiple_of((head ^ other) * inner, inner), inner)])
        for other, weight in enumerate((w0, w1, w2, w3))
    ]
    for copy in start_all(pairs, sems):
        copy.wait()


def arrange(weights):
    inner, width = weights[0].shape
    anywhere = pl.BlockSpec(memory_space=pl.ANY)
    return pl.pallas_call(
        arrange_kernel,
        in_specs=[anywhere] * 4,
        out_specs=pl.BlockSpec(memory_space=pltpu.VMEM),
        out_shape=jax.ShapeDtypeStruct((4 * inner, width), bf16),
        scratch_shapes=[pltpu.SemaphoreType.DMA((4,))],
        compiler_params=pltpu.CompilerParams(vmem_limit_bytes=10 * MIB),
        cost_estimate=pl.CostEstimate(flops=0, bytes_accessed=8 * MIB, transcendentals=0),
        name="arrange",
    )(*weights)


def block_kernel(
    first, att0, att1, att2, att3, weight_ref, tokens_hbm, gain_ref, gate_ref, up_ref, down_ref,
    residual_out, mine_ref, other_ref,
    residual_ref, tokens_ref, attended_ref, normed_ref, hidden_ref, sums_ref, sems,
):
    rows, width = residual_ref.shape
    inner = att0.shape[1]
    half = rows // 2
    head = lax.axis_index("head")
    core = lax.rem(head, 2)
    near = pl.ds(pl.multiple_of(core * half, half), half)
    away = pl.ds(pl.multiple_of((1 - core) * half, half), half)
    copies = start_all([(tokens_hbm.at[first : first + rows], tokens_ref)], sems)
    for other, att in enumerate((att0, att1, att2, att3)):
        place = pl.ds(pl.multiple_of((head ^ other) * inner, inner), inner)
        attended_ref[:, place] = att[...]
    for start in range(0, width, 512):
        cols = slice(start, start + 512)
        residual_ref[:, cols] = dot(attended_ref[...], weight_ref[:, cols])
    copies[0].wait()
    gain = gain_ref[...].reshape(1, -1)

    def norm(index, carry):
        here = pl.ds(pl.multiple_of(index * 32, 32), 32)
        x = tokens_ref[here, :].astype(f32) + residual_ref[here, :]
        residual_ref[here, :] = x
        scale = lax.rsqrt(jnp.mean(x * x, axis=-1, keepdims=True) + epsilon)
        normed_ref[here, :] = (x * scale * gain).astype(bf16)
        return carry

    lax.fori_loop(0, rows // 32, norm, 0, unroll=2)
    for start in range(0, gate_ref.shape[1], 256):
        cols = slice(start, start + 256)
        gate = dot(normed_ref[...], gate_ref[:, cols])
        up = dot(normed_ref[...], up_ref[:, cols])
        hidden_ref[:, cols] = (gate / (1.0 + jnp.exp(-gate)) * up).astype(bf16)
    for start in range(0, width, 512):
        cols = slice(start, start + 512)
        sums_ref[:, cols] = dot(hidden_ref[...], down_ref[:, cols])
    residual_out[...] = residual_ref[near, :]
    mine_ref[...] = sums_ref[near, :]
    other_ref[...] = sums_ref[away, :].astype(bf16)


def block(first, attended, weight, tokens, gain, w_gate, w_up, w_down):
    rows, inner = attended[0].shape
    width = tokens.shape[1]
    hidden = w_gate.shape[1]
    vmem = pl.BlockSpec(memory_space=pltpu.VMEM)
    hbm = pl.BlockSpec(memory_space=pltpu.HBM)
    half = jax.ShapeDtypeStruct((rows // 2, width), f32)
    return pl.pallas_call(
        functools.partial(block_kernel, first),
        in_specs=[vmem] * 5 + [hbm] + [vmem] * 4,
        out_specs=[vmem] * 3,
        out_shape=[half, half, jax.ShapeDtypeStruct((rows // 2, width), bf16)],
        scratch_shapes=[
            pltpu.VMEM((rows, width), f32),
            pltpu.VMEM((rows, width), bf16),
            pltpu.VMEM((rows, 4 * inner), bf16),
            pltpu.VMEM((rows, width), bf16),
            pltpu.VMEM((rows, hidden), bf16),
            pltpu.VMEM((rows, width), f32),
            pltpu.SemaphoreType.DMA((1,)),
        ],
        compiler_params=pltpu.CompilerParams(vmem_limit_bytes=20 * MIB),
        cost_estimate=pl.CostEstimate(
            flops=2 * rows * width * (4 * inner + 3 * hidden), bytes_accessed=16 * MIB,
            transcendentals=rows * hidden,
        ),
        name="block",
    )(*attended, weight, in_hbm(tokens), gain, w_gate, w_up, w_down)


def finish_kernel(*refs):
    parts, out_ref = refs[:-1], refs[-1]
    core = lax.axis_index("head") % 2
    first = 0
    for index in range(0, len(parts), 2):
        half = parts[index].shape[0]
        for part, place in ((parts[index], core), (parts[index + 1], 1 - core)):
            rows = pl.ds(pl.multiple_of(first + place * half, half), half)
            out_ref[rows, :] = part[...]
        first += 2 * half


def finish(parts):
    vmem = pl.BlockSpec(memory_space=pltpu.VMEM)
    rows, width = sum(part.shape[0] for part in parts), parts[0].shape[1]
    return pl.pallas_call(
        finish_kernel,
        in_specs=[vmem] * len(parts),
        out_specs=vmem,
        out_shape=jax.ShapeDtypeStruct((rows, width), parts[0].dtype),
        compiler_params=pltpu.CompilerParams(vmem_limit_bytes=12 * MIB),
        name="finish",
    )(*parts)


def swap_core(value):
    return lax.ppermute(value, "head", [(i, i ^ 1) for i in range(4)])


def swap_chip(value):
    return lax.ppermute(value, "head", [(i, i ^ 2) for i in range(4)])


def shards(
    tokens, parents, page_request, page_fill, keys_pool, values_pool, decay_pool,
    gain_attn, w_query, w_key, w_value, w_forget, forget_bias, w_out,
    gain_ffn, w_gate, w_up, w_down,
):
    steps, rows, width = tokens.shape
    inner = w_query.shape[0]
    local_count = rows // BEAMS
    span = steps * BEAMS
    groups = lax.axis_size("group")
    capacity = (SPILL + groups - 2) // (groups - 1)
    decay = decay_pool.transpose(1, 0, 2)

    def exchange(value):
        return lax.all_to_all(value, "group", split_axis=0, concat_axis=0, tiled=True)

    ids = exchange(jnp.broadcast_to(page_request, (groups, 1, page_request.shape[0])))
    w_out_far = swap_chip(w_out)
    q_near, q, normed = queries_of(tokens, gain_attn, w_query)
    table, asked = ask(page_request, ids, q_near, span, capacity)
    asked_rows = exchange(asked.reshape(groups, capacity * span, inner)).reshape(asked.shape)
    own = own_pages(page_request, page_fill, q, keys_pool, values_pool, decay, span)
    asked_rows, own = lax.optimization_barrier((asked_rows, own))
    payload = hosted_pages(
        page_request, page_fill, asked_rows, keys_pool, values_pool, decay, groups, capacity, local_count
    )
    payload, normed = lax.optimization_barrier((payload, normed))
    back = exchange(payload)
    logs, averages = fresh(parents, forget_bias, normed, w_key, w_value, w_forget, q, own)
    weight = arrange([w_out, swap_core(w_out), w_out_far, swap_core(w_out_far)])
    logs, weight = lax.optimization_barrier((logs, weight))

    flat = tokens.reshape(steps * rows, width)
    each = steps // PARTS
    attended = []
    for index in range(PARTS):
        attended.extend(merge(index, table, back, logs, averages, each, capacity))
    heres = [attended[0], attended[1], jnp.concatenate(attended[2:], axis=0)]
    fars = [swap_chip(here) for here in heres]
    residual, mine, other, chip, far_chip = [], [], [], [], []
    first = 0
    for index, (here, far) in enumerate(zip(heres, fars)):
        gathered = [here, swap_core(here), far, swap_core(far)]
        if index:
            gathered, other[-1] = lax.optimization_barrier((gathered, other[-1]))
        if index > 1:
            gathered, chip[0] = lax.optimization_barrier((gathered, chip[0]))
        outs = block(first, gathered, weight, flat, gain_ffn, w_gate, w_up, w_down)
        for values, out in zip((residual, mine, other), outs):
            values.append(out)
        first += here.shape[0]
        if index:
            chip.append((mine[-2] + swap_core(other[-2]).astype(f32)).astype(bf16))
    chip.append((mine[-1] + swap_core(other[-1]).astype(f32)).astype(bf16))
    parts = []
    for index in range(len(chip)):
        if index:
            chip[index], far_chip[-1] = lax.optimization_barrier((chip[index], far_chip[-1]))
        far_chip.append(swap_chip(chip[index]))
    for index in range(len(chip)):
        both = chip[index].astype(f32) + far_chip[index].astype(f32)
        done = (residual[index] + both).astype(bf16)
        parts.extend([done, swap_core(done)])
    return finish(parts).reshape(steps, rows, width)


def solution(mesh):
    return jax.shard_map(
        shards,
        mesh=mesh,
        in_specs=(
            P(None, "group", None),
            P(None, "group"),
            P("group"),
            P("group"),
            P("group", "head", None),
            P("group", "head", None),
            P("group", "head", None),
            P(),
            P("head", None),
            P("head", None),
            P("head", None),
            P(None, "head"),
            P("head"),
            P("head", None),
            P(),
            P(None, "head"),
            P(None, "head"),
            P("head", None),
        ),
        out_specs=P(None, "group", None),
        check_vma=False,
    )
```

```python
import functools

import jax
import jax.numpy as jnp
from jax import lax
from jax.experimental import pallas as pl
from jax.experimental.pallas import tpu as pltpu
from jax.sharding import PartitionSpec as P

BEAMS = 8
OWNED_SLOTS = 32
SPILL = 16
PAGE_BLOCK = 16
PARTS = 2
TAIL_ROWS = 16
MIB = 1 << 20

epsilon = 1e-05
masked_score = -1e30
f32 = jnp.float32
bf16 = jnp.bfloat16

NN = (((1,), (0,)), ((), ()))
NT = (((1,), (1,)), ((), ()))
SMEM = pl.BlockSpec(memory_space=pltpu.SMEM)


def dot(a, b, dims=NN):
    return lax.dot_general(a, b, dims, preferred_element_type=f32)


def lanes(shape):
    return lax.broadcasted_iota(jnp.int32, shape, len(shape) - 1)


def sublanes(shape):
    return lax.broadcasted_iota(jnp.int32, shape, len(shape) - 2)


def in_hbm(array):
    return pltpu.with_memory_space_constraint(array, pltpu.HBM)


def in_vmem(array):
    return pltpu.with_memory_space_constraint(array, pltpu.VMEM)


def start_all(pairs, sems):
    copies = [pltpu.make_async_copy(s, t, sems.at[i]) for i, (s, t) in enumerate(pairs)]
    for copy in copies:
        copy.start()
    return copies


def fill_table(local_count, capacity, first, ids_ref, table_ref):
    groups = ids_ref.shape[0]
    for slot in range(groups * capacity):
        table_ref[slot] = -1

    def group(index, carry):
        rank = jnp.int32(0)
        for page in range(SPILL):
            local = ids_ref[index, 0, OWNED_SLOTS + page] - first
            mine = (local >= 0) & (local < local_count)

            @pl.when(mine)
            def _():
                table_ref[index * capacity + rank] = local

            rank = rank + mine.astype(jnp.int32)
        return carry

    lax.fori_loop(0, groups, group, 0)


def query_kernel(
    tokens_hbm, gain_ref, wq_hbm, q_ref, q_hbm, normed_hbm,
    tokens_ref, wq_ref, normed_ref, sems, out_sems,
):
    steps, rows, _ = tokens_ref.shape
    span = steps * BEAMS
    cut = rows // 2
    copies = start_all(
        [
            (tokens_hbm.at[:, :cut], tokens_ref.at[:, :cut]),
            (tokens_hbm.at[:, cut:], tokens_ref.at[:, cut:]),
            (wq_hbm, wq_ref),
        ],
        sems,
    )
    gain = gain_ref[...].reshape(1, -1)

    def pair(index, carry):
        slabs = []
        for step in range(steps):
            x = tokens_ref[step, pl.ds(pl.multiple_of(index * 16, 16), 16), :].astype(f32)
            scale = lax.rsqrt(jnp.mean(x * x, axis=-1, keepdims=True) + epsilon)
            slabs.append(x * scale * gain)
        for half in range(2):
            part = jnp.concatenate([s[half * 8 : half * 8 + 8] for s in slabs], axis=0)
            start = pl.multiple_of((index * 2 + half) * span, span)
            normed_ref[pl.ds(start, span), :] = part.astype(bf16)
        return carry

    copies[0].wait()
    lax.fori_loop(0, cut // 16, pair, 0, unroll=2)
    copies[1].wait()
    lax.fori_loop(cut // 16, rows // 16, pair, 0, unroll=2)
    leaving = start_all([(normed_ref, normed_hbm)], out_sems)
    copies[2].wait()
    query = dot(normed_ref[...], wq_ref[...], NT).astype(bf16)
    q_ref[...] = (query.astype(f32) * 0.125).astype(bf16)
    last = pltpu.make_async_copy(q_ref, q_hbm, out_sems.at[1])
    last.start()
    leaving[0].wait()
    last.wait()


def queries_of(tokens, gain, w_query):
    steps, rows, width = tokens.shape
    inner = w_query.shape[0]
    total = steps * rows
    hbm = pl.BlockSpec(memory_space=pltpu.HBM)
    vmem = pl.BlockSpec(memory_space=pltpu.VMEM)
    return pl.pallas_call(
        query_kernel,
        in_specs=[hbm, vmem, hbm],
        out_specs=[vmem, hbm, hbm],
        out_shape=[
            pltpu.VMEM((total, inner), bf16),
            pltpu.HBM((total, inner), bf16),
            pltpu.HBM((total, width), bf16),
        ],
        scratch_shapes=[
            pltpu.VMEM(tokens.shape, bf16),
            pltpu.VMEM(w_query.shape, bf16),
            pltpu.VMEM((total, width), bf16),
            pltpu.SemaphoreType.DMA((3,)),
            pltpu.SemaphoreType.DMA((2,)),
        ],
        compiler_params=pltpu.CompilerParams(vmem_limit_bytes=12 * MIB),
        cost_estimate=pl.CostEstimate(
            flops=2 * total * width * inner, bytes_accessed=6 * MIB, transcendentals=total
        ),
        name="queries",
    )(in_hbm(tokens), gain, in_hbm(w_query))


def ask_kernel(capacity, request_ref, ids_ref, q_ref, table_ref, out_ref):
    slots, span, _ = out_ref.shape
    local_count = q_ref.shape[0] // span
    first = request_ref[0] // local_count * local_count
    fill_table(local_count, capacity, first, ids_ref, table_ref)
    for slot in range(slots):
        start = jnp.maximum(table_ref[slot], 0) * span
        out_ref[slot] = q_ref[pl.ds(pl.multiple_of(start, span), span), :]


def ask(request, ids, q, span, capacity):
    slots = ids.shape[0] * capacity
    vmem = pl.BlockSpec(memory_space=pltpu.VMEM)
    return pl.pallas_call(
        functools.partial(ask_kernel, capacity),
        in_specs=[SMEM, SMEM, vmem],
        out_specs=[SMEM, vmem],
        out_shape=[
            jax.ShapeDtypeStruct((slots,), jnp.int32),
            jax.ShapeDtypeStruct((slots, span, q.shape[1]), bf16),
        ],
        compiler_params=pltpu.CompilerParams(vmem_limit_bytes=8 * MIB),
        name="ask",
    )(request, ids, in_vmem(q))


def half_masks(rows):
    low = lanes((rows, 128)) < 64
    return low.astype(f32).astype(bf16), jnp.logical_not(low).astype(f32).astype(bf16)


def stacked(pair_rows, masks):
    return jnp.concatenate([pair_rows * masks[0], pair_rows * masks[1]], axis=0)


def side_by_side(values, rows):
    low = lanes((rows, 128)) < 64
    top = jnp.broadcast_to(values[:rows], (rows, 128))
    bottom = jnp.broadcast_to(values[rows:], (rows, 128))
    return jnp.where(low, top, bottom)


def absorb(state, rows, columns, top, total, numer):
    top_ref, total_ref, numer_ref = state
    old = top_ref[rows, columns]
    new = jnp.maximum(old, top)
    keep = jnp.exp(old - new)
    add = jnp.exp(top - new)
    top_ref[rows, columns] = new
    total_ref[rows, columns] = total_ref[rows, columns] * keep + total * add
    numer_ref[rows, columns] = numer_ref[rows, columns] * keep + numer * add


def history(parents_ref, q_ref, k_ref, v_ref, forget_ref, state, scores_ref, weights_ref):
    transitions, rows = parents_ref.shape
    span = (transitions + 1) * BEAMS
    pack = 128 // span
    square = (128, 128)
    diagonal = sublanes(square) == lanes(square)
    columns = []
    for step in range(transitions):
        row = parents_ref[step : step + 1, :].astype(f32)
        columns.append(
            jnp.sum(jnp.where(diagonal, jnp.broadcast_to(row, square), 0.0), axis=1, keepdims=True)
        )
    lane8 = lanes((8, 128)).astype(f32)
    masks = half_masks(128)
    low = lanes(square) < 64
    top_ref, total_ref, numer_ref = state
    groups = rows // BEAMS // pack
    pairs = q_ref.shape[1] // 128
    for group in range(groups):
        slabs = []
        for member in range(pack):
            first = (group * pack + member) * BEAMS
            slabs.append(jnp.zeros((8, 128), f32))
            for step in range(transitions):
                wanted = columns[step][first : first + 8] + float(member * span + step * 8)
                slabs.append(jnp.where(lane8 == wanted, 1.0, 0.0))
        parent = jnp.concatenate(slabs, axis=0)
        parent16 = parent.astype(bf16)
        one = diagonal.astype(f32) + parent
        two = dot(parent16, parent16)
        ancestors = one + dot(two.astype(bf16), one.astype(bf16))
        here = pl.ds(group * 128, 128)
        running = lax.dot_general(
            ancestors, forget_ref[here, :], NN,
            precision=lax.Precision.HIGHEST, preferred_element_type=f32,
        ).T
        hidden = jnp.where(ancestors > 0.5, 0.0, masked_score)
        for pair in range(pairs):
            cols = pl.ds(pair * 128, 128)
            raw = dot(stacked(q_ref[here, cols], masks), k_ref[here, cols], NT)
            for half in range(2):
                head = pair * 2 + half
                scores_ref[group * pairs + pair, half] = raw[half * 128 : half * 128 + 128] + (
                    hidden - running[head : head + 1]
                )
    for group in range(groups):
        here = pl.ds(group * 128, 128)
        for pair in range(pairs):
            cols = pl.ds(pair * 128, 128)
            tops, totals = [], []
            for half in range(2):
                scores = scores_ref[group * pairs + pair, half]
                top = jnp.broadcast_to(jnp.max(scores, axis=-1, keepdims=True), square)
                weights = jnp.exp(scores - top)
                weights_ref[group * pairs + pair, pl.ds(half * 128, 128), :] = weights.astype(bf16)
                tops.append(top)
                totals.append(jnp.broadcast_to(jnp.sum(weights, axis=-1, keepdims=True), square))
            top_ref[here, cols] = jnp.where(low, *tops)
            total_ref[here, cols] = jnp.where(low, *totals)
    for group in range(groups):
        here = pl.ds(group * 128, 128)
        for pair in range(pairs):
            cols = pl.ds(pair * 128, 128)
            numer = dot(weights_ref[group * pairs + pair], v_ref[here, cols])
            numer_ref[here, cols] = jnp.where(low, numer[:128], numer[128:])


def fresh_kernel(
    parents_ref, bias_ref, normed_hbm, wk_hbm, wv_hbm, wf_hbm, q_hbm, top_hbm, total_hbm, numer_hbm,
    logs_hbm, averages_hbm,
    normed_ref, wk_ref, wv_ref, wf_ref, q_ref, top_own, total_own, numer_own,
    k_ref, v_ref, forget_ref, top_ref, total_ref, numer_ref, scores_ref, weights_ref,
    logs_ref, averages_ref, sems, out_sems,
):
    copies = start_all(
        [
            (normed_hbm, normed_ref), (wk_hbm, wk_ref), (wv_hbm, wv_ref), (wf_hbm, wf_ref),
            (q_hbm, q_ref), (top_hbm, top_own), (total_hbm, total_own), (numer_hbm, numer_own),
        ],
        sems,
    )
    copies[0].wait()
    copies[1].wait()
    k_ref[...] = dot(normed_ref[...], wk_ref[...], NT).astype(bf16)
    copies[2].wait()
    v_ref[...] = dot(normed_ref[...], wv_ref[...], NT).astype(bf16)
    copies[3].wait()
    gate = dot(normed_ref[...], wf_ref[...], NT) + bias_ref[...]
    forget = jnp.minimum(gate, 0.0) - jnp.log1p(jnp.exp(-jnp.abs(gate)))
    forget_ref[...] = jnp.zeros_like(forget_ref)
    forget_ref[:, : forget.shape[1]] = forget
    copies[4].wait()
    state = (top_ref, total_ref, numer_ref)
    history(parents_ref, q_ref, k_ref, v_ref, forget_ref, state, scores_ref, weights_ref)
    for copy in copies[5:]:
        copy.wait()

    parts, _, part = logs_ref.shape[:3]
    span = parts * part

    def join(index, carry):
        rows = pl.ds(pl.multiple_of(index * span, span), span)
        absorb(state, rows, slice(None), top_own[rows, :], total_own[rows, :], numer_own[rows, :])
        total = total_ref[rows, :]
        logs = top_ref[rows, :] + jnp.log(total)
        averages = numer_ref[rows, :] / total
        for number in range(parts):
            logs_ref[number, index] = logs[number * part : number * part + part]
            averages_ref[number, index] = averages[number * part : number * part + part]
        return carry

    lax.fori_loop(0, logs_ref.shape[1], join, 0, unroll=2)
    for copy in start_all([(logs_ref, logs_hbm), (averages_ref, averages_hbm)], out_sems):
        copy.wait()


def fresh(parents, bias, normed, w_key, w_value, w_forget, q, own):
    rows, inner = q.shape
    span = (parents.shape[0] + 1) * BEAMS
    vmem = pl.BlockSpec(memory_space=pltpu.VMEM)
    hbm = pl.BlockSpec(memory_space=pltpu.HBM)
    big = [normed, w_key, w_value, w_forget.T, q, *own]
    wide = pltpu.VMEM((rows, inner), f32)
    out = (PARTS, rows // span, span // PARTS, inner)
    tiles = rows * inner // (128 * 128)
    return pl.pallas_call(
        fresh_kernel,
        in_specs=[vmem, vmem] + [hbm] * len(big),
        out_specs=[hbm] * 2,
        out_shape=[pltpu.HBM(out, f32)] * 2,
        scratch_shapes=[pltpu.VMEM(x.shape, x.dtype) for x in big]
        + [pltpu.VMEM((rows, inner), bf16)] * 2
        + [pltpu.VMEM((rows, 128), f32), wide, wide, wide]
        + [pltpu.VMEM((tiles, 2, 128, 128), f32), pltpu.VMEM((tiles, 256, 128), bf16)]
        + [pltpu.VMEM(out, f32)] * 2
        + [pltpu.SemaphoreType.DMA((len(big),)), pltpu.SemaphoreType.DMA((2,))],
        compiler_params=pltpu.CompilerParams(vmem_limit_bytes=24 * MIB),
        cost_estimate=pl.CostEstimate(
            flops=4 * rows * normed.shape[1] * inner, bytes_accessed=12 * MIB,
            transcendentals=8 * rows * inner,
        ),
        name="fresh",
    )(parents, bias.reshape(1, -1), *[in_hbm(x) for x in big])


def page_weights(queries, fills, keys_ref, decay_ref, scores_ref, weights_ref, tops_ref):
    span = queries[0][0].shape[0]
    masks = half_masks(span)
    lane = lanes((1, 128))
    decay = [decay_ref[head].astype(f32) for head in range(decay_ref.shape[0])]
    for page, pairs in enumerate(queries):
        valid = lane < fills[page]
        for pair, query in enumerate(pairs):
            raw = dot(stacked(query, masks), keys_ref[page, pl.ds(pair * 128, 128), :])
            for half in range(2):
                head = pair * 2 + half
                bias = jnp.where(valid, decay[head][page : page + 1], masked_score)
                scores_ref[page, pl.ds(head * span, span), :] = (
                    raw[half * span : half * span + span] + bias
                )
    for page in range(len(queries)):
        for head in range(decay_ref.shape[0]):
            rows = pl.ds(head * span, span)
            scores = scores_ref[page, rows, :]
            top = jnp.broadcast_to(jnp.max(scores, axis=-1, keepdims=True), scores.shape)
            tops_ref[page, rows, :] = top
            weights = jnp.exp(scores - top)
            weights_ref[page, rows, :] = weights.astype(bf16)
            scores_ref[page, rows, :] = jnp.broadcast_to(
                jnp.sum(weights, axis=-1, keepdims=True), scores.shape
            )


def page_sums(page, pair, span, values_ref, scores_ref, weights_ref, tops_ref):
    low = lanes((span, 128)) < 64
    first, second = pl.ds(pair * 2 * span, span), pl.ds((pair * 2 + 1) * span, span)
    numer = dot(
        weights_ref[page, pl.ds(pair * 2 * span, 2 * span), :],
        values_ref[page, pl.ds(pair * 128, 128), :],
        NT,
    )
    top = jnp.where(low, tops_ref[page, first, :], tops_ref[page, second, :])
    total = jnp.where(low, scores_ref[page, first, :], scores_ref[page, second, :])
    return top, total, jnp.where(low, numer[:span], numer[span:])


def page_scratch(pages, span, heads):
    rows = span * heads
    return [
        pltpu.VMEM((pages, rows, 128), f32),
        pltpu.VMEM((pages, rows, 128), bf16),
        pltpu.VMEM((pages, rows, 128), f32),
    ]


def own_kernel(
    request_ref, fill_ref, q_ref, keys_ref, values_ref, decay_ref,
    top_ref, total_ref, numer_ref, *scratch,
):
    state = (top_ref, total_ref, numer_ref)
    span = scratch[0].shape[1] // decay_ref.shape[0]
    local_count = q_ref.shape[0] // span
    pairs = q_ref.shape[1] // 128

    block = pl.program_id(0)

    @pl.when(block == 0)
    def _():
        top_ref[...] = jnp.full_like(top_ref, masked_score)
        total_ref[...] = jnp.zeros_like(total_ref)
        numer_ref[...] = jnp.zeros_like(numer_ref)

    places, queries, fills = [], [], []
    for page in range(PAGE_BLOCK):
        index = block * PAGE_BLOCK + page
        local = lax.rem(request_ref[index], local_count)
        rows = pl.ds(pl.multiple_of(local * span, span), span)
        places.append(rows)
        queries.append([q_ref[rows, pl.ds(pair * 128, 128)] for pair in range(pairs)])
        fills.append(fill_ref[index])
    page_weights(queries, fills, keys_ref, decay_ref, *scratch)
    for page, rows in enumerate(places):
        for pair in range(pairs):
            sums = page_sums(page, pair, span, values_ref, *scratch)
            absorb(state, rows, pl.ds(pair * 128, 128), *sums)


def page_cost(pages, keys, rows):
    inner, length = keys.shape[1:]
    return pl.CostEstimate(
        flops=pages * rows * inner * length * 8,
        bytes_accessed=pages * inner * length * 4,
        transcendentals=pages * rows * inner * length // 64,
    )


def own_pages(request, fill, q, keys, values, decay, span):
    pool = pl.BlockSpec((PAGE_BLOCK,) + keys.shape[1:], lambda i: (i, 0, 0))
    decay_spec = pl.BlockSpec((decay.shape[0], PAGE_BLOCK, decay.shape[2]), lambda i: (0, i, 0))
    rows = pl.BlockSpec(q.shape, lambda i: (0, 0))
    return pl.pallas_call(
        own_kernel,
        grid=(OWNED_SLOTS // PAGE_BLOCK,),
        in_specs=[SMEM, SMEM, rows, pool, pool, decay_spec],
        out_specs=[rows] * 3,
        out_shape=[pltpu.HBM(q.shape, f32)] * 3,
        scratch_shapes=page_scratch(PAGE_BLOCK, span, decay.shape[0]),
        compiler_params=pltpu.CompilerParams(vmem_limit_bytes=20 * MIB),
        cost_estimate=page_cost(OWNED_SLOTS, keys, 64),
        name="own_pages",
    )(request, fill, in_hbm(q), in_hbm(keys), in_hbm(values), decay)


def hosted_kernel(
    local_count, capacity, request_ref, fill_ref, q_ref, keys_ref, values_ref, decay_ref,
    out_ref, tail_ref, count_ref, *scratch,
):
    span, inner = q_ref.shape[1:]
    pairs = inner // 128
    heads = decay_ref.shape[0]
    groups = out_ref.shape[0]
    out_ref[...] = jnp.zeros_like(out_ref)
    tail_ref[...] = jnp.zeros_like(tail_ref)
    for owner in range(groups):
        count_ref[owner] = 0
    places, queries, fills = [], [], []
    for page in range(SPILL):
        owner = request_ref[OWNED_SLOTS + page] // local_count
        rank = count_ref[owner]
        count_ref[owner] = rank + 1
        places.append((owner, rank))
        slot = owner * capacity + rank
        queries.append([q_ref[slot, :, pl.ds(pair * 128, 128)] for pair in range(pairs)])
        fills.append(fill_ref[OWNED_SLOTS + page])
    page_weights(queries, fills, keys_ref, decay_ref, *scratch)
    scores_ref, _, tops_ref = scratch
    lane = lanes((span, 128))
    for page, (owner, rank) in enumerate(places):
        here = pl.ds(pl.multiple_of(rank * span, span), span)
        for pair in range(pairs):
            _, total, numer = page_sums(page, pair, span, values_ref, *scratch)
            out_ref[owner, here, pl.ds(pair * 128, 128)] = (numer / total).astype(bf16)
        tail = tail_ref[owner]
        base = rank * (3 * heads)
        for head in range(heads):
            rows = pl.ds(head * span, span)
            rest = tops_ref[page, rows, :] + jnp.log(scores_ref[page, rows, :])
            for piece in range(3):
                part = rest.astype(bf16).astype(f32)
                rest = rest - part
                tail = jnp.where(lane == base + piece * heads + head, part, tail)
        tail_ref[owner] = tail
    first = capacity * span
    for owner in range(groups):
        tail = tail_ref[owner].astype(bf16)
        for part in range(span // TAIL_ROWS):
            out_ref[owner, first : first + TAIL_ROWS, part * 128 : part * 128 + 128] = tail[
                part * TAIL_ROWS : part * TAIL_ROWS + TAIL_ROWS
            ]


def hosted_pages(request, fill, asked_rows, keys, values, decay, groups, capacity, local_count):
    count, span, inner = asked_rows.shape
    shift = OWNED_SLOTS // SPILL
    pool = pl.BlockSpec((SPILL,) + keys.shape[1:], lambda i: (shift, 0, 0))
    decay_spec = pl.BlockSpec((decay.shape[0], SPILL, decay.shape[2]), lambda i: (0, shift, 0))
    out_shape = (groups, capacity * span + TAIL_ROWS, inner)
    return pl.pallas_call(
        functools.partial(hosted_kernel, local_count, capacity),
        grid=(1,),
        in_specs=[
            SMEM, SMEM, pl.BlockSpec(asked_rows.shape, lambda i: (0, 0, 0)), pool, pool, decay_spec
        ],
        out_specs=pl.BlockSpec(out_shape, lambda i: (0, 0, 0)),
        out_shape=jax.ShapeDtypeStruct(out_shape, bf16),
        scratch_shapes=[pltpu.VMEM((groups, span, 128), f32), pltpu.SMEM((groups,), jnp.int32)]
        + page_scratch(SPILL, span, decay.shape[0]),
        compiler_params=pltpu.CompilerParams(vmem_limit_bytes=24 * MIB),
        cost_estimate=page_cost(SPILL, keys, 64),
        name="hosted_pages",
    )(request, fill, asked_rows, in_hbm(keys), in_hbm(values), decay)


def merge_kernel(capacity, steps, part, table_ref, back_ref, log_hbm, average_hbm, *refs):
    loads = []
    if part == PARTS - 1:
        mixes, others, refs = refs[:4], refs[4:7], refs[7:]
        *refs, load_sems = refs
        out_ref, weight_ref, *targets = refs[:5]
        scratch = refs[5:]
        height = mixes[0].shape[0]
        head = lax.axis_index("head")
        pairs = [
            (mix, weight_ref.at[pl.ds(pl.multiple_of((head ^ other) * height, height), height)])
            for other, mix in enumerate(mixes)
        ]
        pairs.extend(zip(others, targets))
    else:
        out_ref, *scratch = refs
    top_ref, total_ref, numer_ref, tops_ref, sems = scratch
    groups, _, inner = back_ref.shape
    rows = steps * BEAMS
    span = PARTS * rows
    heads = inner // 64
    state = (top_ref, total_ref, numer_ref)
    copies = start_all([(log_hbm.at[part], top_ref), (average_hbm.at[part], numer_ref)], sems)
    if part == PARTS - 1:
        loads = start_all(pairs, load_sems)
    total_ref[...] = jnp.ones_like(total_ref)
    first = capacity * span
    tails = jnp.concatenate(
        [
            back_ref[owner, first : first + TAIL_ROWS, part * 128 : part * 128 + 128]
            for owner in range(groups)
        ],
        axis=0,
    )
    source, target = sublanes((128, inner)), lanes((128, inner)) // 64
    for rank in range(capacity):
        hit = source < 0
        for piece in range(3):
            hit = hit | (source == target + (rank * 3 + piece) * heads)
        tops_ref[:, rank * inner : rank * inner + inner] = dot(tails, hit.astype(f32).astype(bf16))
    for copy in copies:
        copy.wait()
    for owner in range(groups):
        for rank in range(capacity):
            local = table_ref[owner * capacity + rank]
            bias = jnp.where(local >= 0, 0.0, masked_score)
            top = tops_ref[owner * rows : owner * rows + rows, rank * inner : rank * inner + inner]
            start = rank * span + part * rows
            average = back_ref[owner, start : start + rows, :].astype(f32)
            here = pl.ds(pl.multiple_of(jnp.maximum(local, 0) * rows, rows), rows)
            absorb(state, here, slice(None), top + bias, 1.0, average)
    for index in range(top_ref.shape[0] // (2 * rows)):
        parts = []
        for half in range(2):
            here = slice((index * 2 + half) * rows, (index * 2 + half + 1) * rows)
            parts.append(numer_ref[here, :] / total_ref[here, :])
        for step in range(steps):
            both = jnp.concatenate([p[step * 8 : step * 8 + 8] for p in parts], axis=0)
            start = step * (top_ref.shape[0] // steps) + index * 16
            out_ref[start : start + 16, :] = both.astype(bf16)
    for copy in loads:
        copy.wait()


def merge(part, table, back, logs, averages, steps, capacity, mixes=(), others=()):
    _, requests, span, inner = logs.shape
    rows = requests * span
    logs, averages = (x.reshape(PARTS, rows, inner) for x in (logs, averages))
    vmem = pl.BlockSpec(memory_space=pltpu.VMEM)
    hbm = pl.BlockSpec(memory_space=pltpu.HBM)
    loads = [*mixes, *others]
    kept = [jax.ShapeDtypeStruct(x.shape, x.dtype) for x in others]
    if mixes:
        kept = [jax.ShapeDtypeStruct((4 * inner, mixes[0].shape[1]), bf16)] + kept
    return pl.pallas_call(
        functools.partial(merge_kernel, capacity, steps, part),
        in_specs=[SMEM, vmem, hbm, hbm]
        + [pl.BlockSpec(memory_space=pl.ANY)] * len(mixes)
        + [hbm] * len(others),
        out_shape=[jax.ShapeDtypeStruct((rows, inner), bf16)] + kept,
        scratch_shapes=[pltpu.VMEM((rows, inner), f32)] * 3
        + [pltpu.VMEM((back.shape[0] * span, capacity * inner), f32), pltpu.SemaphoreType.DMA((2,))]
        + [pltpu.SemaphoreType.DMA((len(loads),))] * bool(loads),
        compiler_params=pltpu.CompilerParams(vmem_limit_bytes=10 * MIB),
        cost_estimate=pl.CostEstimate(
            flops=40 * rows * inner, bytes_accessed=8 * MIB, transcendentals=4 * rows * inner
        ),
        name="merge",
    )(table, back, in_hbm(logs), in_hbm(averages), *mixes, *[in_hbm(x) for x in others])


def block_kernel(
    first, att0, att1, att2, att3, weight_ref, tokens_hbm, gain_ref, gate_ref, up_ref, down_ref,
    residual_out, mine_ref, other_ref,
    residual_ref, tokens_ref, attended_ref, normed_ref, hidden_ref, sums_ref, sems,
):
    rows, width = residual_ref.shape
    inner = att0.shape[1]
    half = rows // 2
    head = lax.axis_index("head")
    core = lax.rem(head, 2)
    near = pl.ds(pl.multiple_of(core * half, half), half)
    away = pl.ds(pl.multiple_of((1 - core) * half, half), half)
    copies = start_all([(tokens_hbm.at[first : first + rows], tokens_ref)], sems)
    for other, att in enumerate((att0, att1, att2, att3)):
        place = pl.ds(pl.multiple_of((head ^ other) * inner, inner), inner)
        attended_ref[:, place] = att[...]
    for start in range(0, width, 512):
        cols = slice(start, start + 512)
        residual_ref[:, cols] = dot(attended_ref[...], weight_ref[:, cols])
    copies[0].wait()
    gain = gain_ref[...].reshape(1, -1)

    def norm(index, carry):
        here = pl.ds(pl.multiple_of(index * 32, 32), 32)
        x = tokens_ref[here, :].astype(f32) + residual_ref[here, :]
        residual_ref[here, :] = x
        scale = lax.rsqrt(jnp.mean(x * x, axis=-1, keepdims=True) + epsilon)
        normed_ref[here, :] = (x * scale * gain).astype(bf16)
        return carry

    lax.fori_loop(0, rows // 32, norm, 0, unroll=2)
    for start in range(0, gate_ref.shape[1], 256):
        cols = slice(start, start + 256)
        gate = dot(normed_ref[...], gate_ref[:, cols])
        up = dot(normed_ref[...], up_ref[:, cols])
        hidden_ref[:, cols] = (gate / (1.0 + jnp.exp(-gate)) * up).astype(bf16)
    for start in range(0, width, 512):
        cols = slice(start, start + 512)
        sums_ref[:, cols] = dot(hidden_ref[...], down_ref[:, cols])
    residual_out[...] = residual_ref[near, :]
    mine_ref[...] = sums_ref[near, :]
    other_ref[...] = sums_ref[away, :].astype(bf16)


def block(first, attended, weight, tokens, gain, w_gate, w_up, w_down):
    rows, inner = attended[0].shape
    width = tokens.shape[1]
    hidden = w_gate.shape[1]
    vmem = pl.BlockSpec(memory_space=pltpu.VMEM)
    hbm = pl.BlockSpec(memory_space=pltpu.HBM)
    half = jax.ShapeDtypeStruct((rows // 2, width), f32)
    return pl.pallas_call(
        functools.partial(block_kernel, first),
        in_specs=[vmem] * 5 + [hbm] + [vmem] * 4,
        out_specs=[vmem] * 3,
        out_shape=[half, half, jax.ShapeDtypeStruct((rows // 2, width), bf16)],
        scratch_shapes=[
            pltpu.VMEM((rows, width), f32),
            pltpu.VMEM((rows, width), bf16),
            pltpu.VMEM((rows, 4 * inner), bf16),
            pltpu.VMEM((rows, width), bf16),
            pltpu.VMEM((rows, hidden), bf16),
            pltpu.VMEM((rows, width), f32),
            pltpu.SemaphoreType.DMA((1,)),
        ],
        compiler_params=pltpu.CompilerParams(vmem_limit_bytes=20 * MIB),
        cost_estimate=pl.CostEstimate(
            flops=2 * rows * width * (4 * inner + 3 * hidden), bytes_accessed=16 * MIB,
            transcendentals=rows * hidden,
        ),
        name="block",
    )(*attended, weight, in_hbm(tokens), gain, w_gate, w_up, w_down)


def finish_kernel(*refs):
    parts, out_ref = refs[:-1], refs[-1]
    core = lax.axis_index("head") % 2
    first = 0
    for index in range(0, len(parts), 2):
        half = parts[index].shape[0]
        for part, place in ((parts[index], core), (parts[index + 1], 1 - core)):
            rows = pl.ds(pl.multiple_of(first + place * half, half), half)
            out_ref[rows, :] = part[...]
        first += 2 * half


def finish(parts):
    vmem = pl.BlockSpec(memory_space=pltpu.VMEM)
    rows, width = sum(part.shape[0] for part in parts), parts[0].shape[1]
    return pl.pallas_call(
        finish_kernel,
        in_specs=[vmem] * len(parts),
        out_specs=vmem,
        out_shape=jax.ShapeDtypeStruct((rows, width), parts[0].dtype),
        compiler_params=pltpu.CompilerParams(vmem_limit_bytes=12 * MIB),
        name="finish",
    )(*parts)


def swap_core(value):
    return lax.ppermute(value, "head", [(i, i ^ 1) for i in range(4)])


def swap_chip(value):
    return lax.ppermute(value, "head", [(i, i ^ 2) for i in range(4)])


def shards(
    tokens, parents, page_request, page_fill, keys_pool, values_pool, decay_pool,
    gain_attn, w_query, w_key, w_value, w_forget, forget_bias, w_out,
    gain_ffn, w_gate, w_up, w_down,
):
    steps, rows, width = tokens.shape
    inner = w_query.shape[0]
    local_count = rows // BEAMS
    span = steps * BEAMS
    groups = lax.axis_size("group")
    capacity = (SPILL + groups - 2) // (groups - 1)
    decay = decay_pool.transpose(1, 0, 2)

    def exchange(value):
        return lax.all_to_all(value, "group", split_axis=0, concat_axis=0, tiled=True)

    ids = exchange(jnp.broadcast_to(page_request, (groups, 1, page_request.shape[0])))
    q_near, q, normed = queries_of(tokens, gain_attn, w_query)
    table, asked = ask(page_request, ids, q_near, span, capacity)
    asked, w_out = lax.optimization_barrier((asked, w_out))
    w_out_far = swap_chip(w_out)
    asked_rows = exchange(asked.reshape(groups, capacity * span, inner)).reshape(asked.shape)
    own = own_pages(page_request, page_fill, q, keys_pool, values_pool, decay, span)
    asked_rows, own = lax.optimization_barrier((asked_rows, own))
    payload = hosted_pages(
        page_request, page_fill, asked_rows, keys_pool, values_pool, decay, groups, capacity, local_count
    )
    payload, normed = lax.optimization_barrier((payload, normed))
    back = exchange(payload)
    logs, averages = fresh(parents, forget_bias, normed, w_key, w_value, w_forget, q, own)
    mixes = [w_out, swap_core(w_out), w_out_far, swap_core(w_out_far)]
    logs, mixes = lax.optimization_barrier((logs, mixes))

    flat = tokens.reshape(steps * rows, width)
    each = steps // PARTS
    heres = list(merge(0, table, back, logs, averages, each, capacity))
    back, heres[0] = lax.optimization_barrier((back, heres[0]))
    here, *weights = merge(
        1, table, back, logs, averages, each, capacity, mixes, [w_gate, w_up, w_down]
    )
    heres.append(here)
    fars = [swap_chip(here) for here in heres]
    fars[0], heres[1] = lax.optimization_barrier((fars[0], heres[1]))

    def block_of(index):
        here, far = heres[index], fars[index]
        gathered = [here, swap_core(here), far, swap_core(far)]
        if index:
            gathered, chip[0] = lax.optimization_barrier((gathered, chip[0]))
        return block(
            index * here.shape[0], gathered, weights[0], flat, gain_ffn, *weights[1:]
        )

    def chip_sum(mine, other):
        return (mine + swap_core(other).astype(f32)).astype(bf16)

    chip, residual = [None] * PARTS, [None] * PARTS
    residual[0], mine, other = block_of(0)
    other, fars[1] = lax.optimization_barrier((other, fars[1]))
    chip[0] = chip_sum(mine, other)
    most = chip[0].shape[0] // 4 * 3
    chip_most, chip_rest = chip[0][:most], chip[0][most:]
    far_most, far_rest = swap_chip(chip_most), swap_chip(chip_rest)
    residual[1], mine, other = block_of(1)
    other, far_most = lax.optimization_barrier((other, far_most))
    chip[1] = chip_sum(mine, other)
    chip[1], far_rest = lax.optimization_barrier((chip[1], far_rest))
    far_chip = [jnp.concatenate([far_most, far_rest], axis=0), swap_chip(chip[1])]
    parts = []
    for index in range(PARTS):
        both = chip[index].astype(f32) + far_chip[index].astype(f32)
        done = (residual[index] + both).astype(bf16)
        parts.extend([done, swap_core(done)])
    return finish(parts).reshape(steps, rows, width)


def solution(mesh):
    return jax.shard_map(
        shards,
        mesh=mesh,
        in_specs=(
            P(None, "group", None),
            P(None, "group"),
            P("group"),
            P("group"),
            P("group", "head", None),
            P("group", "head", None),
            P("group", "head", None),
            P(),
            P("head", None),
            P("head", None),
            P("head", None),
            P(None, "head"),
            P("head"),
            P("head", None),
            P(),
            P(None, "head"),
            P(None, "head"),
            P("head", None),
        ),
        out_specs=P(None, "group", None),
        check_vma=False,
    )
```

```python
import functools

import jax
import jax.numpy as jnp
from jax import lax
from jax.experimental import pallas as pl
from jax.experimental.pallas import tpu as pltpu
from jax.sharding import PartitionSpec as P

BEAMS = 8
OWNED_SLOTS = 32
SPILL = 16
PAGE_BLOCK = 16
PARTS = 2
MIB = 1 << 20

epsilon = 1e-05
masked_score = -1e30
f32 = jnp.float32
bf16 = jnp.bfloat16

NN = (((1,), (0,)), ((), ()))
NT = (((1,), (1,)), ((), ()))
SMEM = pl.BlockSpec(memory_space=pltpu.SMEM)


def dot(a, b, dims=NN):
    return lax.dot_general(a, b, dims, preferred_element_type=f32)


def lanes(shape):
    return lax.broadcasted_iota(jnp.int32, shape, len(shape) - 1)


def sublanes(shape):
    return lax.broadcasted_iota(jnp.int32, shape, len(shape) - 2)


def in_hbm(array):
    return pltpu.with_memory_space_constraint(array, pltpu.HBM)


def in_vmem(array):
    return pltpu.with_memory_space_constraint(array, pltpu.VMEM)


def start_all(pairs, sems):
    copies = [pltpu.make_async_copy(s, t, sems.at[i]) for i, (s, t) in enumerate(pairs)]
    for copy in copies:
        copy.start()
    return copies


def fill_table(local_count, capacity, first, ids_ref, table_ref):
    groups = ids_ref.shape[0]
    for slot in range(groups * capacity):
        table_ref[slot] = -1

    def group(index, carry):
        rank = jnp.int32(0)
        for page in range(SPILL):
            local = ids_ref[index, 0, OWNED_SLOTS + page] - first
            mine = (local >= 0) & (local < local_count)

            @pl.when(mine)
            def _():
                table_ref[index * capacity + rank] = local

            rank = rank + mine.astype(jnp.int32)
        return carry

    lax.fori_loop(0, groups, group, 0)


def query_kernel(
    tokens_hbm, gain_ref, wq_hbm, q_ref, q_hbm, normed_hbm,
    tokens_ref, wq_ref, normed_ref, sems, out_sems,
):
    steps, rows, _ = tokens_ref.shape
    span = steps * BEAMS
    cut = rows // 2
    copies = start_all(
        [
            (tokens_hbm.at[:, :cut], tokens_ref.at[:, :cut]),
            (tokens_hbm.at[:, cut:], tokens_ref.at[:, cut:]),
            (wq_hbm, wq_ref),
        ],
        sems,
    )
    gain = gain_ref[...].reshape(1, -1)

    def pair(index, carry):
        slabs = []
        for step in range(steps):
            x = tokens_ref[step, pl.ds(pl.multiple_of(index * 16, 16), 16), :].astype(f32)
            scale = lax.rsqrt(jnp.mean(x * x, axis=-1, keepdims=True) + epsilon)
            slabs.append(x * scale * gain)
        for half in range(2):
            part = jnp.concatenate([s[half * 8 : half * 8 + 8] for s in slabs], axis=0)
            start = pl.multiple_of((index * 2 + half) * span, span)
            normed_ref[pl.ds(start, span), :] = part.astype(bf16)
        return carry

    copies[0].wait()
    lax.fori_loop(0, cut // 16, pair, 0, unroll=2)
    copies[1].wait()
    lax.fori_loop(cut // 16, rows // 16, pair, 0, unroll=2)
    leaving = start_all([(normed_ref, normed_hbm)], out_sems)
    copies[2].wait()
    query = dot(normed_ref[...], wq_ref[...], NT).astype(bf16)
    q_ref[...] = (query.astype(f32) * 0.125).astype(bf16)
    last = pltpu.make_async_copy(q_ref, q_hbm, out_sems.at[1])
    last.start()
    leaving[0].wait()
    last.wait()


def queries_of(tokens, gain, w_query):
    steps, rows, width = tokens.shape
    inner = w_query.shape[0]
    total = steps * rows
    hbm = pl.BlockSpec(memory_space=pltpu.HBM)
    vmem = pl.BlockSpec(memory_space=pltpu.VMEM)
    return pl.pallas_call(
        query_kernel,
        in_specs=[hbm, vmem, hbm],
        out_specs=[vmem, hbm, hbm],
        out_shape=[
            pltpu.VMEM((total, inner), bf16),
            pltpu.HBM((total, inner), bf16),
            pltpu.HBM((total, width), bf16),
        ],
        scratch_shapes=[
            pltpu.VMEM(tokens.shape, bf16),
            pltpu.VMEM(w_query.shape, bf16),
            pltpu.VMEM((total, width), bf16),
            pltpu.SemaphoreType.DMA((3,)),
            pltpu.SemaphoreType.DMA((2,)),
        ],
        compiler_params=pltpu.CompilerParams(vmem_limit_bytes=12 * MIB),
        cost_estimate=pl.CostEstimate(
            flops=2 * total * width * inner, bytes_accessed=6 * MIB, transcendentals=total
        ),
        name="queries",
    )(in_hbm(tokens), gain, in_hbm(w_query))


def ask_kernel(capacity, request_ref, ids_ref, q_ref, table_ref, out_ref):
    slots, span, _ = out_ref.shape
    local_count = q_ref.shape[0] // span
    first = request_ref[0] // local_count * local_count
    fill_table(local_count, capacity, first, ids_ref, table_ref)
    for slot in range(slots):
        start = jnp.maximum(table_ref[slot], 0) * span
        out_ref[slot] = q_ref[pl.ds(pl.multiple_of(start, span), span), :]


def ask(request, ids, q, span, capacity):
    slots = ids.shape[0] * capacity
    vmem = pl.BlockSpec(memory_space=pltpu.VMEM)
    return pl.pallas_call(
        functools.partial(ask_kernel, capacity),
        in_specs=[SMEM, SMEM, vmem],
        out_specs=[SMEM, vmem],
        out_shape=[
            jax.ShapeDtypeStruct((slots,), jnp.int32),
            jax.ShapeDtypeStruct((slots, span, q.shape[1]), bf16),
        ],
        compiler_params=pltpu.CompilerParams(vmem_limit_bytes=8 * MIB),
        name="ask",
    )(request, ids, in_vmem(q))


def half_masks(rows):
    low = lanes((rows, 128)) < 64
    return low.astype(f32).astype(bf16), jnp.logical_not(low).astype(f32).astype(bf16)


def stacked(pair_rows, masks):
    return jnp.concatenate([pair_rows * masks[0], pair_rows * masks[1]], axis=0)


def side_by_side(values, rows):
    low = lanes((rows, 128)) < 64
    top = jnp.broadcast_to(values[:rows], (rows, 128))
    bottom = jnp.broadcast_to(values[rows:], (rows, 128))
    return jnp.where(low, top, bottom)


def absorb(state, rows, columns, top, total, numer):
    top_ref, total_ref, numer_ref = state
    old = top_ref[rows, columns]
    new = jnp.maximum(old, top)
    keep = jnp.exp(old - new)
    add = jnp.exp(top - new)
    top_ref[rows, columns] = new
    total_ref[rows, columns] = total_ref[rows, columns] * keep + total * add
    numer_ref[rows, columns] = numer_ref[rows, columns] * keep + numer * add


def history(parents_ref, q_ref, k_ref, v_ref, forget_ref, state, scores_ref, weights_ref):
    transitions, rows = parents_ref.shape
    span = (transitions + 1) * BEAMS
    pack = 128 // span
    square = (128, 128)
    diagonal = sublanes(square) == lanes(square)
    columns = []
    for step in range(transitions):
        row = parents_ref[step : step + 1, :].astype(f32)
        columns.append(
            jnp.sum(jnp.where(diagonal, jnp.broadcast_to(row, square), 0.0), axis=1, keepdims=True)
        )
    lane8 = lanes((8, 128)).astype(f32)
    masks = half_masks(128)
    low = lanes(square) < 64
    top_ref, total_ref, numer_ref = state
    groups = rows // BEAMS // pack
    pairs = q_ref.shape[1] // 128
    for group in range(groups):
        slabs = []
        for member in range(pack):
            first = (group * pack + member) * BEAMS
            slabs.append(jnp.zeros((8, 128), f32))
            for step in range(transitions):
                wanted = columns[step][first : first + 8] + float(member * span + step * 8)
                slabs.append(jnp.where(lane8 == wanted, 1.0, 0.0))
        parent = jnp.concatenate(slabs, axis=0)
        parent16 = parent.astype(bf16)
        one = diagonal.astype(f32) + parent
        two = dot(parent16, parent16)
        ancestors = one + dot(two.astype(bf16), one.astype(bf16))
        here = pl.ds(group * 128, 128)
        running = lax.dot_general(
            ancestors, forget_ref[here, :], NN,
            precision=lax.Precision.HIGHEST, preferred_element_type=f32,
        ).T
        hidden = jnp.where(ancestors > 0.5, 0.0, masked_score)
        for pair in range(pairs):
            cols = pl.ds(pair * 128, 128)
            raw = dot(stacked(q_ref[here, cols], masks), k_ref[here, cols], NT)
            for half in range(2):
                head = pair * 2 + half
                scores_ref[group * pairs + pair, half] = raw[half * 128 : half * 128 + 128] + (
                    hidden - running[head : head + 1]
                )
    for group in range(groups):
        here = pl.ds(group * 128, 128)
        for pair in range(pairs):
            cols = pl.ds(pair * 128, 128)
            tops, totals = [], []
            for half in range(2):
                scores = scores_ref[group * pairs + pair, half]
                top = jnp.broadcast_to(jnp.max(scores, axis=-1, keepdims=True), square)
                weights = jnp.exp(scores - top)
                weights_ref[group * pairs + pair, pl.ds(half * 128, 128), :] = weights.astype(bf16)
                tops.append(top)
                totals.append(jnp.broadcast_to(jnp.sum(weights, axis=-1, keepdims=True), square))
            top_ref[here, cols] = jnp.where(low, *tops)
            total_ref[here, cols] = jnp.where(low, *totals)
    for group in range(groups):
        here = pl.ds(group * 128, 128)
        for pair in range(pairs):
            cols = pl.ds(pair * 128, 128)
            numer = dot(weights_ref[group * pairs + pair], v_ref[here, cols])
            numer_ref[here, cols] = jnp.where(low, numer[:128], numer[128:])


def fresh_kernel(
    parents_ref, bias_ref, normed_hbm, wk_hbm, wv_hbm, wf_hbm, q_hbm, top_hbm, total_hbm, numer_hbm,
    logs_hbm, averages_hbm,
    normed_ref, wk_ref, wv_ref, wf_ref, q_ref, top_own, total_own, numer_own,
    k_ref, v_ref, forget_ref, top_ref, total_ref, numer_ref, scores_ref, weights_ref,
    logs_ref, averages_ref, sems, out_sems,
):
    copies = start_all(
        [
            (normed_hbm, normed_ref), (wk_hbm, wk_ref), (wv_hbm, wv_ref), (wf_hbm, wf_ref),
            (q_hbm, q_ref), (top_hbm, top_own), (total_hbm, total_own), (numer_hbm, numer_own),
        ],
        sems,
    )
    copies[0].wait()
    copies[1].wait()
    k_ref[...] = dot(normed_ref[...], wk_ref[...], NT).astype(bf16)
    copies[2].wait()
    v_ref[...] = dot(normed_ref[...], wv_ref[...], NT).astype(bf16)
    copies[3].wait()
    gate = dot(normed_ref[...], wf_ref[...], NT) + bias_ref[...]
    forget = jnp.minimum(gate, 0.0) - jnp.log1p(jnp.exp(-jnp.abs(gate)))
    forget_ref[...] = jnp.zeros_like(forget_ref)
    forget_ref[:, : forget.shape[1]] = forget
    copies[4].wait()
    state = (top_ref, total_ref, numer_ref)
    history(parents_ref, q_ref, k_ref, v_ref, forget_ref, state, scores_ref, weights_ref)
    for copy in copies[5:]:
        copy.wait()

    parts, _, part = logs_ref.shape[:3]
    span = parts * part

    def join(index, carry):
        rows = pl.ds(pl.multiple_of(index * span, span), span)
        absorb(state, rows, slice(None), top_own[rows, :], total_own[rows, :], numer_own[rows, :])
        total = total_ref[rows, :]
        logs = top_ref[rows, :] + jnp.log(total)
        averages = numer_ref[rows, :] / total
        for number in range(parts):
            logs_ref[number, index] = logs[number * part : number * part + part]
            averages_ref[number, index] = averages[number * part : number * part + part]
        return carry

    lax.fori_loop(0, logs_ref.shape[1], join, 0, unroll=2)
    for copy in start_all([(logs_ref, logs_hbm), (averages_ref, averages_hbm)], out_sems):
        copy.wait()


def fresh(parents, bias, normed, w_key, w_value, w_forget, q, own):
    rows, inner = q.shape
    span = (parents.shape[0] + 1) * BEAMS
    vmem = pl.BlockSpec(memory_space=pltpu.VMEM)
    hbm = pl.BlockSpec(memory_space=pltpu.HBM)
    big = [normed, w_key, w_value, w_forget.T, q, *own]
    wide = pltpu.VMEM((rows, inner), f32)
    out = (PARTS, rows // span, span // PARTS, inner)
    tiles = rows * inner // (128 * 128)
    return pl.pallas_call(
        fresh_kernel,
        in_specs=[vmem, vmem] + [hbm] * len(big),
        out_specs=[hbm] * 2,
        out_shape=[pltpu.HBM(out, f32)] * 2,
        scratch_shapes=[pltpu.VMEM(x.shape, x.dtype) for x in big]
        + [pltpu.VMEM((rows, inner), bf16)] * 2
        + [pltpu.VMEM((rows, 128), f32), wide, wide, wide]
        + [pltpu.VMEM((tiles, 2, 128, 128), f32), pltpu.VMEM((tiles, 256, 128), bf16)]
        + [pltpu.VMEM(out, f32)] * 2
        + [pltpu.SemaphoreType.DMA((len(big),)), pltpu.SemaphoreType.DMA((2,))],
        compiler_params=pltpu.CompilerParams(vmem_limit_bytes=24 * MIB),
        cost_estimate=pl.CostEstimate(
            flops=4 * rows * normed.shape[1] * inner, bytes_accessed=12 * MIB,
            transcendentals=8 * rows * inner,
        ),
        name="fresh",
    )(parents, bias.reshape(1, -1), *[in_hbm(x) for x in big])


def page_weights(queries, fills, keys_ref, decay_ref, scores_ref, weights_ref, tops_ref):
    span = queries[0][0].shape[0]
    masks = half_masks(span)
    lane = lanes((1, 128))
    decay = [decay_ref[head].astype(f32) for head in range(decay_ref.shape[0])]
    for page, pairs in enumerate(queries):
        valid = lane < fills[page]
        for pair, query in enumerate(pairs):
            raw = dot(stacked(query, masks), keys_ref[page, pl.ds(pair * 128, 128), :])
            for half in range(2):
                head = pair * 2 + half
                bias = jnp.where(valid, decay[head][page : page + 1], masked_score)
                scores_ref[page, pl.ds(head * span, span), :] = (
                    raw[half * span : half * span + span] + bias
                )
    for page in range(len(queries)):
        for head in range(decay_ref.shape[0]):
            rows = pl.ds(head * span, span)
            scores = scores_ref[page, rows, :]
            top = jnp.broadcast_to(jnp.max(scores, axis=-1, keepdims=True), scores.shape)
            tops_ref[page, rows, :] = top
            weights = jnp.exp(scores - top)
            weights_ref[page, rows, :] = weights.astype(bf16)
            scores_ref[page, rows, :] = jnp.broadcast_to(
                jnp.sum(weights, axis=-1, keepdims=True), scores.shape
            )


def page_sums(page, pair, span, values_ref, scores_ref, weights_ref, tops_ref):
    low = lanes((span, 128)) < 64
    first, second = pl.ds(pair * 2 * span, span), pl.ds((pair * 2 + 1) * span, span)
    numer = dot(
        weights_ref[page, pl.ds(pair * 2 * span, 2 * span), :],
        values_ref[page, pl.ds(pair * 128, 128), :],
        NT,
    )
    top = jnp.where(low, tops_ref[page, first, :], tops_ref[page, second, :])
    total = jnp.where(low, scores_ref[page, first, :], scores_ref[page, second, :])
    return top, total, jnp.where(low, numer[:span], numer[span:])


def page_scratch(pages, span, heads):
    rows = span * heads
    return [
        pltpu.VMEM((pages, rows, 128), f32),
        pltpu.VMEM((pages, rows, 128), bf16),
        pltpu.VMEM((pages, rows, 128), f32),
    ]


def own_kernel(
    request_ref, fill_ref, q_ref, keys_ref, values_ref, decay_ref,
    top_ref, total_ref, numer_ref, *scratch,
):
    state = (top_ref, total_ref, numer_ref)
    span = scratch[0].shape[1] // decay_ref.shape[0]
    local_count = q_ref.shape[0] // span
    pairs = q_ref.shape[1] // 128

    block = pl.program_id(0)

    @pl.when(block == 0)
    def _():
        top_ref[...] = jnp.full_like(top_ref, masked_score)
        total_ref[...] = jnp.zeros_like(total_ref)
        numer_ref[...] = jnp.zeros_like(numer_ref)

    places, queries, fills = [], [], []
    for page in range(PAGE_BLOCK):
        index = block * PAGE_BLOCK + page
        local = lax.rem(request_ref[index], local_count)
        rows = pl.ds(pl.multiple_of(local * span, span), span)
        places.append(rows)
        queries.append([q_ref[rows, pl.ds(pair * 128, 128)] for pair in range(pairs)])
        fills.append(fill_ref[index])
    page_weights(queries, fills, keys_ref, decay_ref, *scratch)
    for page, rows in enumerate(places):
        for pair in range(pairs):
            sums = page_sums(page, pair, span, values_ref, *scratch)
            absorb(state, rows, pl.ds(pair * 128, 128), *sums)


def page_cost(pages, keys, rows):
    inner, length = keys.shape[1:]
    return pl.CostEstimate(
        flops=pages * rows * inner * length * 8,
        bytes_accessed=pages * inner * length * 4,
        transcendentals=pages * rows * inner * length // 64,
    )


def own_pages(request, fill, q, keys, values, decay, span):
    pool = pl.BlockSpec((PAGE_BLOCK,) + keys.shape[1:], lambda i: (i, 0, 0))
    decay_spec = pl.BlockSpec((decay.shape[0], PAGE_BLOCK, decay.shape[2]), lambda i: (0, i, 0))
    rows = pl.BlockSpec(q.shape, lambda i: (0, 0))
    return pl.pallas_call(
        own_kernel,
        grid=(OWNED_SLOTS // PAGE_BLOCK,),
        in_specs=[SMEM, SMEM, rows, pool, pool, decay_spec],
        out_specs=[rows] * 3,
        out_shape=[pltpu.HBM(q.shape, f32)] * 3,
        scratch_shapes=page_scratch(PAGE_BLOCK, span, decay.shape[0]),
        compiler_params=pltpu.CompilerParams(vmem_limit_bytes=20 * MIB),
        cost_estimate=page_cost(OWNED_SLOTS, keys, 64),
        name="own_pages",
    )(request, fill, in_hbm(q), in_hbm(keys), in_hbm(values), decay)


def hosted_kernel(
    local_count, capacity, request_ref, fill_ref, q_ref, keys_ref, values_ref, decay_ref,
    out_ref, tail_ref, count_ref, *scratch,
):
    span, inner = q_ref.shape[1:]
    pairs = inner // 128
    heads = decay_ref.shape[0]
    groups = out_ref.shape[0]
    half = span // PARTS
    slot_rows = pairs * span
    out_ref[...] = jnp.zeros_like(out_ref)
    tail_ref[...] = jnp.zeros_like(tail_ref)
    for owner in range(groups):
        count_ref[owner] = 0
    places, queries, fills = [], [], []
    for page in range(SPILL):
        owner = request_ref[OWNED_SLOTS + page] // local_count
        rank = count_ref[owner]
        count_ref[owner] = rank + 1
        places.append((owner, rank))
        slot = owner * capacity + rank
        queries.append([q_ref[slot, :, pl.ds(pair * 128, 128)] for pair in range(pairs)])
        fills.append(fill_ref[OWNED_SLOTS + page])
    page_weights(queries, fills, keys_ref, decay_ref, *scratch)
    scores_ref, _, tops_ref = scratch
    lane = lanes((half, 128))
    for page, (owner, rank) in enumerate(places):
        for pair in range(pairs):
            _, total, numer = page_sums(page, pair, span, values_ref, *scratch)
            here = pl.ds(pl.multiple_of(rank * slot_rows + pair * span, span), span)
            out_ref[owner, here, :] = (numer / total).astype(bf16)
        tail = tail_ref[owner]
        base = rank * (3 * heads)
        for head in range(heads):
            rows = pl.ds(head * span, span)
            rest = tops_ref[page, rows, :] + jnp.log(scores_ref[page, rows, :])
            rest = jnp.where(lane < 64, rest[:half], rest[half:])
            for piece in range(3):
                part = rest.astype(bf16).astype(f32)
                rest = rest - part
                tail = jnp.where(lane % 64 == base + piece * heads + head, part, tail)
        tail_ref[owner] = tail
    first = capacity * slot_rows
    for owner in range(groups):
        out_ref[owner, first : first + half, :] = tail_ref[owner].astype(bf16)


def hosted_pages(request, fill, asked_rows, keys, values, decay, groups, capacity, local_count):
    count, span, inner = asked_rows.shape
    shift = OWNED_SLOTS // SPILL
    pool = pl.BlockSpec((SPILL,) + keys.shape[1:], lambda i: (shift, 0, 0))
    decay_spec = pl.BlockSpec((decay.shape[0], SPILL, decay.shape[2]), lambda i: (0, shift, 0))
    out_shape = (groups, capacity * span * inner // 128 + span // PARTS, 128)
    return pl.pallas_call(
        functools.partial(hosted_kernel, local_count, capacity),
        grid=(1,),
        in_specs=[
            SMEM, SMEM, pl.BlockSpec(asked_rows.shape, lambda i: (0, 0, 0)), pool, pool, decay_spec
        ],
        out_specs=pl.BlockSpec(out_shape, lambda i: (0, 0, 0)),
        out_shape=jax.ShapeDtypeStruct(out_shape, bf16),
        scratch_shapes=[pltpu.VMEM((groups, span // PARTS, 128), f32), pltpu.SMEM((groups,), jnp.int32)]
        + page_scratch(SPILL, span, decay.shape[0]),
        compiler_params=pltpu.CompilerParams(vmem_limit_bytes=24 * MIB),
        cost_estimate=page_cost(SPILL, keys, 64),
        name="hosted_pages",
    )(request, fill, asked_rows, in_hbm(keys), in_hbm(values), decay)


def merge_kernel(capacity, steps, part, heads, table_ref, back_ref, log_hbm, average_hbm, *refs):
    top_ref, total_ref, numer_ref, tops_ref, sems, load_sems = refs[-6:]
    count = load_sems.shape[0]
    sources, (out_ref, *targets) = refs[:count], refs[count:-6]
    groups = back_ref.shape[0]
    inner = heads * 64
    rows = steps * BEAMS
    span = PARTS * rows
    state = (top_ref, total_ref, numer_ref)
    copies = start_all([(log_hbm.at[part], top_ref), (average_hbm.at[part], numer_ref)], sems)
    pairs = []
    if part == 0:
        weight_ref, *targets = targets
        height = sources[0].shape[0]
        head = lax.axis_index("head")
        for other in range(4):
            place = pl.ds(pl.multiple_of((head ^ other) * height, height), height)
            pairs.append((sources[other], weight_ref.at[place]))
        sources = sources[4:]
    pairs.extend(zip(sources, targets))
    loads = start_all(pairs, load_sems)
    total_ref[...] = jnp.ones_like(total_ref)
    slot_rows = (inner // 128) * span
    first = capacity * slot_rows
    tails = jnp.concatenate(
        [back_ref[owner, first : first + rows, :] for owner in range(groups)], axis=0
    )
    source, target = sublanes((128, inner)), lanes((128, inner)) // 64
    for rank in range(capacity):
        hit = source < 0
        for piece in range(3):
            hit = hit | (source == target + part * 64 + (rank * 3 + piece) * heads)
        tops_ref[:, rank * inner : rank * inner + inner] = dot(tails, hit.astype(f32).astype(bf16))
    for copy in copies:
        copy.wait()
    for owner in range(groups):
        for rank in range(capacity):
            local = table_ref[owner * capacity + rank]
            bias = jnp.where(local >= 0, 0.0, masked_score)
            top = tops_ref[owner * rows : owner * rows + rows, rank * inner : rank * inner + inner]
            starts = [rank * slot_rows + pair * span + part * rows for pair in range(inner // 128)]
            average = jnp.concatenate(
                [back_ref[owner, start : start + rows, :].astype(f32) for start in starts], axis=1
            )
            here = pl.ds(pl.multiple_of(jnp.maximum(local, 0) * rows, rows), rows)
            absorb(state, here, slice(None), top + bias, 1.0, average)
    for index in range(top_ref.shape[0] // (2 * rows)):
        parts = []
        for half in range(2):
            here = slice((index * 2 + half) * rows, (index * 2 + half + 1) * rows)
            parts.append(numer_ref[here, :] / total_ref[here, :])
        for step in range(steps):
            both = jnp.concatenate([p[step * 8 : step * 8 + 8] for p in parts], axis=0)
            start = step * (top_ref.shape[0] // steps) + index * 16
            out_ref[start : start + 16, :] = both.astype(bf16)
    for copy in loads:
        copy.wait()


def merge(part, table, back, logs, averages, steps, capacity, sources):
    _, requests, span, inner = logs.shape
    rows = requests * span
    logs, averages = (x.reshape(PARTS, rows, inner) for x in (logs, averages))
    vmem = pl.BlockSpec(memory_space=pltpu.VMEM)
    hbm = pl.BlockSpec(memory_space=pltpu.HBM)
    anywhere = pl.BlockSpec(memory_space=pl.ANY)
    mixes = sources[:4] if part == 0 else []
    others = sources[len(mixes) :]
    kept = [jax.ShapeDtypeStruct(x.shape, x.dtype) for x in others]
    if mixes:
        kept = [jax.ShapeDtypeStruct((4 * inner, mixes[0].shape[1]), bf16)] + kept
    return pl.pallas_call(
        functools.partial(merge_kernel, capacity, steps, part, inner // 64),
        in_specs=[SMEM, vmem, hbm, hbm] + [anywhere] * len(mixes) + [hbm] * len(others),
        out_shape=[jax.ShapeDtypeStruct((rows, inner), bf16)] + kept,
        scratch_shapes=[pltpu.VMEM((rows, inner), f32)] * 3
        + [
            pltpu.VMEM((back.shape[0] * span, capacity * inner), f32),
            pltpu.SemaphoreType.DMA((2,)),
            pltpu.SemaphoreType.DMA((len(sources),)),
        ],
        compiler_params=pltpu.CompilerParams(vmem_limit_bytes=10 * MIB),
        cost_estimate=pl.CostEstimate(
            flops=40 * rows * inner, bytes_accessed=8 * MIB, transcendentals=4 * rows * inner
        ),
        name="merge",
    )(table, back, in_hbm(logs), in_hbm(averages), *mixes, *[in_hbm(x) for x in others])


def block_kernel(
    first, att0, att1, att2, att3, weight_ref, tokens_ref, gain_ref, gate_ref, up_ref, down_ref,
    residual_out, mine_ref, other_ref,
    residual_ref, attended_ref, scaled_ref, hidden_ref, sums_ref,
):
    rows, width = residual_ref.shape
    inner = att0.shape[1]
    half = rows // 2
    head = lax.axis_index("head")
    core = lax.rem(head, 2)
    near = pl.ds(pl.multiple_of(core * half, half), half)
    away = pl.ds(pl.multiple_of((1 - core) * half, half), half)
    for other, att in enumerate((att0, att1, att2, att3)):
        place = pl.ds(pl.multiple_of((head ^ other) * inner, inner), inner)
        attended_ref[:, place] = att[...]
    gain = gain_ref[...].reshape(1, -1)
    squares = jnp.zeros((rows, 1), f32)
    for start in range(0, width, 512):
        cols = slice(start, start + 512)
        x = tokens_ref[first : first + rows, cols].astype(f32) + dot(attended_ref[...], weight_ref[:, cols])
        residual_ref[:, cols] = x
        scaled_ref[:, cols] = (x * gain[:, cols]).astype(bf16)
        squares = squares + jnp.sum(x * x, axis=-1, keepdims=True)
    scale = lax.rsqrt(squares / width + epsilon)
    for start in range(0, gate_ref.shape[1], 256):
        cols = slice(start, start + 256)
        gate = dot(scaled_ref[...], gate_ref[:, cols]) * scale
        up = dot(scaled_ref[...], up_ref[:, cols]) * scale
        hidden_ref[:, cols] = (gate / (1.0 + jnp.exp(-gate)) * up).astype(bf16)
    residual_out[...] = residual_ref[near, :]
    for start in range(0, width, 512):
        cols = slice(start, start + 512)
        sums_ref[:, cols] = dot(hidden_ref[...], down_ref[:, cols])
    mine_ref[...] = sums_ref[near, :]
    other_ref[...] = sums_ref[away, :].astype(bf16)


def block(first, attended, weight, tokens, gain, w_gate, w_up, w_down):
    rows, inner = attended[0].shape
    width = tokens.shape[1]
    hidden = w_gate.shape[1]
    vmem = pl.BlockSpec(memory_space=pltpu.VMEM)
    half = jax.ShapeDtypeStruct((rows // 2, width), f32)
    return pl.pallas_call(
        functools.partial(block_kernel, first),
        in_specs=[vmem] * 10,
        out_specs=[vmem] * 3,
        out_shape=[half, half, jax.ShapeDtypeStruct((rows // 2, width), bf16)],
        scratch_shapes=[
            pltpu.VMEM((rows, width), f32),
            pltpu.VMEM((rows, 4 * inner), bf16),
            pltpu.VMEM((rows, width), bf16),
            pltpu.VMEM((rows, hidden), bf16),
            pltpu.VMEM((rows, width), f32),
        ],
        compiler_params=pltpu.CompilerParams(vmem_limit_bytes=20 * MIB),
        cost_estimate=pl.CostEstimate(
            flops=2 * rows * width * (4 * inner + 3 * hidden), bytes_accessed=16 * MIB,
            transcendentals=rows * hidden,
        ),
        name="block",
    )(*attended, weight, tokens, gain, w_gate, w_up, w_down)


def finish_kernel(*refs):
    parts, out_ref = refs[:-1], refs[-1]
    core = lax.axis_index("head") % 2
    first = 0
    for index in range(0, len(parts), 2):
        half = parts[index].shape[0]
        for part, place in ((parts[index], core), (parts[index + 1], 1 - core)):
            rows = pl.ds(pl.multiple_of(first + place * half, half), half)
            out_ref[rows, :] = part[...]
        first += 2 * half


def finish(parts):
    vmem = pl.BlockSpec(memory_space=pltpu.VMEM)
    rows, width = sum(part.shape[0] for part in parts), parts[0].shape[1]
    return pl.pallas_call(
        finish_kernel,
        in_specs=[vmem] * len(parts),
        out_specs=vmem,
        out_shape=jax.ShapeDtypeStruct((rows, width), parts[0].dtype),
        compiler_params=pltpu.CompilerParams(vmem_limit_bytes=12 * MIB),
        name="finish",
    )(*parts)


def swap_core(value):
    return lax.ppermute(value, "head", [(i, i ^ 1) for i in range(4)])


def swap_chip(value):
    return lax.ppermute(value, "head", [(i, i ^ 2) for i in range(4)])


def shards(
    tokens, parents, page_request, page_fill, keys_pool, values_pool, decay_pool,
    gain_attn, w_query, w_key, w_value, w_forget, forget_bias, w_out,
    gain_ffn, w_gate, w_up, w_down,
):
    steps, rows, width = tokens.shape
    inner = w_query.shape[0]
    local_count = rows // BEAMS
    span = steps * BEAMS
    groups = lax.axis_size("group")
    capacity = (SPILL + groups - 2) // (groups - 1)
    decay = decay_pool.transpose(1, 0, 2)

    def exchange(value):
        return lax.all_to_all(value, "group", split_axis=0, concat_axis=0, tiled=True)

    ids = exchange(jnp.broadcast_to(page_request, (groups, 1, page_request.shape[0])))
    q_near, q, normed = queries_of(tokens, gain_attn, w_query)
    table, asked = ask(page_request, ids, q_near, span, capacity)
    asked, w_out = lax.optimization_barrier((asked, w_out))
    w_out_far = swap_chip(w_out)
    asked_rows = exchange(asked.reshape(groups, capacity * span, inner)).reshape(asked.shape)
    own = own_pages(page_request, page_fill, q, keys_pool, values_pool, decay, span)
    asked_rows, own = lax.optimization_barrier((asked_rows, own))
    payload = hosted_pages(
        page_request, page_fill, asked_rows, keys_pool, values_pool, decay, groups, capacity, local_count
    )
    payload, normed = lax.optimization_barrier((payload, normed))
    back = exchange(payload)
    logs, averages = fresh(parents, forget_bias, normed, w_key, w_value, w_forget, q, own)
    mixes = [w_out, swap_core(w_out), w_out_far, swap_core(w_out_far)]
    logs, mixes = lax.optimization_barrier((logs, mixes))

    flat = tokens.reshape(steps * rows, width)
    each = steps // PARTS
    sums = (table, back, logs, averages, each, capacity)
    here, weight = merge(0, *sums, mixes)
    heres = [here]
    back, heres[0] = lax.optimization_barrier((back, heres[0]))
    sums = (table, back, logs, averages, each, capacity)
    here, w_gate, w_up, w_down, flat = merge(1, *sums, [w_gate, w_up, w_down, flat])
    heres.append(here)
    fars = [swap_chip(here) for here in heres]
    fars[0], heres[1] = lax.optimization_barrier((fars[0], heres[1]))

    def block_of(index):
        here, far = heres[index], fars[index]
        gathered = [here, swap_core(here), far, swap_core(far)]
        if index:
            gathered, chip[0] = lax.optimization_barrier((gathered, chip[0]))
        first = index * here.shape[0]
        return block(first, gathered, weight, flat, gain_ffn, w_gate, w_up, w_down)

    def chip_sum(mine, other):
        return (mine + swap_core(other).astype(f32)).astype(bf16)

    chip, residual = [None] * PARTS, [None] * PARTS
    residual[0], mine, other = block_of(0)
    other, fars[1] = lax.optimization_barrier((other, fars[1]))
    chip[0] = chip_sum(mine, other)
    most = chip[0].shape[0] // 8 * 5
    chip_most, chip_rest = chip[0][:most], chip[0][most:]
    far_most, far_rest = swap_chip(chip_most), swap_chip(chip_rest)
    residual[1], mine, other = block_of(1)
    other, far_most = lax.optimization_barrier((other, far_most))
    chip[1] = chip_sum(mine, other)
    far_chip = [jnp.concatenate([far_most, far_rest], axis=0), swap_chip(chip[1])]
    parts = []
    for index in range(PARTS):
        both = chip[index].astype(f32) + far_chip[index].astype(f32)
        done = (residual[index] + both).astype(bf16)
        parts.extend([done, swap_core(done)])
    return finish(parts).reshape(steps, rows, width)


def solution(mesh):
    return jax.shard_map(
        shards,
        mesh=mesh,
        in_specs=(
            P(None, "group", None),
            P(None, "group"),
            P("group"),
            P("group"),
            P("group", "head", None),
            P("group", "head", None),
            P("group", "head", None),
            P(),
            P("head", None),
            P("head", None),
            P("head", None),
            P(None, "head"),
            P("head"),
            P("head", None),
            P(),
            P(None, "head"),
            P(None, "head"),
            P("head", None),
        ),
        out_specs=P(None, "group", None),
        check_vma=False,
    )
```

```python
import functools

import jax
import jax.numpy as jnp
from jax import lax
from jax.experimental import pallas as pl
from jax.experimental.pallas import tpu as pltpu
from jax.sharding import PartitionSpec as P

BEAMS = 8
OWNED_SLOTS = 32
SPILL = 16
PAGE_BLOCK = 16
PARTS = 2
MIB = 1 << 20

epsilon = 1e-05
masked_score = -1e30
f32 = jnp.float32
bf16 = jnp.bfloat16

NN = (((1,), (0,)), ((), ()))
NT = (((1,), (1,)), ((), ()))
SMEM = pl.BlockSpec(memory_space=pltpu.SMEM)


def dot(a, b, dims=NN):
    return lax.dot_general(a, b, dims, preferred_element_type=f32)


def lanes(shape):
    return lax.broadcasted_iota(jnp.int32, shape, len(shape) - 1)


def sublanes(shape):
    return lax.broadcasted_iota(jnp.int32, shape, len(shape) - 2)


def in_hbm(array):
    return pltpu.with_memory_space_constraint(array, pltpu.HBM)


def in_vmem(array):
    return pltpu.with_memory_space_constraint(array, pltpu.VMEM)


def start_all(pairs, sems):
    copies = [pltpu.make_async_copy(s, t, sems.at[i]) for i, (s, t) in enumerate(pairs)]
    for copy in copies:
        copy.start()
    return copies


def fill_table(local_count, capacity, first, ids_ref, table_ref):
    groups = ids_ref.shape[0]
    for slot in range(groups * capacity):
        table_ref[slot] = -1

    def group(index, carry):
        rank = jnp.int32(0)
        for page in range(SPILL):
            local = ids_ref[index, 0, OWNED_SLOTS + page] - first
            mine = (local >= 0) & (local < local_count)

            @pl.when(mine)
            def _():
                table_ref[index * capacity + rank] = local

            rank = rank + mine.astype(jnp.int32)
        return carry

    lax.fori_loop(0, groups, group, 0)


def query_kernel(
    tokens_hbm, gain_ref, wq_hbm, q_ref, q_hbm, normed_hbm,
    tokens_ref, wq_ref, normed_ref, sems, out_sems,
):
    steps, rows, _ = tokens_ref.shape
    span = steps * BEAMS
    cut = rows // 2
    copies = start_all(
        [
            (tokens_hbm.at[:, :cut], tokens_ref.at[:, :cut]),
            (tokens_hbm.at[:, cut:], tokens_ref.at[:, cut:]),
            (wq_hbm, wq_ref),
        ],
        sems,
    )
    gain = gain_ref[...].reshape(1, -1)

    def pair(index, carry):
        slabs = []
        for step in range(steps):
            x = tokens_ref[step, pl.ds(pl.multiple_of(index * 16, 16), 16), :].astype(f32)
            scale = lax.rsqrt(jnp.mean(x * x, axis=-1, keepdims=True) + epsilon)
            slabs.append(x * scale * gain)
        for half in range(2):
            part = jnp.concatenate([s[half * 8 : half * 8 + 8] for s in slabs], axis=0)
            start = pl.multiple_of((index * 2 + half) * span, span)
            normed_ref[pl.ds(start, span), :] = part.astype(bf16)
        return carry

    copies[0].wait()
    lax.fori_loop(0, cut // 16, pair, 0, unroll=2)
    copies[1].wait()
    lax.fori_loop(cut // 16, rows // 16, pair, 0, unroll=2)
    leaving = start_all([(normed_ref, normed_hbm)], out_sems)
    copies[2].wait()
    query = dot(normed_ref[...], wq_ref[...], NT).astype(bf16)
    q_ref[...] = (query.astype(f32) * 0.125).astype(bf16)
    last = pltpu.make_async_copy(q_ref, q_hbm, out_sems.at[1])
    last.start()
    leaving[0].wait()
    last.wait()


def queries_of(tokens, gain, w_query):
    steps, rows, width = tokens.shape
    inner = w_query.shape[0]
    total = steps * rows
    hbm = pl.BlockSpec(memory_space=pltpu.HBM)
    vmem = pl.BlockSpec(memory_space=pltpu.VMEM)
    return pl.pallas_call(
        query_kernel,
        in_specs=[hbm, vmem, hbm],
        out_specs=[vmem, hbm, hbm],
        out_shape=[
            pltpu.VMEM((total, inner), bf16),
            pltpu.HBM((total, inner), bf16),
            pltpu.HBM((total, width), bf16),
        ],
        scratch_shapes=[
            pltpu.VMEM(tokens.shape, bf16),
            pltpu.VMEM(w_query.shape, bf16),
            pltpu.VMEM((total, width), bf16),
            pltpu.SemaphoreType.DMA((3,)),
            pltpu.SemaphoreType.DMA((2,)),
        ],
        compiler_params=pltpu.CompilerParams(vmem_limit_bytes=12 * MIB),
        cost_estimate=pl.CostEstimate(
            flops=2 * total * width * inner, bytes_accessed=6 * MIB, transcendentals=total
        ),
        name="queries",
    )(in_hbm(tokens), gain, in_hbm(w_query))


def ask_kernel(capacity, request_ref, ids_ref, q_ref, table_ref, out_ref):
    slots, span, _ = out_ref.shape
    local_count = q_ref.shape[0] // span
    first = request_ref[0] // local_count * local_count
    fill_table(local_count, capacity, first, ids_ref, table_ref)
    for slot in range(slots):
        start = jnp.maximum(table_ref[slot], 0) * span
        out_ref[slot] = q_ref[pl.ds(pl.multiple_of(start, span), span), :]


def ask(request, ids, q, span, capacity):
    slots = ids.shape[0] * capacity
    vmem = pl.BlockSpec(memory_space=pltpu.VMEM)
    return pl.pallas_call(
        functools.partial(ask_kernel, capacity),
        in_specs=[SMEM, SMEM, vmem],
        out_specs=[SMEM, vmem],
        out_shape=[
            jax.ShapeDtypeStruct((slots,), jnp.int32),
            jax.ShapeDtypeStruct((slots, span, q.shape[1]), bf16),
        ],
        compiler_params=pltpu.CompilerParams(vmem_limit_bytes=8 * MIB),
        name="ask",
    )(request, ids, in_vmem(q))


def half_masks(rows):
    low = lanes((rows, 128)) < 64
    return low.astype(f32).astype(bf16), jnp.logical_not(low).astype(f32).astype(bf16)


def stacked(pair_rows, masks):
    return jnp.concatenate([pair_rows * masks[0], pair_rows * masks[1]], axis=0)


def side_by_side(values, rows):
    low = lanes((rows, 128)) < 64
    top = jnp.broadcast_to(values[:rows], (rows, 128))
    bottom = jnp.broadcast_to(values[rows:], (rows, 128))
    return jnp.where(low, top, bottom)


def absorb(state, rows, columns, top, total, numer):
    top_ref, total_ref, numer_ref = state
    old = top_ref[rows, columns]
    new = jnp.maximum(old, top)
    keep = jnp.exp(old - new)
    add = jnp.exp(top - new)
    top_ref[rows, columns] = new
    total_ref[rows, columns] = total_ref[rows, columns] * keep + total * add
    numer_ref[rows, columns] = numer_ref[rows, columns] * keep + numer * add


def history(parents_ref, q_ref, k_ref, v_ref, forget_ref, state, scores_ref, weights_ref):
    transitions, rows = parents_ref.shape
    span = (transitions + 1) * BEAMS
    pack = 128 // span
    square = (128, 128)
    diagonal = sublanes(square) == lanes(square)
    columns = []
    for step in range(transitions):
        row = parents_ref[step : step + 1, :].astype(f32)
        columns.append(
            jnp.sum(jnp.where(diagonal, jnp.broadcast_to(row, square), 0.0), axis=1, keepdims=True)
        )
    lane8 = lanes((8, 128)).astype(f32)
    masks = half_masks(128)
    low = lanes(square) < 64
    top_ref, total_ref, numer_ref = state
    groups = rows // BEAMS // pack
    pairs = q_ref.shape[1] // 128
    for group in range(groups):
        slabs = []
        for member in range(pack):
            first = (group * pack + member) * BEAMS
            slabs.append(jnp.zeros((8, 128), f32))
            for step in range(transitions):
                wanted = columns[step][first : first + 8] + float(member * span + step * 8)
                slabs.append(jnp.where(lane8 == wanted, 1.0, 0.0))
        parent = jnp.concatenate(slabs, axis=0)
        parent16 = parent.astype(bf16)
        one = diagonal.astype(f32) + parent
        two = dot(parent16, parent16)
        ancestors = one + dot(two.astype(bf16), one.astype(bf16))
        here = pl.ds(group * 128, 128)
        running = lax.dot_general(
            ancestors, forget_ref[here, :], NN,
            precision=lax.Precision.HIGHEST, preferred_element_type=f32,
        ).T
        hidden = jnp.where(ancestors > 0.5, 0.0, masked_score)
        for pair in range(pairs):
            cols = pl.ds(pair * 128, 128)
            raw = dot(stacked(q_ref[here, cols], masks), k_ref[here, cols], NT)
            for half in range(2):
                head = pair * 2 + half
                scores_ref[group * pairs + pair, half] = raw[half * 128 : half * 128 + 128] + (
                    hidden - running[head : head + 1]
                )
    for group in range(groups):
        here = pl.ds(group * 128, 128)
        for pair in range(pairs):
            cols = pl.ds(pair * 128, 128)
            tops, totals = [], []
            for half in range(2):
                scores = scores_ref[group * pairs + pair, half]
                top = jnp.broadcast_to(jnp.max(scores, axis=-1, keepdims=True), square)
                weights = jnp.exp(scores - top)
                weights_ref[group * pairs + pair, pl.ds(half * 128, 128), :] = weights.astype(bf16)
                tops.append(top)
                totals.append(jnp.broadcast_to(jnp.sum(weights, axis=-1, keepdims=True), square))
            top_ref[here, cols] = jnp.where(low, *tops)
            total_ref[here, cols] = jnp.where(low, *totals)
    for group in range(groups):
        here = pl.ds(group * 128, 128)
        for pair in range(pairs):
            cols = pl.ds(pair * 128, 128)
            numer = dot(weights_ref[group * pairs + pair], v_ref[here, cols])
            numer_ref[here, cols] = jnp.where(low, numer[:128], numer[128:])


def fresh_kernel(
    parents_ref, bias_ref, normed_hbm, wk_hbm, wv_hbm, wf_hbm, q_hbm, top_hbm, total_hbm, numer_hbm,
    logs_hbm, averages_hbm,
    normed_ref, wk_ref, wv_ref, wf_ref, q_ref, top_own, total_own, numer_own,
    k_ref, v_ref, forget_ref, top_ref, total_ref, numer_ref, scores_ref, weights_ref,
    logs_ref, averages_ref, sems, out_sems,
):
    copies = start_all(
        [
            (normed_hbm, normed_ref), (wk_hbm, wk_ref), (wv_hbm, wv_ref), (wf_hbm, wf_ref),
            (q_hbm, q_ref), (top_hbm, top_own), (total_hbm, total_own), (numer_hbm, numer_own),
        ],
        sems,
    )
    copies[0].wait()
    copies[1].wait()
    k_ref[...] = dot(normed_ref[...], wk_ref[...], NT).astype(bf16)
    copies[2].wait()
    v_ref[...] = dot(normed_ref[...], wv_ref[...], NT).astype(bf16)
    copies[3].wait()
    gate = dot(normed_ref[...], wf_ref[...], NT) + bias_ref[...]
    forget = jnp.minimum(gate, 0.0) - jnp.log1p(jnp.exp(-jnp.abs(gate)))
    forget_ref[...] = jnp.zeros_like(forget_ref)
    forget_ref[:, : forget.shape[1]] = forget
    copies[4].wait()
    state = (top_ref, total_ref, numer_ref)
    history(parents_ref, q_ref, k_ref, v_ref, forget_ref, state, scores_ref, weights_ref)
    for copy in copies[5:]:
        copy.wait()

    parts, _, part = logs_ref.shape[:3]
    span = parts * part

    def join(index, carry):
        rows = pl.ds(pl.multiple_of(index * span, span), span)
        absorb(state, rows, slice(None), top_own[rows, :], total_own[rows, :], numer_own[rows, :])
        total = total_ref[rows, :]
        logs = top_ref[rows, :] + jnp.log(total)
        averages = numer_ref[rows, :] / total
        for number in range(parts):
            logs_ref[number, index] = logs[number * part : number * part + part]
            averages_ref[number, index] = averages[number * part : number * part + part]
        return carry

    lax.fori_loop(0, logs_ref.shape[1], join, 0, unroll=2)
    for copy in start_all([(logs_ref, logs_hbm), (averages_ref, averages_hbm)], out_sems):
        copy.wait()


def fresh(parents, bias, normed, w_key, w_value, w_forget, q, own):
    rows, inner = q.shape
    span = (parents.shape[0] + 1) * BEAMS
    vmem = pl.BlockSpec(memory_space=pltpu.VMEM)
    hbm = pl.BlockSpec(memory_space=pltpu.HBM)
    big = [normed, w_key, w_value, w_forget.T, q, *own]
    wide = pltpu.VMEM((rows, inner), f32)
    out = (PARTS, rows // span, span // PARTS, inner)
    tiles = rows * inner // (128 * 128)
    return pl.pallas_call(
        fresh_kernel,
        in_specs=[vmem, vmem] + [hbm] * len(big),
        out_specs=[hbm] * 2,
        out_shape=[pltpu.HBM(out, f32)] * 2,
        scratch_shapes=[pltpu.VMEM(x.shape, x.dtype) for x in big]
        + [pltpu.VMEM((rows, inner), bf16)] * 2
        + [pltpu.VMEM((rows, 128), f32), wide, wide, wide]
        + [pltpu.VMEM((tiles, 2, 128, 128), f32), pltpu.VMEM((tiles, 256, 128), bf16)]
        + [pltpu.VMEM(out, f32)] * 2
        + [pltpu.SemaphoreType.DMA((len(big),)), pltpu.SemaphoreType.DMA((2,))],
        compiler_params=pltpu.CompilerParams(vmem_limit_bytes=24 * MIB),
        cost_estimate=pl.CostEstimate(
            flops=4 * rows * normed.shape[1] * inner, bytes_accessed=12 * MIB,
            transcendentals=8 * rows * inner,
        ),
        name="fresh",
    )(parents, bias.reshape(1, -1), *[in_hbm(x) for x in big])


def page_weights(queries, fills, keys_ref, decay_ref, scores_ref, weights_ref, tops_ref):
    span = queries[0][0].shape[0]
    masks = half_masks(span)
    lane = lanes((1, 128))
    decay = [decay_ref[head].astype(f32) for head in range(decay_ref.shape[0])]
    for page, pairs in enumerate(queries):
        valid = lane < fills[page]
        for pair, query in enumerate(pairs):
            raw = dot(stacked(query, masks), keys_ref[page, pl.ds(pair * 128, 128), :])
            for half in range(2):
                head = pair * 2 + half
                bias = jnp.where(valid, decay[head][page : page + 1], masked_score)
                scores_ref[page, pl.ds(head * span, span), :] = (
                    raw[half * span : half * span + span] + bias
                )
    for page in range(len(queries)):
        for head in range(decay_ref.shape[0]):
            rows = pl.ds(head * span, span)
            scores = scores_ref[page, rows, :]
            top = jnp.broadcast_to(jnp.max(scores, axis=-1, keepdims=True), scores.shape)
            tops_ref[page, rows, :] = top
            weights = jnp.exp(scores - top)
            weights_ref[page, rows, :] = weights.astype(bf16)
            scores_ref[page, rows, :] = jnp.broadcast_to(
                jnp.sum(weights, axis=-1, keepdims=True), scores.shape
            )


def page_sums(page, pair, span, values_ref, scores_ref, weights_ref, tops_ref):
    low = lanes((span, 128)) < 64
    first, second = pl.ds(pair * 2 * span, span), pl.ds((pair * 2 + 1) * span, span)
    numer = dot(
        weights_ref[page, pl.ds(pair * 2 * span, 2 * span), :],
        values_ref[page, pl.ds(pair * 128, 128), :],
        NT,
    )
    top = jnp.where(low, tops_ref[page, first, :], tops_ref[page, second, :])
    total = jnp.where(low, scores_ref[page, first, :], scores_ref[page, second, :])
    return top, total, jnp.where(low, numer[:span], numer[span:])


def page_scratch(pages, span, heads):
    rows = span * heads
    return [
        pltpu.VMEM((pages, rows, 128), f32),
        pltpu.VMEM((pages, rows, 128), bf16),
        pltpu.VMEM((pages, rows, 128), f32),
    ]


def own_kernel(
    request_ref, fill_ref, q_ref, keys_ref, values_ref, decay_ref,
    top_ref, total_ref, numer_ref, *scratch,
):
    state = (top_ref, total_ref, numer_ref)
    span = scratch[0].shape[1] // decay_ref.shape[0]
    local_count = q_ref.shape[0] // span
    pairs = q_ref.shape[1] // 128

    block = pl.program_id(0)

    @pl.when(block == 0)
    def _():
        top_ref[...] = jnp.full_like(top_ref, masked_score)
        total_ref[...] = jnp.zeros_like(total_ref)
        numer_ref[...] = jnp.zeros_like(numer_ref)

    places, queries, fills = [], [], []
    for page in range(PAGE_BLOCK):
        index = block * PAGE_BLOCK + page
        local = lax.rem(request_ref[index], local_count)
        rows = pl.ds(pl.multiple_of(local * span, span), span)
        places.append(rows)
        queries.append([q_ref[rows, pl.ds(pair * 128, 128)] for pair in range(pairs)])
        fills.append(fill_ref[index])
    page_weights(queries, fills, keys_ref, decay_ref, *scratch)
    for page, rows in enumerate(places):
        for pair in range(pairs):
            sums = page_sums(page, pair, span, values_ref, *scratch)
            absorb(state, rows, pl.ds(pair * 128, 128), *sums)


def page_cost(pages, keys, rows):
    inner, length = keys.shape[1:]
    return pl.CostEstimate(
        flops=pages * rows * inner * length * 8,
        bytes_accessed=pages * inner * length * 4,
        transcendentals=pages * rows * inner * length // 64,
    )


def own_pages(request, fill, q, keys, values, decay, span):
    pool = pl.BlockSpec((PAGE_BLOCK,) + keys.shape[1:], lambda i: (i, 0, 0))
    decay_spec = pl.BlockSpec((decay.shape[0], PAGE_BLOCK, decay.shape[2]), lambda i: (0, i, 0))
    rows = pl.BlockSpec(q.shape, lambda i: (0, 0))
    return pl.pallas_call(
        own_kernel,
        grid=(OWNED_SLOTS // PAGE_BLOCK,),
        in_specs=[SMEM, SMEM, rows, pool, pool, decay_spec],
        out_specs=[rows] * 3,
        out_shape=[pltpu.HBM(q.shape, f32)] * 3,
        scratch_shapes=page_scratch(PAGE_BLOCK, span, decay.shape[0]),
        compiler_params=pltpu.CompilerParams(vmem_limit_bytes=20 * MIB),
        cost_estimate=page_cost(OWNED_SLOTS, keys, 64),
        name="own_pages",
    )(request, fill, in_hbm(q), in_hbm(keys), in_hbm(values), decay)


def hosted_kernel(
    local_count, capacity, request_ref, fill_ref, q_ref, keys_ref, values_ref, decay_ref,
    out_ref, tail_ref, count_ref, *scratch,
):
    span, inner = q_ref.shape[1:]
    pairs = inner // 128
    heads = decay_ref.shape[0]
    groups = out_ref.shape[0]
    half = span // PARTS
    slot_rows = pairs * span
    out_ref[...] = jnp.zeros_like(out_ref)
    tail_ref[...] = jnp.zeros_like(tail_ref)
    for owner in range(groups):
        count_ref[owner] = 0
    places, queries, fills = [], [], []
    for page in range(SPILL):
        owner = request_ref[OWNED_SLOTS + page] // local_count
        rank = count_ref[owner]
        count_ref[owner] = rank + 1
        places.append((owner, rank))
        slot = owner * capacity + rank
        queries.append([q_ref[slot, :, pl.ds(pair * 128, 128)] for pair in range(pairs)])
        fills.append(fill_ref[OWNED_SLOTS + page])
    page_weights(queries, fills, keys_ref, decay_ref, *scratch)
    scores_ref, _, tops_ref = scratch
    lane = lanes((half, 128))
    for page, (owner, rank) in enumerate(places):
        for pair in range(pairs):
            _, total, numer = page_sums(page, pair, span, values_ref, *scratch)
            here = pl.ds(pl.multiple_of(rank * slot_rows + pair * span, span), span)
            out_ref[owner, here, :] = (numer / total).astype(bf16)
        tail = tail_ref[owner]
        base = rank * (3 * heads)
        for head in range(heads):
            rows = pl.ds(head * span, span)
            rest = tops_ref[page, rows, :] + jnp.log(scores_ref[page, rows, :])
            rest = jnp.where(lane < 64, rest[:half], rest[half:])
            for piece in range(3):
                part = rest.astype(bf16).astype(f32)
                rest = rest - part
                tail = jnp.where(lane % 64 == base + piece * heads + head, part, tail)
        tail_ref[owner] = tail
    first = capacity * slot_rows
    for owner in range(groups):
        out_ref[owner, first : first + half, :] = tail_ref[owner].astype(bf16)


def hosted_pages(request, fill, asked_rows, keys, values, decay, groups, capacity, local_count):
    count, span, inner = asked_rows.shape
    shift = OWNED_SLOTS // SPILL
    pool = pl.BlockSpec((SPILL,) + keys.shape[1:], lambda i: (shift, 0, 0))
    decay_spec = pl.BlockSpec((decay.shape[0], SPILL, decay.shape[2]), lambda i: (0, shift, 0))
    out_shape = (groups, capacity * span * inner // 128 + span // PARTS, 128)
    return pl.pallas_call(
        functools.partial(hosted_kernel, local_count, capacity),
        grid=(1,),
        in_specs=[
            SMEM, SMEM, pl.BlockSpec(asked_rows.shape, lambda i: (0, 0, 0)), pool, pool, decay_spec
        ],
        out_specs=pl.BlockSpec(out_shape, lambda i: (0, 0, 0)),
        out_shape=jax.ShapeDtypeStruct(out_shape, bf16),
        scratch_shapes=[pltpu.VMEM((groups, span // PARTS, 128), f32), pltpu.SMEM((groups,), jnp.int32)]
        + page_scratch(SPILL, span, decay.shape[0]),
        compiler_params=pltpu.CompilerParams(vmem_limit_bytes=24 * MIB),
        cost_estimate=page_cost(SPILL, keys, 64),
        name="hosted_pages",
    )(request, fill, asked_rows, in_hbm(keys), in_hbm(values), decay)


def merge_kernel(capacity, steps, part, heads, table_ref, back_ref, log_hbm, average_hbm, *refs):
    top_ref, total_ref, numer_ref, tops_ref, sems, load_sems = refs[-6:]
    count = load_sems.shape[0]
    sources, (out_ref, *targets) = refs[:count], refs[count:-6]
    groups = back_ref.shape[0]
    inner = heads * 64
    rows = steps * BEAMS
    span = PARTS * rows
    state = (top_ref, total_ref, numer_ref)
    copies = start_all([(log_hbm.at[part], top_ref), (average_hbm.at[part], numer_ref)], sems)
    pairs = []
    if part == 0:
        weight_ref, *targets = targets
        height = sources[0].shape[0]
        head = lax.axis_index("head")
        for other in range(4):
            place = pl.ds(pl.multiple_of((head ^ other) * height, height), height)
            pairs.append((sources[other], weight_ref.at[place]))
        sources = sources[4:]
    pairs.extend(zip(sources, targets))
    loads = start_all(pairs, load_sems)
    total_ref[...] = jnp.ones_like(total_ref)
    slot_rows = (inner // 128) * span
    first = capacity * slot_rows
    tails = jnp.concatenate(
        [back_ref[owner, first : first + rows, :] for owner in range(groups)], axis=0
    )
    source, target = sublanes((128, inner)), lanes((128, inner)) // 64
    for rank in range(capacity):
        hit = source < 0
        for piece in range(3):
            hit = hit | (source == target + part * 64 + (rank * 3 + piece) * heads)
        tops_ref[:, rank * inner : rank * inner + inner] = dot(tails, hit.astype(f32).astype(bf16))
    for copy in copies:
        copy.wait()
    for owner in range(groups):
        for rank in range(capacity):
            local = table_ref[owner * capacity + rank]
            bias = jnp.where(local >= 0, 0.0, masked_score)
            top = tops_ref[owner * rows : owner * rows + rows, rank * inner : rank * inner + inner]
            starts = [rank * slot_rows + pair * span + part * rows for pair in range(inner // 128)]
            average = jnp.concatenate(
                [back_ref[owner, start : start + rows, :].astype(f32) for start in starts], axis=1
            )
            here = pl.ds(pl.multiple_of(jnp.maximum(local, 0) * rows, rows), rows)
            absorb(state, here, slice(None), top + bias, 1.0, average)
    for index in range(top_ref.shape[0] // (2 * rows)):
        parts = []
        for half in range(2):
            here = slice((index * 2 + half) * rows, (index * 2 + half + 1) * rows)
            parts.append(numer_ref[here, :] / total_ref[here, :])
        for step in range(steps):
            both = jnp.concatenate([p[step * 8 : step * 8 + 8] for p in parts], axis=0)
            start = step * (top_ref.shape[0] // steps) + index * 16
            out_ref[start : start + 16, :] = both.astype(bf16)
    for copy in loads:
        copy.wait()


def merge(part, table, back, logs, averages, steps, capacity, sources):
    _, requests, span, inner = logs.shape
    rows = requests * span
    logs, averages = (x.reshape(PARTS, rows, inner) for x in (logs, averages))
    vmem = pl.BlockSpec(memory_space=pltpu.VMEM)
    hbm = pl.BlockSpec(memory_space=pltpu.HBM)
    anywhere = pl.BlockSpec(memory_space=pl.ANY)
    mixes = sources[:4] if part == 0 else []
    others = sources[len(mixes) :]
    kept = [jax.ShapeDtypeStruct(x.shape, x.dtype) for x in others]
    if mixes:
        kept = [jax.ShapeDtypeStruct((4 * inner, mixes[0].shape[1]), bf16)] + kept
    return pl.pallas_call(
        functools.partial(merge_kernel, capacity, steps, part, inner // 64),
        in_specs=[SMEM, vmem, hbm, hbm] + [anywhere] * len(mixes) + [hbm] * len(others),
        out_shape=[jax.ShapeDtypeStruct((rows, inner), bf16)] + kept,
        scratch_shapes=[pltpu.VMEM((rows, inner), f32)] * 3
        + [
            pltpu.VMEM((back.shape[0] * span, capacity * inner), f32),
            pltpu.SemaphoreType.DMA((2,)),
            pltpu.SemaphoreType.DMA((len(sources),)),
        ],
        compiler_params=pltpu.CompilerParams(vmem_limit_bytes=10 * MIB),
        cost_estimate=pl.CostEstimate(
            flops=40 * rows * inner, bytes_accessed=8 * MIB, transcendentals=4 * rows * inner
        ),
        name="merge",
    )(table, back, in_hbm(logs), in_hbm(averages), *mixes, *[in_hbm(x) for x in others])


def block_kernel(
    first, att0, att1, att2, att3, weight_ref, tokens_ref, gain_ref, gate_ref, up_ref, down_ref,
    residual_out, mine_ref, other_ref,
    residual_ref, attended_ref, scaled_ref, hidden_ref, sums_ref,
):
    rows, width = residual_ref.shape
    inner = att0.shape[1]
    half = rows // 2
    head = lax.axis_index("head")
    core = lax.rem(head, 2)
    near = pl.ds(pl.multiple_of(core * half, half), half)
    away = pl.ds(pl.multiple_of((1 - core) * half, half), half)
    for other, att in enumerate((att0, att1, att2, att3)):
        place = pl.ds(pl.multiple_of((head ^ other) * inner, inner), inner)
        attended_ref[:, place] = att[...]
    gain = gain_ref[...].reshape(1, -1)
    squares = jnp.zeros((rows, 1), f32)
    for start in range(0, width, 512):
        cols = slice(start, start + 512)
        x = tokens_ref[first : first + rows, cols].astype(f32) + dot(attended_ref[...], weight_ref[:, cols])
        residual_ref[:, cols] = x
        scaled_ref[:, cols] = (x * gain[:, cols]).astype(bf16)
        squares = squares + jnp.sum(x * x, axis=-1, keepdims=True)
    scale = lax.rsqrt(squares / width + epsilon)
    for start in range(0, gate_ref.shape[1], 256):
        cols = slice(start, start + 256)
        gate = dot(scaled_ref[...], gate_ref[:, cols]) * scale
        up = dot(scaled_ref[...], up_ref[:, cols]) * scale
        hidden_ref[:, cols] = (gate / (1.0 + jnp.exp(-gate)) * up).astype(bf16)
    residual_out[...] = residual_ref[near, :]
    for start in range(0, width, 512):
        cols = slice(start, start + 512)
        sums_ref[:, cols] = dot(hidden_ref[...], down_ref[:, cols])
    mine_ref[...] = sums_ref[near, :]
    other_ref[...] = sums_ref[away, :].astype(bf16)


def block(first, attended, weight, tokens, gain, w_gate, w_up, w_down):
    rows, inner = attended[0].shape
    width = tokens.shape[1]
    hidden = w_gate.shape[1]
    vmem = pl.BlockSpec(memory_space=pltpu.VMEM)
    half = jax.ShapeDtypeStruct((rows // 2, width), f32)
    return pl.pallas_call(
        functools.partial(block_kernel, first),
        in_specs=[vmem] * 10,
        out_specs=[vmem] * 3,
        out_shape=[half, half, jax.ShapeDtypeStruct((rows // 2, width), bf16)],
        scratch_shapes=[
            pltpu.VMEM((rows, width), f32),
            pltpu.VMEM((rows, 4 * inner), bf16),
            pltpu.VMEM((rows, width), bf16),
            pltpu.VMEM((rows, hidden), bf16),
            pltpu.VMEM((rows, width), f32),
        ],
        compiler_params=pltpu.CompilerParams(vmem_limit_bytes=20 * MIB),
        cost_estimate=pl.CostEstimate(
            flops=2 * rows * width * (4 * inner + 3 * hidden), bytes_accessed=16 * MIB,
            transcendentals=rows * hidden,
        ),
        name="block",
    )(*attended, weight, tokens, gain, w_gate, w_up, w_down)


def finish_kernel(*refs):
    parts, out_ref = refs[:-1], refs[-1]
    core = lax.axis_index("head") % 2
    first = 0
    for index in range(0, len(parts), 2):
        half = parts[index].shape[0]
        for part, place in ((parts[index], core), (parts[index + 1], 1 - core)):
            rows = pl.ds(pl.multiple_of(first + place * half, half), half)
            out_ref[rows, :] = part[...]
        first += 2 * half


def finish(parts):
    vmem = pl.BlockSpec(memory_space=pltpu.VMEM)
    rows, width = sum(part.shape[0] for part in parts), parts[0].shape[1]
    return pl.pallas_call(
        finish_kernel,
        in_specs=[vmem] * len(parts),
        out_specs=vmem,
        out_shape=jax.ShapeDtypeStruct((rows, width), parts[0].dtype),
        compiler_params=pltpu.CompilerParams(vmem_limit_bytes=12 * MIB),
        name="finish",
    )(*parts)


def swap_core(value):
    return lax.ppermute(value, "head", [(i, i ^ 1) for i in range(4)])


def swap_chip(value):
    return lax.ppermute(value, "head", [(i, i ^ 2) for i in range(4)])


def shards(
    tokens, parents, page_request, page_fill, keys_pool, values_pool, decay_pool,
    gain_attn, w_query, w_key, w_value, w_forget, forget_bias, w_out,
    gain_ffn, w_gate, w_up, w_down,
):
    steps, rows, width = tokens.shape
    inner = w_query.shape[0]
    local_count = rows // BEAMS
    span = steps * BEAMS
    groups = lax.axis_size("group")
    capacity = (SPILL + groups - 2) // (groups - 1)
    decay = decay_pool.transpose(1, 0, 2)

    def exchange(value):
        return lax.all_to_all(value, "group", split_axis=0, concat_axis=0, tiled=True)

    ids = exchange(jnp.broadcast_to(page_request, (groups, 1, page_request.shape[0])))
    q_near, q, normed = queries_of(tokens, gain_attn, w_query)
    table, asked = ask(page_request, ids, q_near, span, capacity)
    asked, w_out = lax.optimization_barrier((asked, w_out))
    w_out_far = swap_chip(w_out)
    asked_rows = exchange(asked.reshape(groups, capacity * span, inner)).reshape(asked.shape)
    own = own_pages(page_request, page_fill, q, keys_pool, values_pool, decay, span)
    asked_rows, own = lax.optimization_barrier((asked_rows, own))
    payload = hosted_pages(
        page_request, page_fill, asked_rows, keys_pool, values_pool, decay, groups, capacity, local_count
    )
    payload, normed, w_out_far = lax.optimization_barrier((payload, normed, w_out_far))
    back = exchange(payload)
    logs, averages = fresh(parents, forget_bias, normed, w_key, w_value, w_forget, q, own)
    mixes = [w_out, swap_core(w_out), w_out_far, swap_core(w_out_far)]
    logs, mixes = lax.optimization_barrier((logs, mixes))

    flat = tokens.reshape(steps * rows, width)
    each = steps // PARTS
    sums = (table, back, logs, averages, each, capacity)
    here, weight = merge(0, *sums, mixes)
    heres = [here]
    back, heres[0] = lax.optimization_barrier((back, heres[0]))
    sums = (table, back, logs, averages, each, capacity)
    here, w_gate, w_up, w_down, flat = merge(1, *sums, [w_gate, w_up, w_down, flat])
    heres.append(here)
    fars = [swap_chip(here) for here in heres]
    fars[0], heres[1] = lax.optimization_barrier((fars[0], heres[1]))

    def block_of(index):
        here, far = heres[index], fars[index]
        gathered = [here, swap_core(here), far, swap_core(far)]
        if index:
            gathered, chip[0] = lax.optimization_barrier((gathered, chip[0]))
        first = index * here.shape[0]
        return block(first, gathered, weight, flat, gain_ffn, w_gate, w_up, w_down)

    def chip_sum(mine, other):
        return (mine + swap_core(other).astype(f32)).astype(bf16)

    chip, residual = [None] * PARTS, [None] * PARTS
    residual[0], mine, other = block_of(0)
    other, fars[1] = lax.optimization_barrier((other, fars[1]))
    chip[0] = chip_sum(mine, other)
    most = chip[0].shape[0] // 8 * 5
    chip_most, chip_rest = chip[0][:most], chip[0][most:]
    far_most, far_rest = swap_chip(chip_most), swap_chip(chip_rest)
    residual[1], mine, other = block_of(1)
    other, far_most = lax.optimization_barrier((other, far_most))
    chip[1] = chip_sum(mine, other)
    far_chip = [jnp.concatenate([far_most, far_rest], axis=0), swap_chip(chip[1])]
    parts = []
    for index in range(PARTS):
        both = chip[index].astype(f32) + far_chip[index].astype(f32)
        done = (residual[index] + both).astype(bf16)
        parts.extend([done, swap_core(done)])
    return finish(parts).reshape(steps, rows, width)


def solution(mesh):
    return jax.shard_map(
        shards,
        mesh=mesh,
        in_specs=(
            P(None, "group", None),
            P(None, "group"),
            P("group"),
            P("group"),
            P("group", "head", None),
            P("group", "head", None),
            P("group", "head", None),
            P(),
            P("head", None),
            P("head", None),
            P("head", None),
            P(None, "head"),
            P("head"),
            P("head", None),
            P(),
            P(None, "head"),
            P(None, "head"),
            P("head", None),
        ),
        out_specs=P(None, "group", None),
        check_vma=False,
    )
```

```python
import functools

import jax
import jax.numpy as jnp
from jax import lax
from jax.experimental import pallas as pl
from jax.experimental.pallas import tpu as pltpu
from jax.sharding import PartitionSpec as P

BEAMS = 8
OWNED_SLOTS = 32
SPILL = 16
PAGE_BLOCK = 16
PARTS = 2
MIB = 1 << 20

epsilon = 1e-05
masked_score = -1e30
f32 = jnp.float32
bf16 = jnp.bfloat16

NN = (((1,), (0,)), ((), ()))
NT = (((1,), (1,)), ((), ()))
SMEM = pl.BlockSpec(memory_space=pltpu.SMEM)


def dot(a, b, dims=NN):
    return lax.dot_general(a, b, dims, preferred_element_type=f32)


def lanes(shape):
    return lax.broadcasted_iota(jnp.int32, shape, len(shape) - 1)


def sublanes(shape):
    return lax.broadcasted_iota(jnp.int32, shape, len(shape) - 2)


def in_hbm(array):
    return pltpu.with_memory_space_constraint(array, pltpu.HBM)


def in_vmem(array):
    return pltpu.with_memory_space_constraint(array, pltpu.VMEM)


def start_all(pairs, sems):
    copies = [pltpu.make_async_copy(s, t, sems.at[i]) for i, (s, t) in enumerate(pairs)]
    for copy in copies:
        copy.start()
    return copies


def fill_table(local_count, capacity, first, ids_ref, table_ref):
    groups = ids_ref.shape[0]
    for slot in range(groups * capacity):
        table_ref[slot] = -1

    def group(index, carry):
        rank = jnp.int32(0)
        for page in range(SPILL):
            local = ids_ref[index, 0, OWNED_SLOTS + page] - first
            mine = (local >= 0) & (local < local_count)

            @pl.when(mine)
            def _():
                table_ref[index * capacity + rank] = local

            rank = rank + mine.astype(jnp.int32)
        return carry

    lax.fori_loop(0, groups, group, 0)


def query_kernel(
    tokens_hbm, gain_ref, wq_hbm, request_ref, q_ref, q_hbm, normed_hbm, ids_ref,
    tokens_ref, wq_ref, normed_ref, sems, out_sems,
):
    steps, rows, _ = tokens_ref.shape
    span = steps * BEAMS
    cut = rows // 2
    copies = start_all(
        [
            (tokens_hbm.at[:, :cut], tokens_ref.at[:, :cut]),
            (tokens_hbm.at[:, cut:], tokens_ref.at[:, cut:]),
            (wq_hbm, wq_ref),
        ],
        sems,
    )
    for group in range(ids_ref.shape[0]):
        ids_ref[group] = request_ref[...]
    gain = gain_ref[...].reshape(1, -1)

    def pair(index, carry):
        slabs = []
        for step in range(steps):
            x = tokens_ref[step, pl.ds(pl.multiple_of(index * 16, 16), 16), :].astype(f32)
            scale = lax.rsqrt(jnp.mean(x * x, axis=-1, keepdims=True) + epsilon)
            slabs.append(x * scale * gain)
        for half in range(2):
            part = jnp.concatenate([s[half * 8 : half * 8 + 8] for s in slabs], axis=0)
            start = pl.multiple_of((index * 2 + half) * span, span)
            normed_ref[pl.ds(start, span), :] = part.astype(bf16)
        return carry

    copies[0].wait()
    lax.fori_loop(0, cut // 16, pair, 0, unroll=2)
    copies[1].wait()
    lax.fori_loop(cut // 16, rows // 16, pair, 0, unroll=2)
    leaving = start_all([(normed_ref, normed_hbm)], out_sems)
    copies[2].wait()
    query = dot(normed_ref[...], wq_ref[...], NT).astype(bf16)
    q_ref[...] = (query.astype(f32) * 0.125).astype(bf16)
    last = pltpu.make_async_copy(q_ref, q_hbm, out_sems.at[1])
    last.start()
    leaving[0].wait()
    last.wait()


def queries_of(tokens, gain, w_query, request, groups):
    steps, rows, width = tokens.shape
    inner = w_query.shape[0]
    total = steps * rows
    hbm = pl.BlockSpec(memory_space=pltpu.HBM)
    vmem = pl.BlockSpec(memory_space=pltpu.VMEM)
    return pl.pallas_call(
        query_kernel,
        in_specs=[hbm, vmem, hbm, vmem],
        out_specs=[vmem, hbm, hbm, vmem],
        out_shape=[
            pltpu.VMEM((total, inner), bf16),
            pltpu.HBM((total, inner), bf16),
            pltpu.HBM((total, width), bf16),
            jax.ShapeDtypeStruct((groups, 1, request.shape[0]), jnp.int32),
        ],
        scratch_shapes=[
            pltpu.VMEM(tokens.shape, bf16),
            pltpu.VMEM(w_query.shape, bf16),
            pltpu.VMEM((total, width), bf16),
            pltpu.SemaphoreType.DMA((3,)),
            pltpu.SemaphoreType.DMA((2,)),
        ],
        compiler_params=pltpu.CompilerParams(vmem_limit_bytes=12 * MIB),
        cost_estimate=pl.CostEstimate(
            flops=2 * total * width * inner, bytes_accessed=6 * MIB, transcendentals=total
        ),
        name="queries",
    )(in_hbm(tokens), gain, in_hbm(w_query), request.reshape(1, -1))


def ask_kernel(capacity, request_ref, ids_ref, q_ref, table_ref, out_ref):
    slots, span, _ = out_ref.shape
    local_count = q_ref.shape[0] // span
    first = request_ref[0] // local_count * local_count
    fill_table(local_count, capacity, first, ids_ref, table_ref)
    for slot in range(slots):
        start = jnp.maximum(table_ref[slot], 0) * span
        out_ref[slot] = q_ref[pl.ds(pl.multiple_of(start, span), span), :]


def ask(request, ids, q, span, capacity):
    slots = ids.shape[0] * capacity
    vmem = pl.BlockSpec(memory_space=pltpu.VMEM)
    return pl.pallas_call(
        functools.partial(ask_kernel, capacity),
        in_specs=[SMEM, SMEM, vmem],
        out_specs=[SMEM, vmem],
        out_shape=[
            jax.ShapeDtypeStruct((slots,), jnp.int32),
            jax.ShapeDtypeStruct((slots, span, q.shape[1]), bf16),
        ],
        compiler_params=pltpu.CompilerParams(vmem_limit_bytes=8 * MIB),
        name="ask",
    )(request, ids, in_vmem(q))


def half_masks(rows):
    low = lanes((rows, 128)) < 64
    return low.astype(f32).astype(bf16), jnp.logical_not(low).astype(f32).astype(bf16)


def stacked(pair_rows, masks):
    return jnp.concatenate([pair_rows * masks[0], pair_rows * masks[1]], axis=0)


def side_by_side(values, rows):
    low = lanes((rows, 128)) < 64
    top = jnp.broadcast_to(values[:rows], (rows, 128))
    bottom = jnp.broadcast_to(values[rows:], (rows, 128))
    return jnp.where(low, top, bottom)


def absorb(state, rows, columns, top, total, numer):
    top_ref, total_ref, numer_ref = state
    old = top_ref[rows, columns]
    new = jnp.maximum(old, top)
    keep = jnp.exp(old - new)
    add = jnp.exp(top - new)
    top_ref[rows, columns] = new
    total_ref[rows, columns] = total_ref[rows, columns] * keep + total * add
    numer_ref[rows, columns] = numer_ref[rows, columns] * keep + numer * add


def history(parents_ref, q_ref, k_ref, v_ref, forget_ref, state, scores_ref, weights_ref):
    transitions, rows = parents_ref.shape
    span = (transitions + 1) * BEAMS
    pack = 128 // span
    square = (128, 128)
    diagonal = sublanes(square) == lanes(square)
    columns = []
    for step in range(transitions):
        row = parents_ref[step : step + 1, :].astype(f32)
        columns.append(
            jnp.sum(jnp.where(diagonal, jnp.broadcast_to(row, square), 0.0), axis=1, keepdims=True)
        )
    lane8 = lanes((8, 128)).astype(f32)
    masks = half_masks(128)
    low = lanes(square) < 64
    top_ref, total_ref, numer_ref = state
    groups = rows // BEAMS // pack
    pairs = q_ref.shape[1] // 128
    for group in range(groups):
        slabs = []
        for member in range(pack):
            first = (group * pack + member) * BEAMS
            slabs.append(jnp.zeros((8, 128), f32))
            for step in range(transitions):
                wanted = columns[step][first : first + 8] + float(member * span + step * 8)
                slabs.append(jnp.where(lane8 == wanted, 1.0, 0.0))
        parent = jnp.concatenate(slabs, axis=0)
        parent16 = parent.astype(bf16)
        one = diagonal.astype(f32) + parent
        two = dot(parent16, parent16)
        ancestors = one + dot(two.astype(bf16), one.astype(bf16))
        here = pl.ds(group * 128, 128)
        running = lax.dot_general(
            ancestors, forget_ref[here, :], NN,
            precision=lax.Precision.HIGHEST, preferred_element_type=f32,
        ).T
        hidden = jnp.where(ancestors > 0.5, 0.0, masked_score)
        for pair in range(pairs):
            cols = pl.ds(pair * 128, 128)
            raw = dot(stacked(q_ref[here, cols], masks), k_ref[here, cols], NT)
            for half in range(2):
                head = pair * 2 + half
                scores_ref[group * pairs + pair, half] = raw[half * 128 : half * 128 + 128] + (
                    hidden - running[head : head + 1]
                )
    for group in range(groups):
        here = pl.ds(group * 128, 128)
        for pair in range(pairs):
            cols = pl.ds(pair * 128, 128)
            tops, totals = [], []
            for half in range(2):
                scores = scores_ref[group * pairs + pair, half]
                top = jnp.broadcast_to(jnp.max(scores, axis=-1, keepdims=True), square)
                weights = jnp.exp(scores - top)
                weights_ref[group * pairs + pair, pl.ds(half * 128, 128), :] = weights.astype(bf16)
                tops.append(top)
                totals.append(jnp.broadcast_to(jnp.sum(weights, axis=-1, keepdims=True), square))
            top_ref[here, cols] = jnp.where(low, *tops)
            total_ref[here, cols] = jnp.where(low, *totals)
    for group in range(groups):
        here = pl.ds(group * 128, 128)
        for pair in range(pairs):
            cols = pl.ds(pair * 128, 128)
            numer = dot(weights_ref[group * pairs + pair], v_ref[here, cols])
            numer_ref[here, cols] = jnp.where(low, numer[:128], numer[128:])


def fresh_kernel(
    parents_ref, bias_ref, normed_hbm, wk_hbm, wv_hbm, wf_hbm, q_hbm, top_hbm, total_hbm, numer_hbm,
    logs_hbm, averages_hbm,
    normed_ref, wk_ref, wv_ref, wf_ref, q_ref, top_own, total_own, numer_own,
    k_ref, v_ref, forget_ref, top_ref, total_ref, numer_ref, scores_ref, weights_ref,
    logs_ref, averages_ref, sems, out_sems,
):
    copies = start_all(
        [
            (normed_hbm, normed_ref), (wk_hbm, wk_ref), (wv_hbm, wv_ref), (wf_hbm, wf_ref),
            (q_hbm, q_ref), (top_hbm, top_own), (total_hbm, total_own), (numer_hbm, numer_own),
        ],
        sems,
    )
    copies[0].wait()
    copies[1].wait()
    k_ref[...] = dot(normed_ref[...], wk_ref[...], NT).astype(bf16)
    copies[2].wait()
    v_ref[...] = dot(normed_ref[...], wv_ref[...], NT).astype(bf16)
    copies[3].wait()
    gate = dot(normed_ref[...], wf_ref[...], NT) + bias_ref[...]
    forget = jnp.minimum(gate, 0.0) - jnp.log1p(jnp.exp(-jnp.abs(gate)))
    forget_ref[...] = jnp.zeros_like(forget_ref)
    forget_ref[:, : forget.shape[1]] = forget
    copies[4].wait()
    state = (top_ref, total_ref, numer_ref)
    history(parents_ref, q_ref, k_ref, v_ref, forget_ref, state, scores_ref, weights_ref)
    for copy in copies[5:]:
        copy.wait()

    parts, _, part = logs_ref.shape[:3]
    span = parts * part

    def join(index, carry):
        rows = pl.ds(pl.multiple_of(index * span, span), span)
        absorb(state, rows, slice(None), top_own[rows, :], total_own[rows, :], numer_own[rows, :])
        total = total_ref[rows, :]
        logs = top_ref[rows, :] + jnp.log(total)
        averages = numer_ref[rows, :] / total
        for number in range(parts):
            logs_ref[number, index] = logs[number * part : number * part + part]
            averages_ref[number, index] = averages[number * part : number * part + part]
        return carry

    lax.fori_loop(0, logs_ref.shape[1], join, 0, unroll=2)
    for copy in start_all([(logs_ref, logs_hbm), (averages_ref, averages_hbm)], out_sems):
        copy.wait()


def fresh(parents, bias, normed, w_key, w_value, w_forget, q, own):
    rows, inner = q.shape
    span = (parents.shape[0] + 1) * BEAMS
    vmem = pl.BlockSpec(memory_space=pltpu.VMEM)
    hbm = pl.BlockSpec(memory_space=pltpu.HBM)
    big = [normed, w_key, w_value, w_forget.T, q, *own]
    wide = pltpu.VMEM((rows, inner), f32)
    out = (PARTS, rows // span, span // PARTS, inner)
    tiles = rows * inner // (128 * 128)
    return pl.pallas_call(
        fresh_kernel,
        in_specs=[vmem, vmem] + [hbm] * len(big),
        out_specs=[hbm] * 2,
        out_shape=[pltpu.HBM(out, f32)] * 2,
        scratch_shapes=[pltpu.VMEM(x.shape, x.dtype) for x in big]
        + [pltpu.VMEM((rows, inner), bf16)] * 2
        + [pltpu.VMEM((rows, 128), f32), wide, wide, wide]
        + [pltpu.VMEM((tiles, 2, 128, 128), f32), pltpu.VMEM((tiles, 256, 128), bf16)]
        + [pltpu.VMEM(out, f32)] * 2
        + [pltpu.SemaphoreType.DMA((len(big),)), pltpu.SemaphoreType.DMA((2,))],
        compiler_params=pltpu.CompilerParams(vmem_limit_bytes=24 * MIB),
        cost_estimate=pl.CostEstimate(
            flops=4 * rows * normed.shape[1] * inner, bytes_accessed=12 * MIB,
            transcendentals=8 * rows * inner,
        ),
        name="fresh",
    )(parents, bias.reshape(1, -1), *[in_hbm(x) for x in big])


def page_weights(queries, fills, keys_ref, decay_ref, scores_ref, weights_ref, tops_ref):
    span = queries[0][0].shape[0]
    masks = half_masks(span)
    lane = lanes((1, 128))
    decay = [decay_ref[head].astype(f32) for head in range(decay_ref.shape[0])]
    for page, pairs in enumerate(queries):
        valid = lane < fills[page]
        for pair, query in enumerate(pairs):
            raw = dot(stacked(query, masks), keys_ref[page, pl.ds(pair * 128, 128), :])
            for half in range(2):
                head = pair * 2 + half
                bias = jnp.where(valid, decay[head][page : page + 1], masked_score)
                scores_ref[page, pl.ds(head * span, span), :] = (
                    raw[half * span : half * span + span] + bias
                )
    for page in range(len(queries)):
        for head in range(decay_ref.shape[0]):
            rows = pl.ds(head * span, span)
            scores = scores_ref[page, rows, :]
            top = jnp.broadcast_to(jnp.max(scores, axis=-1, keepdims=True), scores.shape)
            tops_ref[page, rows, :] = top
            weights = jnp.exp(scores - top)
            weights_ref[page, rows, :] = weights.astype(bf16)
            scores_ref[page, rows, :] = jnp.broadcast_to(
                jnp.sum(weights, axis=-1, keepdims=True), scores.shape
            )


def page_sums(page, pair, span, values_ref, scores_ref, weights_ref, tops_ref):
    low = lanes((span, 128)) < 64
    first, second = pl.ds(pair * 2 * span, span), pl.ds((pair * 2 + 1) * span, span)
    numer = dot(
        weights_ref[page, pl.ds(pair * 2 * span, 2 * span), :],
        values_ref[page, pl.ds(pair * 128, 128), :],
        NT,
    )
    top = jnp.where(low, tops_ref[page, first, :], tops_ref[page, second, :])
    total = jnp.where(low, scores_ref[page, first, :], scores_ref[page, second, :])
    return top, total, jnp.where(low, numer[:span], numer[span:])


def page_scratch(pages, span, heads):
    rows = span * heads
    return [
        pltpu.VMEM((pages, rows, 128), f32),
        pltpu.VMEM((pages, rows, 128), bf16),
        pltpu.VMEM((pages, rows, 128), f32),
    ]


def own_kernel(
    request_ref, fill_ref, q_ref, keys_ref, values_ref, decay_ref,
    top_ref, total_ref, numer_ref, *scratch,
):
    state = (top_ref, total_ref, numer_ref)
    span = scratch[0].shape[1] // decay_ref.shape[0]
    local_count = q_ref.shape[0] // span
    pairs = q_ref.shape[1] // 128

    block = pl.program_id(0)

    @pl.when(block == 0)
    def _():
        top_ref[...] = jnp.full_like(top_ref, masked_score)
        total_ref[...] = jnp.zeros_like(total_ref)
        numer_ref[...] = jnp.zeros_like(numer_ref)

    places, queries, fills = [], [], []
    for page in range(PAGE_BLOCK):
        index = block * PAGE_BLOCK + page
        local = lax.rem(request_ref[index], local_count)
        rows = pl.ds(pl.multiple_of(local * span, span), span)
        places.append(rows)
        queries.append([q_ref[rows, pl.ds(pair * 128, 128)] for pair in range(pairs)])
        fills.append(fill_ref[index])
    page_weights(queries, fills, keys_ref, decay_ref, *scratch)
    for page, rows in enumerate(places):
        for pair in range(pairs):
            sums = page_sums(page, pair, span, values_ref, *scratch)
            absorb(state, rows, pl.ds(pair * 128, 128), *sums)


def page_cost(pages, keys, rows):
    inner, length = keys.shape[1:]
    return pl.CostEstimate(
        flops=pages * rows * inner * length * 8,
        bytes_accessed=pages * inner * length * 4,
        transcendentals=pages * rows * inner * length // 64,
    )


def own_pages(request, fill, q, keys, values, decay, span):
    pool = pl.BlockSpec((PAGE_BLOCK,) + keys.shape[1:], lambda i: (i, 0, 0))
    decay_spec = pl.BlockSpec((decay.shape[0], PAGE_BLOCK, decay.shape[2]), lambda i: (0, i, 0))
    rows = pl.BlockSpec(q.shape, lambda i: (0, 0))
    return pl.pallas_call(
        own_kernel,
        grid=(OWNED_SLOTS // PAGE_BLOCK,),
        in_specs=[SMEM, SMEM, rows, pool, pool, decay_spec],
        out_specs=[rows] * 3,
        out_shape=[pltpu.HBM(q.shape, f32)] * 3,
        scratch_shapes=page_scratch(PAGE_BLOCK, span, decay.shape[0]),
        compiler_params=pltpu.CompilerParams(vmem_limit_bytes=20 * MIB),
        cost_estimate=page_cost(OWNED_SLOTS, keys, 64),
        name="own_pages",
    )(request, fill, in_hbm(q), in_hbm(keys), in_hbm(values), decay)


def hosted_kernel(
    local_count, capacity, request_ref, fill_ref, q_ref, keys_ref, values_ref, decay_ref,
    out_ref, tail_ref, count_ref, *scratch,
):
    span, inner = q_ref.shape[1:]
    pairs = inner // 128
    heads = decay_ref.shape[0]
    groups = out_ref.shape[0]
    half = span // PARTS
    slot_rows = pairs * span
    out_ref[...] = jnp.zeros_like(out_ref)
    tail_ref[...] = jnp.zeros_like(tail_ref)
    for owner in range(groups):
        count_ref[owner] = 0
    places, queries, fills = [], [], []
    for page in range(SPILL):
        owner = request_ref[OWNED_SLOTS + page] // local_count
        rank = count_ref[owner]
        count_ref[owner] = rank + 1
        places.append((owner, rank))
        slot = owner * capacity + rank
        queries.append([q_ref[slot, :, pl.ds(pair * 128, 128)] for pair in range(pairs)])
        fills.append(fill_ref[OWNED_SLOTS + page])
    page_weights(queries, fills, keys_ref, decay_ref, *scratch)
    scores_ref, _, tops_ref = scratch
    lane = lanes((half, 128))
    for page, (owner, rank) in enumerate(places):
        for pair in range(pairs):
            _, total, numer = page_sums(page, pair, span, values_ref, *scratch)
            here = pl.ds(pl.multiple_of(rank * slot_rows + pair * span, span), span)
            out_ref[owner, here, :] = (numer / total).astype(bf16)
        tail = tail_ref[owner]
        base = rank * (3 * heads)
        for head in range(heads):
            rows = pl.ds(head * span, span)
            rest = tops_ref[page, rows, :] + jnp.log(scores_ref[page, rows, :])
            rest = jnp.where(lane < 64, rest[:half], rest[half:])
            for piece in range(3):
                part = rest.astype(bf16).astype(f32)
                rest = rest - part
                tail = jnp.where(lane % 64 == base + piece * heads + head, part, tail)
        tail_ref[owner] = tail
    first = capacity * slot_rows
    for owner in range(groups):
        out_ref[owner, first : first + half, :] = tail_ref[owner].astype(bf16)


def hosted_pages(request, fill, asked_rows, keys, values, decay, groups, capacity, local_count):
    count, span, inner = asked_rows.shape
    shift = OWNED_SLOTS // SPILL
    pool = pl.BlockSpec((SPILL,) + keys.shape[1:], lambda i: (shift, 0, 0))
    decay_spec = pl.BlockSpec((decay.shape[0], SPILL, decay.shape[2]), lambda i: (0, shift, 0))
    out_shape = (groups, capacity * span * inner // 128 + span // PARTS, 128)
    return pl.pallas_call(
        functools.partial(hosted_kernel, local_count, capacity),
        grid=(1,),
        in_specs=[
            SMEM, SMEM, pl.BlockSpec(asked_rows.shape, lambda i: (0, 0, 0)), pool, pool, decay_spec
        ],
        out_specs=pl.BlockSpec(out_shape, lambda i: (0, 0, 0)),
        out_shape=jax.ShapeDtypeStruct(out_shape, bf16),
        scratch_shapes=[pltpu.VMEM((groups, span // PARTS, 128), f32), pltpu.SMEM((groups,), jnp.int32)]
        + page_scratch(SPILL, span, decay.shape[0]),
        compiler_params=pltpu.CompilerParams(vmem_limit_bytes=24 * MIB),
        cost_estimate=page_cost(SPILL, keys, 64),
        name="hosted_pages",
    )(request, fill, asked_rows, in_hbm(keys), in_hbm(values), decay)


def merge_kernel(capacity, steps, part, heads, table_ref, back_ref, log_hbm, average_hbm, *refs):
    top_ref, total_ref, numer_ref, tops_ref, sems, load_sems = refs[-6:]
    count = load_sems.shape[0]
    sources, (out_ref, *targets) = refs[:count], refs[count:-6]
    groups = back_ref.shape[0]
    inner = heads * 64
    rows = steps * BEAMS
    span = PARTS * rows
    state = (top_ref, total_ref, numer_ref)
    copies = start_all([(log_hbm.at[part], top_ref), (average_hbm.at[part], numer_ref)], sems)
    pairs = []
    if part == 0:
        weight_ref, *targets = targets
        height = sources[0].shape[0]
        head = lax.axis_index("head")
        for other in range(4):
            place = pl.ds(pl.multiple_of((head ^ other) * height, height), height)
            pairs.append((sources[other], weight_ref.at[place]))
        sources = sources[4:]
    pairs.extend(zip(sources, targets))
    loads = start_all(pairs, load_sems)
    total_ref[...] = jnp.ones_like(total_ref)
    slot_rows = (inner // 128) * span
    first = capacity * slot_rows
    tails = jnp.concatenate(
        [back_ref[owner, first : first + rows, :] for owner in range(groups)], axis=0
    )
    source, target = sublanes((128, inner)), lanes((128, inner)) // 64
    for rank in range(capacity):
        hit = source < 0
        for piece in range(3):
            hit = hit | (source == target + part * 64 + (rank * 3 + piece) * heads)
        tops_ref[:, rank * inner : rank * inner + inner] = dot(tails, hit.astype(f32).astype(bf16))
    for copy in copies:
        copy.wait()
    for owner in range(groups):
        for rank in range(capacity):
            local = table_ref[owner * capacity + rank]
            bias = jnp.where(local >= 0, 0.0, masked_score)
            top = tops_ref[owner * rows : owner * rows + rows, rank * inner : rank * inner + inner]
            starts = [rank * slot_rows + pair * span + part * rows for pair in range(inner // 128)]
            average = jnp.concatenate(
                [back_ref[owner, start : start + rows, :].astype(f32) for start in starts], axis=1
            )
            here = pl.ds(pl.multiple_of(jnp.maximum(local, 0) * rows, rows), rows)
            absorb(state, here, slice(None), top + bias, 1.0, average)
    for index in range(top_ref.shape[0] // (2 * rows)):
        parts = []
        for half in range(2):
            here = slice((index * 2 + half) * rows, (index * 2 + half + 1) * rows)
            parts.append(numer_ref[here, :] / total_ref[here, :])
        for step in range(steps):
            both = jnp.concatenate([p[step * 8 : step * 8 + 8] for p in parts], axis=0)
            start = step * (top_ref.shape[0] // steps) + index * 16
            out_ref[start : start + 16, :] = both.astype(bf16)
    for copy in loads:
        copy.wait()


def merge(part, table, back, logs, averages, steps, capacity, sources):
    _, requests, span, inner = logs.shape
    rows = requests * span
    logs, averages = (x.reshape(PARTS, rows, inner) for x in (logs, averages))
    vmem = pl.BlockSpec(memory_space=pltpu.VMEM)
    hbm = pl.BlockSpec(memory_space=pltpu.HBM)
    anywhere = pl.BlockSpec(memory_space=pl.ANY)
    mixes = sources[:4] if part == 0 else []
    others = sources[len(mixes) :]
    kept = [jax.ShapeDtypeStruct(x.shape, x.dtype) for x in others]
    if mixes:
        kept = [jax.ShapeDtypeStruct((4 * inner, mixes[0].shape[1]), bf16)] + kept
    return pl.pallas_call(
        functools.partial(merge_kernel, capacity, steps, part, inner // 64),
        in_specs=[SMEM, vmem, hbm, hbm] + [anywhere] * len(mixes) + [hbm] * len(others),
        out_shape=[jax.ShapeDtypeStruct((rows, inner), bf16)] + kept,
        scratch_shapes=[pltpu.VMEM((rows, inner), f32)] * 3
        + [
            pltpu.VMEM((back.shape[0] * span, capacity * inner), f32),
            pltpu.SemaphoreType.DMA((2,)),
            pltpu.SemaphoreType.DMA((len(sources),)),
        ],
        compiler_params=pltpu.CompilerParams(vmem_limit_bytes=10 * MIB),
        cost_estimate=pl.CostEstimate(
            flops=40 * rows * inner, bytes_accessed=8 * MIB, transcendentals=4 * rows * inner
        ),
        name="merge",
    )(table, back, in_hbm(logs), in_hbm(averages), *mixes, *[in_hbm(x) for x in others])


def block_kernel(
    first, att0, att1, att2, att3, weight_ref, tokens_ref, gain_ref, gate_ref, up_ref, down_ref,
    residual_out, mine_ref, other_ref,
    residual_ref, attended_ref, scaled_ref, hidden_ref, sums_ref,
):
    rows, width = residual_ref.shape
    inner = att0.shape[1]
    half = rows // 2
    head = lax.axis_index("head")
    core = lax.rem(head, 2)
    near = pl.ds(pl.multiple_of(core * half, half), half)
    away = pl.ds(pl.multiple_of((1 - core) * half, half), half)
    for other, att in enumerate((att0, att1, att2, att3)):
        place = pl.ds(pl.multiple_of((head ^ other) * inner, inner), inner)
        attended_ref[:, place] = att[...]
    gain = gain_ref[...].reshape(1, -1)
    squares = jnp.zeros((rows, 1), f32)
    for start in range(0, width, 512):
        cols = slice(start, start + 512)
        x = tokens_ref[first : first + rows, cols].astype(f32) + dot(attended_ref[...], weight_ref[:, cols])
        residual_ref[:, cols] = x
        scaled_ref[:, cols] = (x * gain[:, cols]).astype(bf16)
        squares = squares + jnp.sum(x * x, axis=-1, keepdims=True)
    scale = lax.rsqrt(squares / width + epsilon)
    for start in range(0, gate_ref.shape[1], 256):
        cols = slice(start, start + 256)
        gate = dot(scaled_ref[...], gate_ref[:, cols]) * scale
        up = dot(scaled_ref[...], up_ref[:, cols]) * scale
        hidden_ref[:, cols] = (gate / (1.0 + jnp.exp(-gate)) * up).astype(bf16)
    residual_out[...] = residual_ref[near, :]
    for start in range(0, width, 512):
        cols = slice(start, start + 512)
        sums_ref[:, cols] = dot(hidden_ref[...], down_ref[:, cols])
    mine_ref[...] = sums_ref[near, :]
    other_ref[...] = sums_ref[away, :].astype(bf16)


def block(first, attended, weight, tokens, gain, w_gate, w_up, w_down):
    rows, inner = attended[0].shape
    width = tokens.shape[1]
    hidden = w_gate.shape[1]
    vmem = pl.BlockSpec(memory_space=pltpu.VMEM)
    half = jax.ShapeDtypeStruct((rows // 2, width), f32)
    return pl.pallas_call(
        functools.partial(block_kernel, first),
        in_specs=[vmem] * 10,
        out_specs=[vmem] * 3,
        out_shape=[half, half, jax.ShapeDtypeStruct((rows // 2, width), bf16)],
        scratch_shapes=[
            pltpu.VMEM((rows, width), f32),
            pltpu.VMEM((rows, 4 * inner), bf16),
            pltpu.VMEM((rows, width), bf16),
            pltpu.VMEM((rows, hidden), bf16),
            pltpu.VMEM((rows, width), f32),
        ],
        compiler_params=pltpu.CompilerParams(vmem_limit_bytes=20 * MIB),
        cost_estimate=pl.CostEstimate(flops=0, bytes_accessed=0, transcendentals=0),
        name="block",
    )(*attended, weight, tokens, gain, w_gate, w_up, w_down)


def finish_kernel(*refs):
    parts, out_ref = refs[:-1], refs[-1]
    core = lax.axis_index("head") % 2
    first = 0
    for index in range(0, len(parts), 2):
        half = parts[index].shape[0]
        for part, place in ((parts[index], core), (parts[index + 1], 1 - core)):
            rows = pl.ds(pl.multiple_of(first + place * half, half), half)
            out_ref[rows, :] = part[...]
        first += 2 * half


def finish(parts):
    vmem = pl.BlockSpec(memory_space=pltpu.VMEM)
    rows, width = sum(part.shape[0] for part in parts), parts[0].shape[1]
    return pl.pallas_call(
        finish_kernel,
        in_specs=[vmem] * len(parts),
        out_specs=vmem,
        out_shape=jax.ShapeDtypeStruct((rows, width), parts[0].dtype),
        compiler_params=pltpu.CompilerParams(vmem_limit_bytes=12 * MIB),
        name="finish",
    )(*parts)


def swap_core(value):
    return lax.ppermute(value, "head", [(i, i ^ 1) for i in range(4)])


def swap_chip(value):
    return lax.ppermute(value, "head", [(i, i ^ 2) for i in range(4)])


def shards(
    tokens, parents, page_request, page_fill, keys_pool, values_pool, decay_pool,
    gain_attn, w_query, w_key, w_value, w_forget, forget_bias, w_out,
    gain_ffn, w_gate, w_up, w_down,
):
    steps, rows, width = tokens.shape
    inner = w_query.shape[0]
    local_count = rows // BEAMS
    span = steps * BEAMS
    groups = lax.axis_size("group")
    capacity = (SPILL + groups - 2) // (groups - 1)
    decay = decay_pool.transpose(1, 0, 2)

    def exchange(value):
        return lax.all_to_all(value, "group", split_axis=0, concat_axis=0, tiled=True)

    q_near, q, normed, ids = queries_of(tokens, gain_attn, w_query, page_request, groups)
    ids = exchange(ids)
    table, asked = ask(page_request, ids, q_near, span, capacity)
    asked_rows = exchange(asked.reshape(groups, capacity * span, inner)).reshape(asked.shape)
    asked, q = lax.optimization_barrier((asked, q))
    own = own_pages(page_request, page_fill, q, keys_pool, values_pool, decay, span)
    own, w_sent = lax.optimization_barrier((own, w_out))
    w_out_far = swap_chip(w_sent)
    asked_rows, own = lax.optimization_barrier((asked_rows, own))
    payload = hosted_pages(
        page_request, page_fill, asked_rows, keys_pool, values_pool, decay, groups, capacity, local_count
    )
    payload, normed = lax.optimization_barrier((payload, normed))
    back = exchange(payload)
    logs, averages = fresh(parents, forget_bias, normed, w_key, w_value, w_forget, q, own)
    logs, w_out_far = lax.optimization_barrier((logs, w_out_far))
    mixes = [w_out, swap_core(w_out), w_out_far, swap_core(w_out_far)]
    logs, mixes = lax.optimization_barrier((logs, mixes))

    flat = tokens.reshape(steps * rows, width)
    each = steps // PARTS
    sums = (table, back, logs, averages, each, capacity)
    here, weight = merge(0, *sums, mixes)
    heres = [here]
    back, heres[0] = lax.optimization_barrier((back, heres[0]))
    sums = (table, back, logs, averages, each, capacity)
    here, w_gate, w_up, w_down, flat = merge(1, *sums, [w_gate, w_up, w_down, flat])
    heres.append(here)
    fars = [swap_chip(here) for here in heres]
    fars[0], heres[1] = lax.optimization_barrier((fars[0], heres[1]))

    def block_of(index):
        here, far = heres[index], fars[index]
        gathered = [here, swap_core(here), far, swap_core(far)]
        if index:
            gathered, chip[0] = lax.optimization_barrier((gathered, chip[0]))
        first = index * here.shape[0]
        return block(first, gathered, weight, flat, gain_ffn, w_gate, w_up, w_down)

    def chip_sum(mine, other):
        return (mine + swap_core(other).astype(f32)).astype(bf16)

    chip, residual = [None] * PARTS, [None] * PARTS
    residual[0], mine, other = block_of(0)
    other, fars[1] = lax.optimization_barrier((other, fars[1]))
    chip[0] = chip_sum(mine, other)
    most = chip[0].shape[0] // 8 * 5
    chip_most, chip_rest = chip[0][:most], chip[0][most:]
    far_most, far_rest = swap_chip(chip_most), swap_chip(chip_rest)
    residual[1], mine, other = block_of(1)
    other, far_most = lax.optimization_barrier((other, far_most))
    chip[1] = chip_sum(mine, other)
    far_chip = [jnp.concatenate([far_most, far_rest], axis=0), swap_chip(chip[1])]
    parts = []
    for index in range(PARTS):
        both = chip[index].astype(f32) + far_chip[index].astype(f32)
        done = (residual[index] + both).astype(bf16)
        parts.extend([done, swap_core(done)])
    return finish(parts).reshape(steps, rows, width)


def solution(mesh):
    return jax.shard_map(
        shards,
        mesh=mesh,
        in_specs=(
            P(None, "group", None),
            P(None, "group"),
            P("group"),
            P("group"),
            P("group", "head", None),
            P("group", "head", None),
            P("group", "head", None),
            P(),
            P("head", None),
            P("head", None),
            P("head", None),
            P(None, "head"),
            P("head"),
            P("head", None),
            P(),
            P(None, "head"),
            P(None, "head"),
            P("head", None),
        ),
        out_specs=P(None, "group", None),
        check_vma=False,
    )
```

```python
import functools

import jax
import jax.numpy as jnp
from jax import lax
from jax.experimental import pallas as pl
from jax.experimental.pallas import tpu as pltpu
from jax.sharding import PartitionSpec as P

BEAMS = 8
OWNED_SLOTS = 32
SPILL = 16
PAGE_BLOCK = 16
PARTS = 2
MIB = 1 << 20

epsilon = 1e-05
masked_score = -1e30
f32 = jnp.float32
bf16 = jnp.bfloat16

NN = (((1,), (0,)), ((), ()))
NT = (((1,), (1,)), ((), ()))
SMEM = pl.BlockSpec(memory_space=pltpu.SMEM)


def dot(a, b, dims=NN):
    return lax.dot_general(a, b, dims, preferred_element_type=f32)


def lanes(shape):
    return lax.broadcasted_iota(jnp.int32, shape, len(shape) - 1)


def sublanes(shape):
    return lax.broadcasted_iota(jnp.int32, shape, len(shape) - 2)


def in_hbm(array):
    return pltpu.with_memory_space_constraint(array, pltpu.HBM)


def in_vmem(array):
    return pltpu.with_memory_space_constraint(array, pltpu.VMEM)


def start_all(pairs, sems):
    copies = [pltpu.make_async_copy(s, t, sems.at[i]) for i, (s, t) in enumerate(pairs)]
    for copy in copies:
        copy.start()
    return copies


def fill_table(local_count, capacity, first, ids_ref, table_ref):
    groups = ids_ref.shape[0]
    for slot in range(groups * capacity):
        table_ref[slot] = -1

    def group(index, carry):
        rank = jnp.int32(0)
        for page in range(SPILL):
            local = ids_ref[index, 0, OWNED_SLOTS + page] - first
            mine = (local >= 0) & (local < local_count)

            @pl.when(mine)
            def _():
                table_ref[index * capacity + rank] = local

            rank = rank + mine.astype(jnp.int32)
        return carry

    lax.fori_loop(0, groups, group, 0)


def query_kernel(
    tokens_hbm, gain_ref, wq_hbm, q_ref, q_hbm, normed_hbm,
    tokens_ref, wq_ref, normed_ref, sems, out_sems,
):
    steps, rows, _ = tokens_ref.shape
    span = steps * BEAMS
    cut = rows // 2
    copies = start_all(
        [
            (tokens_hbm.at[:, :cut], tokens_ref.at[:, :cut]),
            (tokens_hbm.at[:, cut:], tokens_ref.at[:, cut:]),
            (wq_hbm, wq_ref),
        ],
        sems,
    )
    gain = gain_ref[...].reshape(1, -1)

    def pair(index, carry):
        slabs = []
        for step in range(steps):
            x = tokens_ref[step, pl.ds(pl.multiple_of(index * 16, 16), 16), :].astype(f32)
            scale = lax.rsqrt(jnp.mean(x * x, axis=-1, keepdims=True) + epsilon)
            slabs.append(x * scale * gain)
        for half in range(2):
            part = jnp.concatenate([s[half * 8 : half * 8 + 8] for s in slabs], axis=0)
            start = pl.multiple_of((index * 2 + half) * span, span)
            normed_ref[pl.ds(start, span), :] = part.astype(bf16)
        return carry

    copies[0].wait()
    lax.fori_loop(0, cut // 16, pair, 0, unroll=2)
    copies[1].wait()
    lax.fori_loop(cut // 16, rows // 16, pair, 0, unroll=2)
    leaving = start_all([(normed_ref, normed_hbm)], out_sems)
    copies[2].wait()
    query = dot(normed_ref[...], wq_ref[...], NT).astype(bf16)
    q_ref[...] = (query.astype(f32) * 0.125).astype(bf16)
    last = pltpu.make_async_copy(q_ref, q_hbm, out_sems.at[1])
    last.start()
    leaving[0].wait()
    last.wait()


def queries_of(tokens, gain, w_query):
    steps, rows, width = tokens.shape
    inner = w_query.shape[0]
    total = steps * rows
    hbm = pl.BlockSpec(memory_space=pltpu.HBM)
    vmem = pl.BlockSpec(memory_space=pltpu.VMEM)
    return pl.pallas_call(
        query_kernel,
        in_specs=[hbm, vmem, hbm],
        out_specs=[vmem, hbm, hbm],
        out_shape=[
            pltpu.VMEM((total, inner), bf16),
            pltpu.HBM((total, inner), bf16),
            pltpu.HBM((total, width), bf16),
        ],
        scratch_shapes=[
            pltpu.VMEM(tokens.shape, bf16),
            pltpu.VMEM(w_query.shape, bf16),
            pltpu.VMEM((total, width), bf16),
            pltpu.SemaphoreType.DMA((3,)),
            pltpu.SemaphoreType.DMA((2,)),
        ],
        compiler_params=pltpu.CompilerParams(vmem_limit_bytes=12 * MIB),
        cost_estimate=pl.CostEstimate(
            flops=2 * total * width * inner, bytes_accessed=6 * MIB, transcendentals=total
        ),
        name="queries",
    )(in_hbm(tokens), gain, in_hbm(w_query))


def ask_kernel(capacity, request_ref, ids_ref, q_ref, table_ref, out_ref):
    slots, span, _ = out_ref.shape
    local_count = q_ref.shape[0] // span
    first = request_ref[0] // local_count * local_count
    fill_table(local_count, capacity, first, ids_ref, table_ref)
    for slot in range(slots):
        start = jnp.maximum(table_ref[slot], 0) * span
        out_ref[slot] = q_ref[pl.ds(pl.multiple_of(start, span), span), :]


def ask(request, ids, q, span, capacity):
    slots = ids.shape[0] * capacity
    vmem = pl.BlockSpec(memory_space=pltpu.VMEM)
    return pl.pallas_call(
        functools.partial(ask_kernel, capacity),
        in_specs=[SMEM, SMEM, vmem],
        out_specs=[SMEM, vmem],
        out_shape=[
            jax.ShapeDtypeStruct((slots,), jnp.int32),
            jax.ShapeDtypeStruct((slots, span, q.shape[1]), bf16),
        ],
        compiler_params=pltpu.CompilerParams(vmem_limit_bytes=8 * MIB),
        name="ask",
    )(request, ids, in_vmem(q))


def half_masks(rows):
    low = lanes((rows, 128)) < 64
    return low.astype(f32).astype(bf16), jnp.logical_not(low).astype(f32).astype(bf16)


def stacked(pair_rows, masks):
    return jnp.concatenate([pair_rows * masks[0], pair_rows * masks[1]], axis=0)


def side_by_side(values, rows):
    low = lanes((rows, 128)) < 64
    top = jnp.broadcast_to(values[:rows], (rows, 128))
    bottom = jnp.broadcast_to(values[rows:], (rows, 128))
    return jnp.where(low, top, bottom)


def absorb(state, rows, columns, top, total, numer):
    top_ref, total_ref, numer_ref = state
    old = top_ref[rows, columns]
    new = jnp.maximum(old, top)
    keep = jnp.exp(old - new)
    add = jnp.exp(top - new)
    top_ref[rows, columns] = new
    total_ref[rows, columns] = total_ref[rows, columns] * keep + total * add
    numer_ref[rows, columns] = numer_ref[rows, columns] * keep + numer * add


def history(parents_ref, q_ref, k_ref, v_ref, forget_ref, state, scores_ref, weights_ref):
    transitions, rows = parents_ref.shape
    span = (transitions + 1) * BEAMS
    pack = 128 // span
    square = (128, 128)
    diagonal = sublanes(square) == lanes(square)
    columns = []
    for step in range(transitions):
        row = parents_ref[step : step + 1, :].astype(f32)
        columns.append(
            jnp.sum(jnp.where(diagonal, jnp.broadcast_to(row, square), 0.0), axis=1, keepdims=True)
        )
    lane8 = lanes((8, 128)).astype(f32)
    masks = half_masks(128)
    low = lanes(square) < 64
    top_ref, total_ref, numer_ref = state
    groups = rows // BEAMS // pack
    pairs = q_ref.shape[1] // 128
    for group in range(groups):
        slabs = []
        for member in range(pack):
            first = (group * pack + member) * BEAMS
            slabs.append(jnp.zeros((8, 128), f32))
            for step in range(transitions):
                wanted = columns[step][first : first + 8] + float(member * span + step * 8)
                slabs.append(jnp.where(lane8 == wanted, 1.0, 0.0))
        parent = jnp.concatenate(slabs, axis=0)
        parent16 = parent.astype(bf16)
        one = diagonal.astype(f32) + parent
        two = dot(parent16, parent16)
        ancestors = one + dot(two.astype(bf16), one.astype(bf16))
        here = pl.ds(group * 128, 128)
        running = lax.dot_general(
            ancestors, forget_ref[here, :], NN,
            precision=lax.Precision.HIGHEST, preferred_element_type=f32,
        ).T
        hidden = jnp.where(ancestors > 0.5, 0.0, masked_score)
        for pair in range(pairs):
            cols = pl.ds(pair * 128, 128)
            raw = dot(stacked(q_ref[here, cols], masks), k_ref[here, cols], NT)
            for half in range(2):
                head = pair * 2 + half
                scores_ref[group * pairs + pair, half] = raw[half * 128 : half * 128 + 128] + (
                    hidden - running[head : head + 1]
                )
    for group in range(groups):
        here = pl.ds(group * 128, 128)
        for pair in range(pairs):
            cols = pl.ds(pair * 128, 128)
            tops, totals = [], []
            for half in range(2):
                scores = scores_ref[group * pairs + pair, half]
                top = jnp.broadcast_to(jnp.max(scores, axis=-1, keepdims=True), square)
                weights = jnp.exp(scores - top)
                weights_ref[group * pairs + pair, pl.ds(half * 128, 128), :] = weights.astype(bf16)
                tops.append(top)
                totals.append(jnp.broadcast_to(jnp.sum(weights, axis=-1, keepdims=True), square))
            top_ref[here, cols] = jnp.where(low, *tops)
            total_ref[here, cols] = jnp.where(low, *totals)
    for group in range(groups):
        here = pl.ds(group * 128, 128)
        for pair in range(pairs):
            cols = pl.ds(pair * 128, 128)
            numer = dot(weights_ref[group * pairs + pair], v_ref[here, cols])
            numer_ref[here, cols] = jnp.where(low, numer[:128], numer[128:])


def fresh_kernel(
    parents_ref, bias_ref, normed_hbm, wk_hbm, wv_hbm, wf_hbm, q_hbm, top_hbm, total_hbm, numer_hbm,
    logs_hbm, averages_hbm,
    normed_ref, wk_ref, wv_ref, wf_ref, q_ref, top_own, total_own, numer_own,
    k_ref, v_ref, forget_ref, top_ref, total_ref, numer_ref, scores_ref, weights_ref,
    logs_ref, averages_ref, sems, out_sems,
):
    copies = start_all(
        [
            (normed_hbm, normed_ref), (wk_hbm, wk_ref), (wv_hbm, wv_ref), (wf_hbm, wf_ref),
            (q_hbm, q_ref), (top_hbm, top_own), (total_hbm, total_own), (numer_hbm, numer_own),
        ],
        sems,
    )
    copies[0].wait()
    copies[1].wait()
    k_ref[...] = dot(normed_ref[...], wk_ref[...], NT).astype(bf16)
    copies[2].wait()
    v_ref[...] = dot(normed_ref[...], wv_ref[...], NT).astype(bf16)
    copies[3].wait()
    gate = dot(normed_ref[...], wf_ref[...], NT) + bias_ref[...]
    forget = jnp.minimum(gate, 0.0) - jnp.log1p(jnp.exp(-jnp.abs(gate)))
    forget_ref[...] = jnp.zeros_like(forget_ref)
    forget_ref[:, : forget.shape[1]] = forget
    copies[4].wait()
    state = (top_ref, total_ref, numer_ref)
    history(parents_ref, q_ref, k_ref, v_ref, forget_ref, state, scores_ref, weights_ref)
    for copy in copies[5:]:
        copy.wait()

    parts, _, part = logs_ref.shape[:3]
    span = parts * part

    def join(index, carry):
        rows = pl.ds(pl.multiple_of(index * span, span), span)
        absorb(state, rows, slice(None), top_own[rows, :], total_own[rows, :], numer_own[rows, :])
        total = total_ref[rows, :]
        logs = top_ref[rows, :] + jnp.log(total)
        averages = numer_ref[rows, :] / total
        for number in range(parts):
            logs_ref[number, index] = logs[number * part : number * part + part]
            averages_ref[number, index] = averages[number * part : number * part + part]
        return carry

    lax.fori_loop(0, logs_ref.shape[1], join, 0, unroll=2)
    for copy in start_all([(logs_ref, logs_hbm), (averages_ref, averages_hbm)], out_sems):
        copy.wait()


def fresh(parents, bias, normed, w_key, w_value, w_forget, q, own):
    rows, inner = q.shape
    span = (parents.shape[0] + 1) * BEAMS
    vmem = pl.BlockSpec(memory_space=pltpu.VMEM)
    hbm = pl.BlockSpec(memory_space=pltpu.HBM)
    big = [normed, w_key, w_value, w_forget.T, q, *own]
    wide = pltpu.VMEM((rows, inner), f32)
    out = (PARTS, rows // span, span // PARTS, inner)
    tiles = rows * inner // (128 * 128)
    return pl.pallas_call(
        fresh_kernel,
        in_specs=[vmem, vmem] + [hbm] * len(big),
        out_specs=[hbm] * 2,
        out_shape=[pltpu.HBM(out, f32)] * 2,
        scratch_shapes=[pltpu.VMEM(x.shape, x.dtype) for x in big]
        + [pltpu.VMEM((rows, inner), bf16)] * 2
        + [pltpu.VMEM((rows, 128), f32), wide, wide, wide]
        + [pltpu.VMEM((tiles, 2, 128, 128), f32), pltpu.VMEM((tiles, 256, 128), bf16)]
        + [pltpu.VMEM(out, f32)] * 2
        + [pltpu.SemaphoreType.DMA((len(big),)), pltpu.SemaphoreType.DMA((2,))],
        compiler_params=pltpu.CompilerParams(vmem_limit_bytes=24 * MIB),
        cost_estimate=pl.CostEstimate(
            flops=4 * rows * normed.shape[1] * inner, bytes_accessed=12 * MIB,
            transcendentals=8 * rows * inner,
        ),
        name="fresh",
    )(parents, bias.reshape(1, -1), *[in_hbm(x) for x in big])


def page_weights(queries, fills, keys_ref, decay_ref, scores_ref, weights_ref, tops_ref):
    span = queries[0][0].shape[0]
    masks = half_masks(span)
    lane = lanes((1, 128))
    decay = [decay_ref[head].astype(f32) for head in range(decay_ref.shape[0])]
    for page, pairs in enumerate(queries):
        valid = lane < fills[page]
        for pair, query in enumerate(pairs):
            raw = dot(stacked(query, masks), keys_ref[page, pl.ds(pair * 128, 128), :])
            for half in range(2):
                head = pair * 2 + half
                bias = jnp.where(valid, decay[head][page : page + 1], masked_score)
                scores_ref[page, pl.ds(head * span, span), :] = (
                    raw[half * span : half * span + span] + bias
                )
    for page in range(len(queries)):
        for head in range(decay_ref.shape[0]):
            rows = pl.ds(head * span, span)
            scores = scores_ref[page, rows, :]
            top = jnp.broadcast_to(jnp.max(scores, axis=-1, keepdims=True), scores.shape)
            tops_ref[page, rows, :] = top
            weights = jnp.exp(scores - top)
            weights_ref[page, rows, :] = weights.astype(bf16)
            scores_ref[page, rows, :] = jnp.broadcast_to(
                jnp.sum(weights, axis=-1, keepdims=True), scores.shape
            )


def page_sums(page, pair, span, values_ref, scores_ref, weights_ref, tops_ref):
    low = lanes((span, 128)) < 64
    first, second = pl.ds(pair * 2 * span, span), pl.ds((pair * 2 + 1) * span, span)
    numer = dot(
        weights_ref[page, pl.ds(pair * 2 * span, 2 * span), :],
        values_ref[page, pl.ds(pair * 128, 128), :],
        NT,
    )
    top = jnp.where(low, tops_ref[page, first, :], tops_ref[page, second, :])
    total = jnp.where(low, scores_ref[page, first, :], scores_ref[page, second, :])
    return top, total, jnp.where(low, numer[:span], numer[span:])


def page_scratch(pages, span, heads):
    rows = span * heads
    return [
        pltpu.VMEM((pages, rows, 128), f32),
        pltpu.VMEM((pages, rows, 128), bf16),
        pltpu.VMEM((pages, rows, 128), f32),
    ]


def own_kernel(
    request_ref, fill_ref, q_ref, keys_ref, values_ref, decay_ref,
    top_ref, total_ref, numer_ref, *scratch,
):
    state = (top_ref, total_ref, numer_ref)
    span = scratch[0].shape[1] // decay_ref.shape[0]
    local_count = q_ref.shape[0] // span
    pairs = q_ref.shape[1] // 128

    block = pl.program_id(0)

    @pl.when(block == 0)
    def _():
        top_ref[...] = jnp.full_like(top_ref, masked_score)
        total_ref[...] = jnp.zeros_like(total_ref)
        numer_ref[...] = jnp.zeros_like(numer_ref)

    places, queries, fills = [], [], []
    for page in range(PAGE_BLOCK):
        index = block * PAGE_BLOCK + page
        local = lax.rem(request_ref[index], local_count)
        rows = pl.ds(pl.multiple_of(local * span, span), span)
        places.append(rows)
        queries.append([q_ref[rows, pl.ds(pair * 128, 128)] for pair in range(pairs)])
        fills.append(fill_ref[index])
    page_weights(queries, fills, keys_ref, decay_ref, *scratch)
    for page, rows in enumerate(places):
        for pair in range(pairs):
            sums = page_sums(page, pair, span, values_ref, *scratch)
            absorb(state, rows, pl.ds(pair * 128, 128), *sums)


def page_cost(pages, keys, rows):
    inner, length = keys.shape[1:]
    return pl.CostEstimate(
        flops=pages * rows * inner * length * 8,
        bytes_accessed=pages * inner * length * 4,
        transcendentals=pages * rows * inner * length // 64,
    )


def own_pages(request, fill, q, keys, values, decay, span):
    pool = pl.BlockSpec((PAGE_BLOCK,) + keys.shape[1:], lambda i: (i, 0, 0))
    decay_spec = pl.BlockSpec((decay.shape[0], PAGE_BLOCK, decay.shape[2]), lambda i: (0, i, 0))
    rows = pl.BlockSpec(q.shape, lambda i: (0, 0))
    return pl.pallas_call(
        own_kernel,
        grid=(OWNED_SLOTS // PAGE_BLOCK,),
        in_specs=[SMEM, SMEM, rows, pool, pool, decay_spec],
        out_specs=[rows] * 3,
        out_shape=[pltpu.HBM(q.shape, f32)] * 3,
        scratch_shapes=page_scratch(PAGE_BLOCK, span, decay.shape[0]),
        compiler_params=pltpu.CompilerParams(vmem_limit_bytes=20 * MIB),
        cost_estimate=page_cost(OWNED_SLOTS, keys, 64),
        name="own_pages",
    )(request, fill, in_hbm(q), in_hbm(keys), in_hbm(values), decay)


def hosted_kernel(
    local_count, capacity, request_ref, fill_ref, q_ref, keys_ref, values_ref, decay_ref,
    out_ref, tail_ref, count_ref, *scratch,
):
    span, inner = q_ref.shape[1:]
    pairs = inner // 128
    heads = decay_ref.shape[0]
    groups = out_ref.shape[0]
    half = span // PARTS
    slot_rows = pairs * span
    out_ref[...] = jnp.zeros_like(out_ref)
    tail_ref[...] = jnp.zeros_like(tail_ref)
    for owner in range(groups):
        count_ref[owner] = 0
    places, queries, fills = [], [], []
    for page in range(SPILL):
        owner = request_ref[OWNED_SLOTS + page] // local_count
        rank = count_ref[owner]
        count_ref[owner] = rank + 1
        places.append((owner, rank))
        slot = owner * capacity + rank
        queries.append([q_ref[slot, :, pl.ds(pair * 128, 128)] for pair in range(pairs)])
        fills.append(fill_ref[OWNED_SLOTS + page])
    page_weights(queries, fills, keys_ref, decay_ref, *scratch)
    scores_ref, _, tops_ref = scratch
    lane = lanes((half, 128))
    for page, (owner, rank) in enumerate(places):
        for pair in range(pairs):
            _, total, numer = page_sums(page, pair, span, values_ref, *scratch)
            here = pl.ds(pl.multiple_of(rank * slot_rows + pair * span, span), span)
            out_ref[owner, here, :] = (numer / total).astype(bf16)
        tail = tail_ref[owner]
        base = rank * (3 * heads)
        for head in range(heads):
            rows = pl.ds(head * span, span)
            rest = tops_ref[page, rows, :] + jnp.log(scores_ref[page, rows, :])
            rest = jnp.where(lane < 64, rest[:half], rest[half:])
            for piece in range(3):
                part = rest.astype(bf16).astype(f32)
                rest = rest - part
                tail = jnp.where(lane % 64 == base + piece * heads + head, part, tail)
        tail_ref[owner] = tail
    first = capacity * slot_rows
    for owner in range(groups):
        out_ref[owner, first : first + half, :] = tail_ref[owner].astype(bf16)


def hosted_pages(request, fill, asked_rows, keys, values, decay, groups, capacity, local_count):
    count, span, inner = asked_rows.shape
    shift = OWNED_SLOTS // SPILL
    pool = pl.BlockSpec((SPILL,) + keys.shape[1:], lambda i: (shift, 0, 0))
    decay_spec = pl.BlockSpec((decay.shape[0], SPILL, decay.shape[2]), lambda i: (0, shift, 0))
    out_shape = (groups, capacity * span * inner // 128 + span // PARTS, 128)
    return pl.pallas_call(
        functools.partial(hosted_kernel, local_count, capacity),
        grid=(1,),
        in_specs=[
            SMEM, SMEM, pl.BlockSpec(asked_rows.shape, lambda i: (0, 0, 0)), pool, pool, decay_spec
        ],
        out_specs=pl.BlockSpec(out_shape, lambda i: (0, 0, 0)),
        out_shape=jax.ShapeDtypeStruct(out_shape, bf16),
        scratch_shapes=[pltpu.VMEM((groups, span // PARTS, 128), f32), pltpu.SMEM((groups,), jnp.int32)]
        + page_scratch(SPILL, span, decay.shape[0]),
        compiler_params=pltpu.CompilerParams(vmem_limit_bytes=24 * MIB),
        cost_estimate=page_cost(SPILL, keys, 64),
        name="hosted_pages",
    )(request, fill, asked_rows, in_hbm(keys), in_hbm(values), decay)


def merge_kernel(capacity, steps, part, heads, table_ref, back_ref, log_hbm, average_hbm, *refs):
    top_ref, total_ref, numer_ref, tops_ref, sems, load_sems = refs[-6:]
    count = load_sems.shape[0]
    sources, (out_ref, *targets) = refs[:count], refs[count:-6]
    groups = back_ref.shape[0]
    inner = heads * 64
    rows = steps * BEAMS
    span = PARTS * rows
    state = (top_ref, total_ref, numer_ref)
    copies = start_all([(log_hbm.at[part], top_ref), (average_hbm.at[part], numer_ref)], sems)
    pairs = []
    if part == 0:
        weight_ref, *targets = targets
        height = sources[0].shape[0]
        head = lax.axis_index("head")
        for other in range(4):
            place = pl.ds(pl.multiple_of((head ^ other) * height, height), height)
            pairs.append((sources[other], weight_ref.at[place]))
        sources = sources[4:]
    pairs.extend(zip(sources, targets))
    loads = start_all(pairs, load_sems)
    total_ref[...] = jnp.ones_like(total_ref)
    slot_rows = (inner // 128) * span
    first = capacity * slot_rows
    tails = jnp.concatenate(
        [back_ref[owner, first : first + rows, :] for owner in range(groups)], axis=0
    )
    source, target = sublanes((128, inner)), lanes((128, inner)) // 64
    for rank in range(capacity):
        hit = source < 0
        for piece in range(3):
            hit = hit | (source == target + part * 64 + (rank * 3 + piece) * heads)
        tops_ref[:, rank * inner : rank * inner + inner] = dot(tails, hit.astype(f32).astype(bf16))
    for copy in copies:
        copy.wait()
    for owner in range(groups):
        for rank in range(capacity):
            local = table_ref[owner * capacity + rank]
            bias = jnp.where(local >= 0, 0.0, masked_score)
            top = tops_ref[owner * rows : owner * rows + rows, rank * inner : rank * inner + inner]
            starts = [rank * slot_rows + pair * span + part * rows for pair in range(inner // 128)]
            average = jnp.concatenate(
                [back_ref[owner, start : start + rows, :].astype(f32) for start in starts], axis=1
            )
            here = pl.ds(pl.multiple_of(jnp.maximum(local, 0) * rows, rows), rows)
            absorb(state, here, slice(None), top + bias, 1.0, average)
    for index in range(top_ref.shape[0] // (2 * rows)):
        parts = []
        for half in range(2):
            here = slice((index * 2 + half) * rows, (index * 2 + half + 1) * rows)
            parts.append(numer_ref[here, :] / total_ref[here, :])
        for step in range(steps):
            both = jnp.concatenate([p[step * 8 : step * 8 + 8] for p in parts], axis=0)
            start = step * (top_ref.shape[0] // steps) + index * 16
            out_ref[start : start + 16, :] = both.astype(bf16)
    for copy in loads:
        copy.wait()


def merge(part, table, back, logs, averages, steps, capacity, sources):
    _, requests, span, inner = logs.shape
    rows = requests * span
    logs, averages = (x.reshape(PARTS, rows, inner) for x in (logs, averages))
    vmem = pl.BlockSpec(memory_space=pltpu.VMEM)
    hbm = pl.BlockSpec(memory_space=pltpu.HBM)
    anywhere = pl.BlockSpec(memory_space=pl.ANY)
    mixes = sources[:4] if part == 0 else []
    others = sources[len(mixes) :]
    kept = [jax.ShapeDtypeStruct(x.shape, x.dtype) for x in others]
    if mixes:
        kept = [jax.ShapeDtypeStruct((4 * inner, mixes[0].shape[1]), bf16)] + kept
    return pl.pallas_call(
        functools.partial(merge_kernel, capacity, steps, part, inner // 64),
        in_specs=[SMEM, vmem, hbm, hbm] + [anywhere] * len(mixes) + [hbm] * len(others),
        out_shape=[jax.ShapeDtypeStruct((rows, inner), bf16)] + kept,
        scratch_shapes=[pltpu.VMEM((rows, inner), f32)] * 3
        + [
            pltpu.VMEM((back.shape[0] * span, capacity * inner), f32),
            pltpu.SemaphoreType.DMA((2,)),
            pltpu.SemaphoreType.DMA((len(sources),)),
        ],
        compiler_params=pltpu.CompilerParams(vmem_limit_bytes=10 * MIB),
        cost_estimate=pl.CostEstimate(
            flops=40 * rows * inner, bytes_accessed=8 * MIB, transcendentals=4 * rows * inner
        ),
        name="merge",
    )(table, back, in_hbm(logs), in_hbm(averages), *mixes, *[in_hbm(x) for x in others])


def block_kernel(
    first, att0, att1, att2, att3, weight_ref, tokens_ref, gain_ref, gate_ref, up_ref, down_ref,
    residual_out, mine_ref, other_ref,
    residual_ref, attended_ref, scaled_ref, hidden_ref, sums_ref,
):
    rows, width = residual_ref.shape
    inner = att0.shape[1]
    half = rows // 2
    head = lax.axis_index("head")
    core = lax.rem(head, 2)
    near = pl.ds(pl.multiple_of(core * half, half), half)
    away = pl.ds(pl.multiple_of((1 - core) * half, half), half)
    for other, att in enumerate((att0, att1, att2, att3)):
        place = pl.ds(pl.multiple_of((head ^ other) * inner, inner), inner)
        attended_ref[:, place] = att[...]
    gain = gain_ref[...].reshape(1, -1)
    squares = jnp.zeros((rows, 1), f32)
    for start in range(0, width, 512):
        cols = slice(start, start + 512)
        x = tokens_ref[first : first + rows, cols].astype(f32) + dot(attended_ref[...], weight_ref[:, cols])
        residual_ref[:, cols] = x
        scaled_ref[:, cols] = (x * gain[:, cols]).astype(bf16)
        squares = squares + jnp.sum(x * x, axis=-1, keepdims=True)
    scale = lax.rsqrt(squares / width + epsilon)
    for start in range(0, gate_ref.shape[1], 256):
        cols = slice(start, start + 256)
        gate = dot(scaled_ref[...], gate_ref[:, cols]) * scale
        up = dot(scaled_ref[...], up_ref[:, cols]) * scale
        hidden_ref[:, cols] = (gate / (1.0 + jnp.exp(-gate)) * up).astype(bf16)
    residual_out[...] = residual_ref[near, :]
    for start in range(0, width, 512):
        cols = slice(start, start + 512)
        sums_ref[:, cols] = dot(hidden_ref[...], down_ref[:, cols])
    mine_ref[...] = sums_ref[near, :]
    other_ref[...] = sums_ref[away, :].astype(bf16)


def block(first, attended, weight, tokens, gain, w_gate, w_up, w_down):
    rows, inner = attended[0].shape
    width = tokens.shape[1]
    hidden = w_gate.shape[1]
    vmem = pl.BlockSpec(memory_space=pltpu.VMEM)
    half = jax.ShapeDtypeStruct((rows // 2, width), f32)
    return pl.pallas_call(
        functools.partial(block_kernel, first),
        in_specs=[vmem] * 10,
        out_specs=[vmem] * 3,
        out_shape=[half, half, jax.ShapeDtypeStruct((rows // 2, width), bf16)],
        scratch_shapes=[
            pltpu.VMEM((rows, width), f32),
            pltpu.VMEM((rows, 4 * inner), bf16),
            pltpu.VMEM((rows, width), bf16),
            pltpu.VMEM((rows, hidden), bf16),
            pltpu.VMEM((rows, width), f32),
        ],
        compiler_params=pltpu.CompilerParams(vmem_limit_bytes=20 * MIB),
        cost_estimate=pl.CostEstimate(flops=0, bytes_accessed=0, transcendentals=0),
        name="block",
    )(*attended, weight, tokens, gain, w_gate, w_up, w_down)


def finish_kernel(*refs):
    parts, out_ref = refs[:-1], refs[-1]
    core = lax.axis_index("head") % 2
    first = 0
    for index in range(0, len(parts), 2):
        half = parts[index].shape[0]
        for part, place in ((parts[index], core), (parts[index + 1], 1 - core)):
            rows = pl.ds(pl.multiple_of(first + place * half, half), half)
            out_ref[rows, :] = part[...]
        first += 2 * half


def finish(parts):
    vmem = pl.BlockSpec(memory_space=pltpu.VMEM)
    rows, width = sum(part.shape[0] for part in parts), parts[0].shape[1]
    return pl.pallas_call(
        finish_kernel,
        in_specs=[vmem] * len(parts),
        out_specs=vmem,
        out_shape=jax.ShapeDtypeStruct((rows, width), parts[0].dtype),
        compiler_params=pltpu.CompilerParams(vmem_limit_bytes=12 * MIB),
        name="finish",
    )(*parts)


def swap_core(value):
    return lax.ppermute(value, "head", [(i, i ^ 1) for i in range(4)])


def swap_chip(value):
    return lax.ppermute(value, "head", [(i, i ^ 2) for i in range(4)])


def shards(
    tokens, parents, page_request, page_fill, keys_pool, values_pool, decay_pool,
    gain_attn, w_query, w_key, w_value, w_forget, forget_bias, w_out,
    gain_ffn, w_gate, w_up, w_down,
):
    steps, rows, width = tokens.shape
    inner = w_query.shape[0]
    local_count = rows // BEAMS
    span = steps * BEAMS
    groups = lax.axis_size("group")
    capacity = (SPILL + groups - 2) // (groups - 1)
    decay = decay_pool.transpose(1, 0, 2)

    def exchange(value):
        return lax.all_to_all(value, "group", split_axis=0, concat_axis=0, tiled=True)

    ids = exchange(jnp.broadcast_to(page_request, (groups, 1, page_request.shape[0])))
    q_near, q, normed = queries_of(tokens, gain_attn, w_query)
    table, asked = ask(page_request, ids, q_near, span, capacity)
    asked, w_out = lax.optimization_barrier((asked, w_out))
    w_out_far = swap_chip(w_out)
    asked_rows = exchange(asked.reshape(groups, capacity * span, inner)).reshape(asked.shape)
    own = own_pages(page_request, page_fill, q, keys_pool, values_pool, decay, span)
    asked_rows, own = lax.optimization_barrier((asked_rows, own))
    payload = hosted_pages(
        page_request, page_fill, asked_rows, keys_pool, values_pool, decay, groups, capacity, local_count
    )
    payload, normed = lax.optimization_barrier((payload, normed))
    normed, w_out_far = lax.optimization_barrier((normed, w_out_far))
    back = exchange(payload)
    logs, averages = fresh(parents, forget_bias, normed, w_key, w_value, w_forget, q, own)
    mixes = [w_out, swap_core(w_out), w_out_far, swap_core(w_out_far)]
    logs, mixes = lax.optimization_barrier((logs, mixes))

    flat = tokens.reshape(steps * rows, width)
    each = steps // PARTS
    sums = (table, back, logs, averages, each, capacity)
    here, weight = merge(0, *sums, mixes)
    heres = [here]
    back, heres[0] = lax.optimization_barrier((back, heres[0]))
    sums = (table, back, logs, averages, each, capacity)
    here, w_gate, w_up, w_down, flat = merge(1, *sums, [w_gate, w_up, w_down, flat])
    heres.append(here)
    fars = [swap_chip(here) for here in heres]
    fars[0], heres[1] = lax.optimization_barrier((fars[0], heres[1]))

    def block_of(index):
        here, far = heres[index], fars[index]
        gathered = [here, swap_core(here), far, swap_core(far)]
        if index:
            gathered, chip[0] = lax.optimization_barrier((gathered, chip[0]))
        first = index * here.shape[0]
        return block(first, gathered, weight, flat, gain_ffn, w_gate, w_up, w_down)

    def chip_sum(mine, other):
        return (mine + swap_core(other).astype(f32)).astype(bf16)

    chip, residual = [None] * PARTS, [None] * PARTS
    residual[0], mine, other = block_of(0)
    other, fars[1] = lax.optimization_barrier((other, fars[1]))
    chip[0] = chip_sum(mine, other)
    most = chip[0].shape[0] // 2
    chip_most, chip_rest = chip[0][:most], chip[0][most:]
    far_most, far_rest = swap_chip(chip_most), swap_chip(chip_rest)
    residual[1], mine, other = block_of(1)
    other, far_most = lax.optimization_barrier((other, far_most))
    chip[1] = chip_sum(mine, other)
    far_chip = [jnp.concatenate([far_most, far_rest], axis=0), swap_chip(chip[1])]
    parts = []
    for index in range(PARTS):
        both = chip[index].astype(f32) + far_chip[index].astype(f32)
        done = (residual[index] + both).astype(bf16)
        parts.extend([done, swap_core(done)])
    return finish(parts).reshape(steps, rows, width)


def solution(mesh):
    return jax.shard_map(
        shards,
        mesh=mesh,
        in_specs=(
            P(None, "group", None),
            P(None, "group"),
            P("group"),
            P("group"),
            P("group", "head", None),
            P("group", "head", None),
            P("group", "head", None),
            P(),
            P("head", None),
            P("head", None),
            P("head", None),
            P(None, "head"),
            P("head"),
            P("head", None),
            P(),
            P(None, "head"),
            P(None, "head"),
            P("head", None),
        ),
        out_specs=P(None, "group", None),
        check_vma=False,
    )
```

```python
import functools

import jax
import jax.numpy as jnp
from jax import lax
from jax.experimental import pallas as pl
from jax.experimental.pallas import tpu as pltpu
from jax.sharding import PartitionSpec as P

BEAMS = 8
OWNED_SLOTS = 32
SPILL = 16
PAGE_BLOCK = 16
PARTS = 2
MIB = 1 << 20

epsilon = 1e-05
masked_score = -1e30
f32 = jnp.float32
bf16 = jnp.bfloat16

NN = (((1,), (0,)), ((), ()))
NT = (((1,), (1,)), ((), ()))
SMEM = pl.BlockSpec(memory_space=pltpu.SMEM)


def dot(a, b, dims=NN):
    return lax.dot_general(a, b, dims, preferred_element_type=f32)


def lanes(shape):
    return lax.broadcasted_iota(jnp.int32, shape, len(shape) - 1)


def sublanes(shape):
    return lax.broadcasted_iota(jnp.int32, shape, len(shape) - 2)


def in_hbm(array):
    return pltpu.with_memory_space_constraint(array, pltpu.HBM)


def in_vmem(array):
    return pltpu.with_memory_space_constraint(array, pltpu.VMEM)


def start_all(pairs, sems):
    copies = [pltpu.make_async_copy(s, t, sems.at[i]) for i, (s, t) in enumerate(pairs)]
    for copy in copies:
        copy.start()
    return copies


def fill_table(local_count, capacity, first, ids_ref, table_ref):
    groups = ids_ref.shape[0]
    for slot in range(groups * capacity):
        table_ref[slot] = -1

    def group(index, carry):
        rank = jnp.int32(0)
        for page in range(SPILL):
            local = ids_ref[index, 0, OWNED_SLOTS + page] - first
            mine = (local >= 0) & (local < local_count)

            @pl.when(mine)
            def _():
                table_ref[index * capacity + rank] = local

            rank = rank + mine.astype(jnp.int32)
        return carry

    lax.fori_loop(0, groups, group, 0)


def query_kernel(
    tokens_hbm, gain_ref, wq_hbm, q_ref, q_hbm, normed_hbm,
    tokens_ref, wq_ref, normed_ref, sems, out_sems,
):
    steps, rows, _ = tokens_ref.shape
    span = steps * BEAMS
    cut = rows // 2
    copies = start_all(
        [
            (tokens_hbm.at[:, :cut], tokens_ref.at[:, :cut]),
            (tokens_hbm.at[:, cut:], tokens_ref.at[:, cut:]),
            (wq_hbm, wq_ref),
        ],
        sems,
    )
    gain = gain_ref[...].reshape(1, -1)

    def pair(index, carry):
        slabs = []
        for step in range(steps):
            x = tokens_ref[step, pl.ds(pl.multiple_of(index * 16, 16), 16), :].astype(f32)
            scale = lax.rsqrt(jnp.mean(x * x, axis=-1, keepdims=True) + epsilon)
            slabs.append(x * scale * gain)
        for half in range(2):
            part = jnp.concatenate([s[half * 8 : half * 8 + 8] for s in slabs], axis=0)
            start = pl.multiple_of((index * 2 + half) * span, span)
            normed_ref[pl.ds(start, span), :] = part.astype(bf16)
        return carry

    copies[0].wait()
    lax.fori_loop(0, cut // 16, pair, 0, unroll=2)
    copies[1].wait()
    lax.fori_loop(cut // 16, rows // 16, pair, 0, unroll=2)
    leaving = start_all([(normed_ref, normed_hbm)], out_sems)
    copies[2].wait()
    query = dot(normed_ref[...], wq_ref[...], NT).astype(bf16)
    q_ref[...] = (query.astype(f32) * 0.125).astype(bf16)
    last = pltpu.make_async_copy(q_ref, q_hbm, out_sems.at[1])
    last.start()
    leaving[0].wait()
    last.wait()


def queries_of(tokens, gain, w_query):
    steps, rows, width = tokens.shape
    inner = w_query.shape[0]
    total = steps * rows
    hbm = pl.BlockSpec(memory_space=pltpu.HBM)
    vmem = pl.BlockSpec(memory_space=pltpu.VMEM)
    return pl.pallas_call(
        query_kernel,
        in_specs=[hbm, vmem, hbm],
        out_specs=[vmem, hbm, hbm],
        out_shape=[
            pltpu.VMEM((total, inner), bf16),
            pltpu.HBM((total, inner), bf16),
            pltpu.HBM((total, width), bf16),
        ],
        scratch_shapes=[
            pltpu.VMEM(tokens.shape, bf16),
            pltpu.VMEM(w_query.shape, bf16),
            pltpu.VMEM((total, width), bf16),
            pltpu.SemaphoreType.DMA((3,)),
            pltpu.SemaphoreType.DMA((2,)),
        ],
        compiler_params=pltpu.CompilerParams(vmem_limit_bytes=12 * MIB),
        cost_estimate=pl.CostEstimate(
            flops=2 * total * width * inner, bytes_accessed=6 * MIB, transcendentals=total
        ),
        name="queries",
    )(in_hbm(tokens), gain, in_hbm(w_query))


def ask_kernel(capacity, request_ref, ids_ref, q_ref, table_ref, out_ref):
    slots, span, _ = out_ref.shape
    local_count = q_ref.shape[0] // span
    first = request_ref[0] // local_count * local_count
    fill_table(local_count, capacity, first, ids_ref, table_ref)
    for slot in range(slots):
        start = jnp.maximum(table_ref[slot], 0) * span
        out_ref[slot] = q_ref[pl.ds(pl.multiple_of(start, span), span), :]


def ask(request, ids, q, span, capacity):
    slots = ids.shape[0] * capacity
    vmem = pl.BlockSpec(memory_space=pltpu.VMEM)
    return pl.pallas_call(
        functools.partial(ask_kernel, capacity),
        in_specs=[SMEM, SMEM, vmem],
        out_specs=[SMEM, vmem],
        out_shape=[
            jax.ShapeDtypeStruct((slots,), jnp.int32),
            jax.ShapeDtypeStruct((slots, span, q.shape[1]), bf16),
        ],
        compiler_params=pltpu.CompilerParams(vmem_limit_bytes=8 * MIB),
        name="ask",
    )(request, ids, in_vmem(q))


def half_masks(rows):
    low = lanes((rows, 128)) < 64
    return low.astype(f32).astype(bf16), jnp.logical_not(low).astype(f32).astype(bf16)


def stacked(pair_rows, masks):
    return jnp.concatenate([pair_rows * masks[0], pair_rows * masks[1]], axis=0)


def side_by_side(values, rows):
    low = lanes((rows, 128)) < 64
    top = jnp.broadcast_to(values[:rows], (rows, 128))
    bottom = jnp.broadcast_to(values[rows:], (rows, 128))
    return jnp.where(low, top, bottom)


def absorb(state, rows, columns, top, total, numer):
    top_ref, total_ref, numer_ref = state
    old = top_ref[rows, columns]
    new = jnp.maximum(old, top)
    keep = jnp.exp(old - new)
    add = jnp.exp(top - new)
    top_ref[rows, columns] = new
    total_ref[rows, columns] = total_ref[rows, columns] * keep + total * add
    numer_ref[rows, columns] = numer_ref[rows, columns] * keep + numer * add


def history(parents_ref, q_ref, k_ref, v_ref, forget_ref, state, scores_ref, weights_ref):
    transitions, rows = parents_ref.shape
    span = (transitions + 1) * BEAMS
    pack = 128 // span
    square = (128, 128)
    diagonal = sublanes(square) == lanes(square)
    columns = []
    for step in range(transitions):
        row = parents_ref[step : step + 1, :].astype(f32)
        columns.append(
            jnp.sum(jnp.where(diagonal, jnp.broadcast_to(row, square), 0.0), axis=1, keepdims=True)
        )
    lane8 = lanes((8, 128)).astype(f32)
    masks = half_masks(128)
    low = lanes(square) < 64
    top_ref, total_ref, numer_ref = state
    groups = rows // BEAMS // pack
    pairs = q_ref.shape[1] // 128
    for group in range(groups):
        slabs = []
        for member in range(pack):
            first = (group * pack + member) * BEAMS
            slabs.append(jnp.zeros((8, 128), f32))
            for step in range(transitions):
                wanted = columns[step][first : first + 8] + float(member * span + step * 8)
                slabs.append(jnp.where(lane8 == wanted, 1.0, 0.0))
        parent = jnp.concatenate(slabs, axis=0)
        parent16 = parent.astype(bf16)
        one = diagonal.astype(f32) + parent
        two = dot(parent16, parent16)
        ancestors = one + dot(two.astype(bf16), one.astype(bf16))
        here = pl.ds(group * 128, 128)
        running = lax.dot_general(
            ancestors, forget_ref[here, :], NN,
            precision=lax.Precision.HIGHEST, preferred_element_type=f32,
        ).T
        hidden = jnp.where(ancestors > 0.5, 0.0, masked_score)
        for pair in range(pairs):
            cols = pl.ds(pair * 128, 128)
            raw = dot(stacked(q_ref[here, cols], masks), k_ref[here, cols], NT)
            for half in range(2):
                head = pair * 2 + half
                scores_ref[group * pairs + pair, half] = raw[half * 128 : half * 128 + 128] + (
                    hidden - running[head : head + 1]
                )
    for group in range(groups):
        here = pl.ds(group * 128, 128)
        for pair in range(pairs):
            cols = pl.ds(pair * 128, 128)
            tops, totals = [], []
            for half in range(2):
                scores = scores_ref[group * pairs + pair, half]
                top = jnp.broadcast_to(jnp.max(scores, axis=-1, keepdims=True), square)
                weights = jnp.exp(scores - top)
                weights_ref[group * pairs + pair, pl.ds(half * 128, 128), :] = weights.astype(bf16)
                tops.append(top)
                totals.append(jnp.broadcast_to(jnp.sum(weights, axis=-1, keepdims=True), square))
            top_ref[here, cols] = jnp.where(low, *tops)
            total_ref[here, cols] = jnp.where(low, *totals)
    for group in range(groups):
        here = pl.ds(group * 128, 128)
        for pair in range(pairs):
            cols = pl.ds(pair * 128, 128)
            numer = dot(weights_ref[group * pairs + pair], v_ref[here, cols])
            numer_ref[here, cols] = jnp.where(low, numer[:128], numer[128:])


def fresh_kernel(
    parents_ref, bias_ref, normed_hbm, wk_hbm, wv_hbm, wf_hbm, q_hbm, top_hbm, total_hbm, numer_hbm,
    logs_hbm, averages_hbm,
    normed_ref, wk_ref, wv_ref, wf_ref, q_ref, top_own, total_own, numer_own,
    k_ref, v_ref, forget_ref, top_ref, total_ref, numer_ref, scores_ref, weights_ref,
    logs_ref, averages_ref, sems, out_sems,
):
    copies = start_all(
        [
            (normed_hbm, normed_ref), (wk_hbm, wk_ref), (wv_hbm, wv_ref), (wf_hbm, wf_ref),
            (q_hbm, q_ref), (top_hbm, top_own), (total_hbm, total_own), (numer_hbm, numer_own),
        ],
        sems,
    )
    copies[0].wait()
    copies[1].wait()
    k_ref[...] = dot(normed_ref[...], wk_ref[...], NT).astype(bf16)
    copies[2].wait()
    v_ref[...] = dot(normed_ref[...], wv_ref[...], NT).astype(bf16)
    copies[3].wait()
    gate = dot(normed_ref[...], wf_ref[...], NT) + bias_ref[...]
    forget = jnp.minimum(gate, 0.0) - jnp.log1p(jnp.exp(-jnp.abs(gate)))
    forget_ref[...] = jnp.zeros_like(forget_ref)
    forget_ref[:, : forget.shape[1]] = forget
    copies[4].wait()
    state = (top_ref, total_ref, numer_ref)
    history(parents_ref, q_ref, k_ref, v_ref, forget_ref, state, scores_ref, weights_ref)
    for copy in copies[5:]:
        copy.wait()

    parts, _, part = logs_ref.shape[:3]
    span = parts * part

    def join(index, carry):
        rows = pl.ds(pl.multiple_of(index * span, span), span)
        absorb(state, rows, slice(None), top_own[rows, :], total_own[rows, :], numer_own[rows, :])
        total = total_ref[rows, :]
        logs = top_ref[rows, :] + jnp.log(total)
        averages = numer_ref[rows, :] / total
        for number in range(parts):
            logs_ref[number, index] = logs[number * part : number * part + part]
            averages_ref[number, index] = averages[number * part : number * part + part]
        return carry

    lax.fori_loop(0, logs_ref.shape[1], join, 0, unroll=2)
    for copy in start_all([(logs_ref, logs_hbm), (averages_ref, averages_hbm)], out_sems):
        copy.wait()


def fresh(parents, bias, normed, w_key, w_value, w_forget, q, own):
    rows, inner = q.shape
    span = (parents.shape[0] + 1) * BEAMS
    vmem = pl.BlockSpec(memory_space=pltpu.VMEM)
    hbm = pl.BlockSpec(memory_space=pltpu.HBM)
    big = [normed, w_key, w_value, w_forget.T, q, *own]
    wide = pltpu.VMEM((rows, inner), f32)
    out = (PARTS, rows // span, span // PARTS, inner)
    tiles = rows * inner // (128 * 128)
    return pl.pallas_call(
        fresh_kernel,
        in_specs=[vmem, vmem] + [hbm] * len(big),
        out_specs=[hbm] * 2,
        out_shape=[pltpu.HBM(out, f32)] * 2,
        scratch_shapes=[pltpu.VMEM(x.shape, x.dtype) for x in big]
        + [pltpu.VMEM((rows, inner), bf16)] * 2
        + [pltpu.VMEM((rows, 128), f32), wide, wide, wide]
        + [pltpu.VMEM((tiles, 2, 128, 128), f32), pltpu.VMEM((tiles, 256, 128), bf16)]
        + [pltpu.VMEM(out, f32)] * 2
        + [pltpu.SemaphoreType.DMA((len(big),)), pltpu.SemaphoreType.DMA((2,))],
        compiler_params=pltpu.CompilerParams(vmem_limit_bytes=24 * MIB),
        cost_estimate=pl.CostEstimate(
            flops=4 * rows * normed.shape[1] * inner, bytes_accessed=12 * MIB,
            transcendentals=8 * rows * inner,
        ),
        name="fresh",
    )(parents, bias.reshape(1, -1), *[in_hbm(x) for x in big])


def page_weights(queries, fills, keys_ref, decay_ref, scores_ref, weights_ref, tops_ref):
    span = queries[0][0].shape[0]
    masks = half_masks(span)
    lane = lanes((1, 128))
    decay = [decay_ref[head].astype(f32) for head in range(decay_ref.shape[0])]
    for page, pairs in enumerate(queries):
        valid = lane < fills[page]
        for pair, query in enumerate(pairs):
            raw = dot(stacked(query, masks), keys_ref[page, pl.ds(pair * 128, 128), :])
            for half in range(2):
                head = pair * 2 + half
                bias = jnp.where(valid, decay[head][page : page + 1], masked_score)
                scores_ref[page, pl.ds(head * span, span), :] = (
                    raw[half * span : half * span + span] + bias
                )
    for page in range(len(queries)):
        for head in range(decay_ref.shape[0]):
            rows = pl.ds(head * span, span)
            scores = scores_ref[page, rows, :]
            top = jnp.broadcast_to(jnp.max(scores, axis=-1, keepdims=True), scores.shape)
            tops_ref[page, rows, :] = top
            weights = jnp.exp(scores - top)
            weights_ref[page, rows, :] = weights.astype(bf16)
            scores_ref[page, rows, :] = jnp.broadcast_to(
                jnp.sum(weights, axis=-1, keepdims=True), scores.shape
            )


def page_sums(page, pair, span, values_ref, scores_ref, weights_ref, tops_ref):
    low = lanes((span, 128)) < 64
    first, second = pl.ds(pair * 2 * span, span), pl.ds((pair * 2 + 1) * span, span)
    numer = dot(
        weights_ref[page, pl.ds(pair * 2 * span, 2 * span), :],
        values_ref[page, pl.ds(pair * 128, 128), :],
        NT,
    )
    top = jnp.where(low, tops_ref[page, first, :], tops_ref[page, second, :])
    total = jnp.where(low, scores_ref[page, first, :], scores_ref[page, second, :])
    return top, total, jnp.where(low, numer[:span], numer[span:])


def page_scratch(pages, span, heads):
    rows = span * heads
    return [
        pltpu.VMEM((pages, rows, 128), f32),
        pltpu.VMEM((pages, rows, 128), bf16),
        pltpu.VMEM((pages, rows, 128), f32),
    ]


def own_kernel(
    request_ref, fill_ref, q_ref, keys_ref, values_ref, decay_ref,
    top_ref, total_ref, numer_ref, *scratch,
):
    state = (top_ref, total_ref, numer_ref)
    span = scratch[0].shape[1] // decay_ref.shape[0]
    local_count = q_ref.shape[0] // span
    pairs = q_ref.shape[1] // 128

    block = pl.program_id(0)

    @pl.when(block == 0)
    def _():
        top_ref[...] = jnp.full_like(top_ref, masked_score)
        total_ref[...] = jnp.zeros_like(total_ref)
        numer_ref[...] = jnp.zeros_like(numer_ref)

    places, queries, fills = [], [], []
    for page in range(PAGE_BLOCK):
        index = block * PAGE_BLOCK + page
        local = lax.rem(request_ref[index], local_count)
        rows = pl.ds(pl.multiple_of(local * span, span), span)
        places.append(rows)
        queries.append([q_ref[rows, pl.ds(pair * 128, 128)] for pair in range(pairs)])
        fills.append(fill_ref[index])
    page_weights(queries, fills, keys_ref, decay_ref, *scratch)
    for page, rows in enumerate(places):
        for pair in range(pairs):
            sums = page_sums(page, pair, span, values_ref, *scratch)
            absorb(state, rows, pl.ds(pair * 128, 128), *sums)


def page_cost(pages, keys, rows):
    inner, length = keys.shape[1:]
    return pl.CostEstimate(
        flops=pages * rows * inner * length * 8,
        bytes_accessed=pages * inner * length * 4,
        transcendentals=pages * rows * inner * length // 64,
    )


def own_pages(request, fill, q, keys, values, decay, span):
    pool = pl.BlockSpec((PAGE_BLOCK,) + keys.shape[1:], lambda i: (i, 0, 0))
    decay_spec = pl.BlockSpec((decay.shape[0], PAGE_BLOCK, decay.shape[2]), lambda i: (0, i, 0))
    rows = pl.BlockSpec(q.shape, lambda i: (0, 0))
    return pl.pallas_call(
        own_kernel,
        grid=(OWNED_SLOTS // PAGE_BLOCK,),
        in_specs=[SMEM, SMEM, rows, pool, pool, decay_spec],
        out_specs=[rows] * 3,
        out_shape=[pltpu.HBM(q.shape, f32)] * 3,
        scratch_shapes=page_scratch(PAGE_BLOCK, span, decay.shape[0]),
        compiler_params=pltpu.CompilerParams(vmem_limit_bytes=20 * MIB),
        cost_estimate=page_cost(OWNED_SLOTS, keys, 64),
        name="own_pages",
    )(request, fill, in_hbm(q), in_hbm(keys), in_hbm(values), decay)


def hosted_kernel(
    local_count, capacity, request_ref, fill_ref, q_ref, keys_ref, values_ref, decay_ref,
    out_ref, tail_ref, count_ref, *scratch,
):
    span, inner = q_ref.shape[1:]
    pairs = inner // 128
    heads = decay_ref.shape[0]
    groups = out_ref.shape[0]
    half = span // PARTS
    slot_rows = pairs * span
    out_ref[...] = jnp.zeros_like(out_ref)
    tail_ref[...] = jnp.zeros_like(tail_ref)
    for owner in range(groups):
        count_ref[owner] = 0
    places, queries, fills = [], [], []
    for page in range(SPILL):
        owner = request_ref[OWNED_SLOTS + page] // local_count
        rank = count_ref[owner]
        count_ref[owner] = rank + 1
        places.append((owner, rank))
        slot = owner * capacity + rank
        queries.append([q_ref[slot, :, pl.ds(pair * 128, 128)] for pair in range(pairs)])
        fills.append(fill_ref[OWNED_SLOTS + page])
    page_weights(queries, fills, keys_ref, decay_ref, *scratch)
    scores_ref, _, tops_ref = scratch
    lane = lanes((half, 128))
    for page, (owner, rank) in enumerate(places):
        for pair in range(pairs):
            _, total, numer = page_sums(page, pair, span, values_ref, *scratch)
            here = pl.ds(pl.multiple_of(rank * slot_rows + pair * span, span), span)
            out_ref[owner, here, :] = (numer / total).astype(bf16)
        tail = tail_ref[owner]
        base = rank * (3 * heads)
        for head in range(heads):
            rows = pl.ds(head * span, span)
            rest = tops_ref[page, rows, :] + jnp.log(scores_ref[page, rows, :])
            rest = jnp.where(lane < 64, rest[:half], rest[half:])
            for piece in range(3):
                part = rest.astype(bf16).astype(f32)
                rest = rest - part
                tail = jnp.where(lane % 64 == base + piece * heads + head, part, tail)
        tail_ref[owner] = tail
    first = capacity * slot_rows
    for owner in range(groups):
        out_ref[owner, first : first + half, :] = tail_ref[owner].astype(bf16)


def hosted_pages(request, fill, asked_rows, keys, values, decay, groups, capacity, local_count):
    count, span, inner = asked_rows.shape
    shift = OWNED_SLOTS // SPILL
    pool = pl.BlockSpec((SPILL,) + keys.shape[1:], lambda i: (shift, 0, 0))
    decay_spec = pl.BlockSpec((decay.shape[0], SPILL, decay.shape[2]), lambda i: (0, shift, 0))
    out_shape = (groups, capacity * span * inner // 128 + span // PARTS, 128)
    return pl.pallas_call(
        functools.partial(hosted_kernel, local_count, capacity),
        grid=(1,),
        in_specs=[
            SMEM, SMEM, pl.BlockSpec(asked_rows.shape, lambda i: (0, 0, 0)), pool, pool, decay_spec
        ],
        out_specs=pl.BlockSpec(out_shape, lambda i: (0, 0, 0)),
        out_shape=jax.ShapeDtypeStruct(out_shape, bf16),
        scratch_shapes=[pltpu.VMEM((groups, span // PARTS, 128), f32), pltpu.SMEM((groups,), jnp.int32)]
        + page_scratch(SPILL, span, decay.shape[0]),
        compiler_params=pltpu.CompilerParams(vmem_limit_bytes=24 * MIB),
        cost_estimate=page_cost(SPILL, keys, 64),
        name="hosted_pages",
    )(request, fill, asked_rows, in_hbm(keys), in_hbm(values), decay)


def merge_kernel(capacity, steps, part, heads, table_ref, back_ref, log_hbm, average_hbm, *refs):
    sources, targets, load_sems = [], [], None
    if len(refs) > 6:
        *refs, load_sems = refs
        count = load_sems.shape[0]
        sources, refs = refs[:count], refs[count:]
        targets, refs = refs[1:-5], (refs[0], *refs[-5:])
    out_ref, top_ref, total_ref, numer_ref, tops_ref, sems = refs
    groups = back_ref.shape[0]
    inner = heads * 64
    rows = steps * BEAMS
    span = PARTS * rows
    state = (top_ref, total_ref, numer_ref)
    copies = start_all([(log_hbm.at[part], top_ref), (average_hbm.at[part], numer_ref)], sems)
    pairs = []
    if sources:
        weight_ref, *targets = targets
        height = sources[0].shape[0]
        head = lax.axis_index("head")
        for other in range(4):
            place = pl.ds(pl.multiple_of((head ^ other) * height, height), height)
            pairs.append((sources[other], weight_ref.at[place]))
        sources = sources[4:]
    pairs.extend(zip(sources, targets))
    loads = start_all(pairs, load_sems)
    total_ref[...] = jnp.ones_like(total_ref)
    slot_rows = (inner // 128) * span
    first = capacity * slot_rows
    tails = jnp.concatenate(
        [back_ref[owner, first : first + rows, :] for owner in range(groups)], axis=0
    )
    source, target = sublanes((128, inner)), lanes((128, inner)) // 64
    for rank in range(capacity):
        hit = source < 0
        for piece in range(3):
            hit = hit | (source == target + part * 64 + (rank * 3 + piece) * heads)
        tops_ref[:, rank * inner : rank * inner + inner] = dot(tails, hit.astype(f32).astype(bf16))
    for copy in copies:
        copy.wait()
    for owner in range(groups):
        for rank in range(capacity):
            local = table_ref[owner * capacity + rank]
            bias = jnp.where(local >= 0, 0.0, masked_score)
            top = tops_ref[owner * rows : owner * rows + rows, rank * inner : rank * inner + inner]
            starts = [rank * slot_rows + pair * span + part * rows for pair in range(inner // 128)]
            average = jnp.concatenate(
                [back_ref[owner, start : start + rows, :].astype(f32) for start in starts], axis=1
            )
            here = pl.ds(pl.multiple_of(jnp.maximum(local, 0) * rows, rows), rows)
            absorb(state, here, slice(None), top + bias, 1.0, average)
    for index in range(top_ref.shape[0] // (2 * rows)):
        parts = []
        for half in range(2):
            here = slice((index * 2 + half) * rows, (index * 2 + half + 1) * rows)
            parts.append(numer_ref[here, :] / total_ref[here, :])
        for step in range(steps):
            both = jnp.concatenate([p[step * 8 : step * 8 + 8] for p in parts], axis=0)
            start = step * (top_ref.shape[0] // steps) + index * 16
            out_ref[start : start + 16, :] = both.astype(bf16)
    for copy in loads:
        copy.wait()


def merge(part, table, back, logs, averages, steps, capacity, sources):
    _, requests, span, inner = logs.shape
    rows = requests * span
    logs, averages = (x.reshape(PARTS, rows, inner) for x in (logs, averages))
    vmem = pl.BlockSpec(memory_space=pltpu.VMEM)
    hbm = pl.BlockSpec(memory_space=pltpu.HBM)
    anywhere = pl.BlockSpec(memory_space=pl.ANY)
    mixes = sources[:4]
    others = sources[len(mixes) :]
    kept = [jax.ShapeDtypeStruct(x.shape, x.dtype) for x in others]
    if mixes:
        kept = [jax.ShapeDtypeStruct((4 * inner, mixes[0].shape[1]), bf16)] + kept
    return pl.pallas_call(
        functools.partial(merge_kernel, capacity, steps, part, inner // 64),
        in_specs=[SMEM, vmem, hbm, hbm] + [anywhere] * len(mixes) + [hbm] * len(others),
        out_shape=[jax.ShapeDtypeStruct((rows, inner), bf16)] + kept,
        scratch_shapes=[pltpu.VMEM((rows, inner), f32)] * 3
        + [
            pltpu.VMEM((back.shape[0] * span, capacity * inner), f32),
            pltpu.SemaphoreType.DMA((2,)),
        ]
        + [pltpu.SemaphoreType.DMA((len(sources),))] * bool(sources),
        compiler_params=pltpu.CompilerParams(vmem_limit_bytes=10 * MIB),
        cost_estimate=pl.CostEstimate(
            flops=40 * rows * inner, bytes_accessed=8 * MIB, transcendentals=4 * rows * inner
        ),
        name="merge",
    )(table, back, in_hbm(logs), in_hbm(averages), *mixes, *[in_hbm(x) for x in others])


def block_kernel(
    first, att0, att1, att2, att3, weight_ref, tokens_ref, gain_ref, gate_ref, up_ref, down_ref,
    residual_out, mine_ref, other_ref,
    residual_ref, attended_ref, scaled_ref, hidden_ref, sums_ref,
):
    rows, width = residual_ref.shape
    inner = att0.shape[1]
    half = rows // 2
    head = lax.axis_index("head")
    core = lax.rem(head, 2)
    near = pl.ds(pl.multiple_of(core * half, half), half)
    away = pl.ds(pl.multiple_of((1 - core) * half, half), half)
    for other, att in enumerate((att0, att1, att2, att3)):
        place = pl.ds(pl.multiple_of((head ^ other) * inner, inner), inner)
        attended_ref[:, place] = att[...]
    gain = gain_ref[...].reshape(1, -1)
    squares = jnp.zeros((rows, 1), f32)
    for start in range(0, width, 512):
        cols = slice(start, start + 512)
        x = tokens_ref[first : first + rows, cols].astype(f32) + dot(attended_ref[...], weight_ref[:, cols])
        residual_ref[:, cols] = x
        scaled_ref[:, cols] = (x * gain[:, cols]).astype(bf16)
        squares = squares + jnp.sum(x * x, axis=-1, keepdims=True)
    scale = lax.rsqrt(squares / width + epsilon)
    for start in range(0, gate_ref.shape[1], 256):
        cols = slice(start, start + 256)
        gate = dot(scaled_ref[...], gate_ref[:, cols]) * scale
        up = dot(scaled_ref[...], up_ref[:, cols]) * scale
        hidden_ref[:, cols] = (gate / (1.0 + jnp.exp(-gate)) * up).astype(bf16)
    residual_out[...] = residual_ref[near, :]
    for start in range(0, width, 512):
        cols = slice(start, start + 512)
        sums_ref[:, cols] = dot(hidden_ref[...], down_ref[:, cols])
    mine_ref[...] = sums_ref[near, :]
    other_ref[...] = sums_ref[away, :].astype(bf16)


def block(first, attended, weight, tokens, gain, w_gate, w_up, w_down):
    rows, inner = attended[0].shape
    width = tokens.shape[1]
    hidden = w_gate.shape[1]
    vmem = pl.BlockSpec(memory_space=pltpu.VMEM)
    half = jax.ShapeDtypeStruct((rows // 2, width), f32)
    return pl.pallas_call(
        functools.partial(block_kernel, first),
        in_specs=[vmem] * 10,
        out_specs=[vmem] * 3,
        out_shape=[half, half, jax.ShapeDtypeStruct((rows // 2, width), bf16)],
        scratch_shapes=[
            pltpu.VMEM((rows, width), f32),
            pltpu.VMEM((rows, 4 * inner), bf16),
            pltpu.VMEM((rows, width), bf16),
            pltpu.VMEM((rows, hidden), bf16),
            pltpu.VMEM((rows, width), f32),
        ],
        compiler_params=pltpu.CompilerParams(vmem_limit_bytes=20 * MIB),
        cost_estimate=pl.CostEstimate(flops=0, bytes_accessed=0, transcendentals=0),
        name="block",
    )(*attended, weight, tokens, gain, w_gate, w_up, w_down)


def finish_kernel(first, half, places, *refs):
    count = 2 * len(places)
    parts, out_ref, sems = refs[-2 - count : -2], refs[-2], refs[-1]
    core = lax.axis_index("head") % 2
    pairs = []
    for index, place in enumerate(places):
        for part, owner in ((parts[2 * index], core), (parts[2 * index + 1], 1 - core)):
            start = pl.multiple_of(first + owner * half + place, 16)
            pairs.append((part, out_ref.at[pl.ds(start, part.shape[0])]))
    for copy in start_all(pairs, sems):
        copy.wait()


def finish(first, half, pieces, rows, before=()):
    vmem = pl.BlockSpec(memory_space=pltpu.VMEM)
    hbm = pl.BlockSpec(memory_space=pltpu.HBM)
    places, parts = [], []
    for place, done in pieces:
        places.append(place)
        parts.extend([done, swap_core(done)])
    width = parts[0].shape[1]
    return pl.pallas_call(
        functools.partial(finish_kernel, first, half, places),
        in_specs=[hbm] * len(before) + [vmem] * len(parts),
        out_specs=hbm,
        out_shape=pltpu.HBM((rows, width), parts[0].dtype),
        input_output_aliases={0: 0} if before else {},
        scratch_shapes=[pltpu.SemaphoreType.DMA((len(parts),))],
        compiler_params=pltpu.CompilerParams(vmem_limit_bytes=8 * MIB),
        name="finish",
    )(*[in_hbm(x) for x in before], *parts)


def swap_core(value):
    return lax.ppermute(value, "head", [(i, i ^ 1) for i in range(4)])


def swap_chip(value):
    return lax.ppermute(value, "head", [(i, i ^ 2) for i in range(4)])


def shards(
    tokens, parents, page_request, page_fill, keys_pool, values_pool, decay_pool,
    gain_attn, w_query, w_key, w_value, w_forget, forget_bias, w_out,
    gain_ffn, w_gate, w_up, w_down,
):
    steps, rows, width = tokens.shape
    inner = w_query.shape[0]
    local_count = rows // BEAMS
    span = steps * BEAMS
    groups = lax.axis_size("group")
    capacity = (SPILL + groups - 2) // (groups - 1)
    decay = decay_pool.transpose(1, 0, 2)

    def exchange(value):
        return lax.all_to_all(value, "group", split_axis=0, concat_axis=0, tiled=True)

    ids = exchange(jnp.broadcast_to(page_request, (groups, 1, page_request.shape[0])))
    q_near, q, normed = queries_of(tokens, gain_attn, w_query)
    table, asked = ask(page_request, ids, q_near, span, capacity)
    asked_rows = exchange(asked.reshape(groups, capacity * span, inner)).reshape(asked.shape)
    asked, q = lax.optimization_barrier((asked, q))
    own = own_pages(page_request, page_fill, q, keys_pool, values_pool, decay, span)
    own, w_sent = lax.optimization_barrier((own, w_out))
    w_out_far = swap_chip(w_sent)
    asked_rows, own = lax.optimization_barrier((asked_rows, own))
    payload = hosted_pages(
        page_request, page_fill, asked_rows, keys_pool, values_pool, decay, groups, capacity, local_count
    )
    payload, normed = lax.optimization_barrier((payload, normed))
    back = exchange(payload)
    logs, averages = fresh(parents, forget_bias, normed, w_key, w_value, w_forget, q, own)
    back, w_out_far = lax.optimization_barrier((back, w_out_far))
    mixes = [w_out, swap_core(w_out), w_out_far, swap_core(w_out_far)]

    flat = tokens.reshape(steps * rows, width)
    each = steps // PARTS
    sums = (table, back, logs, averages, each, capacity)
    heres = list(merge(0, *sums, []))
    back, heres[0] = lax.optimization_barrier((back, heres[0]))
    sums = (table, back, logs, averages, each, capacity)
    here, weight, w_gate, w_up, w_down, flat = merge(1, *sums, mixes + [w_gate, w_up, w_down, flat])
    heres.append(here)
    fars = [swap_chip(here) for here in heres]
    fars[0], heres[1] = lax.optimization_barrier((fars[0], heres[1]))

    def block_of(index):
        here, far = heres[index], fars[index]
        gathered = [here, swap_core(here), far, swap_core(far)]
        if index:
            gathered, chip[0] = lax.optimization_barrier((gathered, chip[0]))
        first = index * here.shape[0]
        return block(first, gathered, weight, flat, gain_ffn, w_gate, w_up, w_down)

    def chip_sum(mine, other):
        return (mine + swap_core(other).astype(f32)).astype(bf16)

    chip, residual = [None] * PARTS, [None] * PARTS
    residual[0], mine, other = block_of(0)
    other, fars[1] = lax.optimization_barrier((other, fars[1]))
    chip[0] = chip_sum(mine, other)
    most = chip[0].shape[0] // 2
    chip_most, chip_rest = chip[0][:most], chip[0][most:]
    far_most, far_rest = swap_chip(chip_most), swap_chip(chip_rest)
    residual[1], mine, other = block_of(1)
    other, far_most = lax.optimization_barrier((other, far_most))
    chip[1] = chip_sum(mine, other)
    half = chip[1].shape[0]
    cut = half // 4 * 3
    far_first, far_last = swap_chip(chip[1][:cut]), swap_chip(chip[1][cut:])

    def done(residual, chip, far):
        return (residual + (chip.astype(f32) + far.astype(f32))).astype(bf16)

    pieces = [
        (0, done(residual[0][:most], chip_most, far_most)),
        (most, done(residual[0][most:], chip_rest, far_rest)),
    ]
    result = finish(0, half, pieces, steps * rows)
    pieces = [
        (0, done(residual[1][:cut], chip[1][:cut], far_first)),
        (cut, done(residual[1][cut:], chip[1][cut:], far_last)),
    ]
    result = finish(2 * half, half, pieces, steps * rows, [result])
    return result.reshape(steps, rows, width)


def solution(mesh):
    return jax.shard_map(
        shards,
        mesh=mesh,
        in_specs=(
            P(None, "group", None),
            P(None, "group"),
            P("group"),
            P("group"),
            P("group", "head", None),
            P("group", "head", None),
            P("group", "head", None),
            P(),
            P("head", None),
            P("head", None),
            P("head", None),
            P(None, "head"),
            P("head"),
            P("head", None),
            P(),
            P(None, "head"),
            P(None, "head"),
            P("head", None),
        ),
        out_specs=P(None, "group", None),
        check_vma=False,
    )
```

```python
import functools

import jax
import jax.numpy as jnp
from jax import lax
from jax.experimental import pallas as pl
from jax.experimental.pallas import tpu as pltpu
from jax.sharding import PartitionSpec as P

BEAMS = 8
OWNED_SLOTS = 32
SPILL = 16
PAGE_BLOCK = 16
PARTS = 2
MIB = 1 << 20

epsilon = 1e-05
masked_score = -1e30
f32 = jnp.float32
bf16 = jnp.bfloat16

NN = (((1,), (0,)), ((), ()))
NT = (((1,), (1,)), ((), ()))
SMEM = pl.BlockSpec(memory_space=pltpu.SMEM)


def dot(a, b, dims=NN):
    return lax.dot_general(a, b, dims, preferred_element_type=f32)


def lanes(shape):
    return lax.broadcasted_iota(jnp.int32, shape, len(shape) - 1)


def sublanes(shape):
    return lax.broadcasted_iota(jnp.int32, shape, len(shape) - 2)


def in_hbm(array):
    return pltpu.with_memory_space_constraint(array, pltpu.HBM)


def in_vmem(array):
    return pltpu.with_memory_space_constraint(array, pltpu.VMEM)


def start_all(pairs, sems):
    copies = [pltpu.make_async_copy(s, t, sems.at[i]) for i, (s, t) in enumerate(pairs)]
    for copy in copies:
        copy.start()
    return copies


def fill_table(local_count, capacity, first, ids_ref, table_ref):
    groups = ids_ref.shape[0]
    for slot in range(groups * capacity):
        table_ref[slot] = -1

    def group(index, carry):
        rank = jnp.int32(0)
        for page in range(SPILL):
            local = ids_ref[index, 0, OWNED_SLOTS + page] - first
            mine = (local >= 0) & (local < local_count)

            @pl.when(mine)
            def _():
                table_ref[index * capacity + rank] = local

            rank = rank + mine.astype(jnp.int32)
        return carry

    lax.fori_loop(0, groups, group, 0)


def query_kernel(
    tokens_hbm, gain_ref, wq_hbm, q_ref, q_hbm, normed_hbm,
    tokens_ref, wq_ref, normed_ref, sems, out_sems,
):
    steps, rows, _ = tokens_ref.shape
    span = steps * BEAMS
    cut = rows // 2
    copies = start_all(
        [
            (tokens_hbm.at[:, :cut], tokens_ref.at[:, :cut]),
            (tokens_hbm.at[:, cut:], tokens_ref.at[:, cut:]),
            (wq_hbm, wq_ref),
        ],
        sems,
    )
    gain = gain_ref[...].reshape(1, -1)

    def pair(index, carry):
        slabs = []
        for step in range(steps):
            x = tokens_ref[step, pl.ds(pl.multiple_of(index * 16, 16), 16), :].astype(f32)
            scale = lax.rsqrt(jnp.mean(x * x, axis=-1, keepdims=True) + epsilon)
            slabs.append(x * scale * gain)
        for half in range(2):
            part = jnp.concatenate([s[half * 8 : half * 8 + 8] for s in slabs], axis=0)
            start = pl.multiple_of((index * 2 + half) * span, span)
            normed_ref[pl.ds(start, span), :] = part.astype(bf16)
        return carry

    copies[0].wait()
    lax.fori_loop(0, cut // 16, pair, 0, unroll=2)
    copies[1].wait()
    lax.fori_loop(cut // 16, rows // 16, pair, 0, unroll=2)
    leaving = start_all([(normed_ref, normed_hbm)], out_sems)
    copies[2].wait()
    query = dot(normed_ref[...], wq_ref[...], NT).astype(bf16)
    q_ref[...] = (query.astype(f32) * 0.125).astype(bf16)
    last = pltpu.make_async_copy(q_ref, q_hbm, out_sems.at[1])
    last.start()
    leaving[0].wait()
    last.wait()


def queries_of(tokens, gain, w_query):
    steps, rows, width = tokens.shape
    inner = w_query.shape[0]
    total = steps * rows
    hbm = pl.BlockSpec(memory_space=pltpu.HBM)
    vmem = pl.BlockSpec(memory_space=pltpu.VMEM)
    return pl.pallas_call(
        query_kernel,
        in_specs=[hbm, vmem, hbm],
        out_specs=[vmem, hbm, hbm],
        out_shape=[
            pltpu.VMEM((total, inner), bf16),
            pltpu.HBM((total, inner), bf16),
            pltpu.HBM((total, width), bf16),
        ],
        scratch_shapes=[
            pltpu.VMEM(tokens.shape, bf16),
            pltpu.VMEM(w_query.shape, bf16),
            pltpu.VMEM((total, width), bf16),
            pltpu.SemaphoreType.DMA((3,)),
            pltpu.SemaphoreType.DMA((2,)),
        ],
        compiler_params=pltpu.CompilerParams(vmem_limit_bytes=12 * MIB),
        cost_estimate=pl.CostEstimate(
            flops=2 * total * width * inner, bytes_accessed=6 * MIB, transcendentals=total
        ),
        name="queries",
    )(in_hbm(tokens), gain, in_hbm(w_query))


def ask_kernel(capacity, request_ref, ids_ref, q_ref, table_ref, out_ref):
    slots, span, _ = out_ref.shape
    local_count = q_ref.shape[0] // span
    first = request_ref[0] // local_count * local_count
    fill_table(local_count, capacity, first, ids_ref, table_ref)
    for slot in range(slots):
        start = jnp.maximum(table_ref[slot], 0) * span
        out_ref[slot] = q_ref[pl.ds(pl.multiple_of(start, span), span), :]


def ask(request, ids, q, span, capacity):
    slots = ids.shape[0] * capacity
    vmem = pl.BlockSpec(memory_space=pltpu.VMEM)
    return pl.pallas_call(
        functools.partial(ask_kernel, capacity),
        in_specs=[SMEM, SMEM, vmem],
        out_specs=[SMEM, vmem],
        out_shape=[
            jax.ShapeDtypeStruct((slots,), jnp.int32),
            jax.ShapeDtypeStruct((slots, span, q.shape[1]), bf16),
        ],
        compiler_params=pltpu.CompilerParams(vmem_limit_bytes=8 * MIB),
        name="ask",
    )(request, ids, in_vmem(q))


def half_masks(rows):
    low = lanes((rows, 128)) < 64
    return low.astype(f32).astype(bf16), jnp.logical_not(low).astype(f32).astype(bf16)


def stacked(pair_rows, masks):
    return jnp.concatenate([pair_rows * masks[0], pair_rows * masks[1]], axis=0)


def side_by_side(values, rows):
    low = lanes((rows, 128)) < 64
    top = jnp.broadcast_to(values[:rows], (rows, 128))
    bottom = jnp.broadcast_to(values[rows:], (rows, 128))
    return jnp.where(low, top, bottom)


def absorb(state, rows, columns, top, total, numer):
    top_ref, total_ref, numer_ref = state
    old = top_ref[rows, columns]
    new = jnp.maximum(old, top)
    keep = jnp.exp(old - new)
    add = jnp.exp(top - new)
    top_ref[rows, columns] = new
    total_ref[rows, columns] = total_ref[rows, columns] * keep + total * add
    numer_ref[rows, columns] = numer_ref[rows, columns] * keep + numer * add


def history(parents_ref, q_ref, k_ref, v_ref, forget_ref, state, scores_ref, weights_ref):
    transitions, rows = parents_ref.shape
    span = (transitions + 1) * BEAMS
    pack = 128 // span
    square = (128, 128)
    diagonal = sublanes(square) == lanes(square)
    columns = []
    for step in range(transitions):
        row = parents_ref[step : step + 1, :].astype(f32)
        columns.append(
            jnp.sum(jnp.where(diagonal, jnp.broadcast_to(row, square), 0.0), axis=1, keepdims=True)
        )
    lane8 = lanes((8, 128)).astype(f32)
    masks = half_masks(128)
    low = lanes(square) < 64
    top_ref, total_ref, numer_ref = state
    groups = rows // BEAMS // pack
    pairs = q_ref.shape[1] // 128
    for group in range(groups):
        slabs = []
        for member in range(pack):
            first = (group * pack + member) * BEAMS
            slabs.append(jnp.zeros((8, 128), f32))
            for step in range(transitions):
                wanted = columns[step][first : first + 8] + float(member * span + step * 8)
                slabs.append(jnp.where(lane8 == wanted, 1.0, 0.0))
        parent = jnp.concatenate(slabs, axis=0)
        parent16 = parent.astype(bf16)
        one = diagonal.astype(f32) + parent
        two = dot(parent16, parent16)
        ancestors = one + dot(two.astype(bf16), one.astype(bf16))
        here = pl.ds(group * 128, 128)
        running = lax.dot_general(
            ancestors, forget_ref[here, :], NN,
            precision=lax.Precision.HIGHEST, preferred_element_type=f32,
        ).T
        hidden = jnp.where(ancestors > 0.5, 0.0, masked_score)
        for pair in range(pairs):
            cols = pl.ds(pair * 128, 128)
            raw = dot(stacked(q_ref[here, cols], masks), k_ref[here, cols], NT)
            for half in range(2):
                head = pair * 2 + half
                scores_ref[group * pairs + pair, half] = raw[half * 128 : half * 128 + 128] + (
                    hidden - running[head : head + 1]
                )
    for group in range(groups):
        here = pl.ds(group * 128, 128)
        for pair in range(pairs):
            cols = pl.ds(pair * 128, 128)
            tops, totals = [], []
            for half in range(2):
                scores = scores_ref[group * pairs + pair, half]
                top = jnp.broadcast_to(jnp.max(scores, axis=-1, keepdims=True), square)
                weights = jnp.exp(scores - top)
                weights_ref[group * pairs + pair, pl.ds(half * 128, 128), :] = weights.astype(bf16)
                tops.append(top)
                totals.append(jnp.broadcast_to(jnp.sum(weights, axis=-1, keepdims=True), square))
            top_ref[here, cols] = jnp.where(low, *tops)
            total_ref[here, cols] = jnp.where(low, *totals)
    for group in range(groups):
        here = pl.ds(group * 128, 128)
        for pair in range(pairs):
            cols = pl.ds(pair * 128, 128)
            numer = dot(weights_ref[group * pairs + pair], v_ref[here, cols])
            numer_ref[here, cols] = jnp.where(low, numer[:128], numer[128:])


def fresh_kernel(
    parents_ref, bias_ref, normed_hbm, wk_hbm, wv_hbm, wf_hbm, q_hbm, top_hbm, total_hbm, numer_hbm,
    logs_hbm, averages_hbm,
    normed_ref, wk_ref, wv_ref, wf_ref, q_ref, top_own, total_own, numer_own,
    k_ref, v_ref, forget_ref, top_ref, total_ref, numer_ref, scores_ref, weights_ref,
    logs_ref, averages_ref, sems, out_sems,
):
    copies = start_all(
        [
            (normed_hbm, normed_ref), (wk_hbm, wk_ref), (wv_hbm, wv_ref), (wf_hbm, wf_ref),
            (q_hbm, q_ref), (top_hbm, top_own), (total_hbm, total_own), (numer_hbm, numer_own),
        ],
        sems,
    )
    copies[0].wait()
    copies[1].wait()
    k_ref[...] = dot(normed_ref[...], wk_ref[...], NT).astype(bf16)
    copies[2].wait()
    v_ref[...] = dot(normed_ref[...], wv_ref[...], NT).astype(bf16)
    copies[3].wait()
    gate = dot(normed_ref[...], wf_ref[...], NT) + bias_ref[...]
    forget = jnp.minimum(gate, 0.0) - jnp.log1p(jnp.exp(-jnp.abs(gate)))
    forget_ref[...] = jnp.zeros_like(forget_ref)
    forget_ref[:, : forget.shape[1]] = forget
    copies[4].wait()
    state = (top_ref, total_ref, numer_ref)
    history(parents_ref, q_ref, k_ref, v_ref, forget_ref, state, scores_ref, weights_ref)
    for copy in copies[5:]:
        copy.wait()

    parts, _, part = logs_ref.shape[:3]
    span = parts * part

    def join(index, carry):
        rows = pl.ds(pl.multiple_of(index * span, span), span)
        absorb(state, rows, slice(None), top_own[rows, :], total_own[rows, :], numer_own[rows, :])
        total = total_ref[rows, :]
        logs = top_ref[rows, :] + jnp.log(total)
        averages = numer_ref[rows, :] / total
        for number in range(parts):
            logs_ref[number, index] = logs[number * part : number * part + part]
            averages_ref[number, index] = averages[number * part : number * part + part]
        return carry

    lax.fori_loop(0, logs_ref.shape[1], join, 0, unroll=2)
    for copy in start_all([(logs_ref, logs_hbm), (averages_ref, averages_hbm)], out_sems):
        copy.wait()


def fresh(parents, bias, normed, w_key, w_value, w_forget, q, own):
    rows, inner = q.shape
    span = (parents.shape[0] + 1) * BEAMS
    vmem = pl.BlockSpec(memory_space=pltpu.VMEM)
    hbm = pl.BlockSpec(memory_space=pltpu.HBM)
    big = [normed, w_key, w_value, w_forget.T, q, *own]
    wide = pltpu.VMEM((rows, inner), f32)
    out = (PARTS, rows // span, span // PARTS, inner)
    tiles = rows * inner // (128 * 128)
    return pl.pallas_call(
        fresh_kernel,
        in_specs=[vmem, vmem] + [hbm] * len(big),
        out_specs=[hbm] * 2,
        out_shape=[pltpu.HBM(out, f32)] * 2,
        scratch_shapes=[pltpu.VMEM(x.shape, x.dtype) for x in big]
        + [pltpu.VMEM((rows, inner), bf16)] * 2
        + [pltpu.VMEM((rows, 128), f32), wide, wide, wide]
        + [pltpu.VMEM((tiles, 2, 128, 128), f32), pltpu.VMEM((tiles, 256, 128), bf16)]
        + [pltpu.VMEM(out, f32)] * 2
        + [pltpu.SemaphoreType.DMA((len(big),)), pltpu.SemaphoreType.DMA((2,))],
        compiler_params=pltpu.CompilerParams(vmem_limit_bytes=24 * MIB),
        cost_estimate=pl.CostEstimate(
            flops=4 * rows * normed.shape[1] * inner, bytes_accessed=12 * MIB,
            transcendentals=8 * rows * inner,
        ),
        name="fresh",
    )(parents, bias.reshape(1, -1), *[in_hbm(x) for x in big])


def page_weights(queries, fills, keys_ref, decay_ref, scores_ref, weights_ref, tops_ref):
    span = queries[0][0].shape[0]
    masks = half_masks(span)
    lane = lanes((1, 128))
    decay = [decay_ref[head].astype(f32) for head in range(decay_ref.shape[0])]
    for page, pairs in enumerate(queries):
        valid = lane < fills[page]
        for pair, query in enumerate(pairs):
            raw = dot(stacked(query, masks), keys_ref[page, pl.ds(pair * 128, 128), :])
            for half in range(2):
                head = pair * 2 + half
                bias = jnp.where(valid, decay[head][page : page + 1], masked_score)
                scores_ref[page, pl.ds(head * span, span), :] = (
                    raw[half * span : half * span + span] + bias
                )
    for page in range(len(queries)):
        for head in range(decay_ref.shape[0]):
            rows = pl.ds(head * span, span)
            scores = scores_ref[page, rows, :]
            top = jnp.broadcast_to(jnp.max(scores, axis=-1, keepdims=True), scores.shape)
            tops_ref[page, rows, :] = top
            weights = jnp.exp(scores - top)
            weights_ref[page, rows, :] = weights.astype(bf16)
            scores_ref[page, rows, :] = jnp.broadcast_to(
                jnp.sum(weights, axis=-1, keepdims=True), scores.shape
            )


def page_sums(page, pair, span, values_ref, scores_ref, weights_ref, tops_ref):
    low = lanes((span, 128)) < 64
    first, second = pl.ds(pair * 2 * span, span), pl.ds((pair * 2 + 1) * span, span)
    numer = dot(
        weights_ref[page, pl.ds(pair * 2 * span, 2 * span), :],
        values_ref[page, pl.ds(pair * 128, 128), :],
        NT,
    )
    top = jnp.where(low, tops_ref[page, first, :], tops_ref[page, second, :])
    total = jnp.where(low, scores_ref[page, first, :], scores_ref[page, second, :])
    return top, total, jnp.where(low, numer[:span], numer[span:])


def page_scratch(pages, span, heads):
    rows = span * heads
    return [
        pltpu.VMEM((pages, rows, 128), f32),
        pltpu.VMEM((pages, rows, 128), bf16),
        pltpu.VMEM((pages, rows, 128), f32),
    ]


def own_kernel(
    request_ref, fill_ref, q_ref, keys_ref, values_ref, decay_ref,
    top_ref, total_ref, numer_ref, *scratch,
):
    state = (top_ref, total_ref, numer_ref)
    span = scratch[0].shape[1] // decay_ref.shape[0]
    local_count = q_ref.shape[0] // span
    pairs = q_ref.shape[1] // 128

    block = pl.program_id(0)

    @pl.when(block == 0)
    def _():
        top_ref[...] = jnp.full_like(top_ref, masked_score)
        total_ref[...] = jnp.zeros_like(total_ref)
        numer_ref[...] = jnp.zeros_like(numer_ref)

    places, queries, fills = [], [], []
    for page in range(PAGE_BLOCK):
        index = block * PAGE_BLOCK + page
        local = lax.rem(request_ref[index], local_count)
        rows = pl.ds(pl.multiple_of(local * span, span), span)
        places.append(rows)
        queries.append([q_ref[rows, pl.ds(pair * 128, 128)] for pair in range(pairs)])
        fills.append(fill_ref[index])
    page_weights(queries, fills, keys_ref, decay_ref, *scratch)
    for page, rows in enumerate(places):
        for pair in range(pairs):
            sums = page_sums(page, pair, span, values_ref, *scratch)
            absorb(state, rows, pl.ds(pair * 128, 128), *sums)


def page_cost(pages, keys, rows):
    inner, length = keys.shape[1:]
    return pl.CostEstimate(
        flops=pages * rows * inner * length * 8,
        bytes_accessed=pages * inner * length * 4,
        transcendentals=pages * rows * inner * length // 64,
    )


def own_pages(request, fill, q, keys, values, decay, span):
    pool = pl.BlockSpec((PAGE_BLOCK,) + keys.shape[1:], lambda i: (i, 0, 0))
    decay_spec = pl.BlockSpec((decay.shape[0], PAGE_BLOCK, decay.shape[2]), lambda i: (0, i, 0))
    rows = pl.BlockSpec(q.shape, lambda i: (0, 0))
    return pl.pallas_call(
        own_kernel,
        grid=(OWNED_SLOTS // PAGE_BLOCK,),
        in_specs=[SMEM, SMEM, rows, pool, pool, decay_spec],
        out_specs=[rows] * 3,
        out_shape=[pltpu.HBM(q.shape, f32)] * 3,
        scratch_shapes=page_scratch(PAGE_BLOCK, span, decay.shape[0]),
        compiler_params=pltpu.CompilerParams(vmem_limit_bytes=20 * MIB),
        cost_estimate=page_cost(OWNED_SLOTS, keys, 64),
        name="own_pages",
    )(request, fill, in_hbm(q), in_hbm(keys), in_hbm(values), decay)


def hosted_kernel(
    local_count, capacity, request_ref, fill_ref, q_ref, keys_ref, values_ref, decay_ref,
    out_ref, tail_ref, count_ref, *scratch,
):
    span, inner = q_ref.shape[1:]
    pairs = inner // 128
    heads = decay_ref.shape[0]
    groups = out_ref.shape[0]
    half = span // PARTS
    slot_rows = pairs * span
    out_ref[...] = jnp.zeros_like(out_ref)
    tail_ref[...] = jnp.zeros_like(tail_ref)
    for owner in range(groups):
        count_ref[owner] = 0
    places, queries, fills = [], [], []
    for page in range(SPILL):
        owner = request_ref[OWNED_SLOTS + page] // local_count
        rank = count_ref[owner]
        count_ref[owner] = rank + 1
        places.append((owner, rank))
        slot = owner * capacity + rank
        queries.append([q_ref[slot, :, pl.ds(pair * 128, 128)] for pair in range(pairs)])
        fills.append(fill_ref[OWNED_SLOTS + page])
    page_weights(queries, fills, keys_ref, decay_ref, *scratch)
    scores_ref, _, tops_ref = scratch
    lane = lanes((half, 128))
    for page, (owner, rank) in enumerate(places):
        for pair in range(pairs):
            _, total, numer = page_sums(page, pair, span, values_ref, *scratch)
            here = pl.ds(pl.multiple_of(rank * slot_rows + pair * span, span), span)
            out_ref[owner, here, :] = (numer / total).astype(bf16)
        tail = tail_ref[owner]
        base = rank * (3 * heads)
        for head in range(heads):
            rows = pl.ds(head * span, span)
            rest = tops_ref[page, rows, :] + jnp.log(scores_ref[page, rows, :])
            rest = jnp.where(lane < 64, rest[:half], rest[half:])
            for piece in range(3):
                part = rest.astype(bf16).astype(f32)
                rest = rest - part
                tail = jnp.where(lane % 64 == base + piece * heads + head, part, tail)
        tail_ref[owner] = tail
    first = capacity * slot_rows
    for owner in range(groups):
        out_ref[owner, first : first + half, :] = tail_ref[owner].astype(bf16)


def hosted_pages(request, fill, asked_rows, keys, values, decay, groups, capacity, local_count):
    count, span, inner = asked_rows.shape
    shift = OWNED_SLOTS // SPILL
    pool = pl.BlockSpec((SPILL,) + keys.shape[1:], lambda i: (shift, 0, 0))
    decay_spec = pl.BlockSpec((decay.shape[0], SPILL, decay.shape[2]), lambda i: (0, shift, 0))
    out_shape = (groups, capacity * span * inner // 128 + span // PARTS, 128)
    return pl.pallas_call(
        functools.partial(hosted_kernel, local_count, capacity),
        grid=(1,),
        in_specs=[
            SMEM, SMEM, pl.BlockSpec(asked_rows.shape, lambda i: (0, 0, 0)), pool, pool, decay_spec
        ],
        out_specs=pl.BlockSpec(out_shape, lambda i: (0, 0, 0)),
        out_shape=jax.ShapeDtypeStruct(out_shape, bf16),
        scratch_shapes=[pltpu.VMEM((groups, span // PARTS, 128), f32), pltpu.SMEM((groups,), jnp.int32)]
        + page_scratch(SPILL, span, decay.shape[0]),
        compiler_params=pltpu.CompilerParams(vmem_limit_bytes=24 * MIB),
        cost_estimate=page_cost(SPILL, keys, 64),
        name="hosted_pages",
    )(request, fill, asked_rows, in_hbm(keys), in_hbm(values), decay)


def merge_kernel(capacity, steps, part, heads, table_ref, back_ref, log_hbm, average_hbm, *refs):
    sources, targets, load_sems = [], [], None
    if len(refs) > 6:
        *refs, load_sems = refs
        count = load_sems.shape[0]
        sources, refs = refs[:count], refs[count:]
        targets, refs = refs[1:-5], (refs[0], *refs[-5:])
    out_ref, top_ref, total_ref, numer_ref, tops_ref, sems = refs
    groups = back_ref.shape[0]
    inner = heads * 64
    rows = steps * BEAMS
    span = PARTS * rows
    state = (top_ref, total_ref, numer_ref)
    copies = start_all([(log_hbm.at[part], top_ref), (average_hbm.at[part], numer_ref)], sems)
    pairs = []
    if sources:
        weight_ref, *targets = targets
        height = sources[0].shape[0]
        head = lax.axis_index("head")
        for other in range(4):
            place = pl.ds(pl.multiple_of((head ^ other) * height, height), height)
            pairs.append((sources[other], weight_ref.at[place]))
        sources = sources[4:]
    pairs.extend(zip(sources, targets))
    loads = start_all(pairs, load_sems)
    total_ref[...] = jnp.ones_like(total_ref)
    slot_rows = (inner // 128) * span
    first = capacity * slot_rows
    tails = jnp.concatenate(
        [back_ref[owner, first : first + rows, :] for owner in range(groups)], axis=0
    )
    source, target = sublanes((128, inner)), lanes((128, inner)) // 64
    for rank in range(capacity):
        hit = source < 0
        for piece in range(3):
            hit = hit | (source == target + part * 64 + (rank * 3 + piece) * heads)
        tops_ref[:, rank * inner : rank * inner + inner] = dot(tails, hit.astype(f32).astype(bf16))
    for copy in copies:
        copy.wait()
    for owner in range(groups):
        for rank in range(capacity):
            local = table_ref[owner * capacity + rank]
            bias = jnp.where(local >= 0, 0.0, masked_score)
            top = tops_ref[owner * rows : owner * rows + rows, rank * inner : rank * inner + inner]
            starts = [rank * slot_rows + pair * span + part * rows for pair in range(inner // 128)]
            average = jnp.concatenate(
                [back_ref[owner, start : start + rows, :].astype(f32) for start in starts], axis=1
            )
            here = pl.ds(pl.multiple_of(jnp.maximum(local, 0) * rows, rows), rows)
            absorb(state, here, slice(None), top + bias, 1.0, average)
    for index in range(top_ref.shape[0] // (2 * rows)):
        parts = []
        for half in range(2):
            here = slice((index * 2 + half) * rows, (index * 2 + half + 1) * rows)
            parts.append(numer_ref[here, :] / total_ref[here, :])
        for step in range(steps):
            both = jnp.concatenate([p[step * 8 : step * 8 + 8] for p in parts], axis=0)
            start = step * (top_ref.shape[0] // steps) + index * 16
            out_ref[start : start + 16, :] = both.astype(bf16)
    for copy in loads:
        copy.wait()


def merge(part, table, back, logs, averages, steps, capacity, sources):
    _, requests, span, inner = logs.shape
    rows = requests * span
    logs, averages = (x.reshape(PARTS, rows, inner) for x in (logs, averages))
    vmem = pl.BlockSpec(memory_space=pltpu.VMEM)
    hbm = pl.BlockSpec(memory_space=pltpu.HBM)
    anywhere = pl.BlockSpec(memory_space=pl.ANY)
    mixes = sources[:4]
    others = sources[len(mixes) :]
    kept = [jax.ShapeDtypeStruct(x.shape, x.dtype) for x in others]
    if mixes:
        kept = [jax.ShapeDtypeStruct((4 * inner, mixes[0].shape[1]), bf16)] + kept
    return pl.pallas_call(
        functools.partial(merge_kernel, capacity, steps, part, inner // 64),
        in_specs=[SMEM, vmem, hbm, hbm] + [anywhere] * len(mixes) + [hbm] * len(others),
        out_shape=[jax.ShapeDtypeStruct((rows, inner), bf16)] + kept,
        scratch_shapes=[pltpu.VMEM((rows, inner), f32)] * 3
        + [
            pltpu.VMEM((back.shape[0] * span, capacity * inner), f32),
            pltpu.SemaphoreType.DMA((2,)),
        ]
        + [pltpu.SemaphoreType.DMA((len(sources),))] * bool(sources),
        compiler_params=pltpu.CompilerParams(vmem_limit_bytes=10 * MIB),
        cost_estimate=pl.CostEstimate(
            flops=40 * rows * inner, bytes_accessed=8 * MIB, transcendentals=4 * rows * inner
        ),
        name="merge",
    )(table, back, in_hbm(logs), in_hbm(averages), *mixes, *[in_hbm(x) for x in others])


def block_kernel(
    first, att0, att1, att2, att3, weight_ref, tokens_ref, gain_ref, gate_ref, up_ref, down_ref,
    residual_out, mine_ref, other_ref,
    residual_ref, attended_ref, scaled_ref, hidden_ref, sums_ref,
):
    rows, width = residual_ref.shape
    inner = att0.shape[1]
    half = rows // 2
    head = lax.axis_index("head")
    core = lax.rem(head, 2)
    near = pl.ds(pl.multiple_of(core * half, half), half)
    away = pl.ds(pl.multiple_of((1 - core) * half, half), half)
    for other, att in enumerate((att0, att1, att2, att3)):
        place = pl.ds(pl.multiple_of((head ^ other) * inner, inner), inner)
        attended_ref[:, place] = att[...]
    gain = gain_ref[...].reshape(1, -1)
    squares = jnp.zeros((rows, 1), f32)
    for start in range(0, width, 512):
        cols = slice(start, start + 512)
        x = tokens_ref[first : first + rows, cols].astype(f32) + dot(attended_ref[...], weight_ref[:, cols])
        residual_ref[:, cols] = x
        scaled_ref[:, cols] = (x * gain[:, cols]).astype(bf16)
        squares = squares + jnp.sum(x * x, axis=-1, keepdims=True)
    scale = lax.rsqrt(squares / width + epsilon)
    for start in range(0, gate_ref.shape[1], 256):
        cols = slice(start, start + 256)
        gate = dot(scaled_ref[...], gate_ref[:, cols]) * scale
        up = dot(scaled_ref[...], up_ref[:, cols]) * scale
        hidden_ref[:, cols] = (gate / (1.0 + jnp.exp(-gate)) * up).astype(bf16)
    residual_out[...] = residual_ref[near, :]
    for start in range(0, width, 512):
        cols = slice(start, start + 512)
        sums_ref[:, cols] = dot(hidden_ref[...], down_ref[:, cols])
    mine_ref[...] = sums_ref[near, :]
    other_ref[...] = sums_ref[away, :].astype(bf16)


def block(first, attended, weight, tokens, gain, w_gate, w_up, w_down):
    rows, inner = attended[0].shape
    width = tokens.shape[1]
    hidden = w_gate.shape[1]
    vmem = pl.BlockSpec(memory_space=pltpu.VMEM)
    half = jax.ShapeDtypeStruct((rows // 2, width), f32)
    return pl.pallas_call(
        functools.partial(block_kernel, first),
        in_specs=[vmem] * 10,
        out_specs=[vmem] * 3,
        out_shape=[half, half, jax.ShapeDtypeStruct((rows // 2, width), bf16)],
        scratch_shapes=[
            pltpu.VMEM((rows, width), f32),
            pltpu.VMEM((rows, 4 * inner), bf16),
            pltpu.VMEM((rows, width), bf16),
            pltpu.VMEM((rows, hidden), bf16),
            pltpu.VMEM((rows, width), f32),
        ],
        compiler_params=pltpu.CompilerParams(vmem_limit_bytes=20 * MIB),
        cost_estimate=pl.CostEstimate(flops=0, bytes_accessed=0, transcendentals=0),
        name="block",
    )(*attended, weight, tokens, gain, w_gate, w_up, w_down)


def finish_kernel(first, half, places, *refs):
    count = 2 * len(places)
    parts, out_ref, sems = refs[-2 - count : -2], refs[-2], refs[-1]
    core = lax.axis_index("head") % 2
    pairs = []
    for index, place in enumerate(places):
        for part, owner in ((parts[2 * index], core), (parts[2 * index + 1], 1 - core)):
            start = pl.multiple_of(first + owner * half + place, 16)
            pairs.append((part, out_ref.at[pl.ds(start, part.shape[0])]))
    for copy in start_all(pairs, sems):
        copy.wait()


def finish(first, half, pieces, rows, before=()):
    vmem = pl.BlockSpec(memory_space=pltpu.VMEM)
    hbm = pl.BlockSpec(memory_space=pltpu.HBM)
    places, parts = [], []
    for place, done in pieces:
        places.append(place)
        parts.extend([done, swap_core(done)])
    width = parts[0].shape[1]
    return pl.pallas_call(
        functools.partial(finish_kernel, first, half, places),
        in_specs=[hbm] * len(before) + [vmem] * len(parts),
        out_specs=hbm,
        out_shape=pltpu.HBM((rows, width), parts[0].dtype),
        input_output_aliases={0: 0} if before else {},
        scratch_shapes=[pltpu.SemaphoreType.DMA((len(parts),))],
        compiler_params=pltpu.CompilerParams(vmem_limit_bytes=8 * MIB),
        name="finish",
    )(*[in_hbm(x) for x in before], *parts)


def swap_core(value):
    return lax.ppermute(value, "head", [(i, i ^ 1) for i in range(4)])


def swap_chip(value):
    return lax.ppermute(value, "head", [(i, i ^ 2) for i in range(4)])


def shards(
    tokens, parents, page_request, page_fill, keys_pool, values_pool, decay_pool,
    gain_attn, w_query, w_key, w_value, w_forget, forget_bias, w_out,
    gain_ffn, w_gate, w_up, w_down,
):
    steps, rows, width = tokens.shape
    inner = w_query.shape[0]
    local_count = rows // BEAMS
    span = steps * BEAMS
    groups = lax.axis_size("group")
    capacity = (SPILL + groups - 2) // (groups - 1)
    decay = decay_pool.transpose(1, 0, 2)

    def exchange(value):
        return lax.all_to_all(value, "group", split_axis=0, concat_axis=0, tiled=True)

    ids = exchange(jnp.broadcast_to(page_request, (groups, 1, page_request.shape[0])))
    q_near, q, normed = queries_of(tokens, gain_attn, w_query)
    table, asked = ask(page_request, ids, q_near, span, capacity)
    asked_rows = exchange(asked.reshape(groups, capacity * span, inner)).reshape(asked.shape)
    asked, q = lax.optimization_barrier((asked, q))
    own = own_pages(page_request, page_fill, q, keys_pool, values_pool, decay, span)
    own, w_sent = lax.optimization_barrier((own, w_out))
    w_out_far = swap_chip(w_sent)
    asked_rows, own = lax.optimization_barrier((asked_rows, own))
    payload = hosted_pages(
        page_request, page_fill, asked_rows, keys_pool, values_pool, decay, groups, capacity, local_count
    )
    payload, normed = lax.optimization_barrier((payload, normed))
    back = exchange(payload)
    logs, averages = fresh(parents, forget_bias, normed, w_key, w_value, w_forget, q, own)
    logs, w_out_far = lax.optimization_barrier((logs, w_out_far))
    mixes = [w_out, swap_core(w_out), w_out_far, swap_core(w_out_far)]

    flat = tokens.reshape(steps * rows, width)
    each = steps // PARTS
    sums = (table, back, logs, averages, each, capacity)
    heres = list(merge(0, *sums, []))
    back, heres[0] = lax.optimization_barrier((back, heres[0]))
    sums = (table, back, logs, averages, each, capacity)
    here, weight, w_gate, w_up, w_down, flat = merge(1, *sums, mixes + [w_gate, w_up, w_down, flat])
    heres.append(here)
    fars = [swap_chip(here) for here in heres]
    fars[0], heres[1] = lax.optimization_barrier((fars[0], heres[1]))

    def block_of(index):
        here, far = heres[index], fars[index]
        gathered = [here, swap_core(here), far, swap_core(far)]
        if index:
            gathered, chip[0] = lax.optimization_barrier((gathered, chip[0]))
        first = index * here.shape[0]
        return block(first, gathered, weight, flat, gain_ffn, w_gate, w_up, w_down)

    def chip_sum(mine, other):
        return (mine + swap_core(other).astype(f32)).astype(bf16)

    chip, residual = [None] * PARTS, [None] * PARTS
    residual[0], mine, other = block_of(0)
    other, fars[1] = lax.optimization_barrier((other, fars[1]))
    chip[0] = chip_sum(mine, other)
    most = chip[0].shape[0] // 2
    chip_most, chip_rest = chip[0][:most], chip[0][most:]
    far_most, far_rest = swap_chip(chip_most), swap_chip(chip_rest)
    residual[1], mine, other = block_of(1)
    other, far_most = lax.optimization_barrier((other, far_most))
    chip[1] = chip_sum(mine, other)
    half = chip[1].shape[0]
    cut = half // 4 * 3
    far_first, far_last = swap_chip(chip[1][:cut]), swap_chip(chip[1][cut:])

    def done(residual, chip, far):
        return (residual + (chip.astype(f32) + far.astype(f32))).astype(bf16)

    pieces = [
        (0, done(residual[0][:most], chip_most, far_most)),
        (most, done(residual[0][most:], chip_rest, far_rest)),
    ]
    result = finish(0, half, pieces, steps * rows)
    pieces = [
        (0, done(residual[1][:cut], chip[1][:cut], far_first)),
        (cut, done(residual[1][cut:], chip[1][cut:], far_last)),
    ]
    result = finish(2 * half, half, pieces, steps * rows, [result])
    return result.reshape(steps, rows, width)


def solution(mesh):
    return jax.shard_map(
        shards,
        mesh=mesh,
        in_specs=(
            P(None, "group", None),
            P(None, "group"),
            P("group"),
            P("group"),
            P("group", "head", None),
            P("group", "head", None),
            P("group", "head", None),
            P(),
            P("head", None),
            P("head", None),
            P("head", None),
            P(None, "head"),
            P("head"),
            P("head", None),
            P(),
            P(None, "head"),
            P(None, "head"),
            P("head", None),
        ),
        out_specs=P(None, "group", None),
        check_vma=False,
    )
```

```python
import functools

import jax
import jax.numpy as jnp
from jax import lax
from jax.experimental import pallas as pl
from jax.experimental.pallas import tpu as pltpu
from jax.sharding import PartitionSpec as P

BEAMS = 8
OWNED_SLOTS = 32
SPILL = 16
PAGE_BLOCK = 16
PARTS = 2
MIB = 1 << 20

epsilon = 1e-05
masked_score = -1e30
f32 = jnp.float32
bf16 = jnp.bfloat16

NN = (((1,), (0,)), ((), ()))
NT = (((1,), (1,)), ((), ()))
SMEM = pl.BlockSpec(memory_space=pltpu.SMEM)


def dot(a, b, dims=NN):
    return lax.dot_general(a, b, dims, preferred_element_type=f32)


def lanes(shape):
    return lax.broadcasted_iota(jnp.int32, shape, len(shape) - 1)


def sublanes(shape):
    return lax.broadcasted_iota(jnp.int32, shape, len(shape) - 2)


def in_hbm(array):
    return pltpu.with_memory_space_constraint(array, pltpu.HBM)


def in_vmem(array):
    return pltpu.with_memory_space_constraint(array, pltpu.VMEM)


def start_all(pairs, sems):
    copies = [pltpu.make_async_copy(s, t, sems.at[i]) for i, (s, t) in enumerate(pairs)]
    for copy in copies:
        copy.start()
    return copies


def fill_table(local_count, capacity, first, ids_ref, table_ref):
    groups = ids_ref.shape[0]
    for slot in range(groups * capacity):
        table_ref[slot] = -1

    def group(index, carry):
        rank = jnp.int32(0)
        for page in range(SPILL):
            local = ids_ref[index, 0, OWNED_SLOTS + page] - first
            mine = (local >= 0) & (local < local_count)

            @pl.when(mine)
            def _():
                table_ref[index * capacity + rank] = local

            rank = rank + mine.astype(jnp.int32)
        return carry

    lax.fori_loop(0, groups, group, 0)


def query_kernel(
    tokens_hbm, gain_ref, wq_hbm, q_ref, q_hbm, normed_hbm,
    tokens_ref, wq_ref, normed_ref, sems, out_sems,
):
    steps, rows, _ = tokens_ref.shape
    span = steps * BEAMS
    cut = rows // 2
    copies = start_all(
        [
            (tokens_hbm.at[:, :cut], tokens_ref.at[:, :cut]),
            (tokens_hbm.at[:, cut:], tokens_ref.at[:, cut:]),
            (wq_hbm, wq_ref),
        ],
        sems,
    )
    gain = gain_ref[...].reshape(1, -1)

    def pair(index, carry):
        slabs = []
        for step in range(steps):
            x = tokens_ref[step, pl.ds(pl.multiple_of(index * 16, 16), 16), :].astype(f32)
            scale = lax.rsqrt(jnp.mean(x * x, axis=-1, keepdims=True) + epsilon)
            slabs.append(x * scale * gain)
        for half in range(2):
            part = jnp.concatenate([s[half * 8 : half * 8 + 8] for s in slabs], axis=0)
            start = pl.multiple_of((index * 2 + half) * span, span)
            normed_ref[pl.ds(start, span), :] = part.astype(bf16)
        return carry

    copies[0].wait()
    lax.fori_loop(0, cut // 16, pair, 0, unroll=2)
    copies[1].wait()
    lax.fori_loop(cut // 16, rows // 16, pair, 0, unroll=2)
    leaving = start_all([(normed_ref, normed_hbm)], out_sems)
    copies[2].wait()
    query = dot(normed_ref[...], wq_ref[...], NT).astype(bf16)
    q_ref[...] = (query.astype(f32) * 0.125).astype(bf16)
    last = pltpu.make_async_copy(q_ref, q_hbm, out_sems.at[1])
    last.start()
    leaving[0].wait()
    last.wait()


def queries_of(tokens, gain, w_query):
    steps, rows, width = tokens.shape
    inner = w_query.shape[0]
    total = steps * rows
    hbm = pl.BlockSpec(memory_space=pltpu.HBM)
    vmem = pl.BlockSpec(memory_space=pltpu.VMEM)
    return pl.pallas_call(
        query_kernel,
        in_specs=[hbm, vmem, hbm],
        out_specs=[vmem, hbm, hbm],
        out_shape=[
            pltpu.VMEM((total, inner), bf16),
            pltpu.HBM((total, inner), bf16),
            pltpu.HBM((total, width), bf16),
        ],
        scratch_shapes=[
            pltpu.VMEM(tokens.shape, bf16),
            pltpu.VMEM(w_query.shape, bf16),
            pltpu.VMEM((total, width), bf16),
            pltpu.SemaphoreType.DMA((3,)),
            pltpu.SemaphoreType.DMA((2,)),
        ],
        compiler_params=pltpu.CompilerParams(vmem_limit_bytes=12 * MIB),
        cost_estimate=pl.CostEstimate(
            flops=2 * total * width * inner, bytes_accessed=6 * MIB, transcendentals=total
        ),
        name="queries",
    )(in_hbm(tokens), gain, in_hbm(w_query))


def ask_kernel(capacity, request_ref, ids_ref, q_ref, table_ref, out_ref):
    slots, span, _ = out_ref.shape
    local_count = q_ref.shape[0] // span
    first = request_ref[0] // local_count * local_count
    fill_table(local_count, capacity, first, ids_ref, table_ref)
    for slot in range(slots):
        start = jnp.maximum(table_ref[slot], 0) * span
        out_ref[slot] = q_ref[pl.ds(pl.multiple_of(start, span), span), :]


def ask(request, ids, q, span, capacity):
    slots = ids.shape[0] * capacity
    vmem = pl.BlockSpec(memory_space=pltpu.VMEM)
    return pl.pallas_call(
        functools.partial(ask_kernel, capacity),
        in_specs=[SMEM, SMEM, vmem],
        out_specs=[SMEM, vmem],
        out_shape=[
            jax.ShapeDtypeStruct((slots,), jnp.int32),
            jax.ShapeDtypeStruct((slots, span, q.shape[1]), bf16),
        ],
        compiler_params=pltpu.CompilerParams(vmem_limit_bytes=8 * MIB),
        name="ask",
    )(request, ids, in_vmem(q))


def half_masks(rows):
    low = lanes((rows, 128)) < 64
    return low.astype(f32).astype(bf16), jnp.logical_not(low).astype(f32).astype(bf16)


def stacked(pair_rows, masks):
    return jnp.concatenate([pair_rows * masks[0], pair_rows * masks[1]], axis=0)


def side_by_side(values, rows):
    low = lanes((rows, 128)) < 64
    top = jnp.broadcast_to(values[:rows], (rows, 128))
    bottom = jnp.broadcast_to(values[rows:], (rows, 128))
    return jnp.where(low, top, bottom)


def absorb(state, rows, columns, top, total, numer):
    top_ref, total_ref, numer_ref = state
    old = top_ref[rows, columns]
    new = jnp.maximum(old, top)
    keep = jnp.exp(old - new)
    add = jnp.exp(top - new)
    top_ref[rows, columns] = new
    total_ref[rows, columns] = total_ref[rows, columns] * keep + total * add
    numer_ref[rows, columns] = numer_ref[rows, columns] * keep + numer * add


def history(parents_ref, q_ref, k_ref, v_ref, forget_ref, state, scores_ref, weights_ref):
    transitions, rows = parents_ref.shape
    span = (transitions + 1) * BEAMS
    pack = 128 // span
    square = (128, 128)
    diagonal = sublanes(square) == lanes(square)
    columns = []
    for step in range(transitions):
        row = parents_ref[step : step + 1, :].astype(f32)
        columns.append(
            jnp.sum(jnp.where(diagonal, jnp.broadcast_to(row, square), 0.0), axis=1, keepdims=True)
        )
    lane8 = lanes((8, 128)).astype(f32)
    masks = half_masks(128)
    low = lanes(square) < 64
    top_ref, total_ref, numer_ref = state
    groups = rows // BEAMS // pack
    pairs = q_ref.shape[1] // 128
    for group in range(groups):
        slabs = []
        for member in range(pack):
            first = (group * pack + member) * BEAMS
            slabs.append(jnp.zeros((8, 128), f32))
            for step in range(transitions):
                wanted = columns[step][first : first + 8] + float(member * span + step * 8)
                slabs.append(jnp.where(lane8 == wanted, 1.0, 0.0))
        parent = jnp.concatenate(slabs, axis=0)
        parent16 = parent.astype(bf16)
        one = diagonal.astype(f32) + parent
        two = dot(parent16, parent16)
        ancestors = one + dot(two.astype(bf16), one.astype(bf16))
        here = pl.ds(group * 128, 128)
        running = lax.dot_general(
            ancestors, forget_ref[here, :], NN,
            precision=lax.Precision.HIGHEST, preferred_element_type=f32,
        ).T
        hidden = jnp.where(ancestors > 0.5, 0.0, masked_score)
        for pair in range(pairs):
            cols = pl.ds(pair * 128, 128)
            raw = dot(stacked(q_ref[here, cols], masks), k_ref[here, cols], NT)
            for half in range(2):
                head = pair * 2 + half
                scores_ref[group * pairs + pair, half] = raw[half * 128 : half * 128 + 128] + (
                    hidden - running[head : head + 1]
                )
    for group in range(groups):
        here = pl.ds(group * 128, 128)
        for pair in range(pairs):
            cols = pl.ds(pair * 128, 128)
            tops, totals = [], []
            for half in range(2):
                scores = scores_ref[group * pairs + pair, half]
                top = jnp.broadcast_to(jnp.max(scores, axis=-1, keepdims=True), square)
                weights = jnp.exp(scores - top)
                weights_ref[group * pairs + pair, pl.ds(half * 128, 128), :] = weights.astype(bf16)
                tops.append(top)
                totals.append(jnp.broadcast_to(jnp.sum(weights, axis=-1, keepdims=True), square))
            top_ref[here, cols] = jnp.where(low, *tops)
            total_ref[here, cols] = jnp.where(low, *totals)
    for group in range(groups):
        here = pl.ds(group * 128, 128)
        for pair in range(pairs):
            cols = pl.ds(pair * 128, 128)
            numer = dot(weights_ref[group * pairs + pair], v_ref[here, cols])
            numer_ref[here, cols] = jnp.where(low, numer[:128], numer[128:])


def fresh_kernel(
    parents_ref, bias_ref, normed_hbm, wk_hbm, wv_hbm, wf_hbm, q_hbm, top_hbm, total_hbm, numer_hbm,
    logs_hbm, averages_hbm,
    normed_ref, wk_ref, wv_ref, wf_ref, q_ref, top_own, total_own, numer_own,
    k_ref, v_ref, forget_ref, top_ref, total_ref, numer_ref, scores_ref, weights_ref,
    logs_ref, averages_ref, sems, out_sems,
):
    copies = start_all(
        [
            (normed_hbm, normed_ref), (wk_hbm, wk_ref), (wv_hbm, wv_ref), (wf_hbm, wf_ref),
            (q_hbm, q_ref), (top_hbm, top_own), (total_hbm, total_own), (numer_hbm, numer_own),
        ],
        sems,
    )
    copies[0].wait()
    copies[1].wait()
    k_ref[...] = dot(normed_ref[...], wk_ref[...], NT).astype(bf16)
    copies[2].wait()
    v_ref[...] = dot(normed_ref[...], wv_ref[...], NT).astype(bf16)
    copies[3].wait()
    gate = dot(normed_ref[...], wf_ref[...], NT) + bias_ref[...]
    forget = jnp.minimum(gate, 0.0) - jnp.log1p(jnp.exp(-jnp.abs(gate)))
    forget_ref[...] = jnp.zeros_like(forget_ref)
    forget_ref[:, : forget.shape[1]] = forget
    copies[4].wait()
    state = (top_ref, total_ref, numer_ref)
    history(parents_ref, q_ref, k_ref, v_ref, forget_ref, state, scores_ref, weights_ref)
    for copy in copies[5:]:
        copy.wait()

    parts, _, part = logs_ref.shape[:3]
    span = parts * part

    def join(index, carry):
        rows = pl.ds(pl.multiple_of(index * span, span), span)
        absorb(state, rows, slice(None), top_own[rows, :], total_own[rows, :], numer_own[rows, :])
        total = total_ref[rows, :]
        logs = top_ref[rows, :] + jnp.log(total)
        averages = numer_ref[rows, :] / total
        for number in range(parts):
            logs_ref[number, index] = logs[number * part : number * part + part]
            averages_ref[number, index] = averages[number * part : number * part + part]
        return carry

    lax.fori_loop(0, logs_ref.shape[1], join, 0, unroll=2)
    for copy in start_all([(logs_ref, logs_hbm), (averages_ref, averages_hbm)], out_sems):
        copy.wait()


def fresh(parents, bias, normed, w_key, w_value, w_forget, q, own):
    rows, inner = q.shape
    span = (parents.shape[0] + 1) * BEAMS
    vmem = pl.BlockSpec(memory_space=pltpu.VMEM)
    hbm = pl.BlockSpec(memory_space=pltpu.HBM)
    big = [normed, w_key, w_value, w_forget.T, q, *own]
    wide = pltpu.VMEM((rows, inner), f32)
    out = (PARTS, rows // span, span // PARTS, inner)
    tiles = rows * inner // (128 * 128)
    return pl.pallas_call(
        fresh_kernel,
        in_specs=[vmem, vmem] + [hbm] * len(big),
        out_specs=[hbm] * 2,
        out_shape=[pltpu.HBM(out, f32)] * 2,
        scratch_shapes=[pltpu.VMEM(x.shape, x.dtype) for x in big]
        + [pltpu.VMEM((rows, inner), bf16)] * 2
        + [pltpu.VMEM((rows, 128), f32), wide, wide, wide]
        + [pltpu.VMEM((tiles, 2, 128, 128), f32), pltpu.VMEM((tiles, 256, 128), bf16)]
        + [pltpu.VMEM(out, f32)] * 2
        + [pltpu.SemaphoreType.DMA((len(big),)), pltpu.SemaphoreType.DMA((2,))],
        compiler_params=pltpu.CompilerParams(vmem_limit_bytes=24 * MIB),
        cost_estimate=pl.CostEstimate(
            flops=4 * rows * normed.shape[1] * inner, bytes_accessed=12 * MIB,
            transcendentals=8 * rows * inner,
        ),
        name="fresh",
    )(parents, bias.reshape(1, -1), *[in_hbm(x) for x in big])


def page_weights(queries, fills, keys_ref, decay_ref, scores_ref, weights_ref, tops_ref):
    span = queries[0][0].shape[0]
    masks = half_masks(span)
    lane = lanes((1, 128))
    decay = [decay_ref[head].astype(f32) for head in range(decay_ref.shape[0])]
    for page, pairs in enumerate(queries):
        valid = lane < fills[page]
        for pair, query in enumerate(pairs):
            raw = dot(stacked(query, masks), keys_ref[page, pl.ds(pair * 128, 128), :])
            for half in range(2):
                head = pair * 2 + half
                bias = jnp.where(valid, decay[head][page : page + 1], masked_score)
                scores_ref[page, pl.ds(head * span, span), :] = (
                    raw[half * span : half * span + span] + bias
                )
    for page in range(len(queries)):
        for head in range(decay_ref.shape[0]):
            rows = pl.ds(head * span, span)
            scores = scores_ref[page, rows, :]
            top = jnp.broadcast_to(jnp.max(scores, axis=-1, keepdims=True), scores.shape)
            tops_ref[page, rows, :] = top
            weights = jnp.exp(scores - top)
            weights_ref[page, rows, :] = weights.astype(bf16)
            scores_ref[page, rows, :] = jnp.broadcast_to(
                jnp.sum(weights, axis=-1, keepdims=True), scores.shape
            )


def page_sums(page, pair, span, values_ref, scores_ref, weights_ref, tops_ref):
    low = lanes((span, 128)) < 64
    first, second = pl.ds(pair * 2 * span, span), pl.ds((pair * 2 + 1) * span, span)
    numer = dot(
        weights_ref[page, pl.ds(pair * 2 * span, 2 * span), :],
        values_ref[page, pl.ds(pair * 128, 128), :],
        NT,
    )
    top = jnp.where(low, tops_ref[page, first, :], tops_ref[page, second, :])
    total = jnp.where(low, scores_ref[page, first, :], scores_ref[page, second, :])
    return top, total, jnp.where(low, numer[:span], numer[span:])


def page_scratch(pages, span, heads):
    rows = span * heads
    return [
        pltpu.VMEM((pages, rows, 128), f32),
        pltpu.VMEM((pages, rows, 128), bf16),
        pltpu.VMEM((pages, rows, 128), f32),
    ]


def own_kernel(
    request_ref, fill_ref, q_ref, keys_ref, values_ref, decay_ref,
    top_ref, total_ref, numer_ref, *scratch,
):
    state = (top_ref, total_ref, numer_ref)
    span = scratch[0].shape[1] // decay_ref.shape[0]
    local_count = q_ref.shape[0] // span
    pairs = q_ref.shape[1] // 128

    block = pl.program_id(0)

    @pl.when(block == 0)
    def _():
        top_ref[...] = jnp.full_like(top_ref, masked_score)
        total_ref[...] = jnp.zeros_like(total_ref)
        numer_ref[...] = jnp.zeros_like(numer_ref)

    places, queries, fills = [], [], []
    for page in range(PAGE_BLOCK):
        index = block * PAGE_BLOCK + page
        local = lax.rem(request_ref[index], local_count)
        rows = pl.ds(pl.multiple_of(local * span, span), span)
        places.append(rows)
        queries.append([q_ref[rows, pl.ds(pair * 128, 128)] for pair in range(pairs)])
        fills.append(fill_ref[index])
    page_weights(queries, fills, keys_ref, decay_ref, *scratch)
    for page, rows in enumerate(places):
        for pair in range(pairs):
            sums = page_sums(page, pair, span, values_ref, *scratch)
            absorb(state, rows, pl.ds(pair * 128, 128), *sums)


def page_cost(pages, keys, rows):
    inner, length = keys.shape[1:]
    return pl.CostEstimate(
        flops=pages * rows * inner * length * 8,
        bytes_accessed=pages * inner * length * 4,
        transcendentals=pages * rows * inner * length // 64,
    )


def own_pages(request, fill, q, keys, values, decay, span):
    pool = pl.BlockSpec((PAGE_BLOCK,) + keys.shape[1:], lambda i: (i, 0, 0))
    decay_spec = pl.BlockSpec((decay.shape[0], PAGE_BLOCK, decay.shape[2]), lambda i: (0, i, 0))
    rows = pl.BlockSpec(q.shape, lambda i: (0, 0))
    return pl.pallas_call(
        own_kernel,
        grid=(OWNED_SLOTS // PAGE_BLOCK,),
        in_specs=[SMEM, SMEM, rows, pool, pool, decay_spec],
        out_specs=[rows] * 3,
        out_shape=[pltpu.HBM(q.shape, f32)] * 3,
        scratch_shapes=page_scratch(PAGE_BLOCK, span, decay.shape[0]),
        compiler_params=pltpu.CompilerParams(vmem_limit_bytes=20 * MIB),
        cost_estimate=page_cost(OWNED_SLOTS, keys, 64),
        name="own_pages",
    )(request, fill, in_hbm(q), in_hbm(keys), in_hbm(values), decay)


def hosted_kernel(
    local_count, capacity, request_ref, fill_ref, q_ref, keys_ref, values_ref, decay_ref,
    out_ref, tail_ref, count_ref, *scratch,
):
    span, inner = q_ref.shape[1:]
    pairs = inner // 128
    heads = decay_ref.shape[0]
    groups = out_ref.shape[0]
    half = span // PARTS
    slot_rows = pairs * span
    out_ref[...] = jnp.zeros_like(out_ref)
    tail_ref[...] = jnp.zeros_like(tail_ref)
    for owner in range(groups):
        count_ref[owner] = 0
    places, queries, fills = [], [], []
    for page in range(SPILL):
        owner = request_ref[OWNED_SLOTS + page] // local_count
        rank = count_ref[owner]
        count_ref[owner] = rank + 1
        places.append((owner, rank))
        slot = owner * capacity + rank
        queries.append([q_ref[slot, :, pl.ds(pair * 128, 128)] for pair in range(pairs)])
        fills.append(fill_ref[OWNED_SLOTS + page])
    page_weights(queries, fills, keys_ref, decay_ref, *scratch)
    scores_ref, _, tops_ref = scratch
    lane = lanes((half, 128))
    for page, (owner, rank) in enumerate(places):
        for pair in range(pairs):
            _, total, numer = page_sums(page, pair, span, values_ref, *scratch)
            here = pl.ds(pl.multiple_of(rank * slot_rows + pair * span, span), span)
            out_ref[owner, here, :] = (numer / total).astype(bf16)
        tail = tail_ref[owner]
        base = rank * (3 * heads)
        for head in range(heads):
            rows = pl.ds(head * span, span)
            rest = tops_ref[page, rows, :] + jnp.log(scores_ref[page, rows, :])
            rest = jnp.where(lane < 64, rest[:half], rest[half:])
            for piece in range(3):
                part = rest.astype(bf16).astype(f32)
                rest = rest - part
                tail = jnp.where(lane % 64 == base + piece * heads + head, part, tail)
        tail_ref[owner] = tail
    first = capacity * slot_rows
    for owner in range(groups):
        out_ref[owner, first : first + half, :] = tail_ref[owner].astype(bf16)


def hosted_pages(request, fill, asked_rows, keys, values, decay, groups, capacity, local_count):
    count, span, inner = asked_rows.shape
    shift = OWNED_SLOTS // SPILL
    pool = pl.BlockSpec((SPILL,) + keys.shape[1:], lambda i: (shift, 0, 0))
    decay_spec = pl.BlockSpec((decay.shape[0], SPILL, decay.shape[2]), lambda i: (0, shift, 0))
    out_shape = (groups, capacity * span * inner // 128 + span // PARTS, 128)
    return pl.pallas_call(
        functools.partial(hosted_kernel, local_count, capacity),
        grid=(1,),
        in_specs=[
            SMEM, SMEM, pl.BlockSpec(asked_rows.shape, lambda i: (0, 0, 0)), pool, pool, decay_spec
        ],
        out_specs=pl.BlockSpec(out_shape, lambda i: (0, 0, 0)),
        out_shape=jax.ShapeDtypeStruct(out_shape, bf16),
        scratch_shapes=[pltpu.VMEM((groups, span // PARTS, 128), f32), pltpu.SMEM((groups,), jnp.int32)]
        + page_scratch(SPILL, span, decay.shape[0]),
        compiler_params=pltpu.CompilerParams(vmem_limit_bytes=24 * MIB),
        cost_estimate=page_cost(SPILL, keys, 64),
        name="hosted_pages",
    )(request, fill, asked_rows, in_hbm(keys), in_hbm(values), decay)


def merge_kernel(capacity, steps, part, heads, table_ref, back_ref, log_hbm, average_hbm, *refs):
    sources, targets, load_sems = [], [], None
    if len(refs) > 6:
        *refs, load_sems = refs
        count = load_sems.shape[0]
        sources, refs = refs[:count], refs[count:]
        targets, refs = refs[1:-5], (refs[0], *refs[-5:])
    out_ref, top_ref, total_ref, numer_ref, tops_ref, sems = refs
    groups = back_ref.shape[0]
    inner = heads * 64
    rows = steps * BEAMS
    span = PARTS * rows
    state = (top_ref, total_ref, numer_ref)
    copies = start_all([(log_hbm.at[part], top_ref), (average_hbm.at[part], numer_ref)], sems)
    pairs = []
    if len(sources) > 4:
        weight_ref, *targets = targets
        height = sources[0].shape[0]
        head = lax.axis_index("head")
        for other in range(4):
            place = pl.ds(pl.multiple_of((head ^ other) * height, height), height)
            pairs.append((sources[other], weight_ref.at[place]))
        sources = sources[4:]
    pairs.extend(zip(sources, targets))
    loads = start_all(pairs, load_sems)
    total_ref[...] = jnp.ones_like(total_ref)
    slot_rows = (inner // 128) * span
    first = capacity * slot_rows
    tails = jnp.concatenate(
        [back_ref[owner, first : first + rows, :] for owner in range(groups)], axis=0
    )
    source, target = sublanes((128, inner)), lanes((128, inner)) // 64
    for rank in range(capacity):
        hit = source < 0
        for piece in range(3):
            hit = hit | (source == target + part * 64 + (rank * 3 + piece) * heads)
        tops_ref[:, rank * inner : rank * inner + inner] = dot(tails, hit.astype(f32).astype(bf16))
    for copy in copies:
        copy.wait()
    for owner in range(groups):
        for rank in range(capacity):
            local = table_ref[owner * capacity + rank]
            bias = jnp.where(local >= 0, 0.0, masked_score)
            top = tops_ref[owner * rows : owner * rows + rows, rank * inner : rank * inner + inner]
            starts = [rank * slot_rows + pair * span + part * rows for pair in range(inner // 128)]
            average = jnp.concatenate(
                [back_ref[owner, start : start + rows, :].astype(f32) for start in starts], axis=1
            )
            here = pl.ds(pl.multiple_of(jnp.maximum(local, 0) * rows, rows), rows)
            absorb(state, here, slice(None), top + bias, 1.0, average)
    for index in range(top_ref.shape[0] // (2 * rows)):
        parts = []
        for half in range(2):
            here = slice((index * 2 + half) * rows, (index * 2 + half + 1) * rows)
            parts.append(numer_ref[here, :] / total_ref[here, :])
        for step in range(steps):
            both = jnp.concatenate([p[step * 8 : step * 8 + 8] for p in parts], axis=0)
            start = step * (top_ref.shape[0] // steps) + index * 16
            out_ref[start : start + 16, :] = both.astype(bf16)
    for copy in loads:
        copy.wait()


def merge(part, table, back, logs, averages, steps, capacity, sources):
    _, requests, span, inner = logs.shape
    rows = requests * span
    logs, averages = (x.reshape(PARTS, rows, inner) for x in (logs, averages))
    vmem = pl.BlockSpec(memory_space=pltpu.VMEM)
    hbm = pl.BlockSpec(memory_space=pltpu.HBM)
    anywhere = pl.BlockSpec(memory_space=pl.ANY)
    mixes = sources[:4] if len(sources) > 4 else []
    others = sources[len(mixes) :]
    kept = [jax.ShapeDtypeStruct(x.shape, x.dtype) for x in others]
    if mixes:
        kept = [jax.ShapeDtypeStruct((4 * inner, mixes[0].shape[1]), bf16)] + kept
    return pl.pallas_call(
        functools.partial(merge_kernel, capacity, steps, part, inner // 64),
        in_specs=[SMEM, vmem, hbm, hbm] + [anywhere] * len(mixes) + [hbm] * len(others),
        out_shape=[jax.ShapeDtypeStruct((rows, inner), bf16)] + kept,
        scratch_shapes=[pltpu.VMEM((rows, inner), f32)] * 3
        + [
            pltpu.VMEM((back.shape[0] * span, capacity * inner), f32),
            pltpu.SemaphoreType.DMA((2,)),
        ]
        + [pltpu.SemaphoreType.DMA((len(sources),))] * bool(sources),
        compiler_params=pltpu.CompilerParams(vmem_limit_bytes=10 * MIB),
        cost_estimate=pl.CostEstimate(
            flops=40 * rows * inner, bytes_accessed=8 * MIB, transcendentals=4 * rows * inner
        ),
        name="merge",
    )(table, back, in_hbm(logs), in_hbm(averages), *mixes, *[in_hbm(x) for x in others])


def block_kernel(
    first, att0, att1, att2, att3, weight_ref, tokens_ref, gain_ref, gate_ref, up_ref, down_ref,
    residual_out, mine_ref, other_ref,
    residual_ref, attended_ref, scaled_ref, hidden_ref, sums_ref,
):
    rows, width = residual_ref.shape
    inner = att0.shape[1]
    half = rows // 2
    head = lax.axis_index("head")
    core = lax.rem(head, 2)
    near = pl.ds(pl.multiple_of(core * half, half), half)
    away = pl.ds(pl.multiple_of((1 - core) * half, half), half)
    for other, att in enumerate((att0, att1, att2, att3)):
        place = pl.ds(pl.multiple_of((head ^ other) * inner, inner), inner)
        attended_ref[:, place] = att[...]
    gain = gain_ref[...].reshape(1, -1)
    squares = jnp.zeros((rows, 1), f32)
    for start in range(0, width, 512):
        cols = slice(start, start + 512)
        x = tokens_ref[first : first + rows, cols].astype(f32) + dot(attended_ref[...], weight_ref[:, cols])
        residual_ref[:, cols] = x
        scaled_ref[:, cols] = (x * gain[:, cols]).astype(bf16)
        squares = squares + jnp.sum(x * x, axis=-1, keepdims=True)
    scale = lax.rsqrt(squares / width + epsilon)
    for start in range(0, gate_ref.shape[1], 256):
        cols = slice(start, start + 256)
        gate = dot(scaled_ref[...], gate_ref[:, cols]) * scale
        up = dot(scaled_ref[...], up_ref[:, cols]) * scale
        hidden_ref[:, cols] = (gate / (1.0 + jnp.exp(-gate)) * up).astype(bf16)
    residual_out[...] = residual_ref[near, :]
    for start in range(0, width, 512):
        cols = slice(start, start + 512)
        sums_ref[:, cols] = dot(hidden_ref[...], down_ref[:, cols])
    mine_ref[...] = sums_ref[near, :]
    other_ref[...] = sums_ref[away, :].astype(bf16)


def block(first, attended, weight, tokens, gain, w_gate, w_up, w_down):
    rows, inner = attended[0].shape
    width = tokens.shape[1]
    hidden = w_gate.shape[1]
    vmem = pl.BlockSpec(memory_space=pltpu.VMEM)
    half = jax.ShapeDtypeStruct((rows // 2, width), f32)
    return pl.pallas_call(
        functools.partial(block_kernel, first),
        in_specs=[vmem] * 10,
        out_specs=[vmem] * 3,
        out_shape=[half, half, jax.ShapeDtypeStruct((rows // 2, width), bf16)],
        scratch_shapes=[
            pltpu.VMEM((rows, width), f32),
            pltpu.VMEM((rows, 4 * inner), bf16),
            pltpu.VMEM((rows, width), bf16),
            pltpu.VMEM((rows, hidden), bf16),
            pltpu.VMEM((rows, width), f32),
        ],
        compiler_params=pltpu.CompilerParams(vmem_limit_bytes=20 * MIB),
        cost_estimate=pl.CostEstimate(flops=0, bytes_accessed=0, transcendentals=0),
        name="block",
    )(*attended, weight, tokens, gain, w_gate, w_up, w_down)


def finish_kernel(first, half, places, *refs):
    count = 2 * len(places)
    parts, out_ref, sems = refs[-2 - count : -2], refs[-2], refs[-1]
    core = lax.axis_index("head") % 2
    pairs = []
    for index, place in enumerate(places):
        for part, owner in ((parts[2 * index], core), (parts[2 * index + 1], 1 - core)):
            start = pl.multiple_of(first + owner * half + place, 16)
            pairs.append((part, out_ref.at[pl.ds(start, part.shape[0])]))
    for copy in start_all(pairs, sems):
        copy.wait()


def finish(first, half, pieces, rows, before=()):
    vmem = pl.BlockSpec(memory_space=pltpu.VMEM)
    hbm = pl.BlockSpec(memory_space=pltpu.HBM)
    places, parts = [], []
    for place, done in pieces:
        places.append(place)
        parts.extend([done, swap_core(done)])
    width = parts[0].shape[1]
    return pl.pallas_call(
        functools.partial(finish_kernel, first, half, places),
        in_specs=[hbm] * len(before) + [vmem] * len(parts),
        out_specs=hbm,
        out_shape=pltpu.HBM((rows, width), parts[0].dtype),
        input_output_aliases={0: 0} if before else {},
        scratch_shapes=[pltpu.SemaphoreType.DMA((len(parts),))],
        compiler_params=pltpu.CompilerParams(vmem_limit_bytes=8 * MIB),
        name="finish",
    )(*[in_hbm(x) for x in before], *parts)


def swap_core(value):
    return lax.ppermute(value, "head", [(i, i ^ 1) for i in range(4)])


def swap_chip(value):
    return lax.ppermute(value, "head", [(i, i ^ 2) for i in range(4)])


def shards(
    tokens, parents, page_request, page_fill, keys_pool, values_pool, decay_pool,
    gain_attn, w_query, w_key, w_value, w_forget, forget_bias, w_out,
    gain_ffn, w_gate, w_up, w_down,
):
    steps, rows, width = tokens.shape
    inner = w_query.shape[0]
    local_count = rows // BEAMS
    span = steps * BEAMS
    groups = lax.axis_size("group")
    capacity = (SPILL + groups - 2) // (groups - 1)
    decay = decay_pool.transpose(1, 0, 2)

    def exchange(value):
        return lax.all_to_all(value, "group", split_axis=0, concat_axis=0, tiled=True)

    ids = exchange(jnp.broadcast_to(page_request, (groups, 1, page_request.shape[0])))
    q_near, q, normed = queries_of(tokens, gain_attn, w_query)
    table, asked = ask(page_request, ids, q_near, span, capacity)
    asked_rows = exchange(asked.reshape(groups, capacity * span, inner)).reshape(asked.shape)
    asked, q = lax.optimization_barrier((asked, q))
    own = own_pages(page_request, page_fill, q, keys_pool, values_pool, decay, span)
    own, w_sent = lax.optimization_barrier((own, w_out))
    w_out_far = swap_chip(w_sent)
    asked_rows, own = lax.optimization_barrier((asked_rows, own))
    payload = hosted_pages(
        page_request, page_fill, asked_rows, keys_pool, values_pool, decay, groups, capacity, local_count
    )
    payload, normed = lax.optimization_barrier((payload, normed))
    back = exchange(payload)
    logs, averages = fresh(parents, forget_bias, normed, w_key, w_value, w_forget, q, own)
    logs, w_out_far = lax.optimization_barrier((logs, w_out_far))
    mixes = [w_out, swap_core(w_out), w_out_far, swap_core(w_out_far)]

    flat = tokens.reshape(steps * rows, width)
    each = steps // PARTS
    sums = (table, back, logs, averages, each, capacity)
    here, flat = merge(0, *sums, [flat])
    heres = [here]
    back, heres[0] = lax.optimization_barrier((back, heres[0]))
    sums = (table, back, logs, averages, each, capacity)
    here, weight, w_gate, w_up, w_down = merge(1, *sums, mixes + [w_gate, w_up, w_down])
    heres.append(here)
    fars = [swap_chip(here) for here in heres]
    fars[0], heres[1] = lax.optimization_barrier((fars[0], heres[1]))

    def block_of(index):
        here, far = heres[index], fars[index]
        gathered = [here, swap_core(here), far, swap_core(far)]
        if index:
            gathered, chip[0] = lax.optimization_barrier((gathered, chip[0]))
        first = index * here.shape[0]
        return block(first, gathered, weight, flat, gain_ffn, w_gate, w_up, w_down)

    def chip_sum(mine, other):
        return (mine + swap_core(other).astype(f32)).astype(bf16)

    chip, residual = [None] * PARTS, [None] * PARTS
    residual[0], mine, other = block_of(0)
    other, fars[1] = lax.optimization_barrier((other, fars[1]))
    chip[0] = chip_sum(mine, other)
    most = chip[0].shape[0] // 8 * 3
    chip_most, chip_rest = chip[0][:most], chip[0][most:]
    far_most, far_rest = swap_chip(chip_most), swap_chip(chip_rest)
    residual[1], mine, other = block_of(1)
    other, far_most = lax.optimization_barrier((other, far_most))
    chip[1] = chip_sum(mine, other)
    half = chip[1].shape[0]
    cut = half // 4 * 3
    far_first, far_last = swap_chip(chip[1][:cut]), swap_chip(chip[1][cut:])

    def done(residual, chip, far):
        return (residual + (chip.astype(f32) + far.astype(f32))).astype(bf16)

    pieces = [
        (0, done(residual[0][:most], chip_most, far_most)),
        (most, done(residual[0][most:], chip_rest, far_rest)),
    ]
    result = finish(0, half, pieces, steps * rows)
    pieces = [
        (0, done(residual[1][:cut], chip[1][:cut], far_first)),
        (cut, done(residual[1][cut:], chip[1][cut:], far_last)),
    ]
    result = finish(2 * half, half, pieces, steps * rows, [result])
    return result.reshape(steps, rows, width)


def solution(mesh):
    return jax.shard_map(
        shards,
        mesh=mesh,
        in_specs=(
            P(None, "group", None),
            P(None, "group"),
            P("group"),
            P("group"),
            P("group", "head", None),
            P("group", "head", None),
            P("group", "head", None),
            P(),
            P("head", None),
            P("head", None),
            P("head", None),
            P(None, "head"),
            P("head"),
            P("head", None),
            P(),
            P(None, "head"),
            P(None, "head"),
            P("head", None),
        ),
        out_specs=P(None, "group", None),
        check_vma=False,
    )
```

```python
import functools

import jax
import jax.numpy as jnp
from jax import lax
from jax.experimental import pallas as pl
from jax.experimental.pallas import tpu as pltpu
from jax.sharding import PartitionSpec as P

BEAMS = 8
OWNED_SLOTS = 32
SPILL = 16
PAGE_BLOCK = 16
PARTS = 2
MIB = 1 << 20

epsilon = 1e-05
masked_score = -1e30
f32 = jnp.float32
bf16 = jnp.bfloat16

NN = (((1,), (0,)), ((), ()))
NT = (((1,), (1,)), ((), ()))
SMEM = pl.BlockSpec(memory_space=pltpu.SMEM)


def dot(a, b, dims=NN):
    return lax.dot_general(a, b, dims, preferred_element_type=f32)


def lanes(shape):
    return lax.broadcasted_iota(jnp.int32, shape, len(shape) - 1)


def sublanes(shape):
    return lax.broadcasted_iota(jnp.int32, shape, len(shape) - 2)


def in_hbm(array):
    return pltpu.with_memory_space_constraint(array, pltpu.HBM)


def in_vmem(array):
    return pltpu.with_memory_space_constraint(array, pltpu.VMEM)


def start_all(pairs, sems):
    copies = [pltpu.make_async_copy(s, t, sems.at[i]) for i, (s, t) in enumerate(pairs)]
    for copy in copies:
        copy.start()
    return copies


def fill_table(local_count, capacity, first, ids_ref, table_ref):
    groups = ids_ref.shape[0]
    for slot in range(groups * capacity + 1):
        table_ref[slot] = -1

    def group(index, carry):
        rank = jnp.int32(0)
        for page in range(SPILL):
            local = ids_ref[index, 0, OWNED_SLOTS + page] - first
            mine = (local >= 0) & (local < local_count)

            slot = jnp.where(mine, index * capacity + rank, groups * capacity)
            table_ref[slot] = local
            rank = rank + mine.astype(jnp.int32)
        return carry

    lax.fori_loop(0, groups, group, 0, unroll=2)


def query_kernel(
    tokens_hbm, gain_ref, wq_hbm, q_ref, q_hbm, normed_hbm,
    tokens_ref, wq_ref, normed_ref, sems, out_sems,
):
    steps, rows, _ = tokens_ref.shape
    span = steps * BEAMS
    cut = rows // 2
    copies = start_all(
        [
            (tokens_hbm.at[:, :cut], tokens_ref.at[:, :cut]),
            (tokens_hbm.at[:, cut:], tokens_ref.at[:, cut:]),
            (wq_hbm, wq_ref),
        ],
        sems,
    )
    gain = gain_ref[...].reshape(1, -1)

    def pair(index, carry):
        slabs = []
        for step in range(steps):
            x = tokens_ref[step, pl.ds(pl.multiple_of(index * 16, 16), 16), :].astype(f32)
            scale = lax.rsqrt(jnp.mean(x * x, axis=-1, keepdims=True) + epsilon)
            slabs.append(x * scale * gain)
        for half in range(2):
            part = jnp.concatenate([s[half * 8 : half * 8 + 8] for s in slabs], axis=0)
            start = pl.multiple_of((index * 2 + half) * span, span)
            normed_ref[pl.ds(start, span), :] = part.astype(bf16)
        return carry

    copies[0].wait()
    lax.fori_loop(0, cut // 16, pair, 0, unroll=2)
    copies[1].wait()
    lax.fori_loop(cut // 16, rows // 16, pair, 0, unroll=2)
    leaving = start_all([(normed_ref, normed_hbm)], out_sems)
    copies[2].wait()
    query = dot(normed_ref[...], wq_ref[...], NT).astype(bf16)
    q_ref[...] = (query.astype(f32) * 0.125).astype(bf16)
    last = pltpu.make_async_copy(q_ref, q_hbm, out_sems.at[1])
    last.start()
    leaving[0].wait()
    last.wait()


def queries_of(tokens, gain, w_query):
    steps, rows, width = tokens.shape
    inner = w_query.shape[0]
    total = steps * rows
    hbm = pl.BlockSpec(memory_space=pltpu.HBM)
    vmem = pl.BlockSpec(memory_space=pltpu.VMEM)
    return pl.pallas_call(
        query_kernel,
        in_specs=[hbm, vmem, hbm],
        out_specs=[vmem, hbm, hbm],
        out_shape=[
            pltpu.VMEM((total, inner), bf16),
            pltpu.HBM((total, inner), bf16),
            pltpu.HBM((total, width), bf16),
        ],
        scratch_shapes=[
            pltpu.VMEM(tokens.shape, bf16),
            pltpu.VMEM(w_query.shape, bf16),
            pltpu.VMEM((total, width), bf16),
            pltpu.SemaphoreType.DMA((3,)),
            pltpu.SemaphoreType.DMA((2,)),
        ],
        compiler_params=pltpu.CompilerParams(vmem_limit_bytes=12 * MIB),
        cost_estimate=pl.CostEstimate(
            flops=2 * total * width * inner, bytes_accessed=6 * MIB, transcendentals=total
        ),
        name="queries",
    )(in_hbm(tokens), gain, in_hbm(w_query))


def ask_kernel(capacity, request_ref, ids_ref, q_ref, table_ref, out_ref):
    slots, span, _ = out_ref.shape
    local_count = q_ref.shape[0] // span
    first = request_ref[0] // local_count * local_count
    fill_table(local_count, capacity, first, ids_ref, table_ref)
    for slot in range(slots):
        start = jnp.maximum(table_ref[slot], 0) * span
        out_ref[slot] = q_ref[pl.ds(pl.multiple_of(start, span), span), :]


def ask(request, ids, q, span, capacity):
    slots = ids.shape[0] * capacity
    vmem = pl.BlockSpec(memory_space=pltpu.VMEM)
    return pl.pallas_call(
        functools.partial(ask_kernel, capacity),
        in_specs=[SMEM, SMEM, vmem],
        out_specs=[SMEM, vmem],
        out_shape=[
            jax.ShapeDtypeStruct((slots + 1,), jnp.int32),
            jax.ShapeDtypeStruct((slots, span, q.shape[1]), bf16),
        ],
        compiler_params=pltpu.CompilerParams(vmem_limit_bytes=8 * MIB),
        name="ask",
    )(request, ids, in_vmem(q))


def half_masks(rows):
    low = lanes((rows, 128)) < 64
    return low.astype(f32).astype(bf16), jnp.logical_not(low).astype(f32).astype(bf16)


def stacked(pair_rows, masks):
    return jnp.concatenate([pair_rows * masks[0], pair_rows * masks[1]], axis=0)


def side_by_side(values, rows):
    low = lanes((rows, 128)) < 64
    top = jnp.broadcast_to(values[:rows], (rows, 128))
    bottom = jnp.broadcast_to(values[rows:], (rows, 128))
    return jnp.where(low, top, bottom)


def absorb(state, rows, columns, top, total, numer):
    top_ref, total_ref, numer_ref = state
    old = top_ref[rows, columns]
    new = jnp.maximum(old, top)
    keep = jnp.exp(old - new)
    add = jnp.exp(top - new)
    top_ref[rows, columns] = new
    total_ref[rows, columns] = total_ref[rows, columns] * keep + total * add
    numer_ref[rows, columns] = numer_ref[rows, columns] * keep + numer * add


def history(parents_ref, q_ref, k_ref, v_ref, forget_ref, state, scores_ref, weights_ref):
    transitions, rows = parents_ref.shape
    span = (transitions + 1) * BEAMS
    pack = 128 // span
    square = (128, 128)
    diagonal = sublanes(square) == lanes(square)
    columns = []
    for step in range(transitions):
        row = parents_ref[step : step + 1, :].astype(f32)
        columns.append(
            jnp.sum(jnp.where(diagonal, jnp.broadcast_to(row, square), 0.0), axis=1, keepdims=True)
        )
    lane8 = lanes((8, 128)).astype(f32)
    masks = half_masks(128)
    low = lanes(square) < 64
    top_ref, total_ref, numer_ref = state
    groups = rows // BEAMS // pack
    pairs = q_ref.shape[1] // 128
    for group in range(groups):
        slabs = []
        for member in range(pack):
            first = (group * pack + member) * BEAMS
            slabs.append(jnp.zeros((8, 128), f32))
            for step in range(transitions):
                wanted = columns[step][first : first + 8] + float(member * span + step * 8)
                slabs.append(jnp.where(lane8 == wanted, 1.0, 0.0))
        parent = jnp.concatenate(slabs, axis=0)
        parent16 = parent.astype(bf16)
        one = diagonal.astype(f32) + parent
        two = dot(parent16, parent16)
        ancestors = one + dot(two.astype(bf16), one.astype(bf16))
        here = pl.ds(group * 128, 128)
        running = lax.dot_general(
            ancestors, forget_ref[here, :], NN,
            precision=lax.Precision.HIGHEST, preferred_element_type=f32,
        ).T
        hidden = jnp.where(ancestors > 0.5, 0.0, masked_score)
        for pair in range(pairs):
            cols = pl.ds(pair * 128, 128)
            raw = dot(stacked(q_ref[here, cols], masks), k_ref[here, cols], NT)
            for half in range(2):
                head = pair * 2 + half
                scores_ref[group * pairs + pair, half] = raw[half * 128 : half * 128 + 128] + (
                    hidden - running[head : head + 1]
                )
    for group in range(groups):
        here = pl.ds(group * 128, 128)
        for pair in range(pairs):
            cols = pl.ds(pair * 128, 128)
            tops, totals = [], []
            for half in range(2):
                scores = scores_ref[group * pairs + pair, half]
                top = jnp.broadcast_to(jnp.max(scores, axis=-1, keepdims=True), square)
                weights = jnp.exp(scores - top)
                weights_ref[group * pairs + pair, pl.ds(half * 128, 128), :] = weights.astype(bf16)
                tops.append(top)
                totals.append(jnp.broadcast_to(jnp.sum(weights, axis=-1, keepdims=True), square))
            top_ref[here, cols] = jnp.where(low, *tops)
            total_ref[here, cols] = jnp.where(low, *totals)
    for group in range(groups):
        here = pl.ds(group * 128, 128)
        for pair in range(pairs):
            cols = pl.ds(pair * 128, 128)
            numer = dot(weights_ref[group * pairs + pair], v_ref[here, cols])
            numer_ref[here, cols] = jnp.where(low, numer[:128], numer[128:])


def fresh_kernel(
    parents_ref, bias_ref, normed_hbm, wk_hbm, wv_hbm, wf_hbm, q_hbm, top_hbm, total_hbm, numer_hbm,
    logs_hbm, averages_hbm,
    normed_ref, wk_ref, wv_ref, wf_ref, q_ref, top_own, total_own, numer_own,
    k_ref, v_ref, forget_ref, top_ref, total_ref, numer_ref, scores_ref, weights_ref,
    logs_ref, averages_ref, sems, out_sems,
):
    copies = start_all(
        [
            (normed_hbm, normed_ref), (wk_hbm, wk_ref), (wv_hbm, wv_ref), (wf_hbm, wf_ref),
            (q_hbm, q_ref), (top_hbm, top_own), (total_hbm, total_own), (numer_hbm, numer_own),
        ],
        sems,
    )
    copies[0].wait()
    copies[1].wait()
    k_ref[...] = dot(normed_ref[...], wk_ref[...], NT).astype(bf16)
    copies[2].wait()
    v_ref[...] = dot(normed_ref[...], wv_ref[...], NT).astype(bf16)
    copies[3].wait()
    gate = dot(normed_ref[...], wf_ref[...], NT) + bias_ref[...]
    forget = jnp.minimum(gate, 0.0) - jnp.log1p(jnp.exp(-jnp.abs(gate)))
    forget_ref[...] = jnp.zeros_like(forget_ref)
    forget_ref[:, : forget.shape[1]] = forget
    copies[4].wait()
    state = (top_ref, total_ref, numer_ref)
    history(parents_ref, q_ref, k_ref, v_ref, forget_ref, state, scores_ref, weights_ref)
    for copy in copies[5:]:
        copy.wait()

    parts, _, part = logs_ref.shape[:3]
    span = parts * part

    def join(index, carry):
        rows = pl.ds(pl.multiple_of(index * span, span), span)
        absorb(state, rows, slice(None), top_own[rows, :], total_own[rows, :], numer_own[rows, :])
        total = total_ref[rows, :]
        logs = top_ref[rows, :] + jnp.log(total)
        averages = numer_ref[rows, :] / total
        for number in range(parts):
            logs_ref[number, index] = logs[number * part : number * part + part]
            averages_ref[number, index] = averages[number * part : number * part + part]
        return carry

    lax.fori_loop(0, logs_ref.shape[1], join, 0, unroll=2)
    for copy in start_all([(logs_ref, logs_hbm), (averages_ref, averages_hbm)], out_sems):
        copy.wait()


def fresh(parents, bias, normed, w_key, w_value, w_forget, q, own):
    rows, inner = q.shape
    span = (parents.shape[0] + 1) * BEAMS
    vmem = pl.BlockSpec(memory_space=pltpu.VMEM)
    hbm = pl.BlockSpec(memory_space=pltpu.HBM)
    big = [normed, w_key, w_value, w_forget.T, q, *own]
    wide = pltpu.VMEM((rows, inner), f32)
    out = (PARTS, rows // span, span // PARTS, inner)
    tiles = rows * inner // (128 * 128)
    return pl.pallas_call(
        fresh_kernel,
        in_specs=[vmem, vmem] + [hbm] * len(big),
        out_specs=[hbm] * 2,
        out_shape=[pltpu.HBM(out, f32)] * 2,
        scratch_shapes=[pltpu.VMEM(x.shape, x.dtype) for x in big]
        + [pltpu.VMEM((rows, inner), bf16)] * 2
        + [pltpu.VMEM((rows, 128), f32), wide, wide, wide]
        + [pltpu.VMEM((tiles, 2, 128, 128), f32), pltpu.VMEM((tiles, 256, 128), bf16)]
        + [pltpu.VMEM(out, f32)] * 2
        + [pltpu.SemaphoreType.DMA((len(big),)), pltpu.SemaphoreType.DMA((2,))],
        compiler_params=pltpu.CompilerParams(vmem_limit_bytes=24 * MIB),
        cost_estimate=pl.CostEstimate(
            flops=4 * rows * normed.shape[1] * inner, bytes_accessed=12 * MIB,
            transcendentals=8 * rows * inner,
        ),
        name="fresh",
    )(parents, bias.reshape(1, -1), *[in_hbm(x) for x in big])


def page_weights(queries, fills, keys_ref, decay_ref, scores_ref, weights_ref, tops_ref):
    span = queries[0][0].shape[0]
    masks = half_masks(span)
    lane = lanes((1, 128))
    decay = [decay_ref[head].astype(f32) for head in range(decay_ref.shape[0])]
    for page, pairs in enumerate(queries):
        valid = lane < fills[page]
        for pair, query in enumerate(pairs):
            raw = dot(stacked(query, masks), keys_ref[page, pl.ds(pair * 128, 128), :])
            for half in range(2):
                head = pair * 2 + half
                bias = jnp.where(valid, decay[head][page : page + 1], masked_score)
                scores_ref[page, pl.ds(head * span, span), :] = (
                    raw[half * span : half * span + span] + bias
                )
    for page in range(len(queries)):
        for head in range(decay_ref.shape[0]):
            rows = pl.ds(head * span, span)
            scores = scores_ref[page, rows, :]
            top = jnp.broadcast_to(jnp.max(scores, axis=-1, keepdims=True), scores.shape)
            tops_ref[page, rows, :] = top
            weights = jnp.exp(scores - top)
            weights_ref[page, rows, :] = weights.astype(bf16)
            scores_ref[page, rows, :] = jnp.broadcast_to(
                jnp.sum(weights, axis=-1, keepdims=True), scores.shape
            )


def page_sums(page, pair, span, values_ref, scores_ref, weights_ref, tops_ref):
    low = lanes((span, 128)) < 64
    first, second = pl.ds(pair * 2 * span, span), pl.ds((pair * 2 + 1) * span, span)
    numer = dot(
        weights_ref[page, pl.ds(pair * 2 * span, 2 * span), :],
        values_ref[page, pl.ds(pair * 128, 128), :],
        NT,
    )
    top = jnp.where(low, tops_ref[page, first, :], tops_ref[page, second, :])
    total = jnp.where(low, scores_ref[page, first, :], scores_ref[page, second, :])
    return top, total, jnp.where(low, numer[:span], numer[span:])


def page_scratch(pages, span, heads):
    rows = span * heads
    return [
        pltpu.VMEM((pages, rows, 128), f32),
        pltpu.VMEM((pages, rows, 128), bf16),
        pltpu.VMEM((pages, rows, 128), f32),
    ]


def own_kernel(
    request_ref, fill_ref, q_ref, keys_ref, values_ref, decay_ref,
    top_ref, total_ref, numer_ref, *scratch,
):
    state = (top_ref, total_ref, numer_ref)
    span = scratch[0].shape[1] // decay_ref.shape[0]
    local_count = q_ref.shape[0] // span
    pairs = q_ref.shape[1] // 128

    block = pl.program_id(0)

    @pl.when(block == 0)
    def _():
        top_ref[...] = jnp.full_like(top_ref, masked_score)
        total_ref[...] = jnp.zeros_like(total_ref)
        numer_ref[...] = jnp.zeros_like(numer_ref)

    places, queries, fills = [], [], []
    for page in range(PAGE_BLOCK):
        index = block * PAGE_BLOCK + page
        local = lax.rem(request_ref[index], local_count)
        rows = pl.ds(pl.multiple_of(local * span, span), span)
        places.append(rows)
        queries.append([q_ref[rows, pl.ds(pair * 128, 128)] for pair in range(pairs)])
        fills.append(fill_ref[index])
    page_weights(queries, fills, keys_ref, decay_ref, *scratch)
    for page, rows in enumerate(places):
        for pair in range(pairs):
            sums = page_sums(page, pair, span, values_ref, *scratch)
            absorb(state, rows, pl.ds(pair * 128, 128), *sums)


def page_cost(pages, keys, rows):
    inner, length = keys.shape[1:]
    return pl.CostEstimate(
        flops=pages * rows * inner * length * 8,
        bytes_accessed=pages * inner * length * 4,
        transcendentals=pages * rows * inner * length // 64,
    )


def own_pages(request, fill, q, keys, values, decay, span):
    pool = pl.BlockSpec((PAGE_BLOCK,) + keys.shape[1:], lambda i: (i, 0, 0))
    decay_spec = pl.BlockSpec((decay.shape[0], PAGE_BLOCK, decay.shape[2]), lambda i: (0, i, 0))
    rows = pl.BlockSpec(q.shape, lambda i: (0, 0))
    return pl.pallas_call(
        own_kernel,
        grid=(OWNED_SLOTS // PAGE_BLOCK,),
        in_specs=[SMEM, SMEM, rows, pool, pool, decay_spec],
        out_specs=[rows] * 3,
        out_shape=[pltpu.HBM(q.shape, f32)] * 3,
        scratch_shapes=page_scratch(PAGE_BLOCK, span, decay.shape[0]),
        compiler_params=pltpu.CompilerParams(vmem_limit_bytes=20 * MIB),
        cost_estimate=page_cost(OWNED_SLOTS, keys, 64),
        name="own_pages",
    )(request, fill, in_hbm(q), in_hbm(keys), in_hbm(values), decay)


def hosted_kernel(
    local_count, capacity, request_ref, fill_ref, q_ref, keys_ref, values_ref, decay_ref,
    out_ref, tail_ref, count_ref, *scratch,
):
    span, inner = q_ref.shape[1:]
    pairs = inner // 128
    heads = decay_ref.shape[0]
    groups = out_ref.shape[0]
    half = span // PARTS
    slot_rows = pairs * span
    out_ref[...] = jnp.zeros_like(out_ref)
    tail_ref[...] = jnp.zeros_like(tail_ref)
    for owner in range(groups):
        count_ref[owner] = 0
    places, queries, fills = [], [], []
    for page in range(SPILL):
        owner = request_ref[OWNED_SLOTS + page] // local_count
        rank = count_ref[owner]
        count_ref[owner] = rank + 1
        places.append((owner, rank))
        slot = owner * capacity + rank
        queries.append([q_ref[slot, :, pl.ds(pair * 128, 128)] for pair in range(pairs)])
        fills.append(fill_ref[OWNED_SLOTS + page])
    page_weights(queries, fills, keys_ref, decay_ref, *scratch)
    scores_ref, _, tops_ref = scratch
    lane = lanes((half, 128))
    for page, (owner, rank) in enumerate(places):
        for pair in range(pairs):
            _, total, numer = page_sums(page, pair, span, values_ref, *scratch)
            here = pl.ds(pl.multiple_of(rank * slot_rows + pair * span, span), span)
            out_ref[owner, here, :] = (numer / total).astype(bf16)
        tail = tail_ref[owner]
        base = rank * (3 * heads)
        for head in range(heads):
            rows = pl.ds(head * span, span)
            rest = tops_ref[page, rows, :] + jnp.log(scores_ref[page, rows, :])
            rest = jnp.where(lane < 64, rest[:half], rest[half:])
            for piece in range(3):
                part = rest.astype(bf16).astype(f32)
                rest = rest - part
                tail = jnp.where(lane % 64 == base + piece * heads + head, part, tail)
        tail_ref[owner] = tail
    first = capacity * slot_rows
    for owner in range(groups):
        out_ref[owner, first : first + half, :] = tail_ref[owner].astype(bf16)


def hosted_pages(request, fill, asked_rows, keys, values, decay, groups, capacity, local_count):
    count, span, inner = asked_rows.shape
    shift = OWNED_SLOTS // SPILL
    pool = pl.BlockSpec((SPILL,) + keys.shape[1:], lambda i: (shift, 0, 0))
    decay_spec = pl.BlockSpec((decay.shape[0], SPILL, decay.shape[2]), lambda i: (0, shift, 0))
    out_shape = (groups, capacity * span * inner // 128 + span // PARTS, 128)
    return pl.pallas_call(
        functools.partial(hosted_kernel, local_count, capacity),
        grid=(1,),
        in_specs=[
            SMEM, SMEM, pl.BlockSpec(asked_rows.shape, lambda i: (0, 0, 0)), pool, pool, decay_spec
        ],
        out_specs=pl.BlockSpec(out_shape, lambda i: (0, 0, 0)),
        out_shape=jax.ShapeDtypeStruct(out_shape, bf16),
        scratch_shapes=[pltpu.VMEM((groups, span // PARTS, 128), f32), pltpu.SMEM((groups,), jnp.int32)]
        + page_scratch(SPILL, span, decay.shape[0]),
        compiler_params=pltpu.CompilerParams(vmem_limit_bytes=24 * MIB),
        cost_estimate=page_cost(SPILL, keys, 64),
        name="hosted_pages",
    )(request, fill, asked_rows, in_hbm(keys), in_hbm(values), decay)


def merge_kernel(capacity, steps, part, heads, table_ref, back_ref, log_hbm, average_hbm, *refs):
    sources, targets, load_sems = [], [], None
    if len(refs) > 6:
        *refs, load_sems = refs
        count = load_sems.shape[0]
        sources, refs = refs[:count], refs[count:]
        targets, refs = refs[1:-5], (refs[0], *refs[-5:])
    out_ref, top_ref, total_ref, numer_ref, tops_ref, sems = refs
    groups = back_ref.shape[0]
    inner = heads * 64
    rows = steps * BEAMS
    span = PARTS * rows
    state = (top_ref, total_ref, numer_ref)
    copies = start_all([(log_hbm.at[part], top_ref), (average_hbm.at[part], numer_ref)], sems)
    pairs = []
    if len(sources) > 4:
        weight_ref, *targets = targets
        height = sources[0].shape[0]
        head = lax.axis_index("head")
        for other in range(4):
            place = pl.ds(pl.multiple_of((head ^ other) * height, height), height)
            pairs.append((sources[other], weight_ref.at[place]))
        sources = sources[4:]
    pairs.extend(zip(sources, targets))
    loads = start_all(pairs, load_sems)
    total_ref[...] = jnp.ones_like(total_ref)
    slot_rows = (inner // 128) * span
    first = capacity * slot_rows
    tails = jnp.concatenate(
        [back_ref[owner, first : first + rows, :] for owner in range(groups)], axis=0
    )
    source, target = sublanes((128, inner)), lanes((128, inner)) // 64
    for rank in range(capacity):
        hit = source < 0
        for piece in range(3):
            hit = hit | (source == target + part * 64 + (rank * 3 + piece) * heads)
        tops_ref[:, rank * inner : rank * inner + inner] = dot(tails, hit.astype(f32).astype(bf16))
    for copy in copies:
        copy.wait()
    for owner in range(groups):
        for rank in range(capacity):
            local = table_ref[owner * capacity + rank]
            bias = jnp.where(local >= 0, 0.0, masked_score)
            top = tops_ref[owner * rows : owner * rows + rows, rank * inner : rank * inner + inner]
            starts = [rank * slot_rows + pair * span + part * rows for pair in range(inner // 128)]
            average = jnp.concatenate(
                [back_ref[owner, start : start + rows, :].astype(f32) for start in starts], axis=1
            )
            here = pl.ds(pl.multiple_of(jnp.maximum(local, 0) * rows, rows), rows)
            absorb(state, here, slice(None), top + bias, 1.0, average)
    for index in range(top_ref.shape[0] // (2 * rows)):
        parts = []
        for half in range(2):
            here = slice((index * 2 + half) * rows, (index * 2 + half + 1) * rows)
            parts.append(numer_ref[here, :] / total_ref[here, :])
        for step in range(steps):
            both = jnp.concatenate([p[step * 8 : step * 8 + 8] for p in parts], axis=0)
            start = step * (top_ref.shape[0] // steps) + index * 16
            out_ref[start : start + 16, :] = both.astype(bf16)
    for copy in loads:
        copy.wait()


def merge(part, table, back, logs, averages, steps, capacity, sources):
    _, requests, span, inner = logs.shape
    rows = requests * span
    logs, averages = (x.reshape(PARTS, rows, inner) for x in (logs, averages))
    vmem = pl.BlockSpec(memory_space=pltpu.VMEM)
    hbm = pl.BlockSpec(memory_space=pltpu.HBM)
    anywhere = pl.BlockSpec(memory_space=pl.ANY)
    mixes = sources[:4] if len(sources) > 4 else []
    others = sources[len(mixes) :]
    kept = [jax.ShapeDtypeStruct(x.shape, x.dtype) for x in others]
    if mixes:
        kept = [jax.ShapeDtypeStruct((4 * inner, mixes[0].shape[1]), bf16)] + kept
    return pl.pallas_call(
        functools.partial(merge_kernel, capacity, steps, part, inner // 64),
        in_specs=[SMEM, vmem, hbm, hbm] + [anywhere] * len(mixes) + [hbm] * len(others),
        out_shape=[jax.ShapeDtypeStruct((rows, inner), bf16)] + kept,
        scratch_shapes=[pltpu.VMEM((rows, inner), f32)] * 3
        + [
            pltpu.VMEM((back.shape[0] * span, capacity * inner), f32),
            pltpu.SemaphoreType.DMA((2,)),
        ]
        + [pltpu.SemaphoreType.DMA((len(sources),))] * bool(sources),
        compiler_params=pltpu.CompilerParams(vmem_limit_bytes=10 * MIB),
        cost_estimate=pl.CostEstimate(
            flops=40 * rows * inner, bytes_accessed=8 * MIB, transcendentals=4 * rows * inner
        ),
        name="merge",
    )(table, back, in_hbm(logs), in_hbm(averages), *mixes, *[in_hbm(x) for x in others])


def block_kernel(
    first, att0, att1, att2, att3, weight_ref, tokens_ref, gain_ref, gate_ref, up_ref, down_ref,
    residual_out, mine_ref, other_ref,
    residual_ref, attended_ref, scaled_ref, hidden_ref, sums_ref,
):
    rows, width = residual_ref.shape
    inner = att0.shape[1]
    half = rows // 2
    head = lax.axis_index("head")
    core = lax.rem(head, 2)
    near = pl.ds(pl.multiple_of(core * half, half), half)
    away = pl.ds(pl.multiple_of((1 - core) * half, half), half)
    for other, att in enumerate((att0, att1, att2, att3)):
        place = pl.ds(pl.multiple_of((head ^ other) * inner, inner), inner)
        attended_ref[:, place] = att[...]
    gain = gain_ref[...].reshape(1, -1)
    squares = jnp.zeros((rows, 1), f32)
    for start in range(0, width, 512):
        cols = slice(start, start + 512)
        x = tokens_ref[first : first + rows, cols].astype(f32) + dot(attended_ref[...], weight_ref[:, cols])
        residual_ref[:, cols] = x
        scaled_ref[:, cols] = (x * gain[:, cols]).astype(bf16)
        squares = squares + jnp.sum(x * x, axis=-1, keepdims=True)
    scale = lax.rsqrt(squares / width + epsilon)
    for start in range(0, gate_ref.shape[1], 256):
        cols = slice(start, start + 256)
        gate = dot(scaled_ref[...], gate_ref[:, cols]) * scale
        up = dot(scaled_ref[...], up_ref[:, cols]) * scale
        hidden_ref[:, cols] = (gate / (1.0 + jnp.exp(-gate)) * up).astype(bf16)
    residual_out[...] = residual_ref[near, :]
    for start in range(0, width, 512):
        cols = slice(start, start + 512)
        sums_ref[:, cols] = dot(hidden_ref[...], down_ref[:, cols])
    mine_ref[...] = sums_ref[near, :]
    other_ref[...] = sums_ref[away, :].astype(bf16)


def block(first, attended, weight, tokens, gain, w_gate, w_up, w_down):
    rows, inner = attended[0].shape
    width = tokens.shape[1]
    hidden = w_gate.shape[1]
    vmem = pl.BlockSpec(memory_space=pltpu.VMEM)
    half = jax.ShapeDtypeStruct((rows // 2, width), f32)
    return pl.pallas_call(
        functools.partial(block_kernel, first),
        in_specs=[vmem] * 10,
        out_specs=[vmem] * 3,
        out_shape=[half, half, jax.ShapeDtypeStruct((rows // 2, width), bf16)],
        scratch_shapes=[
            pltpu.VMEM((rows, width), f32),
            pltpu.VMEM((rows, 4 * inner), bf16),
            pltpu.VMEM((rows, width), bf16),
            pltpu.VMEM((rows, hidden), bf16),
            pltpu.VMEM((rows, width), f32),
        ],
        compiler_params=pltpu.CompilerParams(vmem_limit_bytes=20 * MIB),
        cost_estimate=pl.CostEstimate(flops=0, bytes_accessed=0, transcendentals=0),
        name="block",
    )(*attended, weight, tokens, gain, w_gate, w_up, w_down)


def finish_kernel(first, half, places, *refs):
    count = 2 * len(places)
    parts, out_ref, sems = refs[-2 - count : -2], refs[-2], refs[-1]
    core = lax.axis_index("head") % 2
    pairs = []
    for index, place in enumerate(places):
        for part, owner in ((parts[2 * index], core), (parts[2 * index + 1], 1 - core)):
            start = pl.multiple_of(first + owner * half + place, 16)
            pairs.append((part, out_ref.at[pl.ds(start, part.shape[0])]))
    for copy in start_all(pairs, sems):
        copy.wait()


def finish(first, half, pieces, rows, before=()):
    vmem = pl.BlockSpec(memory_space=pltpu.VMEM)
    hbm = pl.BlockSpec(memory_space=pltpu.HBM)
    places, parts = [], []
    for place, done in pieces:
        places.append(place)
        parts.extend([done, swap_core(done)])
    width = parts[0].shape[1]
    return pl.pallas_call(
        functools.partial(finish_kernel, first, half, places),
        in_specs=[hbm] * len(before) + [vmem] * len(parts),
        out_specs=hbm,
        out_shape=pltpu.HBM((rows, width), parts[0].dtype),
        input_output_aliases={0: 0} if before else {},
        scratch_shapes=[pltpu.SemaphoreType.DMA((len(parts),))],
        compiler_params=pltpu.CompilerParams(vmem_limit_bytes=8 * MIB),
        name="finish",
    )(*[in_hbm(x) for x in before], *parts)


def swap_core(value):
    return lax.ppermute(value, "head", [(i, i ^ 1) for i in range(4)])


def swap_chip(value):
    return lax.ppermute(value, "head", [(i, i ^ 2) for i in range(4)])


def shards(
    tokens, parents, page_request, page_fill, keys_pool, values_pool, decay_pool,
    gain_attn, w_query, w_key, w_value, w_forget, forget_bias, w_out,
    gain_ffn, w_gate, w_up, w_down,
):
    steps, rows, width = tokens.shape
    inner = w_query.shape[0]
    local_count = rows // BEAMS
    span = steps * BEAMS
    groups = lax.axis_size("group")
    capacity = (SPILL + groups - 2) // (groups - 1)
    decay = decay_pool.transpose(1, 0, 2)

    def exchange(value):
        return lax.all_to_all(value, "group", split_axis=0, concat_axis=0, tiled=True)

    ids = exchange(jnp.broadcast_to(page_request, (groups, 1, page_request.shape[0])))
    q_near, q, normed = queries_of(tokens, gain_attn, w_query)
    table, asked = ask(page_request, ids, q_near, span, capacity)
    asked_rows = exchange(asked.reshape(groups, capacity * span, inner)).reshape(asked.shape)
    asked, q = lax.optimization_barrier((asked, q))
    own = own_pages(page_request, page_fill, q, keys_pool, values_pool, decay, span)
    own, w_sent = lax.optimization_barrier((own, w_out))
    w_out_far = swap_chip(w_sent)
    asked_rows, own = lax.optimization_barrier((asked_rows, own))
    payload = hosted_pages(
        page_request, page_fill, asked_rows, keys_pool, values_pool, decay, groups, capacity, local_count
    )
    payload, normed = lax.optimization_barrier((payload, normed))
    back = exchange(payload)
    logs, averages = fresh(parents, forget_bias, normed, w_key, w_value, w_forget, q, own)
    logs, w_out_far = lax.optimization_barrier((logs, w_out_far))
    mixes = [w_out, swap_core(w_out), w_out_far, swap_core(w_out_far)]

    flat = tokens.reshape(steps * rows, width)
    each = steps // PARTS
    sums = (table, back, logs, averages, each, capacity)
    here, flat = merge(0, *sums, [flat])
    heres = [here]
    back, heres[0] = lax.optimization_barrier((back, heres[0]))
    sums = (table, back, logs, averages, each, capacity)
    here, weight, w_gate, w_up, w_down = merge(1, *sums, mixes + [w_gate, w_up, w_down])
    heres.append(here)
    fars = [swap_chip(here) for here in heres]
    fars[0], heres[1] = lax.optimization_barrier((fars[0], heres[1]))

    def block_of(index):
        here, far = heres[index], fars[index]
        gathered = [here, swap_core(here), far, swap_core(far)]
        if index:
            gathered, chip[0] = lax.optimization_barrier((gathered, chip[0]))
        first = index * here.shape[0]
        return block(first, gathered, weight, flat, gain_ffn, w_gate, w_up, w_down)

    def chip_sum(mine, other):
        return (mine + swap_core(other).astype(f32)).astype(bf16)

    chip, residual = [None] * PARTS, [None] * PARTS
    residual[0], mine, other = block_of(0)
    cuts = [0, 48, 96, 128]
    other = jnp.concatenate([swap_core(other[a:b]) for a, b in zip(cuts, cuts[1:])], axis=0)
    chip[0] = (mine + other.astype(f32)).astype(bf16)
    most = chip[0].shape[0] // 8 * 3
    chip_most, chip_rest = chip[0][:most], chip[0][most:]
    far_most, far_rest = swap_chip(chip_most), swap_chip(chip_rest)
    residual[1], mine, other = block_of(1)
    other, far_most = lax.optimization_barrier((other, far_most))
    chip[1] = chip_sum(mine, other)
    half = chip[1].shape[0]
    cut = half // 4 * 3
    far_first, far_last = swap_chip(chip[1][:cut]), swap_chip(chip[1][cut:])

    def done(residual, chip, far):
        return (residual + (chip.astype(f32) + far.astype(f32))).astype(bf16)

    pieces = [
        (0, done(residual[0][:most], chip_most, far_most)),
        (most, done(residual[0][most:], chip_rest, far_rest)),
    ]
    result = finish(0, half, pieces, steps * rows)
    pieces = [
        (0, done(residual[1][:cut], chip[1][:cut], far_first)),
        (cut, done(residual[1][cut:], chip[1][cut:], far_last)),
    ]
    result = finish(2 * half, half, pieces, steps * rows, [result])
    return result.reshape(steps, rows, width)


def solution(mesh):
    return jax.shard_map(
        shards,
        mesh=mesh,
        in_specs=(
            P(None, "group", None),
            P(None, "group"),
            P("group"),
            P("group"),
            P("group", "head", None),
            P("group", "head", None),
            P("group", "head", None),
            P(),
            P("head", None),
            P("head", None),
            P("head", None),
            P(None, "head"),
            P("head"),
            P("head", None),
            P(),
            P(None, "head"),
            P(None, "head"),
            P("head", None),
        ),
        out_specs=P(None, "group", None),
        check_vma=False,
    )
```

```python
import functools

import jax
import jax.numpy as jnp
from jax import lax
from jax.experimental import pallas as pl
from jax.experimental.pallas import tpu as pltpu
from jax.sharding import PartitionSpec as P

BEAMS = 8
OWNED_SLOTS = 32
SPILL = 16
PAGE_BLOCK = 16
PARTS = 2
MIB = 1 << 20

epsilon = 1e-05
masked_score = -1e30
f32 = jnp.float32
bf16 = jnp.bfloat16

NN = (((1,), (0,)), ((), ()))
NT = (((1,), (1,)), ((), ()))
SMEM = pl.BlockSpec(memory_space=pltpu.SMEM)


def dot(a, b, dims=NN):
    return lax.dot_general(a, b, dims, preferred_element_type=f32)


def lanes(shape):
    return lax.broadcasted_iota(jnp.int32, shape, len(shape) - 1)


def sublanes(shape):
    return lax.broadcasted_iota(jnp.int32, shape, len(shape) - 2)


def in_hbm(array):
    return pltpu.with_memory_space_constraint(array, pltpu.HBM)


def in_vmem(array):
    return pltpu.with_memory_space_constraint(array, pltpu.VMEM)


def start_all(pairs, sems):
    copies = [pltpu.make_async_copy(s, t, sems.at[i]) for i, (s, t) in enumerate(pairs)]
    for copy in copies:
        copy.start()
    return copies


def fill_table(local_count, capacity, first, ids_ref, table_ref):
    groups = ids_ref.shape[0]
    for slot in range(groups * capacity + 1):
        table_ref[slot] = -1

    def group(index, carry):
        rank = jnp.int32(0)
        for page in range(SPILL):
            local = ids_ref[index, 0, OWNED_SLOTS + page] - first
            mine = (local >= 0) & (local < local_count)

            slot = jnp.where(mine, index * capacity + rank, groups * capacity)
            table_ref[slot] = local
            rank = rank + mine.astype(jnp.int32)
        return carry

    lax.fori_loop(0, groups, group, 0, unroll=2)


def query_kernel(
    tokens_hbm, gain_ref, wq_hbm, q_ref, q_hbm, normed_hbm,
    tokens_ref, wq_ref, normed_ref, sems, out_sems,
):
    steps, rows, _ = tokens_ref.shape
    span = steps * BEAMS
    cut = rows // 2
    copies = start_all(
        [
            (tokens_hbm.at[:, :cut], tokens_ref.at[:, :cut]),
            (tokens_hbm.at[:, cut:], tokens_ref.at[:, cut:]),
            (wq_hbm, wq_ref),
        ],
        sems,
    )
    gain = gain_ref[...].reshape(1, -1)

    def pair(index, carry):
        slabs = []
        for step in range(steps):
            x = tokens_ref[step, pl.ds(pl.multiple_of(index * 16, 16), 16), :].astype(f32)
            scale = lax.rsqrt(jnp.mean(x * x, axis=-1, keepdims=True) + epsilon)
            slabs.append(x * scale * gain)
        for half in range(2):
            part = jnp.concatenate([s[half * 8 : half * 8 + 8] for s in slabs], axis=0)
            start = pl.multiple_of((index * 2 + half) * span, span)
            normed_ref[pl.ds(start, span), :] = part.astype(bf16)
        return carry

    copies[0].wait()
    lax.fori_loop(0, cut // 16, pair, 0, unroll=2)
    copies[1].wait()
    lax.fori_loop(cut // 16, rows // 16, pair, 0, unroll=2)
    leaving = start_all([(normed_ref, normed_hbm)], out_sems)
    copies[2].wait()
    query = dot(normed_ref[...], wq_ref[...], NT).astype(bf16)
    q_ref[...] = (query.astype(f32) * 0.125).astype(bf16)
    last = pltpu.make_async_copy(q_ref, q_hbm, out_sems.at[1])
    last.start()
    leaving[0].wait()
    last.wait()


def queries_of(tokens, gain, w_query):
    steps, rows, width = tokens.shape
    inner = w_query.shape[0]
    total = steps * rows
    hbm = pl.BlockSpec(memory_space=pltpu.HBM)
    vmem = pl.BlockSpec(memory_space=pltpu.VMEM)
    return pl.pallas_call(
        query_kernel,
        in_specs=[hbm, vmem, hbm],
        out_specs=[vmem, hbm, hbm],
        out_shape=[
            pltpu.VMEM((total, inner), bf16),
            pltpu.HBM((total, inner), bf16),
            pltpu.HBM((total, width), bf16),
        ],
        scratch_shapes=[
            pltpu.VMEM(tokens.shape, bf16),
            pltpu.VMEM(w_query.shape, bf16),
            pltpu.VMEM((total, width), bf16),
            pltpu.SemaphoreType.DMA((3,)),
            pltpu.SemaphoreType.DMA((2,)),
        ],
        compiler_params=pltpu.CompilerParams(vmem_limit_bytes=12 * MIB),
        cost_estimate=pl.CostEstimate(
            flops=2 * total * width * inner, bytes_accessed=6 * MIB, transcendentals=total
        ),
        name="queries",
    )(in_hbm(tokens), gain, in_hbm(w_query))


def ask_kernel(capacity, request_ref, ids_ref, q_ref, table_ref, out_ref):
    slots, span, _ = out_ref.shape
    local_count = q_ref.shape[0] // span
    first = request_ref[0] // local_count * local_count
    fill_table(local_count, capacity, first, ids_ref, table_ref)
    for slot in range(slots):
        start = jnp.maximum(table_ref[slot], 0) * span
        out_ref[slot] = q_ref[pl.ds(pl.multiple_of(start, span), span), :]


def ask(request, ids, q, span, capacity):
    slots = ids.shape[0] * capacity
    vmem = pl.BlockSpec(memory_space=pltpu.VMEM)
    return pl.pallas_call(
        functools.partial(ask_kernel, capacity),
        in_specs=[SMEM, SMEM, vmem],
        out_specs=[SMEM, vmem],
        out_shape=[
            jax.ShapeDtypeStruct((slots + 1,), jnp.int32),
            jax.ShapeDtypeStruct((slots, span, q.shape[1]), bf16),
        ],
        compiler_params=pltpu.CompilerParams(vmem_limit_bytes=8 * MIB),
        name="ask",
    )(request, ids, in_vmem(q))


def half_masks(rows):
    low = lanes((rows, 128)) < 64
    return low.astype(f32).astype(bf16), jnp.logical_not(low).astype(f32).astype(bf16)


def stacked(pair_rows, masks):
    return jnp.concatenate([pair_rows * masks[0], pair_rows * masks[1]], axis=0)


def side_by_side(values, rows):
    low = lanes((rows, 128)) < 64
    top = jnp.broadcast_to(values[:rows], (rows, 128))
    bottom = jnp.broadcast_to(values[rows:], (rows, 128))
    return jnp.where(low, top, bottom)


def absorb(state, rows, columns, top, total, numer):
    top_ref, total_ref, numer_ref = state
    old = top_ref[rows, columns]
    new = jnp.maximum(old, top)
    keep = jnp.exp(old - new)
    add = jnp.exp(top - new)
    top_ref[rows, columns] = new
    total_ref[rows, columns] = total_ref[rows, columns] * keep + total * add
    numer_ref[rows, columns] = numer_ref[rows, columns] * keep + numer * add


def history(parents_ref, q_ref, k_ref, v_ref, forget_ref, state, scores_ref, weights_ref):
    transitions, rows = parents_ref.shape
    span = (transitions + 1) * BEAMS
    pack = 128 // span
    square = (128, 128)
    diagonal = sublanes(square) == lanes(square)
    columns = []
    for step in range(transitions):
        row = parents_ref[step : step + 1, :].astype(f32)
        columns.append(
            jnp.sum(jnp.where(diagonal, jnp.broadcast_to(row, square), 0.0), axis=1, keepdims=True)
        )
    lane8 = lanes((8, 128)).astype(f32)
    masks = half_masks(128)
    low = lanes(square) < 64
    top_ref, total_ref, numer_ref = state
    groups = rows // BEAMS // pack
    pairs = q_ref.shape[1] // 128
    for group in range(groups):
        slabs = []
        for member in range(pack):
            first = (group * pack + member) * BEAMS
            slabs.append(jnp.zeros((8, 128), f32))
            for step in range(transitions):
                wanted = columns[step][first : first + 8] + float(member * span + step * 8)
                slabs.append(jnp.where(lane8 == wanted, 1.0, 0.0))
        parent = jnp.concatenate(slabs, axis=0)
        parent16 = parent.astype(bf16)
        one = diagonal.astype(f32) + parent
        two = dot(parent16, parent16)
        ancestors = one + dot(two.astype(bf16), one.astype(bf16))
        here = pl.ds(group * 128, 128)
        running = lax.dot_general(
            ancestors, forget_ref[here, :], NN,
            precision=lax.Precision.HIGHEST, preferred_element_type=f32,
        ).T
        hidden = jnp.where(ancestors > 0.5, 0.0, masked_score)
        for pair in range(pairs):
            cols = pl.ds(pair * 128, 128)
            raw = dot(stacked(q_ref[here, cols], masks), k_ref[here, cols], NT)
            for half in range(2):
                head = pair * 2 + half
                scores_ref[group * pairs + pair, half] = raw[half * 128 : half * 128 + 128] + (
                    hidden - running[head : head + 1]
                )
    for group in range(groups):
        here = pl.ds(group * 128, 128)
        for pair in range(pairs):
            cols = pl.ds(pair * 128, 128)
            tops, totals = [], []
            for half in range(2):
                scores = scores_ref[group * pairs + pair, half]
                top = jnp.broadcast_to(jnp.max(scores, axis=-1, keepdims=True), square)
                weights = jnp.exp(scores - top)
                weights_ref[group * pairs + pair, pl.ds(half * 128, 128), :] = weights.astype(bf16)
                tops.append(top)
                totals.append(jnp.broadcast_to(jnp.sum(weights, axis=-1, keepdims=True), square))
            top_ref[here, cols] = jnp.where(low, *tops)
            total_ref[here, cols] = jnp.where(low, *totals)
    for group in range(groups):
        here = pl.ds(group * 128, 128)
        for pair in range(pairs):
            cols = pl.ds(pair * 128, 128)
            numer = dot(weights_ref[group * pairs + pair], v_ref[here, cols])
            numer_ref[here, cols] = jnp.where(low, numer[:128], numer[128:])


def fresh_kernel(
    parents_ref, bias_ref, normed_hbm, wk_hbm, wv_hbm, wf_hbm, q_hbm, top_hbm, total_hbm, numer_hbm,
    logs_hbm, averages_hbm,
    normed_ref, wk_ref, wv_ref, wf_ref, q_ref, top_own, total_own, numer_own,
    k_ref, v_ref, forget_ref, top_ref, total_ref, numer_ref, scores_ref, weights_ref,
    logs_ref, averages_ref, sems, out_sems,
):
    copies = start_all(
        [
            (normed_hbm, normed_ref), (wk_hbm, wk_ref), (wv_hbm, wv_ref), (wf_hbm, wf_ref),
            (q_hbm, q_ref), (top_hbm, top_own), (total_hbm, total_own), (numer_hbm, numer_own),
        ],
        sems,
    )
    copies[0].wait()
    copies[1].wait()
    k_ref[...] = dot(normed_ref[...], wk_ref[...], NT).astype(bf16)
    copies[2].wait()
    v_ref[...] = dot(normed_ref[...], wv_ref[...], NT).astype(bf16)
    copies[3].wait()
    gate = dot(normed_ref[...], wf_ref[...], NT) + bias_ref[...]
    forget = jnp.minimum(gate, 0.0) - jnp.log1p(jnp.exp(-jnp.abs(gate)))
    forget_ref[...] = jnp.zeros_like(forget_ref)
    forget_ref[:, : forget.shape[1]] = forget
    copies[4].wait()
    state = (top_ref, total_ref, numer_ref)
    history(parents_ref, q_ref, k_ref, v_ref, forget_ref, state, scores_ref, weights_ref)
    for copy in copies[5:]:
        copy.wait()

    parts, _, part = logs_ref.shape[:3]
    span = parts * part

    def join(index, carry):
        rows = pl.ds(pl.multiple_of(index * span, span), span)
        absorb(state, rows, slice(None), top_own[rows, :], total_own[rows, :], numer_own[rows, :])
        total = total_ref[rows, :]
        logs = top_ref[rows, :] + jnp.log(total)
        averages = numer_ref[rows, :] / total
        for number in range(parts):
            logs_ref[number, index] = logs[number * part : number * part + part]
            averages_ref[number, index] = averages[number * part : number * part + part]
        return carry

    lax.fori_loop(0, logs_ref.shape[1], join, 0, unroll=2)
    for copy in start_all([(logs_ref, logs_hbm), (averages_ref, averages_hbm)], out_sems):
        copy.wait()


def fresh(parents, bias, normed, w_key, w_value, w_forget, q, own):
    rows, inner = q.shape
    span = (parents.shape[0] + 1) * BEAMS
    vmem = pl.BlockSpec(memory_space=pltpu.VMEM)
    hbm = pl.BlockSpec(memory_space=pltpu.HBM)
    big = [normed, w_key, w_value, w_forget.T, q, *own]
    wide = pltpu.VMEM((rows, inner), f32)
    out = (PARTS, rows // span, span // PARTS, inner)
    tiles = rows * inner // (128 * 128)
    return pl.pallas_call(
        fresh_kernel,
        in_specs=[vmem, vmem] + [hbm] * len(big),
        out_specs=[hbm] * 2,
        out_shape=[pltpu.HBM(out, f32)] * 2,
        scratch_shapes=[pltpu.VMEM(x.shape, x.dtype) for x in big]
        + [pltpu.VMEM((rows, inner), bf16)] * 2
        + [pltpu.VMEM((rows, 128), f32), wide, wide, wide]
        + [pltpu.VMEM((tiles, 2, 128, 128), f32), pltpu.VMEM((tiles, 256, 128), bf16)]
        + [pltpu.VMEM(out, f32)] * 2
        + [pltpu.SemaphoreType.DMA((len(big),)), pltpu.SemaphoreType.DMA((2,))],
        compiler_params=pltpu.CompilerParams(vmem_limit_bytes=24 * MIB),
        cost_estimate=pl.CostEstimate(
            flops=4 * rows * normed.shape[1] * inner, bytes_accessed=12 * MIB,
            transcendentals=8 * rows * inner,
        ),
        name="fresh",
    )(parents, bias.reshape(1, -1), *[in_hbm(x) for x in big])


def page_weights(queries, fills, keys_ref, decay_ref, scores_ref, weights_ref, tops_ref):
    span = queries[0][0].shape[0]
    masks = half_masks(span)
    lane = lanes((1, 128))
    decay = [decay_ref[head].astype(f32) for head in range(decay_ref.shape[0])]
    for page, pairs in enumerate(queries):
        valid = lane < fills[page]
        for pair, query in enumerate(pairs):
            raw = dot(stacked(query, masks), keys_ref[page, pl.ds(pair * 128, 128), :])
            for half in range(2):
                head = pair * 2 + half
                bias = jnp.where(valid, decay[head][page : page + 1], masked_score)
                scores_ref[page, pl.ds(head * span, span), :] = (
                    raw[half * span : half * span + span] + bias
                )
    for page in range(len(queries)):
        for head in range(decay_ref.shape[0]):
            rows = pl.ds(head * span, span)
            scores = scores_ref[page, rows, :]
            top = jnp.broadcast_to(jnp.max(scores, axis=-1, keepdims=True), scores.shape)
            tops_ref[page, rows, :] = top
            weights = jnp.exp(scores - top)
            weights_ref[page, rows, :] = weights.astype(bf16)
            scores_ref[page, rows, :] = jnp.broadcast_to(
                jnp.sum(weights, axis=-1, keepdims=True), scores.shape
            )


def page_sums(page, pair, span, values_ref, scores_ref, weights_ref, tops_ref):
    low = lanes((span, 128)) < 64
    first, second = pl.ds(pair * 2 * span, span), pl.ds((pair * 2 + 1) * span, span)
    numer = dot(
        weights_ref[page, pl.ds(pair * 2 * span, 2 * span), :],
        values_ref[page, pl.ds(pair * 128, 128), :],
        NT,
    )
    top = jnp.where(low, tops_ref[page, first, :], tops_ref[page, second, :])
    total = jnp.where(low, scores_ref[page, first, :], scores_ref[page, second, :])
    return top, total, jnp.where(low, numer[:span], numer[span:])


def page_scratch(pages, span, heads):
    rows = span * heads
    return [
        pltpu.VMEM((pages, rows, 128), f32),
        pltpu.VMEM((pages, rows, 128), bf16),
        pltpu.VMEM((pages, rows, 128), f32),
    ]


def own_kernel(
    request_ref, fill_ref, q_ref, keys_ref, values_ref, decay_ref,
    top_ref, total_ref, numer_ref, *scratch,
):
    state = (top_ref, total_ref, numer_ref)
    span = scratch[0].shape[1] // decay_ref.shape[0]
    local_count = q_ref.shape[0] // span
    pairs = q_ref.shape[1] // 128

    block = pl.program_id(0)

    @pl.when(block == 0)
    def _():
        top_ref[...] = jnp.full_like(top_ref, masked_score)
        total_ref[...] = jnp.zeros_like(total_ref)
        numer_ref[...] = jnp.zeros_like(numer_ref)

    places, queries, fills = [], [], []
    for page in range(PAGE_BLOCK):
        index = block * PAGE_BLOCK + page
        local = lax.rem(request_ref[index], local_count)
        rows = pl.ds(pl.multiple_of(local * span, span), span)
        places.append(rows)
        queries.append([q_ref[rows, pl.ds(pair * 128, 128)] for pair in range(pairs)])
        fills.append(fill_ref[index])
    page_weights(queries, fills, keys_ref, decay_ref, *scratch)
    for page, rows in enumerate(places):
        for pair in range(pairs):
            sums = page_sums(page, pair, span, values_ref, *scratch)
            absorb(state, rows, pl.ds(pair * 128, 128), *sums)


def page_cost(pages, keys, rows):
    inner, length = keys.shape[1:]
    return pl.CostEstimate(
        flops=pages * rows * inner * length * 8,
        bytes_accessed=pages * inner * length * 4,
        transcendentals=pages * rows * inner * length // 64,
    )


def own_pages(request, fill, q, keys, values, decay, span):
    pool = pl.BlockSpec((PAGE_BLOCK,) + keys.shape[1:], lambda i: (i, 0, 0))
    decay_spec = pl.BlockSpec((decay.shape[0], PAGE_BLOCK, decay.shape[2]), lambda i: (0, i, 0))
    rows = pl.BlockSpec(q.shape, lambda i: (0, 0))
    return pl.pallas_call(
        own_kernel,
        grid=(OWNED_SLOTS // PAGE_BLOCK,),
        in_specs=[SMEM, SMEM, rows, pool, pool, decay_spec],
        out_specs=[rows] * 3,
        out_shape=[pltpu.HBM(q.shape, f32)] * 3,
        scratch_shapes=page_scratch(PAGE_BLOCK, span, decay.shape[0]),
        compiler_params=pltpu.CompilerParams(vmem_limit_bytes=20 * MIB),
        cost_estimate=page_cost(OWNED_SLOTS, keys, 64),
        name="own_pages",
    )(request, fill, in_hbm(q), in_hbm(keys), in_hbm(values), decay)


def hosted_kernel(
    local_count, capacity, request_ref, fill_ref, q_ref, keys_ref, values_ref, decay_ref,
    out_ref, tail_ref, count_ref, *scratch,
):
    span, inner = q_ref.shape[1:]
    pairs = inner // 128
    heads = decay_ref.shape[0]
    groups = out_ref.shape[0]
    half = span // PARTS
    slot_rows = pairs * span
    out_ref[...] = jnp.zeros_like(out_ref)
    tail_ref[...] = jnp.zeros_like(tail_ref)
    for owner in range(groups):
        count_ref[owner] = 0
    places, queries, fills = [], [], []
    for page in range(SPILL):
        owner = request_ref[OWNED_SLOTS + page] // local_count
        rank = count_ref[owner]
        count_ref[owner] = rank + 1
        places.append((owner, rank))
        slot = owner * capacity + rank
        queries.append([q_ref[slot, :, pl.ds(pair * 128, 128)] for pair in range(pairs)])
        fills.append(fill_ref[OWNED_SLOTS + page])
    page_weights(queries, fills, keys_ref, decay_ref, *scratch)
    scores_ref, _, tops_ref = scratch
    lane = lanes((half, 128))
    for page, (owner, rank) in enumerate(places):
        for pair in range(pairs):
            _, total, numer = page_sums(page, pair, span, values_ref, *scratch)
            here = pl.ds(pl.multiple_of(rank * slot_rows + pair * span, span), span)
            out_ref[owner, here, :] = (numer / total).astype(bf16)
        tail = tail_ref[owner]
        base = rank * (3 * heads)
        for head in range(heads):
            rows = pl.ds(head * span, span)
            rest = tops_ref[page, rows, :] + jnp.log(scores_ref[page, rows, :])
            rest = jnp.where(lane < 64, rest[:half], rest[half:])
            for piece in range(3):
                part = rest.astype(bf16).astype(f32)
                rest = rest - part
                tail = jnp.where(lane % 64 == base + piece * heads + head, part, tail)
        tail_ref[owner] = tail
    first = capacity * slot_rows
    for owner in range(groups):
        out_ref[owner, first : first + half, :] = tail_ref[owner].astype(bf16)


def hosted_pages(request, fill, asked_rows, keys, values, decay, groups, capacity, local_count):
    count, span, inner = asked_rows.shape
    shift = OWNED_SLOTS // SPILL
    pool = pl.BlockSpec((SPILL,) + keys.shape[1:], lambda i: (shift, 0, 0))
    decay_spec = pl.BlockSpec((decay.shape[0], SPILL, decay.shape[2]), lambda i: (0, shift, 0))
    out_shape = (groups, capacity * span * inner // 128 + span // PARTS, 128)
    return pl.pallas_call(
        functools.partial(hosted_kernel, local_count, capacity),
        grid=(1,),
        in_specs=[
            SMEM, SMEM, pl.BlockSpec(asked_rows.shape, lambda i: (0, 0, 0)), pool, pool, decay_spec
        ],
        out_specs=pl.BlockSpec(out_shape, lambda i: (0, 0, 0)),
        out_shape=jax.ShapeDtypeStruct(out_shape, bf16),
        scratch_shapes=[pltpu.VMEM((groups, span // PARTS, 128), f32), pltpu.SMEM((groups,), jnp.int32)]
        + page_scratch(SPILL, span, decay.shape[0]),
        compiler_params=pltpu.CompilerParams(vmem_limit_bytes=24 * MIB),
        cost_estimate=page_cost(SPILL, keys, 64),
        name="hosted_pages",
    )(request, fill, asked_rows, in_hbm(keys), in_hbm(values), decay)


def merge_kernel(capacity, steps, part, heads, table_ref, back_ref, log_hbm, average_hbm, *refs):
    sources, targets, load_sems = [], [], None
    if len(refs) > 6:
        *refs, load_sems = refs
        count = load_sems.shape[0]
        sources, refs = refs[:count], refs[count:]
        targets, refs = refs[1:-5], (refs[0], *refs[-5:])
    out_ref, top_ref, total_ref, numer_ref, tops_ref, sems = refs
    groups = back_ref.shape[0]
    inner = heads * 64
    rows = steps * BEAMS
    span = PARTS * rows
    state = (top_ref, total_ref, numer_ref)
    copies = start_all([(log_hbm.at[part], top_ref), (average_hbm.at[part], numer_ref)], sems)
    pairs = []
    if len(sources) > 4:
        weight_ref, *targets = targets
        height = sources[0].shape[0]
        head = lax.axis_index("head")
        for other in range(4):
            place = pl.ds(pl.multiple_of((head ^ other) * height, height), height)
            pairs.append((sources[other], weight_ref.at[place]))
        sources = sources[4:]
    pairs.extend(zip(sources, targets))
    loads = start_all(pairs, load_sems)
    total_ref[...] = jnp.ones_like(total_ref)
    slot_rows = (inner // 128) * span
    first = capacity * slot_rows
    tails = jnp.concatenate(
        [back_ref[owner, first : first + rows, :] for owner in range(groups)], axis=0
    )
    source, target = sublanes((128, inner)), lanes((128, inner)) // 64
    for rank in range(capacity):
        hit = source < 0
        for piece in range(3):
            hit = hit | (source == target + part * 64 + (rank * 3 + piece) * heads)
        tops_ref[:, rank * inner : rank * inner + inner] = dot(tails, hit.astype(f32).astype(bf16))
    for copy in copies:
        copy.wait()
    for owner in range(groups):
        for rank in range(capacity):
            local = table_ref[owner * capacity + rank]
            bias = jnp.where(local >= 0, 0.0, masked_score)
            top = tops_ref[owner * rows : owner * rows + rows, rank * inner : rank * inner + inner]
            starts = [rank * slot_rows + pair * span + part * rows for pair in range(inner // 128)]
            average = jnp.concatenate(
                [back_ref[owner, start : start + rows, :].astype(f32) for start in starts], axis=1
            )
            here = pl.ds(pl.multiple_of(jnp.maximum(local, 0) * rows, rows), rows)
            absorb(state, here, slice(None), top + bias, 1.0, average)
    for index in range(top_ref.shape[0] // (2 * rows)):
        parts = []
        for half in range(2):
            here = slice((index * 2 + half) * rows, (index * 2 + half + 1) * rows)
            parts.append(numer_ref[here, :] / total_ref[here, :])
        for step in range(steps):
            both = jnp.concatenate([p[step * 8 : step * 8 + 8] for p in parts], axis=0)
            start = step * (top_ref.shape[0] // steps) + index * 16
            out_ref[start : start + 16, :] = both.astype(bf16)
    for copy in loads:
        copy.wait()


def merge(part, table, back, logs, averages, steps, capacity, sources):
    _, requests, span, inner = logs.shape
    rows = requests * span
    logs, averages = (x.reshape(PARTS, rows, inner) for x in (logs, averages))
    vmem = pl.BlockSpec(memory_space=pltpu.VMEM)
    hbm = pl.BlockSpec(memory_space=pltpu.HBM)
    anywhere = pl.BlockSpec(memory_space=pl.ANY)
    mixes = sources[:4] if len(sources) > 4 else []
    others = sources[len(mixes) :]
    kept = [jax.ShapeDtypeStruct(x.shape, x.dtype) for x in others]
    if mixes:
        kept = [jax.ShapeDtypeStruct((4 * inner, mixes[0].shape[1]), bf16)] + kept
    return pl.pallas_call(
        functools.partial(merge_kernel, capacity, steps, part, inner // 64),
        in_specs=[SMEM, vmem, hbm, hbm] + [anywhere] * len(mixes) + [hbm] * len(others),
        out_shape=[jax.ShapeDtypeStruct((rows, inner), bf16)] + kept,
        scratch_shapes=[pltpu.VMEM((rows, inner), f32)] * 3
        + [
            pltpu.VMEM((back.shape[0] * span, capacity * inner), f32),
            pltpu.SemaphoreType.DMA((2,)),
        ]
        + [pltpu.SemaphoreType.DMA((len(sources),))] * bool(sources),
        compiler_params=pltpu.CompilerParams(vmem_limit_bytes=10 * MIB),
        cost_estimate=pl.CostEstimate(
            flops=40 * rows * inner, bytes_accessed=8 * MIB, transcendentals=4 * rows * inner
        ),
        name="merge",
    )(table, back, in_hbm(logs), in_hbm(averages), *mixes, *[in_hbm(x) for x in others])


def block_kernel(
    first, att0, att1, att2, att3, weight_ref, tokens_ref, gain_ref, gate_ref, up_ref, down_ref,
    residual_out, mine_ref, other_ref,
    residual_ref, attended_ref, scaled_ref, hidden_ref, sums_ref,
):
    rows, width = residual_ref.shape
    inner = att0.shape[1]
    half = rows // 2
    head = lax.axis_index("head")
    core = lax.rem(head, 2)
    near = pl.ds(pl.multiple_of(core * half, half), half)
    away = pl.ds(pl.multiple_of((1 - core) * half, half), half)
    for other, att in enumerate((att0, att1, att2, att3)):
        place = pl.ds(pl.multiple_of((head ^ other) * inner, inner), inner)
        attended_ref[:, place] = att[...]
    gain = gain_ref[...].reshape(1, -1)
    squares = jnp.zeros((rows, 1), f32)
    for start in range(0, width, 512):
        cols = slice(start, start + 512)
        x = tokens_ref[first : first + rows, cols].astype(f32) + dot(attended_ref[...], weight_ref[:, cols])
        residual_ref[:, cols] = x
        scaled_ref[:, cols] = (x * gain[:, cols]).astype(bf16)
        squares = squares + jnp.sum(x * x, axis=-1, keepdims=True)
    scale = lax.rsqrt(squares / width + epsilon)
    for start in range(0, gate_ref.shape[1], 256):
        cols = slice(start, start + 256)
        gate = dot(scaled_ref[...], gate_ref[:, cols]) * scale
        up = dot(scaled_ref[...], up_ref[:, cols]) * scale
        hidden_ref[:, cols] = (gate / (1.0 + jnp.exp(-gate)) * up).astype(bf16)
    residual_out[...] = residual_ref[near, :]
    for start in range(0, width, 512):
        cols = slice(start, start + 512)
        sums_ref[:, cols] = dot(hidden_ref[...], down_ref[:, cols])
    mine_ref[...] = sums_ref[near, :]
    other_ref[...] = sums_ref[away, :].astype(bf16)


def block(first, attended, weight, tokens, gain, w_gate, w_up, w_down):
    rows, inner = attended[0].shape
    width = tokens.shape[1]
    hidden = w_gate.shape[1]
    vmem = pl.BlockSpec(memory_space=pltpu.VMEM)
    half = jax.ShapeDtypeStruct((rows // 2, width), f32)
    return pl.pallas_call(
        functools.partial(block_kernel, first),
        in_specs=[vmem] * 10,
        out_specs=[vmem] * 3,
        out_shape=[half, half, jax.ShapeDtypeStruct((rows // 2, width), bf16)],
        scratch_shapes=[
            pltpu.VMEM((rows, width), f32),
            pltpu.VMEM((rows, 4 * inner), bf16),
            pltpu.VMEM((rows, width), bf16),
            pltpu.VMEM((rows, hidden), bf16),
            pltpu.VMEM((rows, width), f32),
        ],
        compiler_params=pltpu.CompilerParams(vmem_limit_bytes=20 * MIB),
        cost_estimate=pl.CostEstimate(flops=0, bytes_accessed=0, transcendentals=0),
        name="block",
    )(*attended, weight, tokens, gain, w_gate, w_up, w_down)


def finish_kernel(first, half, places, *refs):
    count = 2 * len(places)
    parts, out_ref, sems = refs[-2 - count : -2], refs[-2], refs[-1]
    core = lax.axis_index("head") % 2
    pairs = []
    for index, place in enumerate(places):
        for part, owner in ((parts[2 * index], core), (parts[2 * index + 1], 1 - core)):
            start = pl.multiple_of(first + owner * half + place, 16)
            pairs.append((part, out_ref.at[pl.ds(start, part.shape[0])]))
    for copy in start_all(pairs, sems):
        copy.wait()


def finish(first, half, pieces, rows, before=()):
    vmem = pl.BlockSpec(memory_space=pltpu.VMEM)
    hbm = pl.BlockSpec(memory_space=pltpu.HBM)
    places, parts = [], []
    for place, done in pieces:
        places.append(place)
        parts.extend([done, swap_core(done)])
    width = parts[0].shape[1]
    return pl.pallas_call(
        functools.partial(finish_kernel, first, half, places),
        in_specs=[hbm] * len(before) + [vmem] * len(parts),
        out_specs=hbm,
        out_shape=pltpu.HBM((rows, width), parts[0].dtype),
        input_output_aliases={0: 0} if before else {},
        scratch_shapes=[pltpu.SemaphoreType.DMA((len(parts),))],
        compiler_params=pltpu.CompilerParams(vmem_limit_bytes=8 * MIB),
        name="finish",
    )(*[in_hbm(x) for x in before], *parts)


def swap_core(value):
    return lax.ppermute(value, "head", [(i, i ^ 1) for i in range(4)])


def swap_chip(value):
    return lax.ppermute(value, "head", [(i, i ^ 2) for i in range(4)])


def shards(
    tokens, parents, page_request, page_fill, keys_pool, values_pool, decay_pool,
    gain_attn, w_query, w_key, w_value, w_forget, forget_bias, w_out,
    gain_ffn, w_gate, w_up, w_down,
):
    steps, rows, width = tokens.shape
    inner = w_query.shape[0]
    local_count = rows // BEAMS
    span = steps * BEAMS
    groups = lax.axis_size("group")
    capacity = (SPILL + groups - 2) // (groups - 1)
    decay = decay_pool.transpose(1, 0, 2)

    def exchange(value):
        return lax.all_to_all(value, "group", split_axis=0, concat_axis=0, tiled=True)

    ids = exchange(jnp.broadcast_to(page_request, (groups, 1, page_request.shape[0])))
    q_near, q, normed = queries_of(tokens, gain_attn, w_query)
    table, asked = ask(page_request, ids, q_near, span, capacity)
    asked_rows = exchange(asked.reshape(groups, capacity * span, inner)).reshape(asked.shape)
    asked, q = lax.optimization_barrier((asked, q))
    own = own_pages(page_request, page_fill, q, keys_pool, values_pool, decay, span)
    own, w_sent = lax.optimization_barrier((own, w_out))
    w_out_far = swap_chip(w_sent)
    asked_rows, own = lax.optimization_barrier((asked_rows, own))
    payload = hosted_pages(
        page_request, page_fill, asked_rows, keys_pool, values_pool, decay, groups, capacity, local_count
    )
    payload, normed = lax.optimization_barrier((payload, normed))
    back = exchange(payload)
    logs, averages = fresh(parents, forget_bias, normed, w_key, w_value, w_forget, q, own)
    logs, w_out_far = lax.optimization_barrier((logs, w_out_far))
    mixes = [w_out, swap_core(w_out), w_out_far, swap_core(w_out_far)]

    flat = tokens.reshape(steps * rows, width)
    each = steps // PARTS
    sums = (table, back, logs, averages, each, capacity)
    here, flat, w_down = merge(0, *sums, [flat, w_down])
    heres = [here]
    back, heres[0] = lax.optimization_barrier((back, heres[0]))
    sums = (table, back, logs, averages, each, capacity)
    here, weight, w_gate, w_up = merge(1, *sums, mixes + [w_gate, w_up])
    heres.append(here)
    fars = [swap_chip(here) for here in heres]
    fars[0], heres[1] = lax.optimization_barrier((fars[0], heres[1]))

    def block_of(index):
        here, far = heres[index], fars[index]
        gathered = [here, swap_core(here), far, swap_core(far)]
        if index:
            gathered, chip[0] = lax.optimization_barrier((gathered, chip[0]))
        first = index * here.shape[0]
        return block(first, gathered, weight, flat, gain_ffn, w_gate, w_up, w_down)

    def chip_sum(mine, other):
        return (mine + swap_core(other).astype(f32)).astype(bf16)

    chip, residual = [None] * PARTS, [None] * PARTS
    residual[0], mine, other = block_of(0)
    cuts = [0, 48, 96, 128]
    other = jnp.concatenate([swap_core(other[a:b]) for a, b in zip(cuts, cuts[1:])], axis=0)
    chip[0] = (mine + other.astype(f32)).astype(bf16)
    most = chip[0].shape[0] // 8 * 3
    chip_most, chip_rest = chip[0][:most], chip[0][most:]
    far_most, far_rest = swap_chip(chip_most), swap_chip(chip_rest)
    residual[1], mine, other = block_of(1)
    other, far_most = lax.optimization_barrier((other, far_most))
    chip[1] = chip_sum(mine, other)
    half = chip[1].shape[0]
    cut = half // 4 * 3
    far_first, far_last = swap_chip(chip[1][:cut]), swap_chip(chip[1][cut:])

    def done(residual, chip, far):
        return (residual + (chip.astype(f32) + far.astype(f32))).astype(bf16)

    pieces = [
        (0, done(residual[0][:most], chip_most, far_most)),
        (most, done(residual[0][most:], chip_rest, far_rest)),
    ]
    result = finish(0, half, pieces, steps * rows)
    pieces = [
        (0, done(residual[1][:cut], chip[1][:cut], far_first)),
        (cut, done(residual[1][cut:], chip[1][cut:], far_last)),
    ]
    result = finish(2 * half, half, pieces, steps * rows, [result])
    return result.reshape(steps, rows, width)


def solution(mesh):
    return jax.shard_map(
        shards,
        mesh=mesh,
        in_specs=(
            P(None, "group", None),
            P(None, "group"),
            P("group"),
            P("group"),
            P("group", "head", None),
            P("group", "head", None),
            P("group", "head", None),
            P(),
            P("head", None),
            P("head", None),
            P("head", None),
            P(None, "head"),
            P("head"),
            P("head", None),
            P(),
            P(None, "head"),
            P(None, "head"),
            P("head", None),
        ),
        out_specs=P(None, "group", None),
        check_vma=False,
    )
```
